32 devices in a mesh: rep: 8 (over y, x, core), grp: 4 (over z).
Axes of the slice: x: 2, y: 2, z: 4, core: 2. Of those that a mesh axis runs over, the one named last changes fastest.
Arguments:
- tokens: bfloat16 [4096, 1536], P(('rep', 'grp')), may hold values from -6 to 6
- attn_gain: bfloat16 [1536], P('grp'), may hold values from 0.5 to 1.5
- query_key_value_weight: bfloat16 [1536, 2560], P('grp'), may hold values from -0.15625 to 0.15625
- attn_proj: bfloat16 [1536, 1536], P('grp'), may hold values from -1.25 to 1.25
- mlp_gain: bfloat16 [1536], P('grp'), may hold values from 0.5 to 1.5
- w_router: bfloat16 [1536, 16], P('grp'), may hold values from -0.078125 to 0.078125
- w_gate_up: bfloat16 [1536, 16, 1024], P('grp'), may hold values from -0.15625 to 0.15625
- w_down: bfloat16 [1536, 16, 512], P('grp'), may hold values from -1 to 1
- prefix_len: int32 [32], P(('rep', 'grp')), may hold values from 0 to 128
- expert_ids: int32 [4096, 8], P(('rep', 'grp')), may hold values from 0 to 15, all different within a row
- priority: int32 [32, 1024], P(('rep', 'grp')), may hold values from 0 to 1023, each once within a row
- cotangent: bfloat16 [4096, 1536], P(('rep', 'grp')), may hold values from -6 to 6
Outputs:
- output: bfloat16 [4096, 1536], P(('rep', 'grp'))
- grad_tokens: float32 [4096, 1536], P(('rep', 'grp'))
- grad_attn_gain: float32 [1536], P('grp')
- grad_w_qkv: float32 [1536, 2560], P('grp')
- grad_attn_proj: float32 [1536, 1536], P('grp')
- grad_mlp_gain: float32 [1536], P('grp')
- grad_w_router: float32 [1536, 16], P('grp')
- grad_w_gate_up: float32 [1536, 16, 1024], P('grp')
- grad_w_down: float32 [1536, 16, 512], P('grp')
The draws below stay inside these ranges and needn't reach their ends.
Inputs may be any that keep to these rules, and one draw needn't show every extreme that they name: `prefix_len`: positions below a sequence's prefix length attend to one another in both directions. `expert_ids`: the 8 experts of a token are different. `priority`: each row holds every number of 0 to 1023 once.
All inputs are finite; a program needn't handle non-finite values.
Results may differ from the reference program's by a relative error of at most 0.015.
Values may be sent and summed in bfloat16 or wider, within the bound.
A program may use at most 576 MiB of HBM per device.

```python
import jax
import jax.numpy as jnp
from jax import lax

MODEL_WIDTH = 1536
QUERY_HEADS = 24
KEY_VALUE_HEADS = 8
HEAD_WIDTH = 64
HID = 512
TOPK = 8
EXPERTS = 16
TOK_DEV = 128
SEQ = 128
NSEQ = 32
TOKENS = 4096
CAP = 72


def plant(array, stream_key, least, top_value):
    shape = array.shape
    place = [jax.random.randint(jax.random.fold_in(stream_key, axis), (), 0, shape[axis]) for axis in range(len(shape))]
    array = array.at[tuple(place)].set(least)
    longest = shape.index(max(shape))
    place[longest] = (place[longest] + 1) % shape[longest]
    return array.at[tuple(place)].set(top_value)


def levels(rng, dims, split, smallest, high):
    factor_of, own = 1.0, jax.random.fold_in(rng, 6)
    for dim, parts in split:
        draws = jnp.exp(jax.random.uniform(jax.random.fold_in(own, dim), (parts,), jnp.float32, smallest / len(split), high / len(split)))
        factor_of = factor_of * jnp.repeat(draws, dims[dim] // parts).reshape([-1 if axis == dim else 1 for axis in range(len(dims))])
    return factor_of


def picks_of(stream_key, rows, number_of, top, lift):
    sequence = jax.random.permutation(jax.random.fold_in(stream_key, 1), number_of)
    boost = sequence
    for power in range(3):
        boost = boost * boost // number_of
    boost = boost * lift // number_of
    chance = jax.random.randint(jax.random.fold_in(stream_key, 2), (rows, number_of), 0, 4096) + boost
    fixed_rows = jax.random.permutation(jax.random.fold_in(stream_key, 3), rows)[jnp.arange(number_of) % rows]
    chance = jnp.where(jnp.arange(rows)[:, None] == fixed_rows[None, :], 1 << 14, chance)
    merit = chance * number_of + jnp.arange(number_of)
    return lax.top_k(merit.astype(jnp.int32), top)[1].astype(jnp.int32)


def noise(own_key, shape, spread, most, pieces=(), kind=jnp.bfloat16):
    array = spread * jax.random.normal(own_key, shape, jnp.float32)
    if pieces:
        array = array * levels(own_key, shape, pieces, -0.22, 0.18)
    return jnp.clip(array, -most, most).astype(kind)


def setup_inputs(seed: int = 0) -> dict:
    streams_of = jax.random.split(jax.random.key(seed), 13)
    tokens = noise(streams_of[0], (TOKENS, MODEL_WIDTH), 1.0, 6.0, ((0, 32),))
    attn_gain = jnp.clip(1.0 + 0.1 * jax.random.normal(streams_of[1], (MODEL_WIDTH,), jnp.float32), 0.5, 1.5).astype(jnp.bfloat16)
    query_key_value_weight = noise(streams_of[2], (MODEL_WIDTH, (QUERY_HEADS + 2 * KEY_VALUE_HEADS) * HEAD_WIDTH), MODEL_WIDTH ** -0.5, 0.15625, ((0, 4),))
    attn_proj = noise(streams_of[3], (QUERY_HEADS * HEAD_WIDTH, MODEL_WIDTH), (max(QUERY_HEADS * HEAD_WIDTH // 64, 1)) ** -0.5, 1.25, ((0, 4),))
    mlp_gain = jnp.clip(1.0 + 0.1 * jax.random.normal(streams_of[4], (MODEL_WIDTH,), jnp.float32), 0.5, 1.5).astype(jnp.bfloat16)
    w_router = noise(streams_of[5], (MODEL_WIDTH, EXPERTS), (4 * MODEL_WIDTH) ** -0.5, 0.078125, ((0, 4),))
    w_gate_up = noise(streams_of[6], (MODEL_WIDTH, EXPERTS, 2 * HID), MODEL_WIDTH ** -0.5, 0.15625, ((0, 4),))
    w_down = noise(streams_of[7], (MODEL_WIDTH, EXPERTS, HID), (max(HID // 16, 1)) ** -0.5, 1.0, ((0, 4),))
    prefix_len = plant(jax.random.randint(streams_of[8], (NSEQ,), 0, SEQ + 1), jax.random.fold_in(streams_of[8], 1), 0, SEQ).astype(jnp.int32)
    expert_ids = picks_of(streams_of[9], TOKENS, EXPERTS, TOPK, 4096)
    priority = jax.vmap(lambda own: jax.random.permutation(own, TOK_DEV * TOPK))(jax.random.split(streams_of[10], NSEQ)).reshape((NSEQ, TOK_DEV * TOPK)).astype(jnp.int32)
    cotangent = noise(streams_of[11], (TOKENS, MODEL_WIDTH), 1.0, 6.0, ((0, 32),))
    return dict(tokens=tokens, attn_gain=attn_gain, query_key_value_weight=query_key_value_weight, attn_proj=attn_proj, mlp_gain=mlp_gain, w_router=w_router, w_gate_up=w_gate_up, w_down=w_down, prefix_len=prefix_len, expert_ids=expert_ids, priority=priority, cotangent=cotangent)


EPS = 1e-05
HIGH = lax.Precision.HIGHEST

@jax.custom_vjp
def lower_precision(v):
    return lax.optimization_barrier(v.astype(jnp.bfloat16)).astype(jnp.float32)

@jax.custom_vjp
def low_back(v):
    return v

def low_keep(v):
    return (lower_precision(v), None)

def low_pass(kept, grad):
    return (grad,)

def back_keep(v):
    return (v, None)

def back_low(kept, grad):
    return (lower_precision(grad),)
lower_precision.defvjp(low_keep, low_pass)
low_back.defvjp(back_keep, back_low)

def rope_tables(sequence_length, head_size):
    half_width = head_size // 2
    position = jnp.arange(sequence_length, dtype=jnp.float32)[:, None]
    inverse_freq = 10000.0 ** (-jnp.arange(half_width, dtype=jnp.float32) * 2.0 / head_size)
    angles = position * inverse_freq[None, :]
    return (jnp.cos(angles), jnp.sin(angles))

def apply_rotary(values_in, cosine_table, sine_table):
    half_width = values_in.shape[-1] // 2
    front_half = values_in[..., :half_width]
    back_half = values_in[..., half_width:]
    cos_rows = cosine_table[:, None, :]
    sin_rows = sine_table[:, None, :]
    return jnp.concatenate([front_half * cos_rows - back_half * sin_rows, back_half * cos_rows + front_half * sin_rows], axis=-1)

def slot_plan(expert_ids, priority, experts, capacity):
    sequence_length, top_count = expert_ids.shape
    pair_count = sequence_length * top_count
    flat_ids = expert_ids.reshape(pair_count).astype(jnp.int32)
    numbers = jnp.arange(pair_count, dtype=jnp.int32)
    ordering = jnp.zeros((pair_count,), jnp.int32).at[priority.reshape(pair_count).astype(jnp.int32)].set(numbers)
    sorted_ids = flat_ids[ordering]
    one_hot = (sorted_ids[:, None] == jnp.arange(experts, dtype=jnp.int32)[None, :]).astype(jnp.int32)
    rank_rows = lax.optimization_barrier(jnp.sum((jnp.cumsum(one_hot, axis=0) - 1) * one_hot, axis=1)).astype(jnp.int32)
    slot_index = jnp.zeros((pair_count,), jnp.int32).at[ordering].set(rank_rows)
    target = jnp.where(slot_index < capacity, flat_ids * capacity + slot_index, experts * capacity).astype(jnp.int32)
    source_row = jnp.full((experts * capacity + 1,), sequence_length, jnp.int32).at[target].set((numbers // top_count).astype(jnp.int32))
    return (target, source_row[:experts * capacity])

def block_forward(tokens_f, gain_one, qkv_full, proj_full, gain_two, router_full, gate_up_full, down_full, prefix_value, expert_ids, priority):
    sequence_length = tokens_f.shape[0]
    width = tokens_f.shape[1]
    inverse_one = lax.rsqrt(lax.optimization_barrier(jnp.mean(tokens_f * tokens_f, axis=1, keepdims=True)) + EPS)
    act_one = lower_precision(tokens_f * inverse_one * gain_one)
    projected_rows = low_back(jnp.dot(act_one, qkv_full, precision=HIGH))
    query_feature_width = QUERY_HEADS * HEAD_WIDTH
    key_feature_width = KEY_VALUE_HEADS * HEAD_WIDTH
    heads_per_group = QUERY_HEADS // KEY_VALUE_HEADS
    cosine_table, sine_table = rope_tables(sequence_length, HEAD_WIDTH)
    query_rows = lower_precision(apply_rotary(projected_rows[:, :query_feature_width].reshape(sequence_length, QUERY_HEADS, HEAD_WIDTH), cosine_table, sine_table)).reshape(sequence_length, KEY_VALUE_HEADS, heads_per_group, HEAD_WIDTH)
    key_matrix = lower_precision(apply_rotary(projected_rows[:, query_feature_width:query_feature_width + key_feature_width].reshape(sequence_length, KEY_VALUE_HEADS, HEAD_WIDTH), cosine_table, sine_table))
    value_matrix = lower_precision(projected_rows[:, query_feature_width + key_feature_width:].reshape(sequence_length, KEY_VALUE_HEADS, HEAD_WIDTH))
    score_scale = HEAD_WIDTH ** (-0.5)
    row_pos = jnp.arange(sequence_length)[:, None]
    col_pos = jnp.arange(sequence_length)[None, :]
    allowed = (col_pos <= row_pos) | (col_pos < prefix_value)
    scores = low_back(jnp.einsum('shgd,thd->hgst', query_rows, key_matrix, precision=HIGH) * score_scale)
    scores = jnp.where(allowed, scores, -1e+30)
    exps_row = jnp.exp(scores - lax.optimization_barrier(jnp.max(scores, axis=-1, keepdims=True)))
    attn_probs = exps_row / lax.optimization_barrier(jnp.sum(exps_row, axis=-1, keepdims=True))
    attended = jnp.einsum('hgst,thd->shgd', lower_precision(attn_probs), value_matrix, precision=HIGH).reshape(sequence_length, query_feature_width)
    attended = lower_precision(low_back(attended))
    residual = tokens_f + low_back(jnp.dot(attended, proj_full, precision=HIGH))
    inverse_two = lax.rsqrt(lax.optimization_barrier(jnp.mean(residual * residual, axis=1, keepdims=True)) + EPS)
    act_two = lower_precision(residual * inverse_two * gain_two)
    logits = low_back(jnp.dot(act_two, router_full, precision=HIGH))
    choose = (expert_ids[:, :, None] == jnp.arange(EXPERTS, dtype=jnp.int32)[None, None, :]).astype(jnp.float32)
    chosen = lax.optimization_barrier(jnp.sum(choose * logits[:, None, :], axis=2))
    gate_exp = jnp.exp(chosen - lax.optimization_barrier(jnp.max(chosen, axis=1, keepdims=True)))
    gates = gate_exp / lax.optimization_barrier(jnp.sum(gate_exp, axis=1, keepdims=True))
    target, source_row = slot_plan(expert_ids, priority, EXPERTS, CAP)
    padded = jnp.concatenate([act_two, jnp.zeros((1, width), jnp.float32)], axis=0)
    slots_in = padded[source_row].reshape(EXPERTS, CAP, width)
    gate_up = low_back(jnp.einsum('ecd,deh->ech', slots_in, gate_up_full, precision=HIGH))
    gate_part = gate_up[..., :HID]
    up_part = gate_up[..., HID:]
    hidden_low = lower_precision(jax.nn.silu(gate_part) * up_part)
    expert_out = low_back(jnp.einsum('ech,deh->ecd', hidden_low, down_full, precision=HIGH))
    out_pad = jnp.concatenate([expert_out.reshape(EXPERTS * CAP, width), jnp.zeros((1, width), jnp.float32)], axis=0)
    picked = out_pad[target].reshape(sequence_length, TOPK, width)
    return residual + lax.optimization_barrier(jnp.sum(gates[:, :, None] * picked, axis=1))

def reference(tokens, attn_gain, query_key_value_weight, attn_proj, mlp_gain, w_router, w_gate_up, w_down, prefix_len, expert_ids, priority, cotangent):
    tokens_seq = tokens.astype(jnp.float32).reshape(NSEQ, SEQ, MODEL_WIDTH)
    cot_seq = cotangent.astype(jnp.float32).reshape(NSEQ, SEQ, MODEL_WIDTH)
    ids_seq = expert_ids.reshape(NSEQ, SEQ, TOPK)
    params = (attn_gain.astype(jnp.float32), query_key_value_weight.astype(jnp.float32), attn_proj.astype(jnp.float32), mlp_gain.astype(jnp.float32), w_router.astype(jnp.float32), w_gate_up.astype(jnp.float32), w_down.astype(jnp.float32))

    def step(summed, item):
        tokens_one, cot_one, prefix_one, ids_one, priority_one = item

        def forward_one(tokens_f, gain_one, qkv_full, proj_full, gain_two, router_full, gate_up_full, down_full):
            return block_forward(tokens_f, gain_one, qkv_full, proj_full, gain_two, router_full, gate_up_full, down_full, prefix_one, ids_one, priority_one)
        result, pull_back = jax.vjp(forward_one, tokens_one, *params)
        grads = pull_back(cot_one)
        updated = tuple((old + new for old, new in zip(summed, grads[1:])))
        return (updated, (result, grads[0]))
    initial = tuple((jnp.zeros(p_arr.shape, jnp.float32) for p_arr in params))
    summed, (results, grad_rows) = lax.scan(step, initial, (tokens_seq, cot_seq, prefix_len, ids_seq, priority))
    output = results.reshape(NSEQ * SEQ, MODEL_WIDTH).astype(jnp.bfloat16)
    grad_tokens = grad_rows.reshape(NSEQ * SEQ, MODEL_WIDTH)
    return (output, grad_tokens, summed[0], summed[1], summed[2], summed[3], summed[4], summed[5], summed[6])
```

```python
import jax
import jax.numpy as jnp
from jax import lax
from jax.sharding import PartitionSpec as P

QUERY_HEADS = 24
KEY_VALUE_HEADS = 8
HEAD_WIDTH = 64
HID = 512
EXPERTS = 16
CAP = 72
EPS = 1e-05
BF = jnp.bfloat16
F32 = jnp.float32
QPK = QUERY_HEADS // KEY_VALUE_HEADS
BIG = 1 << 20


def dot(a, b):
    return jnp.dot(a, b, preferred_element_type=F32)


def rope_tables(length):
    half = HEAD_WIDTH // 2
    position = jnp.arange(length, dtype=F32)[:, None]
    inverse_freq = 10000.0 ** (-jnp.arange(half, dtype=F32) * 2.0 / HEAD_WIDTH)
    angles = position * inverse_freq[None, :]
    return jnp.cos(angles), jnp.sin(angles)


def rotate(v, cos, sin):
    half = HEAD_WIDTH // 2
    a, b = v[..., :half], v[..., half:]
    return jnp.concatenate([a * cos - b * sin, b * cos + a * sin], axis=-1)


def routing(expert_ids, priority, logits):
    seq, top = expert_ids.shape
    choose = expert_ids[:, :, None] == jnp.arange(EXPERTS, dtype=jnp.int32)[None, None, :]
    chosen = jnp.any(choose, axis=1)
    rank_of = jnp.sum(jnp.where(choose, priority.reshape(seq, top)[:, :, None], 0), axis=1)
    rank_of = jnp.where(chosen, rank_of, BIG)
    slot = jnp.sum((rank_of[None, :, :] < rank_of[:, None, :]).astype(jnp.int32), axis=1)
    kept = chosen & (slot < CAP)
    top_logit = jnp.max(jnp.where(chosen, logits, -jnp.inf), axis=1, keepdims=True)
    gate_exp = jnp.where(chosen, jnp.exp(jnp.where(chosen, logits - top_logit, 0.0)), 0.0)
    gates = gate_exp / jnp.sum(gate_exp, axis=1, keepdims=True)
    return gates, kept


def shards(
    reps,
    grps,
    tokens,
    attn_gain,
    query_key_value_weight,
    attn_proj,
    mlp_gain,
    w_router,
    w_gate_up,
    w_down,
    prefix_len,
    expert_ids,
    priority,
    cotangent,
):
    seq, width = tokens.shape
    own = width // grps
    local_experts = EXPERTS // grps
    heads = KEY_VALUE_HEADS
    groups = None if reps == heads else [list(range(i, i + heads)) for i in range(0, reps, heads)]
    rep, grp = lax.axis_index("rep"), lax.axis_index("grp")
    head = lax.rem(rep, heads)
    qw, hw = QPK * HEAD_WIDTH, HEAD_WIDTH
    q_all = QUERY_HEADS * HEAD_WIDTH

    small = jnp.concatenate([attn_gain[:, None], mlp_gain[:, None], w_router], axis=1)
    small = lax.all_gather(small, "grp", axis=0, tiled=True)
    gain_one, gain_two = small[:, 0].astype(F32)[None, :], small[:, 1].astype(F32)[None, :]
    router = small[:, 2:]
    qkv_cols = jnp.concatenate(
        [
            lax.dynamic_slice_in_dim(query_key_value_weight, head * qw, qw, 1),
            lax.dynamic_slice_in_dim(query_key_value_weight, q_all + head * hw, hw, 1),
            lax.dynamic_slice_in_dim(query_key_value_weight, q_all + heads * hw + head * hw, hw, 1),
        ],
        axis=1,
    )
    qkv_head = lax.all_gather(qkv_cols, "grp", axis=0, tiled=True)
    row = head * qw + jnp.arange(qw)
    mine = (row // own) == grp
    proj_rows = jnp.where(mine[:, None], jnp.take(attn_proj, jnp.where(mine, row - grp * own, 0), axis=0), 0)
    proj_head = lax.psum(proj_rows, "grp")

    piece = own // reps
    gu_piece = lax.dynamic_slice_in_dim(w_gate_up, rep * piece, piece, 0)
    dn_piece = lax.dynamic_slice_in_dim(w_down, rep * piece, piece, 0)
    both = jnp.concatenate([gu_piece, dn_piece], axis=2)
    both = both.reshape(piece, grps, local_experts, 3 * HID).transpose(1, 2, 0, 3)
    both = lax.all_to_all(both, "grp", 0, 0, tiled=True)
    both = lax.all_gather(both, "rep", axis=0, tiled=False)
    both = both.transpose(2, 1, 0, 3, 4).reshape(local_experts, width, 3 * HID)
    wgu, wdn = both[:, :, : 2 * HID], both[:, :, 2 * HID :]

    tokens_f = tokens.astype(F32)
    inverse_one = lax.rsqrt(jnp.mean(tokens_f * tokens_f, axis=1, keepdims=True) + EPS)
    normed_one = tokens_f * inverse_one
    act_one = (normed_one * gain_one).astype(BF)
    act_plane = lax.all_gather(act_one, "rep", axis=0, tiled=True, axis_index_groups=groups)
    prefix_plane = lax.all_gather(prefix_len, "rep", axis=0, tiled=True, axis_index_groups=groups)
    cos, sin = rope_tables(seq)
    projected = dot(act_plane, qkv_head).reshape(heads, seq, QPK + 2, HEAD_WIDTH)
    cos_b, sin_b = cos[None, :, None, :], sin[None, :, None, :]
    turned = rotate(projected[:, :, : QPK + 1], cos_b, sin_b).astype(BF)
    query = turned[:, :, :QPK]
    key = turned[:, :, QPK]
    value = projected[:, :, QPK + 1].astype(BF)
    scale = HEAD_WIDTH ** (-0.5)
    row_pos, col_pos = jnp.arange(seq)[:, None], jnp.arange(seq)[None, :]
    allowed = (col_pos <= row_pos)[None] | (col_pos[None] < prefix_plane[:, None, None])
    scores = jnp.einsum("bsgd,btd->bgst", query, key, preferred_element_type=F32) * scale
    scores = jnp.where(allowed[:, None], scores, -1e30)
    exps = jnp.exp(scores - jnp.max(scores, axis=-1, keepdims=True))
    probs = exps / jnp.sum(exps, axis=-1, keepdims=True)
    probs_low = probs.astype(BF)
    attended = jnp.einsum("bgst,btd->bsgd", probs_low, value, preferred_element_type=F32)
    attended = attended.astype(BF).reshape(heads * seq, qw)
    part = dot(attended, proj_head).astype(BF)
    part = lax.psum_scatter(part, "rep", scatter_dimension=0, tiled=True, axis_index_groups=groups)
    residual = tokens_f + part.astype(F32)
    inverse_two = lax.rsqrt(jnp.mean(residual * residual, axis=1, keepdims=True) + EPS)
    normed_two = residual * inverse_two
    act_two = (normed_two * gain_two).astype(BF)
    gates, kept = routing(expert_ids, priority, dot(act_two, router))

    dy_all = lax.all_gather(cotangent, "grp", axis=0, tiled=True)
    x_all = lax.all_gather(act_two, "grp", axis=0, tiled=True)
    weight = lax.all_gather(jnp.where(kept, gates, 0.0), "grp", axis=0, tiled=True)
    weight = lax.dynamic_slice_in_dim(weight, grp * local_experts, local_experts, 1).T[:, :, None]
    gate_up = jnp.einsum("td,edh->eth", x_all, wgu, preferred_element_type=F32)
    g, u = gate_up[..., :HID], gate_up[..., HID:]
    sig = jax.nn.sigmoid(g)
    silu = g * sig
    hidden = silu * u
    hidden_w = (hidden * weight).astype(BF)
    back = jnp.einsum("td,edh->eth", dy_all, wdn, preferred_element_type=F32)
    grad_gate_part = jnp.sum(back * hidden, axis=2)
    grad_hidden = back * weight
    ggu = jnp.concatenate(
        [grad_hidden * u * sig * (1.0 + g * (1.0 - sig)), grad_hidden * silu], axis=2
    ).astype(BF)
    out_part = jnp.einsum("eth,edh->td", hidden_w, wdn, preferred_element_type=F32).astype(BF)
    gact_part = jnp.einsum("eth,edh->td", ggu, wgu, preferred_element_type=F32).astype(BF)
    gact = lax.psum_scatter(gact_part, "grp", scatter_dimension=0, tiled=True).astype(F32)
    grad_gates = lax.all_to_all(grad_gate_part.T, "grp", 0, 1, tiled=True)
    grad_gates = jnp.where(kept, grad_gates, 0.0)
    gw_gu = jnp.einsum("td,eth->edh", x_all, ggu, preferred_element_type=F32).astype(BF)
    gw_dn = jnp.einsum("td,eth->edh", dy_all, hidden_w, preferred_element_type=F32).astype(BF)
    gw = jnp.concatenate([gw_gu, gw_dn], axis=2)
    gw = gw.reshape(local_experts, grps, reps, piece, 3 * HID).transpose(2, 1, 3, 0, 4)
    gw = gw.reshape(reps * grps * piece, EXPERTS // grps * 3 * HID)
    gw = lax.psum_scatter(gw, "rep", scatter_dimension=0, tiled=True)
    gw = gw.reshape(grps, piece, local_experts, 3 * HID)
    gw = lax.all_to_all(gw, "grp", 0, 0, tiled=True)
    gw = gw.transpose(1, 0, 2, 3).reshape(piece, EXPERTS, 3 * HID)
    gw = lax.all_gather(gw, "rep", axis=0, tiled=True)
    grad_gu = gw[:, :, : 2 * HID].astype(F32)
    grad_dn = gw[:, :, 2 * HID :].astype(F32)
    out = lax.psum_scatter(out_part, "grp", scatter_dimension=0, tiled=True).astype(F32)
    output = (residual + out).astype(BF)

    grad_logits = (gates * (grad_gates - jnp.sum(gates * grad_gates, axis=1, keepdims=True))).astype(BF)
    gact = gact + dot(grad_logits, router.T)
    router_term = dot(act_two.T, grad_logits)
    gain_two_term = jnp.sum(gact * normed_two, axis=0)
    scaled = gact * gain_two
    dy = cotangent.astype(F32)
    grad_residual = dy + inverse_two * (
        scaled - normed_two * jnp.mean(scaled * normed_two, axis=1, keepdims=True)
    )
    gres_low = grad_residual.astype(BF)

    gres_plane = lax.all_gather(gres_low, "rep", axis=0, tiled=True, axis_index_groups=groups)
    proj_term = dot(attended.T, gres_plane)
    grad_att = dot(gres_plane, proj_head.T).astype(BF).reshape(heads, seq, QPK, HEAD_WIDTH)
    grad_value = jnp.einsum("bgst,bsgd->btd", probs_low, grad_att, preferred_element_type=F32)
    grad_probs = jnp.einsum("bsgd,btd->bgst", grad_att, value, preferred_element_type=F32)
    grad_scores = (
        probs * (grad_probs - jnp.sum(probs * grad_probs, axis=-1, keepdims=True))
    ).astype(BF)
    grad_query = jnp.einsum("bgst,btd->bsgd", grad_scores, key, preferred_element_type=F32) * scale
    grad_key = jnp.einsum("bgst,bsgd->btd", grad_scores, query, preferred_element_type=F32) * scale
    turned_back = rotate(
        jnp.concatenate([grad_query, grad_key[:, :, None]], axis=2), cos_b, -sin_b
    )
    gproj = jnp.concatenate([turned_back, grad_value[:, :, None]], axis=2).astype(BF)
    gproj = gproj.reshape(heads * seq, qw + 2 * hw)
    qkv_term = dot(act_plane.T, gproj)
    gact_one = dot(gproj, qkv_head.T).astype(BF)
    gact_one = lax.psum_scatter(
        gact_one, "rep", scatter_dimension=0, tiled=True, axis_index_groups=groups
    ).astype(F32)
    gain_one_term = jnp.sum(gact_one * normed_one, axis=0)
    scaled_one = gact_one * gain_one
    grad_tokens = grad_residual + inverse_one * (
        scaled_one - normed_one * jnp.mean(scaled_one * normed_one, axis=1, keepdims=True)
    )

    qkv_own = lax.psum_scatter(qkv_term.astype(BF), "grp", scatter_dimension=0, tiled=True)
    proj_sum = lax.psum(proj_term.astype(BF), "grp")
    if groups is not None:
        across = [[i + heads * j for j in range(reps // heads)] for i in range(heads)]
        qkv_own = lax.psum(qkv_own, "rep", axis_index_groups=across)
        proj_sum = lax.psum(proj_sum, "rep", axis_index_groups=across)
    qkv_own = lax.all_gather(qkv_own, "rep", axis=0, tiled=False, axis_index_groups=groups)
    qkv_own = qkv_own.astype(F32)
    grad_qkv = jnp.concatenate(
        [
            qkv_own[:, :, lo:hi].transpose(1, 0, 2).reshape(own, -1)
            for lo, hi in ((0, qw), (qw, qw + hw), (qw + hw, qw + 2 * hw))
        ],
        axis=1,
    )
    proj_all = lax.all_gather(proj_sum, "rep", axis=0, tiled=True, axis_index_groups=groups)
    grad_proj = lax.dynamic_slice_in_dim(proj_all, grp * own, own, 0).astype(F32)
    terms = jnp.concatenate([gain_one_term[:, None], gain_two_term[:, None], router_term], axis=1)
    terms = lax.psum(lax.psum_scatter(terms, "grp", scatter_dimension=0, tiled=True), "rep")
    return (
        output,
        grad_tokens,
        terms[:, 0],
        grad_qkv,
        grad_proj,
        terms[:, 1],
        terms[:, 2:],
        grad_gu,
        grad_dn,
    )


def solution(mesh):
    tok, par = ("rep", "grp"), "grp"
    in_specs = (
        P(tok, None),
        P(par),
        P(par, None),
        P(par, None),
        P(par),
        P(par, None),
        P(par, None, None),
        P(par, None, None),
        P(tok),
        P(tok, None),
        P(tok, None),
        P(tok, None),
    )
    out_specs = (
        P(tok, None),
        P(tok, None),
        P(par),
        P(par, None),
        P(par, None),
        P(par),
        P(par, None),
        P(par, None, None),
        P(par, None, None),
    )
    reps, grps = mesh.shape["rep"], mesh.shape["grp"]

    def body(*args):
        return shards(reps, grps, *args)

    return jax.shard_map(body, mesh=mesh, in_specs=in_specs, out_specs=out_specs, check_vma=False)
```

```python
import jax
import jax.numpy as jnp
from jax import lax
from jax.experimental import pallas as pl
from jax.experimental.pallas import tpu as pltpu
from jax.sharding import PartitionSpec as P

QUERY_HEADS = 24
KEY_VALUE_HEADS = 8
HEAD_WIDTH = 64
HID = 512
EXPERTS = 16
CAP = 72
EPS = 1e-05
BF = jnp.bfloat16
F32 = jnp.float32
QPK = QUERY_HEADS // KEY_VALUE_HEADS
BIG = 1 << 20
MESH = pl.DeviceIdType.MESH


def dot(a, b):
    return jnp.dot(a, b, preferred_element_type=F32)


def rope_tables(length):
    half = HEAD_WIDTH // 2
    position = jnp.arange(length, dtype=F32)[:, None]
    inverse_freq = 10000.0 ** (-jnp.arange(half, dtype=F32) * 2.0 / HEAD_WIDTH)
    angles = position * inverse_freq[None, :]
    return jnp.cos(angles), jnp.sin(angles)


def rotate(v, cos, sin):
    half = HEAD_WIDTH // 2
    a, b = v[..., :half], v[..., half:]
    return jnp.concatenate([a * cos - b * sin, b * cos + a * sin], axis=-1)


def routing(expert_ids, priority, logits):
    seq, top = expert_ids.shape
    choose = expert_ids[:, :, None] == jnp.arange(EXPERTS, dtype=jnp.int32)[None, None, :]
    chosen = jnp.any(choose, axis=1)
    rank_of = jnp.sum(jnp.where(choose, priority.reshape(seq, top)[:, :, None], 0), axis=1)
    rank_of = jnp.where(chosen, rank_of, BIG)
    slot = jnp.sum((rank_of[None, :, :] < rank_of[:, None, :]).astype(jnp.int32), axis=1)
    kept = chosen & (slot < CAP)
    top_logit = jnp.max(jnp.where(chosen, logits, -jnp.inf), axis=1, keepdims=True)
    gate_exp = jnp.where(chosen, jnp.exp(jnp.where(chosen, logits - top_logit, 0.0)), 0.0)
    gates = gate_exp / jnp.sum(gate_exp, axis=1, keepdims=True)
    return gates, kept


def place():
    r, z = lax.axis_index("rep"), lax.axis_index("grp")
    return r // 4, (r // 2) % 2, r % 2, z


def flip(bit, by):
    return bit + by * (1 - 2 * bit)


def grads_kernel(nq, x_ref, dy_ref, ggu_ref, hw_ref, gu_out, dn_out,
                 gw, recv1, send2, recv2, zs, zr, ag, sb, ib, st,
                 s1, r1, s2, r2, sz, rz, sa, ra, ss, rs, so):
    y, x, c, z = place()
    half = HID // 2
    wide = 3 * half

    def slot(a, b):
        return flip(y, a * c + b * (1 - c)) * 2 + flip(x, a * (1 - c) + b * c)

    def dev(p, core, zz):
        return (p * 2 + core, zz)

    p0 = slot(0, 0)
    d1, d2, dsib = dev(slot(1, 0), c, z), dev(slot(0, 1), c, z), dev(p0, 1 - c, z)
    zk = [lax.rem(z + k, 4) for k in range(4)]
    barrier = pltpu.get_barrier_semaphore()
    for to in (d1, d2, dsib, dev(p0, c, zk[1]), dev(p0, c, zk[2]), dev(p0, c, zk[3])):
        pl.semaphore_signal(barrier, 1, device_id=to, device_id_type=MESH)
    pl.semaphore_wait(barrier, 6)

    def copy1(q, b):
        return pltpu.make_async_remote_copy(
            gw.at[q // 2, slot(1, b), q % 2], recv1.at[q, b], s1.at[q, b], r1.at[q, b],
            device_id=d1, device_id_type=MESH)

    def copy2(q):
        return pltpu.make_async_remote_copy(
            send2.at[q % 2], recv2.at[q], s2.at[q], r2.at[q], device_id=d2, device_id_type=MESH)

    def copyz(q, k):
        return pltpu.make_async_remote_copy(
            zs.at[q % 2, zk[k]], zr.at[q, z], sz.at[q, k - 1], rz.at[q, k - 1],
            device_id=dev(p0, c, zk[k]), device_id_type=MESH)

    def copya(q, i):
        src, dst = ((0, 1), (0, 2), (1, 3))[i]
        return pltpu.make_async_remote_copy(
            ag.at[q, src], ag.at[q, dst], sa.at[q, i], ra.at[q, i],
            device_id=d1 if i == 0 else d2, device_id_type=MESH)

    def copys(q, i):
        return pltpu.make_async_remote_copy(
            ag.at[q, i], sb.at[q, i], ss.at[q, i], rs.at[q, i], device_id=dsib, device_id_type=MESH)

    def out_copies(q, k, p, core):
        rows = 256
        at = pl.multiple_of(((q // 2) * 128 + p * 32 + (q % 2) * 16) * EXPERTS, rows)
        lo = pl.multiple_of(core * half, half)
        hi = pl.multiple_of(HID + core * half, half)
        pairs = ((gu_out.at[pl.ds(at, rows), pl.ds(lo, half)], 0),
                 (gu_out.at[pl.ds(at, rows), pl.ds(hi, half)], half),
                 (dn_out.at[pl.ds(at, rows), pl.ds(lo, half)], 2 * half))
        return [pltpu.make_async_copy(st.at[k, :, pl.ds(off, half)], ref, so.at[k, i])
                for i, (ref, off) in enumerate(pairs)]

    def emit(q, k, first, p, core, ref):
        @pl.when(jnp.logical_not(first))
        def _():
            for one in out_copies(q, k, p, core):
                one.wait()
        st[k] = ref[...].astype(F32)
        for one in out_copies(q, k, p, core):
            one.start()

    def stage1(q):
        @pl.when(q % 2 == 0)
        def _():
            q3 = q // 2
            xs = jnp.concatenate(
                [x_ref[:, pl.ds(pl.multiple_of(zz * 384 + q3 * 128, 128), 128)] for zz in range(4)], axis=1)
            ds_ = jnp.concatenate(
                [dy_ref[:, pl.ds(pl.multiple_of(zz * 384 + q3 * 128, 128), 128)] for zz in range(4)], axis=1)

            def one(j, _):
                up = lax.dot_general(xs, ggu_ref[j], (((0,), (0,)), ((), ())),
                                     preferred_element_type=F32).astype(BF)
                dn = lax.dot_general(ds_, hw_ref[j], (((0,), (0,)), ((), ())),
                                     preferred_element_type=F32).astype(BF)
                for zz in range(4):
                    for p in range(4):
                        for h in range(2):
                            at = zz * 128 + p * 32 + h * 16
                            gw[q3, p, h, zz, j, :, : 2 * half] = up[at : at + 16]
                            gw[q3, p, h, zz, j, :, 2 * half :] = dn[at : at + 16]
                return 0
            lax.fori_loop(0, 4, one, 0)
        for b in range(2):
            copy1(q, b).start()

    def stage2(q):
        for b in range(2):
            copy1(q, b).wait_recv()

        def one(zz, _):
            send2[q % 2, zz] = (gw[q // 2, slot(0, 1), q % 2, zz].astype(F32)
                                + recv1[q, 1, zz].astype(F32)).astype(BF)
            return 0
        lax.fori_loop(0, 4, one, 0)
        copy2(q).start()

    def stage3(q):
        copy2(q).wait()

        def one(zz, _):
            zs[q % 2, zz] = (gw[q // 2, p0, q % 2, zz].astype(F32) + recv1[q, 0, zz].astype(F32)
                             + recv2[q, zz].astype(F32)).astype(BF)
            return 0
        lax.fori_loop(0, 4, one, 0)
        for k in range(1, 4):
            copyz(q, k).start()
        zr[q, z] = zs[q % 2, z]

    def stage4(q):
        for k in range(1, 4):
            copyz(q, k).wait()
        for zz in range(4):
            for j in range(4):
                for l in range(wide // 128):
                    ib[l, pl.ds(zz * 4 + j, 16, stride=EXPERTS), :] = (
                        zr[q, zz, j, :, l * 128 : (l + 1) * 128].astype(F32))
        for l in range(wide // 128):
            ag[q, 0, :, l * 128 : (l + 1) * 128] = ib[l].astype(BF)
        copya(q, 0).start()
        copys(q, 0).start()

    def stage5(q):
        copya(q, 0).wait_recv()
        copya(q, 1).start()
        copya(q, 2).start()
        copys(q, 1).start()
        emit(q, 0, q == 0, p0, c, ag.at[q, 0])
        emit(q, 1, q == 0, slot(1, 0), c, ag.at[q, 1])

    def stage6(q):
        copya(q, 1).wait_recv()
        copya(q, 2).wait_recv()
        copys(q, 2).start()
        copys(q, 3).start()
        emit(q, 2, q == 0, slot(0, 1), c, ag.at[q, 2])
        emit(q, 3, q == 0, slot(1, 1), c, ag.at[q, 3])

    def stage7(q):
        for i in range(4):
            copys(q, i).wait_recv()
        for i, p in enumerate((p0, slot(0, 1), slot(1, 0), slot(1, 1))):
            emit(q, i, False, p, 1 - c, sb.at[q, i])
        for i in range(4):
            copys(q, i).wait_send()
        for i in range(3):
            copya(q, i).wait_send()
        for b in range(2):
            copy1(q, b).wait_send()

    stages = (stage1, stage2, stage3, stage4, stage5, stage6, stage7)

    def step(t, _):
        for i, stage in enumerate(stages):
            q = t - i

            @pl.when((q >= 0) & (q < nq))
            def _(stage=stage, q=q):
                stage(q)
        return 0

    lax.fori_loop(0, nq + len(stages) - 1, step, 0)
    for k in range(4):
        for one in out_copies(0, k, p0, c):
            one.wait()


def expert_grads(xs, dys, ggu, hw):
    nq, half, wide = 6, HID // 2, 3 * HID // 2
    piece = (4, 4, 16, wide)
    sem = pltpu.SemaphoreType.DMA
    return pl.pallas_call(
        lambda *a: grads_kernel(nq, *a),
        out_shape=(jax.ShapeDtypeStruct((384 * 16, 2 * HID), F32), jax.ShapeDtypeStruct((384 * 16, HID), F32)),
        in_specs=[pl.BlockSpec(memory_space=pltpu.VMEM)] * 4,
        out_specs=[pl.BlockSpec(memory_space=pl.ANY)] * 2,
        scratch_shapes=[
            pltpu.VMEM((3, 4, 2) + piece, BF),
            pltpu.VMEM((nq, 2) + piece, BF),
            pltpu.VMEM((2,) + piece, BF),
            pltpu.VMEM((nq,) + piece, BF),
            pltpu.VMEM((2,) + piece, BF),
            pltpu.VMEM((nq,) + piece, BF),
            pltpu.VMEM((nq, 4, 256, wide), BF),
            pltpu.VMEM((nq, 4, 256, wide), BF),
            pltpu.VMEM((wide // 128, 256, 128), F32),
            pltpu.VMEM((4, 256, wide), F32),
            sem((nq, 2)), sem((nq, 2)), sem((nq,)), sem((nq,)), sem((nq, 3)), sem((nq, 3)),
            sem((nq, 3)), sem((nq, 3)), sem((nq, 4)), sem((nq, 4)), sem((4, 3)),
        ],
        compiler_params=pltpu.CompilerParams(
            collective_id=3, has_side_effects=True, vmem_limit_bytes=62 * 1024 * 1024),
        name="expert_grads",
    )(xs, dys, ggu, hw)


def expert_grads_general(reps, grps, xs, dys, ggu, hw):
    local, half, width = ggu.shape[0], HID // 2, xs.shape[1]
    own = width // grps
    chips = reps // 2
    piece = own // chips
    same_core = [[2 * i + c for i in range(chips)] for c in range(2)]
    pairs = [[2 * i, 2 * i + 1] for i in range(chips)]
    up = jnp.einsum("td,eth->edh", xs, ggu, preferred_element_type=F32).astype(BF)
    down = jnp.einsum("td,eth->edh", dys, hw, preferred_element_type=F32).astype(BF)
    gw = jnp.concatenate([up, down], axis=2)
    gw = gw.reshape(local, grps, chips, piece, 3 * half).transpose(2, 1, 3, 0, 4)
    gw = gw.reshape(chips * grps * piece, local * 3 * half)
    gw = lax.psum_scatter(gw, "rep", scatter_dimension=0, tiled=True, axis_index_groups=same_core)
    gw = lax.all_to_all(gw.reshape(grps, piece, local, 3 * half), "grp", 0, 0, tiled=True)
    gw = gw.transpose(1, 0, 2, 3).reshape(piece, EXPERTS, 3 * half)
    gw = lax.all_gather(gw, "rep", axis=0, tiled=True, axis_index_groups=same_core)
    gw = lax.all_gather(gw, "rep", axis=0, tiled=False, axis_index_groups=pairs).astype(F32)
    gw = gw.reshape(2, own * EXPERTS, 3, half)
    gw = jnp.moveaxis(gw, 0, 2).reshape(own * EXPERTS, 3 * HID)
    return gw[:, : 2 * HID], gw[:, 2 * HID :]


def shards(
    reps,
    grps,
    tokens,
    attn_gain,
    query_key_value_weight,
    attn_proj,
    mlp_gain,
    w_router,
    w_gate_up,
    w_down,
    prefix_len,
    expert_ids,
    priority,
    cotangent,
):
    seq, width = tokens.shape
    own = width // grps
    local_experts = EXPERTS // grps
    heads = KEY_VALUE_HEADS
    groups = None if reps == heads else [list(range(i, i + heads)) for i in range(0, reps, heads)]
    rep, grp = lax.axis_index("rep"), lax.axis_index("grp")
    head = lax.rem(rep, heads)
    qw, hw = QPK * HEAD_WIDTH, HEAD_WIDTH
    q_all = QUERY_HEADS * HEAD_WIDTH

    small = jnp.concatenate([attn_gain[:, None], mlp_gain[:, None], w_router], axis=1)
    small = lax.all_gather(small, "grp", axis=0, tiled=True)
    gain_one, gain_two = small[:, 0].astype(F32)[None, :], small[:, 1].astype(F32)[None, :]
    router = small[:, 2:]
    qkv_cols = jnp.concatenate(
        [
            lax.dynamic_slice_in_dim(query_key_value_weight, head * qw, qw, 1),
            lax.dynamic_slice_in_dim(query_key_value_weight, q_all + head * hw, hw, 1),
            lax.dynamic_slice_in_dim(query_key_value_weight, q_all + heads * hw + head * hw, hw, 1),
        ],
        axis=1,
    )
    qkv_head = lax.all_gather(qkv_cols, "grp", axis=0, tiled=True)
    row = head * qw + jnp.arange(qw)
    mine = (row // own) == grp
    proj_rows = jnp.where(mine[:, None], jnp.take(attn_proj, jnp.where(mine, row - grp * own, 0), axis=0), 0)
    proj_head = lax.psum(proj_rows, "grp")

    core, chip, chips, half = lax.rem(rep, 2), rep // 2, reps // 2, HID // 2
    pairs = [[2 * i, 2 * i + 1] for i in range(chips)]
    same_core = [[2 * i + c for i in range(chips)] for c in range(2)]
    piece = own // chips
    gu_piece = lax.dynamic_slice_in_dim(w_gate_up, chip * piece, piece, 0)
    dn_piece = lax.dynamic_slice_in_dim(w_down, chip * piece, piece, 0)
    both = jnp.concatenate(
        [
            lax.dynamic_slice_in_dim(gu_piece, core * half, half, 2),
            lax.dynamic_slice_in_dim(gu_piece, HID + core * half, half, 2),
            lax.dynamic_slice_in_dim(dn_piece, core * half, half, 2),
        ],
        axis=2,
    )
    both = both.reshape(piece, grps, local_experts, 3 * half).transpose(1, 2, 0, 3)
    both = lax.all_to_all(both, "grp", 0, 0, tiled=True)
    both = lax.all_gather(both, "rep", axis=0, tiled=False, axis_index_groups=same_core)
    both = both.transpose(2, 1, 0, 3, 4).reshape(local_experts, width, 3 * half)
    wgu, wdn = both[:, :, : 2 * half], both[:, :, 2 * half :]

    tokens_f = tokens.astype(F32)
    inverse_one = lax.rsqrt(jnp.mean(tokens_f * tokens_f, axis=1, keepdims=True) + EPS)
    normed_one = tokens_f * inverse_one
    act_one = (normed_one * gain_one).astype(BF)
    act_plane = lax.all_gather(act_one, "rep", axis=0, tiled=True, axis_index_groups=groups)
    prefix_plane = lax.all_gather(prefix_len, "rep", axis=0, tiled=True, axis_index_groups=groups)
    cos, sin = rope_tables(seq)
    projected = dot(act_plane, qkv_head).reshape(heads, seq, QPK + 2, HEAD_WIDTH)
    cos_b, sin_b = cos[None, :, None, :], sin[None, :, None, :]
    turned = rotate(projected[:, :, : QPK + 1], cos_b, sin_b).astype(BF)
    query = turned[:, :, :QPK]
    key = turned[:, :, QPK]
    value = projected[:, :, QPK + 1].astype(BF)
    scale = HEAD_WIDTH ** (-0.5)
    row_pos, col_pos = jnp.arange(seq)[:, None], jnp.arange(seq)[None, :]
    allowed = (col_pos <= row_pos)[None] | (col_pos[None] < prefix_plane[:, None, None])
    scores = jnp.einsum("bsgd,btd->bgst", query, key, preferred_element_type=F32) * scale
    scores = jnp.where(allowed[:, None], scores, -1e30)
    exps = jnp.exp(scores - jnp.max(scores, axis=-1, keepdims=True))
    probs = exps / jnp.sum(exps, axis=-1, keepdims=True)
    probs_low = probs.astype(BF)
    attended = jnp.einsum("bgst,btd->bsgd", probs_low, value, preferred_element_type=F32)
    attended = attended.astype(BF).reshape(heads * seq, qw)
    part = dot(attended, proj_head).astype(BF)
    part = lax.psum_scatter(part, "rep", scatter_dimension=0, tiled=True, axis_index_groups=groups)
    residual = tokens_f + part.astype(F32)
    inverse_two = lax.rsqrt(jnp.mean(residual * residual, axis=1, keepdims=True) + EPS)
    normed_two = residual * inverse_two
    act_two = (normed_two * gain_two).astype(BF)
    gates, kept = routing(expert_ids, priority, dot(act_two, router))

    def column(v):
        v = lax.all_gather(v, "grp", axis=0, tiled=True)
        return lax.all_gather(v, "rep", axis=0, tiled=True, axis_index_groups=pairs)

    def to_owners(v):
        v = lax.psum_scatter(v, "rep", scatter_dimension=0, tiled=True, axis_index_groups=pairs)
        return lax.psum_scatter(v, "grp", scatter_dimension=0, tiled=True).astype(F32)

    dy_all = column(cotangent)
    x_all = column(act_two)
    weight = column(jnp.where(kept, gates, 0.0))
    weight = lax.dynamic_slice_in_dim(weight, grp * local_experts, local_experts, 1).T[:, :, None]
    gate_up = jnp.einsum("td,edh->eth", x_all, wgu, preferred_element_type=F32)
    g, u = gate_up[..., :half], gate_up[..., half:]
    sig = jax.nn.sigmoid(g)
    silu = g * sig
    hidden = silu * u
    hidden_w = (hidden * weight).astype(BF)
    back = jnp.einsum("td,edh->eth", dy_all, wdn, preferred_element_type=F32)
    grad_gate_part = jnp.sum(back * hidden, axis=2)
    grad_hidden = back * weight
    ggu = jnp.concatenate(
        [grad_hidden * u * sig * (1.0 + g * (1.0 - sig)), grad_hidden * silu], axis=2
    ).astype(BF)
    out_part = jnp.einsum("eth,edh->td", hidden_w, wdn, preferred_element_type=F32).astype(BF)
    gact_part = jnp.einsum("eth,edh->td", ggu, wgu, preferred_element_type=F32).astype(BF)
    gact = to_owners(gact_part)
    grad_gates = lax.psum_scatter(
        grad_gate_part.T, "rep", scatter_dimension=0, tiled=True, axis_index_groups=pairs
    )
    grad_gates = lax.all_to_all(grad_gates, "grp", 0, 1, tiled=True)
    grad_gates = jnp.where(kept, grad_gates, 0.0)
    out = to_owners(out_part)
    output = (residual + out).astype(BF)
    if (reps, grps) == (8, 4):
        grad_gu, grad_dn = expert_grads(x_all, dy_all, ggu, hidden_w)
    else:
        grad_gu, grad_dn = expert_grads_general(reps, grps, x_all, dy_all, ggu, hidden_w)
    grad_gu = grad_gu.reshape(own, EXPERTS, 2 * HID)
    grad_dn = grad_dn.reshape(own, EXPERTS, HID)

    grad_logits = (gates * (grad_gates - jnp.sum(gates * grad_gates, axis=1, keepdims=True))).astype(BF)
    gact = gact + dot(grad_logits, router.T)
    router_term = dot(act_two.T, grad_logits)
    gain_two_term = jnp.sum(gact * normed_two, axis=0)
    scaled = gact * gain_two
    dy = cotangent.astype(F32)
    grad_residual = dy + inverse_two * (
        scaled - normed_two * jnp.mean(scaled * normed_two, axis=1, keepdims=True)
    )
    gres_low = grad_residual.astype(BF)

    gres_plane = lax.all_gather(gres_low, "rep", axis=0, tiled=True, axis_index_groups=groups)
    proj_term = dot(attended.T, gres_plane)
    grad_att = dot(gres_plane, proj_head.T).astype(BF).reshape(heads, seq, QPK, HEAD_WIDTH)
    grad_value = jnp.einsum("bgst,bsgd->btd", probs_low, grad_att, preferred_element_type=F32)
    grad_probs = jnp.einsum("bsgd,btd->bgst", grad_att, value, preferred_element_type=F32)
    grad_scores = (
        probs * (grad_probs - jnp.sum(probs * grad_probs, axis=-1, keepdims=True))
    ).astype(BF)
    grad_query = jnp.einsum("bgst,btd->bsgd", grad_scores, key, preferred_element_type=F32) * scale
    grad_key = jnp.einsum("bgst,bsgd->btd", grad_scores, query, preferred_element_type=F32) * scale
    turned_back = rotate(
        jnp.concatenate([grad_query, grad_key[:, :, None]], axis=2), cos_b, -sin_b
    )
    gproj = jnp.concatenate([turned_back, grad_value[:, :, None]], axis=2).astype(BF)
    gproj = gproj.reshape(heads * seq, qw + 2 * hw)
    qkv_term = dot(act_plane.T, gproj)
    gact_one = dot(gproj, qkv_head.T).astype(BF)
    gact_one = lax.psum_scatter(
        gact_one, "rep", scatter_dimension=0, tiled=True, axis_index_groups=groups
    ).astype(F32)
    gain_one_term = jnp.sum(gact_one * normed_one, axis=0)
    scaled_one = gact_one * gain_one
    grad_tokens = grad_residual + inverse_one * (
        scaled_one - normed_one * jnp.mean(scaled_one * normed_one, axis=1, keepdims=True)
    )

    qkv_own = lax.psum_scatter(qkv_term.astype(BF), "grp", scatter_dimension=0, tiled=True)
    proj_sum = lax.psum(proj_term.astype(BF), "grp")
    if groups is not None:
        across = [[i + heads * j for j in range(reps // heads)] for i in range(heads)]
        qkv_own = lax.psum(qkv_own, "rep", axis_index_groups=across)
        proj_sum = lax.psum(proj_sum, "rep", axis_index_groups=across)
    qkv_own = lax.all_gather(qkv_own, "rep", axis=0, tiled=False, axis_index_groups=groups)
    qkv_own = qkv_own.astype(F32)
    grad_qkv = jnp.concatenate(
        [
            qkv_own[:, :, lo:hi].transpose(1, 0, 2).reshape(own, -1)
            for lo, hi in ((0, qw), (qw, qw + hw), (qw + hw, qw + 2 * hw))
        ],
        axis=1,
    )
    proj_all = lax.all_gather(proj_sum, "rep", axis=0, tiled=True, axis_index_groups=groups)
    grad_proj = lax.dynamic_slice_in_dim(proj_all, grp * own, own, 0).astype(F32)
    terms = jnp.concatenate([gain_one_term[:, None], gain_two_term[:, None], router_term], axis=1)
    terms = lax.psum(lax.psum_scatter(terms, "grp", scatter_dimension=0, tiled=True), "rep")
    return (
        output,
        grad_tokens,
        terms[:, 0],
        grad_qkv,
        grad_proj,
        terms[:, 1],
        terms[:, 2:],
        grad_gu,
        grad_dn,
    )


def solution(mesh):
    tok, par = ("rep", "grp"), "grp"
    in_specs = (
        P(tok, None),
        P(par),
        P(par, None),
        P(par, None),
        P(par),
        P(par, None),
        P(par, None, None),
        P(par, None, None),
        P(tok),
        P(tok, None),
        P(tok, None),
        P(tok, None),
    )
    out_specs = (
        P(tok, None),
        P(tok, None),
        P(par),
        P(par, None),
        P(par, None),
        P(par),
        P(par, None),
        P(par, None, None),
        P(par, None, None),
    )
    reps, grps = mesh.shape["rep"], mesh.shape["grp"]

    def body(*args):
        return shards(reps, grps, *args)

    return jax.shard_map(body, mesh=mesh, in_specs=in_specs, out_specs=out_specs, check_vma=False)
```

```python
import jax
import jax.numpy as jnp
from jax import lax
from jax.experimental import pallas as pl
from jax.experimental.pallas import tpu as pltpu
from jax.sharding import PartitionSpec as P

QUERY_HEADS = 24
KEY_VALUE_HEADS = 8
HEAD_WIDTH = 64
HID = 512
EXPERTS = 16
CAP = 72
EPS = 1e-05
BF = jnp.bfloat16
F32 = jnp.float32
QPK = QUERY_HEADS // KEY_VALUE_HEADS
BIG = 1 << 20
MESH = pl.DeviceIdType.MESH


def dot(a, b):
    return jnp.dot(a, b, preferred_element_type=F32)


def rope_tables(length):
    half = HEAD_WIDTH // 2
    position = jnp.arange(length, dtype=F32)[:, None]
    inverse_freq = 10000.0 ** (-jnp.arange(half, dtype=F32) * 2.0 / HEAD_WIDTH)
    angles = position * inverse_freq[None, :]
    return jnp.cos(angles), jnp.sin(angles)


def rotate(v, cos, sin):
    half = HEAD_WIDTH // 2
    a, b = v[..., :half], v[..., half:]
    return jnp.concatenate([a * cos - b * sin, b * cos + a * sin], axis=-1)


def choices(expert_ids, priority):
    seq, top = expert_ids.shape
    choose = expert_ids[:, :, None] == jnp.arange(EXPERTS, dtype=jnp.int32)[None, None, :]
    chosen = jnp.any(choose, axis=1)
    rank_of = jnp.sum(jnp.where(choose, priority.reshape(seq, top)[:, :, None], 0), axis=1)
    rank_of = jnp.where(chosen, rank_of, BIG)
    slot = jnp.sum((rank_of[None, :, :] < rank_of[:, None, :]).astype(jnp.int32), axis=1)
    return chosen, chosen & (slot < CAP)


def routing(expert_ids, priority, logits):
    chosen, kept = choices(expert_ids, priority)
    top_logit = jnp.max(jnp.where(chosen, logits, -jnp.inf), axis=1, keepdims=True)
    gate_exp = jnp.where(chosen, jnp.exp(jnp.where(chosen, logits - top_logit, 0.0)), 0.0)
    gates = gate_exp / jnp.sum(gate_exp, axis=1, keepdims=True)
    return gates, kept


def place():
    r, z = lax.axis_index("rep"), lax.axis_index("grp")
    return r // 4, (r // 2) % 2, r % 2, z


def flip(bit, by):
    return bit + by * (1 - 2 * bit)


def grads_kernel(nq, x_ref, dy_ref, ggu_ref, hw_ref, gu_out, dn_out,
                 gw, recv1, send2, recv2, zs, zr, ag, sb, ib, st,
                 s1, r1, s2, r2, sz, rz, sa, ra, ss, rs, so):
    y, x, c, z = place()
    half = HID // 2
    wide = 3 * half

    def slot(a, b):
        return flip(y, a * c + b * (1 - c)) * 2 + flip(x, a * (1 - c) + b * c)

    def dev(p, core, zz):
        return (p * 2 + core, zz)

    p0 = slot(0, 0)
    d1, d2, dsib = dev(slot(1, 0), c, z), dev(slot(0, 1), c, z), dev(p0, 1 - c, z)
    zk = [lax.rem(z + k, 4) for k in range(4)]
    barrier = pltpu.get_barrier_semaphore()
    for to in (d1, d2, dsib, dev(p0, c, zk[1]), dev(p0, c, zk[2]), dev(p0, c, zk[3])):
        pl.semaphore_signal(barrier, 1, device_id=to, device_id_type=MESH)
    pl.semaphore_wait(barrier, 6)

    def copy1(q, b):
        return pltpu.make_async_remote_copy(
            gw.at[q // 2, slot(1, b), q % 2], recv1.at[q, b], s1.at[q, b], r1.at[q, b],
            device_id=d1, device_id_type=MESH)

    def copy2(q):
        return pltpu.make_async_remote_copy(
            send2.at[q % 2], recv2.at[q], s2.at[q], r2.at[q], device_id=d2, device_id_type=MESH)

    def copyz(q, k):
        return pltpu.make_async_remote_copy(
            zs.at[q % 2, zk[k]], zr.at[q, z], sz.at[q, k - 1], rz.at[q, k - 1],
            device_id=dev(p0, c, zk[k]), device_id_type=MESH)

    def copya(q, i):
        src, dst = ((0, 1), (0, 2), (1, 3))[i]
        return pltpu.make_async_remote_copy(
            ag.at[q, src], ag.at[q, dst], sa.at[q, i], ra.at[q, i],
            device_id=d1 if i == 0 else d2, device_id_type=MESH)

    def copys(q, i):
        return pltpu.make_async_remote_copy(
            ag.at[q, i], sb.at[q, i], ss.at[q, i], rs.at[q, i], device_id=dsib, device_id_type=MESH)

    def out_copies(q, k, p, core):
        rows = 256
        at = pl.multiple_of(((q // 2) * 128 + p * 32 + (q % 2) * 16) * EXPERTS, rows)
        lo = pl.multiple_of(core * half, half)
        hi = pl.multiple_of(HID + core * half, half)
        pairs = ((gu_out.at[pl.ds(at, rows), pl.ds(lo, half)], 0),
                 (gu_out.at[pl.ds(at, rows), pl.ds(hi, half)], half),
                 (dn_out.at[pl.ds(at, rows), pl.ds(lo, half)], 2 * half))
        return [pltpu.make_async_copy(st.at[k, :, pl.ds(off, half)], ref, so.at[k, i])
                for i, (ref, off) in enumerate(pairs)]

    def emit(q, k, first, p, core, ref):
        @pl.when(jnp.logical_not(first))
        def _():
            for one in out_copies(q, k, p, core):
                one.wait()
        st[k] = ref[...].astype(F32)
        for one in out_copies(q, k, p, core):
            one.start()

    def stage1(q):
        @pl.when(q % 2 == 0)
        def _():
            q3 = q // 2
            xs = jnp.concatenate(
                [x_ref[:, pl.ds(pl.multiple_of(zz * 384 + q3 * 128, 128), 128)] for zz in range(4)], axis=1)
            ds_ = jnp.concatenate(
                [dy_ref[:, pl.ds(pl.multiple_of(zz * 384 + q3 * 128, 128), 128)] for zz in range(4)], axis=1)

            def one(j, _):
                up = lax.dot_general(xs, ggu_ref[j], (((0,), (0,)), ((), ())),
                                     preferred_element_type=F32).astype(BF)
                dn = lax.dot_general(ds_, hw_ref[j], (((0,), (0,)), ((), ())),
                                     preferred_element_type=F32).astype(BF)
                for zz in range(4):
                    for p in range(4):
                        for h in range(2):
                            at = zz * 128 + p * 32 + h * 16
                            gw[q3, p, h, zz, j, :, : 2 * half] = up[at : at + 16]
                            gw[q3, p, h, zz, j, :, 2 * half :] = dn[at : at + 16]
                return 0
            lax.fori_loop(0, 4, one, 0)
        for b in range(2):
            copy1(q, b).start()

    def stage2(q):
        for b in range(2):
            copy1(q, b).wait_recv()

        def one(zz, _):
            send2[q % 2, zz] = (gw[q // 2, slot(0, 1), q % 2, zz].astype(F32)
                                + recv1[q, 1, zz].astype(F32)).astype(BF)
            return 0
        lax.fori_loop(0, 4, one, 0)
        copy2(q).start()

    def stage3(q):
        copy2(q).wait()

        def one(zz, _):
            zs[q % 2, zz] = (gw[q // 2, p0, q % 2, zz].astype(F32) + recv1[q, 0, zz].astype(F32)
                             + recv2[q, zz].astype(F32)).astype(BF)
            return 0
        lax.fori_loop(0, 4, one, 0)
        for k in range(1, 4):
            copyz(q, k).start()
        zr[q, z] = zs[q % 2, z]

    def stage4(q):
        for k in range(1, 4):
            copyz(q, k).wait()
        for zz in range(4):
            for j in range(4):
                for l in range(wide // 128):
                    ib[l, pl.ds(zz * 4 + j, 16, stride=EXPERTS), :] = (
                        zr[q, zz, j, :, l * 128 : (l + 1) * 128].astype(F32))
        for l in range(wide // 128):
            ag[q, 0, :, l * 128 : (l + 1) * 128] = ib[l].astype(BF)
        copya(q, 0).start()
        copys(q, 0).start()

    def stage5(q):
        copya(q, 0).wait_recv()
        copya(q, 1).start()
        copya(q, 2).start()
        copys(q, 1).start()
        emit(q, 0, q == 0, p0, c, ag.at[q, 0])
        emit(q, 1, q == 0, slot(1, 0), c, ag.at[q, 1])

    def stage6(q):
        copya(q, 1).wait_recv()
        copya(q, 2).wait_recv()
        copys(q, 2).start()
        copys(q, 3).start()
        emit(q, 2, q == 0, slot(0, 1), c, ag.at[q, 2])
        emit(q, 3, q == 0, slot(1, 1), c, ag.at[q, 3])

    def stage7(q):
        for i in range(4):
            copys(q, i).wait_recv()
        for i, p in enumerate((p0, slot(0, 1), slot(1, 0), slot(1, 1))):
            emit(q, i, False, p, 1 - c, sb.at[q, i])
        for i in range(4):
            copys(q, i).wait_send()
        for i in range(3):
            copya(q, i).wait_send()
        for b in range(2):
            copy1(q, b).wait_send()

    stages = (stage1, stage2, stage3, stage4, stage5, stage6, stage7)

    def step(t, _):
        for i, stage in enumerate(stages):
            q = t - i

            @pl.when((q >= 0) & (q < nq))
            def _(stage=stage, q=q):
                stage(q)
        return 0

    lax.fori_loop(0, nq + len(stages) - 1, step, 0)
    for k in range(4):
        for one in out_copies(0, k, p0, c):
            one.wait()


def expert_grads(xs, dys, ggu, hw):
    nq, half, wide = 6, HID // 2, 3 * HID // 2
    piece = (4, 4, 16, wide)
    sem = pltpu.SemaphoreType.DMA
    return pl.pallas_call(
        lambda *a: grads_kernel(nq, *a),
        out_shape=(jax.ShapeDtypeStruct((384 * 16, 2 * HID), F32), jax.ShapeDtypeStruct((384 * 16, HID), F32)),
        in_specs=[pl.BlockSpec(memory_space=pltpu.VMEM)] * 4,
        out_specs=[pl.BlockSpec(memory_space=pl.ANY)] * 2,
        scratch_shapes=[
            pltpu.VMEM((3, 4, 2) + piece, BF),
            pltpu.VMEM((nq, 2) + piece, BF),
            pltpu.VMEM((2,) + piece, BF),
            pltpu.VMEM((nq,) + piece, BF),
            pltpu.VMEM((2,) + piece, BF),
            pltpu.VMEM((nq,) + piece, BF),
            pltpu.VMEM((nq, 4, 256, wide), BF),
            pltpu.VMEM((nq, 4, 256, wide), BF),
            pltpu.VMEM((wide // 128, 256, 128), F32),
            pltpu.VMEM((4, 256, wide), F32),
            sem((nq, 2)), sem((nq, 2)), sem((nq,)), sem((nq,)), sem((nq, 3)), sem((nq, 3)),
            sem((nq, 3)), sem((nq, 3)), sem((nq, 4)), sem((nq, 4)), sem((4, 3)),
        ],
        compiler_params=pltpu.CompilerParams(
            collective_id=3, has_side_effects=True, vmem_limit_bytes=62 * 1024 * 1024),
        name="expert_grads",
    )(xs, dys, ggu, hw)


def turn(v, cos, sin):
    lane = lax.broadcasted_iota(jnp.int32, v.shape, 1)
    partner = jnp.where(lax.rem(lane, 64) < 32, pltpu.roll(v, 96, 1), pltpu.roll(v, 32, 1))
    return v * cos + partner * sin


def front_kernel(tok, dy, wpiece, qkv_cols, proj, small, masks, prefix, cos_t, sin_t,
                 o_x, o_dy, o_ggu, o_hw, o_act, o_q, o_k, o_v, o_probs, o_att, o_qkvw, o_projw,
                 o_small, o_res, o_gates, o_gact, o_gg, o_out,
                 smalls, qkvw, projw, actp, pre, pr, qs, ks, vs, probs, att, part, sibr, sums, plr,
                 xall, dyall, wgt, wbuf, ggu, hw, gpart, opart, ggp, gsib, osib, ggsib,
                 gsum, osum, ggsum, grecv, orecv, ggrecv, res, gates, gact, ggt, outb,
                 s_small, r_small, s_qkv, r_qkv, s_proj, r_proj, s_wz, r_wz, s_wp, r_wp,
                 s_act, r_act, s_pre, r_pre, s_actc, r_actc, s_prec, r_prec, s_sib, r_sib, s_pl, r_pl,
                 s_x, r_x, s_xc, r_xc, s_y, r_y, s_yc, r_yc, s_w, r_w, s_wc, r_wc,
                 s_g, r_g, s_o, r_o, s_gg, r_gg, s_gc, r_gc, s_oc, r_oc, s_ggc, r_ggc, sl):
    y, x, c, z = place()
    half = HID // 2

    def slot(a, b):
        return flip(y, a * c + b * (1 - c)) * 2 + flip(x, a * (1 - c) + b * c)

    p0, p1, p2, p3 = slot(0, 0), slot(1, 0), slot(0, 1), slot(1, 1)
    peers = (p1, p2, p3)
    d1, d2, dsib = (p1 * 2 + c, z), (p2 * 2 + c, z), (p0 * 2 + 1 - c, z)
    dpl = [(p * 2 + c, z) for p in peers]
    zk = [lax.rem(z + k, 4) for k in range(4)]
    zf = [lax.rem(z + 4 - k, 4) for k in range(4)]
    dz = [(p0 * 2 + c, zz) for zz in zk]

    barrier = pltpu.get_barrier_semaphore()
    for to in dpl + dz[1:] + [dsib]:
        pl.semaphore_signal(barrier, 1, device_id=to, device_id_type=MESH)
    pl.semaphore_wait(barrier, 7)

    def remote(src, dst, s, r, to):
        return pltpu.make_async_remote_copy(src, dst, s, r, device_id=to, device_id_type=MESH)

    def c_small(k):
        return remote(small, smalls.at[z], s_small.at[k - 1], r_small.at[k - 1], dz[k])

    def c_qkv(k):
        return remote(qkv_cols, qkvw.at[pl.ds(pl.multiple_of(z * 384, 384), 384)],
                      s_qkv.at[k - 1], r_qkv.at[k - 1], dz[k])

    def rows(zz, pp):
        return pl.ds(pl.multiple_of(zz * 384 + pp * 96, 96), 96)

    def c_wz(k):
        return remote(wpiece.at[zk[k]], wbuf.at[:, rows(z, p0)], s_wz.at[k - 1], r_wz.at[k - 1], dz[k])

    def c_wp(k, i):
        zz = zf[k]
        who, pp = ((d1, p0), (d2, p0), (d2, p1))[i]
        src = wpiece.at[z] if (k == 0 and i < 2) else wbuf.at[:, rows(zz, pp)]
        return remote(src, wbuf.at[:, rows(zz, pp)], s_wp.at[k, i], r_wp.at[k, i], who)

    up_ok, down_ok = (z >= p0) & (z < 3), (z <= p0) & (z > 0)

    def c_proj(src, d):
        return remote(src, projw, s_proj.at[d], r_proj, (p0 * 2 + c, z + 1 if d == 0 else z - 1))

    def c_act(i):
        return remote(actp.at[c, p0], actp.at[c, p0], s_act.at[i], r_act.at[i], dpl[i])

    def c_pre(i):
        return remote(pre.at[c, p0], pre.at[c, p0], s_pre.at[i], r_pre.at[i], dpl[i])

    def c_actc(i):
        p = (p0, p1, p2, p3)[i]
        return remote(actp.at[c, p], actp.at[c, p], s_actc.at[i], r_actc.at[i], dsib)

    def c_prec(i):
        p = (p0, p1, p2, p3)[i]
        return remote(pre.at[c, p], pre.at[c, p], s_prec.at[i], r_prec.at[i], dsib)

    def c_sib():
        return remote(part, sibr, s_sib, r_sib, dsib)

    def c_pl(i):
        return remote(sums.at[i], plr.at[i], s_pl.at[i], r_pl.at[i], dpl[i])

    def column(buf, s, r, sc, rc):
        def along(k):
            return remote(buf.at[c, z], buf.at[c, z], s.at[k - 1], r.at[k - 1], dz[k])

        def across(k):
            return remote(buf.at[c, zf[k]], buf.at[c, zf[k]], sc.at[k], rc.at[k], dsib)
        return along, across

    x_z, x_c = column(xall, s_x, r_x, s_xc, r_xc)
    y_z, y_c = column(dyall, s_y, r_y, s_yc, r_yc)
    w_z, w_c = column(wgt, s_w, r_w, s_wc, r_wc)

    def back(src, dst, s, r):
        return lambda k: remote(src.at[zk[k]], dst.at[k - 1], s.at[k - 1], r.at[k - 1], dz[k])

    g_z, o_z, gg_z = back(gsum, grecv, s_g, r_g), back(osum, orecv, s_o, r_o), back(ggsum, ggrecv, s_gg, r_gg)
    g_c = remote(gpart, gsib, s_gc, r_gc, dsib)
    o_c = remote(opart, osib, s_oc, r_oc, dsib)
    gg_c = remote(ggp.at[1 - c], ggsib, s_ggc, r_ggc, dsib)

    def weights_a(k):
        if k:
            c_wz(k).wait_recv()
        c_wp(k, 0).start()

    def weights_b(k):
        c_wp(k, 0).wait_recv()
        c_wp(k, 1).start()
        c_wp(k, 2).start()

    for k in (1, 2, 3):
        c_small(k).start()
    local = [pltpu.make_async_copy(small, smalls.at[z], sl.at[0]),
             pltpu.make_async_copy(qkv_cols, qkvw.at[pl.ds(pl.multiple_of(z * 384, 384), 384)], sl.at[1]),
             pltpu.make_async_copy(wpiece.at[z], wbuf.at[:, rows(z, p0)], sl.at[2]),
             pltpu.make_async_copy(dy, dyall.at[c, z], sl.at[3])]
    for one in local:
        one.start()
    for k in (1, 2, 3):
        c_qkv(k).start()
    my_proj = proj.at[pl.ds(pl.multiple_of(c * 192, 192), 192)]
    own_proj = pltpu.make_async_copy(my_proj, projw, sl.at[4])

    @pl.when(z == p0)
    def _():
        own_proj.start()

        @pl.when(z < 3)
        def _():
            c_proj(my_proj, 0).start()

        @pl.when(z > 0)
        def _():
            c_proj(my_proj, 1).start()
    weights_a(0)
    for k in (1, 2, 3):
        c_wz(k).start()

    tok_f = tok[...].astype(F32)
    inv1 = lax.rsqrt(jnp.mean(tok_f * tok_f, axis=1, keepdims=True) + EPS)
    for k in (1, 2, 3):
        c_small(k).wait_recv()
    local[0].wait()
    gain1 = jnp.concatenate([smalls[i, 0:1, :] for i in range(4)], axis=1).astype(F32)
    actp[c, p0] = (tok_f * inv1 * gain1).astype(BF)
    pre[c, p0] = prefix[...]
    for i in range(3):
        c_act(i).start()
        c_pre(i).start()
    c_actc(0).start()
    c_prec(0).start()

    @pl.when(z == p0)
    def _():
        own_proj.wait()

    @pl.when(z != p0)
    def _():
        c_proj(projw, 0).wait_recv()

    @pl.when((z > p0) & (z < 3))
    def _():
        c_proj(projw, 0).start()

    @pl.when((z < p0) & (z > 0))
    def _():
        c_proj(projw, 1).start()

    weights_b(0)
    for i in range(3):
        c_act(i).wait_recv()
        c_pre(i).wait_recv()
        c_actc(i + 1).start()
        c_prec(i + 1).start()
    for k in (1, 2, 3):
        c_qkv(k).wait_recv()
    local[1].wait()
    local[3].wait()
    for k in (1, 2, 3):
        y_z(k).start()
    y_c(0).start()

    row = lax.broadcasted_iota(jnp.int32, (128, 128), 0)
    col = lax.broadcasted_iota(jnp.int32, (128, 128), 1)
    causal = col <= row
    col_f = col.astype(F32)

    def attention(cc):
        pr[...] = jnp.dot(actp[cc].reshape(512, 1536), qkvw[...], preferred_element_type=F32).reshape(4, 128, 320)

        def one(i, _):
            lo = turn(pr[i, :, 0:128], cos_t[...], sin_t[...]).astype(BF)
            hi = turn(pr[i, :, 128:256], cos_t[...], sin_t[...]).astype(BF)
            qs[cc, i, 0:128] = lo[:, 0:64]
            qs[cc, i, 128:256] = lo[:, 64:128]
            qs[cc, i, 256:384] = hi[:, 0:64]
            ks[cc, i] = hi[:, 64:128]
            vs[cc, i] = pr[i, :, 256:320].astype(BF)
            sc = lax.dot_general(qs[cc, i], ks[cc, i], (((1,), (1,)), ((), ())), preferred_element_type=F32)
            allowed = causal | (col_f < pre[cc, i, 0:1, :])
            sc = jnp.where(allowed[None], sc.reshape(3, 128, 128) * (64 ** -0.5), -1e30)
            ex = jnp.exp(sc - jnp.max(sc, axis=-1, keepdims=True))
            pb = (ex / jnp.sum(ex, axis=-1, keepdims=True)).reshape(384, 128)
            probs[cc, i] = pb
            at = jnp.dot(pb.astype(BF), vs[cc, i], preferred_element_type=F32).astype(BF)
            for h in range(3):
                att[cc, i, :, h * 64 : (h + 1) * 64] = at[h * 128 : (h + 1) * 128]
            return 0
        lax.fori_loop(0, 4, one, 0)

    attention(c)
    weights_a(1)
    for i in range(4):
        c_actc(i).wait_recv()
        c_prec(i).wait_recv()
    attention(1 - c)

    def to_sib(i, _):
        part[i] = jnp.dot(att[1 - c, i], projw[...], preferred_element_type=F32).astype(BF)
        return 0
    lax.fori_loop(0, 4, to_sib, 0)
    c_sib().start()
    weights_b(1)
    c_sib().wait_recv()
    for i in range(3):
        sums[i] = (jnp.dot(att[c, peers[i]], projw[...], preferred_element_type=F32)
                   + sibr[peers[i]].astype(F32)).astype(BF)
        c_pl(i).start()
    residual = (tok_f + jnp.dot(att[c, p0], projw[...], preferred_element_type=F32) + sibr[p0].astype(F32))
    weights_a(2)
    for i in range(3):
        c_pl(i).wait_recv()
        residual = residual + plr[i].astype(F32)
    res[...] = residual
    inv2 = lax.rsqrt(jnp.mean(residual * residual, axis=1, keepdims=True) + EPS)
    gain2 = jnp.concatenate([smalls[i, 1:2, :] for i in range(4)], axis=1).astype(F32)
    act2 = (residual * inv2 * gain2).astype(BF)
    xall[c, z] = act2
    for k in (1, 2, 3):
        x_z(k).start()
    x_c(0).start()
    router = jnp.concatenate([smalls[i, 16:32, :] for i in range(4)], axis=1)
    logits = lax.dot_general(act2, router, (((1,), (1,)), ((), ())), preferred_element_type=F32)
    chosen, kept = masks[0] > 0.0, masks[1]
    top = jnp.max(jnp.where(chosen, logits, -1e30), axis=1, keepdims=True)
    ge = jnp.where(chosen, jnp.exp(jnp.where(chosen, logits - top, 0.0)), 0.0)
    gt = ge / jnp.sum(ge, axis=1, keepdims=True)
    gates[...] = gt
    wgt[c, z] = jnp.concatenate([gt * kept, jnp.zeros((128, 112), F32)], axis=1)
    for k in (1, 2, 3):
        w_z(k).start()
    w_c(0).start()
    weights_b(2)
    weights_a(3)
    for k in (1, 2, 3):
        y_z(k).wait_recv()
        y_c(k).start()
    weights_b(3)
    for k in (1, 2, 3):
        x_z(k).wait_recv()
        x_c(k).start()
        w_z(k).wait_recv()
        w_c(k).start()
    local[2].wait()
    for k in range(4):
        c_wp(k, 1).wait_recv()
        c_wp(k, 2).wait_recv()
    for k in range(4):
        x_c(k).wait_recv()
        y_c(k).wait_recv()
        w_c(k).wait_recv()

    lane = lax.broadcasted_iota(jnp.int32, (512, 128), 1)
    ggp[...] = jnp.zeros_like(ggp)

    def expert(n, _):
        j, t = n // 2, lax.rem(n, 2)
        gu = jnp.dot(xall[t].reshape(512, 1536), wbuf[j, :, : 2 * half], preferred_element_type=F32)
        bk = jnp.dot(dyall[t].reshape(512, 1536), wbuf[j, :, 2 * half :], preferred_element_type=F32)
        mine = lane == z * 4 + j
        w = jnp.sum(jnp.where(mine, wgt[t].reshape(512, 128), 0.0), axis=1, keepdims=True)
        g, u = gu[:, :half], gu[:, half:]
        sg = 1.0 / (1.0 + jnp.exp(-g))
        silu = g * sg
        hid = silu * u
        hw[j, pl.ds(pl.multiple_of(t * 512, 512), 512)] = (hid * w).astype(BF)
        ggp[t] = ggp[t] + jnp.where(mine, jnp.sum(bk * hid, axis=1, keepdims=True), 0.0).reshape(4, 128, 128)
        gh = bk * w
        at = pl.ds(pl.multiple_of(t * 512, 512), 512)
        ggu[j, at, :half] = (gh * u * sg * (1.0 + g * (1.0 - sg))).astype(BF)
        ggu[j, at, half:] = (gh * silu).astype(BF)
        return 0
    lax.fori_loop(0, 8, expert, 0)
    saves = []

    def save(src, dst):
        one = pltpu.make_async_copy(src, dst, sl.at[5 + len(saves)])
        one.start()
        saves.append(one)
    for src, dst in ((xall, o_x), (dyall, o_dy), (ggu, o_ggu), (hw, o_hw), (actp, o_act), (qs, o_q), (ks, o_k),
                     (vs, o_v), (probs, o_probs), (att, o_att), (qkvw, o_qkvw), (projw, o_projw),
                     (smalls, o_small), (res, o_res), (gates, o_gates)):
        save(src, dst)

    def block(grad, t, n):
        at = pl.ds(pl.multiple_of(t * 512, 512), 512)
        lanes = pl.ds(pl.multiple_of(n * 256, 256), 256)
        acc = jnp.zeros((512, 256), F32)
        for j in range(4):
            a = ggu[j, at] if grad else hw[j, at]
            b = wbuf[j, lanes, : 2 * half] if grad else wbuf[j, lanes, 2 * half :]
            acc = acc + lax.dot_general(a, b, (((1,), (1,)), ((), ())), preferred_element_type=F32)
        return acc.reshape(4, 128, 256), lanes

    def partial(grad, buf):
        def one(n, _):
            v, lanes = block(grad, 1 - c, n)
            buf[:, :, lanes] = v.astype(BF)
            return 0
        lax.fori_loop(0, 6, one, 0)

    def own(grad, sib, dst):
        def one(n, _):
            v, lanes = block(grad, c, n)
            dst[:, :, lanes] = (v + sib[:, :, lanes].astype(F32)).astype(BF)
            return 0
        lax.fori_loop(0, 6, one, 0)

    gg_c.start()
    partial(True, gpart)
    g_c.start()
    gg_c.wait_recv()
    for k in range(4):
        ggsum[zk[k]] = ggp[c, zk[k]] + ggsib[zk[k]]
    for k in (1, 2, 3):
        gg_z(k).start()
    partial(False, opart)
    o_c.start()
    g_c.wait_recv()
    own(True, gsib, gsum)
    for k in (1, 2, 3):
        g_z(k).start()
    o_c.wait_recv()
    own(False, osib, osum)
    for k in (1, 2, 3):
        o_z(k).start()
    for k in (1, 2, 3):
        gg_z(k).wait_recv()
        g_z(k).wait_recv()
    ggt[...] = (ggsum[z] + ggrecv[0] + ggrecv[1] + ggrecv[2])[:, :EXPERTS]
    save(ggt, o_gg)
    gact[...] = (gsum[z].astype(F32) + grecv[0].astype(F32) + grecv[1].astype(F32) + grecv[2].astype(F32))
    save(gact, o_gact)
    for k in (1, 2, 3):
        o_z(k).wait_recv()
    outb[...] = (res[...] + osum[z].astype(F32) + orecv[0].astype(F32) + orecv[1].astype(F32)
                 + orecv[2].astype(F32)).astype(BF)
    save(outb, o_out)

    for k in (1, 2, 3):
        for one in (c_small(k), c_qkv(k), c_wz(k), x_z(k), y_z(k), w_z(k), g_z(k), o_z(k), gg_z(k)):
            one.wait_send()
    for k in range(4):
        for i in range(3):
            c_wp(k, i).wait_send()
        for one in (c_actc(k), c_prec(k), x_c(k), y_c(k), w_c(k)):
            one.wait_send()
    for i in range(3):
        for one in (c_act(i), c_pre(i), c_pl(i)):
            one.wait_send()
    for one in (c_sib(), g_c, o_c, gg_c):
        one.wait_send()

    @pl.when(up_ok)
    def _():
        c_proj(projw, 0).wait_send()

    @pl.when(down_ok)
    def _():
        c_proj(projw, 1).wait_send()
    for one in saves:
        one.wait()


def front(tok, dy, wpiece, qkv_cols, proj, small, masks, prefix, cos_t, sin_t):
    sem, vm = pltpu.SemaphoreType.DMA, pltpu.VMEM
    out = lambda shape, kind=BF: jax.ShapeDtypeStruct(shape, kind)
    outs = (
        out((2, 4, 128, 1536)), out((2, 4, 128, 1536)), out((4, 1024, 512)), out((4, 1024, 256)),
        out((2, 4, 128, 1536)), out((2, 4, 384, 64)), out((2, 4, 128, 64)), out((2, 4, 128, 64)),
        out((2, 4, 384, 128), F32), out((2, 4, 128, 192)), out((1536, 320)), out((192, 1536)),
        out((4, 32, 384)), out((128, 1536), F32), out((128, 16), F32), out((128, 1536), F32),
        out((128, 16), F32), out((128, 1536)),
    )
    block, quad = vm((2, 4, 128, 1536), BF), vm((4, 128, 1536), BF)
    three = vm((3, 128, 1536), BF)
    scratch = [
        vm((4, 32, 384), BF), vm((1536, 320), BF), vm((192, 1536), BF), block, vm((2, 4, 8, 128), F32),
        vm((4, 128, 320), F32), vm((2, 4, 384, 64), BF), vm((2, 4, 128, 64), BF), vm((2, 4, 128, 64), BF),
        vm((2, 4, 384, 128), F32), vm((2, 4, 128, 192), BF), quad, quad, three, three,
        block, block, vm((2, 4, 128, 128), F32), vm((4, 1536, 768), BF), vm((4, 1024, 512), BF),
        vm((4, 1024, 256), BF), quad, quad, vm((2, 4, 128, 128), F32), quad, quad, vm((4, 128, 128), F32),
        quad, quad, vm((4, 128, 128), F32), three, three, vm((3, 128, 128), F32),
        vm((128, 1536), F32), vm((128, 16), F32), vm((128, 1536), F32), vm((128, 16), F32), vm((128, 1536), BF),
    ]
    n3, n4 = sem((3,)), sem((4,))
    one = sem(())
    sems = [
        n3, n3, n3, n3, sem((2,)), one, n3, n3, sem((4, 3)), sem((4, 3)),
        n3, n3, n3, n3, n4, n4, n4, n4, one, one, n3, n3,
        n3, n3, n4, n4, n3, n3, n4, n4, n3, n3, n4, n4,
        n3, n3, n3, n3, n3, n3, one, one, one, one, one, one, sem((24,)),
    ]
    vmem, any_ = pl.BlockSpec(memory_space=pltpu.VMEM), pl.BlockSpec(memory_space=pl.ANY)
    return pl.pallas_call(
        front_kernel,
        out_shape=outs,
        in_specs=[vmem, any_, any_, any_, any_, any_, vmem, vmem, vmem, vmem],
        out_specs=[any_] * len(outs),
        scratch_shapes=scratch + sems,
        compiler_params=pltpu.CompilerParams(
            collective_id=1, has_side_effects=True, vmem_limit_bytes=62 * 1024 * 1024),
        name="front",
    )(tok, dy, wpiece, qkv_cols, proj, small, masks, prefix, cos_t, sin_t)


def expert_grads_general(reps, grps, xs, dys, ggu, hw):
    local, half, width = ggu.shape[0], HID // 2, xs.shape[1]
    own = width // grps
    chips = reps // 2
    piece = own // chips
    same_core = [[2 * i + c for i in range(chips)] for c in range(2)]
    pairs = [[2 * i, 2 * i + 1] for i in range(chips)]
    up = jnp.einsum("td,eth->edh", xs, ggu, preferred_element_type=F32).astype(BF)
    down = jnp.einsum("td,eth->edh", dys, hw, preferred_element_type=F32).astype(BF)
    gw = jnp.concatenate([up, down], axis=2)
    gw = gw.reshape(local, grps, chips, piece, 3 * half).transpose(2, 1, 3, 0, 4)
    gw = gw.reshape(chips * grps * piece, local * 3 * half)
    gw = lax.psum_scatter(gw, "rep", scatter_dimension=0, tiled=True, axis_index_groups=same_core)
    gw = lax.all_to_all(gw.reshape(grps, piece, local, 3 * half), "grp", 0, 0, tiled=True)
    gw = gw.transpose(1, 0, 2, 3).reshape(piece, EXPERTS, 3 * half)
    gw = lax.all_gather(gw, "rep", axis=0, tiled=True, axis_index_groups=same_core)
    gw = lax.all_gather(gw, "rep", axis=0, tiled=False, axis_index_groups=pairs).astype(F32)
    gw = gw.reshape(2, own * EXPERTS, 3, half)
    gw = jnp.moveaxis(gw, 0, 2).reshape(own * EXPERTS, 3 * HID)
    return gw[:, : 2 * HID], gw[:, 2 * HID :]


def shards_general(
    reps,
    grps,
    tokens,
    attn_gain,
    query_key_value_weight,
    attn_proj,
    mlp_gain,
    w_router,
    w_gate_up,
    w_down,
    prefix_len,
    expert_ids,
    priority,
    cotangent,
):
    seq, width = tokens.shape
    own = width // grps
    local_experts = EXPERTS // grps
    heads = KEY_VALUE_HEADS
    groups = None if reps == heads else [list(range(i, i + heads)) for i in range(0, reps, heads)]
    rep, grp = lax.axis_index("rep"), lax.axis_index("grp")
    head = lax.rem(rep, heads)
    qw, hw = QPK * HEAD_WIDTH, HEAD_WIDTH
    q_all = QUERY_HEADS * HEAD_WIDTH

    small = jnp.concatenate([attn_gain[:, None], mlp_gain[:, None], w_router], axis=1)
    small = lax.all_gather(small, "grp", axis=0, tiled=True)
    gain_one, gain_two = small[:, 0].astype(F32)[None, :], small[:, 1].astype(F32)[None, :]
    router = small[:, 2:]
    qkv_cols = jnp.concatenate(
        [
            lax.dynamic_slice_in_dim(query_key_value_weight, head * qw, qw, 1),
            lax.dynamic_slice_in_dim(query_key_value_weight, q_all + head * hw, hw, 1),
            lax.dynamic_slice_in_dim(query_key_value_weight, q_all + heads * hw + head * hw, hw, 1),
        ],
        axis=1,
    )
    qkv_head = lax.all_gather(qkv_cols, "grp", axis=0, tiled=True)
    row = head * qw + jnp.arange(qw)
    mine = (row // own) == grp
    proj_rows = jnp.where(mine[:, None], jnp.take(attn_proj, jnp.where(mine, row - grp * own, 0), axis=0), 0)
    proj_head = lax.psum(proj_rows, "grp")

    core, chip, chips, half = lax.rem(rep, 2), rep // 2, reps // 2, HID // 2
    pairs = [[2 * i, 2 * i + 1] for i in range(chips)]
    same_core = [[2 * i + c for i in range(chips)] for c in range(2)]
    piece = own // chips
    gu_piece = lax.dynamic_slice_in_dim(w_gate_up, chip * piece, piece, 0)
    dn_piece = lax.dynamic_slice_in_dim(w_down, chip * piece, piece, 0)
    both = jnp.concatenate(
        [
            lax.dynamic_slice_in_dim(gu_piece, core * half, half, 2),
            lax.dynamic_slice_in_dim(gu_piece, HID + core * half, half, 2),
            lax.dynamic_slice_in_dim(dn_piece, core * half, half, 2),
        ],
        axis=2,
    )
    both = both.reshape(piece, grps, local_experts, 3 * half).transpose(1, 2, 0, 3)
    both = lax.all_to_all(both, "grp", 0, 0, tiled=True)
    both = lax.all_gather(both, "rep", axis=0, tiled=False, axis_index_groups=same_core)
    both = both.transpose(2, 1, 0, 3, 4).reshape(local_experts, width, 3 * half)
    wgu, wdn = both[:, :, : 2 * half], both[:, :, 2 * half :]

    tokens_f = tokens.astype(F32)
    inverse_one = lax.rsqrt(jnp.mean(tokens_f * tokens_f, axis=1, keepdims=True) + EPS)
    normed_one = tokens_f * inverse_one
    act_one = (normed_one * gain_one).astype(BF)
    act_plane = lax.all_gather(act_one, "rep", axis=0, tiled=True, axis_index_groups=groups)
    prefix_plane = lax.all_gather(prefix_len, "rep", axis=0, tiled=True, axis_index_groups=groups)
    cos, sin = rope_tables(seq)
    projected = dot(act_plane, qkv_head).reshape(heads, seq, QPK + 2, HEAD_WIDTH)
    cos_b, sin_b = cos[None, :, None, :], sin[None, :, None, :]
    turned = rotate(projected[:, :, : QPK + 1], cos_b, sin_b).astype(BF)
    query = turned[:, :, :QPK]
    key = turned[:, :, QPK]
    value = projected[:, :, QPK + 1].astype(BF)
    scale = HEAD_WIDTH ** (-0.5)
    row_pos, col_pos = jnp.arange(seq)[:, None], jnp.arange(seq)[None, :]
    allowed = (col_pos <= row_pos)[None] | (col_pos[None] < prefix_plane[:, None, None])
    scores = jnp.einsum("bsgd,btd->bgst", query, key, preferred_element_type=F32) * scale
    scores = jnp.where(allowed[:, None], scores, -1e30)
    exps = jnp.exp(scores - jnp.max(scores, axis=-1, keepdims=True))
    probs = exps / jnp.sum(exps, axis=-1, keepdims=True)
    probs_low = probs.astype(BF)
    attended = jnp.einsum("bgst,btd->bsgd", probs_low, value, preferred_element_type=F32)
    attended = attended.astype(BF).reshape(heads * seq, qw)
    part = dot(attended, proj_head).astype(BF)
    part = lax.psum_scatter(part, "rep", scatter_dimension=0, tiled=True, axis_index_groups=groups)
    residual = tokens_f + part.astype(F32)
    inverse_two = lax.rsqrt(jnp.mean(residual * residual, axis=1, keepdims=True) + EPS)
    normed_two = residual * inverse_two
    act_two = (normed_two * gain_two).astype(BF)
    gates, kept = routing(expert_ids, priority, dot(act_two, router))

    def column(v):
        v = lax.all_gather(v, "grp", axis=0, tiled=True)
        return lax.all_gather(v, "rep", axis=0, tiled=True, axis_index_groups=pairs)

    def to_owners(v):
        v = lax.psum_scatter(v, "rep", scatter_dimension=0, tiled=True, axis_index_groups=pairs)
        return lax.psum_scatter(v, "grp", scatter_dimension=0, tiled=True).astype(F32)

    dy_all = column(cotangent)
    x_all = column(act_two)
    weight = column(jnp.where(kept, gates, 0.0))
    weight = lax.dynamic_slice_in_dim(weight, grp * local_experts, local_experts, 1).T[:, :, None]
    gate_up = jnp.einsum("td,edh->eth", x_all, wgu, preferred_element_type=F32)
    g, u = gate_up[..., :half], gate_up[..., half:]
    sig = jax.nn.sigmoid(g)
    silu = g * sig
    hidden = silu * u
    hidden_w = (hidden * weight).astype(BF)
    back = jnp.einsum("td,edh->eth", dy_all, wdn, preferred_element_type=F32)
    grad_gate_part = jnp.sum(back * hidden, axis=2)
    grad_hidden = back * weight
    ggu = jnp.concatenate(
        [grad_hidden * u * sig * (1.0 + g * (1.0 - sig)), grad_hidden * silu], axis=2
    ).astype(BF)
    out_part = jnp.einsum("eth,edh->td", hidden_w, wdn, preferred_element_type=F32).astype(BF)
    gact_part = jnp.einsum("eth,edh->td", ggu, wgu, preferred_element_type=F32).astype(BF)
    gact = to_owners(gact_part)
    grad_gates = lax.psum_scatter(
        grad_gate_part.T, "rep", scatter_dimension=0, tiled=True, axis_index_groups=pairs
    )
    grad_gates = lax.all_to_all(grad_gates, "grp", 0, 1, tiled=True)
    grad_gates = jnp.where(kept, grad_gates, 0.0)
    out = to_owners(out_part)
    output = (residual + out).astype(BF)
    grad_gu, grad_dn = expert_grads_general(reps, grps, x_all, dy_all, ggu, hidden_w)
    grad_gu = grad_gu.reshape(own, EXPERTS, 2 * HID)
    grad_dn = grad_dn.reshape(own, EXPERTS, HID)

    grad_logits = (gates * (grad_gates - jnp.sum(gates * grad_gates, axis=1, keepdims=True))).astype(BF)
    gact = gact + dot(grad_logits, router.T)
    router_term = dot(act_two.T, grad_logits)
    gain_two_term = jnp.sum(gact * normed_two, axis=0)
    scaled = gact * gain_two
    dy = cotangent.astype(F32)
    grad_residual = dy + inverse_two * (
        scaled - normed_two * jnp.mean(scaled * normed_two, axis=1, keepdims=True)
    )
    gres_low = grad_residual.astype(BF)

    gres_plane = lax.all_gather(gres_low, "rep", axis=0, tiled=True, axis_index_groups=groups)
    proj_term = dot(attended.T, gres_plane)
    grad_att = dot(gres_plane, proj_head.T).astype(BF).reshape(heads, seq, QPK, HEAD_WIDTH)
    grad_value = jnp.einsum("bgst,bsgd->btd", probs_low, grad_att, preferred_element_type=F32)
    grad_probs = jnp.einsum("bsgd,btd->bgst", grad_att, value, preferred_element_type=F32)
    grad_scores = (
        probs * (grad_probs - jnp.sum(probs * grad_probs, axis=-1, keepdims=True))
    ).astype(BF)
    grad_query = jnp.einsum("bgst,btd->bsgd", grad_scores, key, preferred_element_type=F32) * scale
    grad_key = jnp.einsum("bgst,bsgd->btd", grad_scores, query, preferred_element_type=F32) * scale
    turned_back = rotate(
        jnp.concatenate([grad_query, grad_key[:, :, None]], axis=2), cos_b, -sin_b
    )
    gproj = jnp.concatenate([turned_back, grad_value[:, :, None]], axis=2).astype(BF)
    gproj = gproj.reshape(heads * seq, qw + 2 * hw)
    qkv_term = dot(act_plane.T, gproj)
    gact_one = dot(gproj, qkv_head.T).astype(BF)
    gact_one = lax.psum_scatter(
        gact_one, "rep", scatter_dimension=0, tiled=True, axis_index_groups=groups
    ).astype(F32)
    gain_one_term = jnp.sum(gact_one * normed_one, axis=0)
    scaled_one = gact_one * gain_one
    grad_tokens = grad_residual + inverse_one * (
        scaled_one - normed_one * jnp.mean(scaled_one * normed_one, axis=1, keepdims=True)
    )

    qkv_own = lax.psum_scatter(qkv_term.astype(BF), "grp", scatter_dimension=0, tiled=True)
    proj_sum = lax.psum(proj_term.astype(BF), "grp")
    if groups is not None:
        across = [[i + heads * j for j in range(reps // heads)] for i in range(heads)]
        qkv_own = lax.psum(qkv_own, "rep", axis_index_groups=across)
        proj_sum = lax.psum(proj_sum, "rep", axis_index_groups=across)
    qkv_own = lax.all_gather(qkv_own, "rep", axis=0, tiled=False, axis_index_groups=groups)
    qkv_own = qkv_own.astype(F32)
    grad_qkv = jnp.concatenate(
        [
            qkv_own[:, :, lo:hi].transpose(1, 0, 2).reshape(own, -1)
            for lo, hi in ((0, qw), (qw, qw + hw), (qw + hw, qw + 2 * hw))
        ],
        axis=1,
    )
    proj_all = lax.all_gather(proj_sum, "rep", axis=0, tiled=True, axis_index_groups=groups)
    grad_proj = lax.dynamic_slice_in_dim(proj_all, grp * own, own, 0).astype(F32)
    terms = jnp.concatenate([gain_one_term[:, None], gain_two_term[:, None], router_term], axis=1)
    terms = lax.psum(lax.psum_scatter(terms, "grp", scatter_dimension=0, tiled=True), "rep")
    return (
        output,
        grad_tokens,
        terms[:, 0],
        grad_qkv,
        grad_proj,
        terms[:, 1],
        terms[:, 2:],
        grad_gu,
        grad_dn,
    )


def shards(
    tokens,
    attn_gain,
    query_key_value_weight,
    attn_proj,
    mlp_gain,
    w_router,
    w_gate_up,
    w_down,
    prefix_len,
    expert_ids,
    priority,
    cotangent,
):
    heads, half, own = KEY_VALUE_HEADS, HID // 2, attn_gain.shape[0]
    qw, hw, q_all = QPK * HEAD_WIDTH, HEAD_WIDTH, QUERY_HEADS * HEAD_WIDTH
    rep = lax.axis_index("rep")
    core, chip = lax.rem(rep, 2), rep // 2
    seq, width = tokens.shape
    small = jnp.concatenate(
        [attn_gain[None], mlp_gain[None], jnp.zeros((14, own), BF), w_router.T], axis=0
    )
    qkv_cols = jnp.concatenate(
        [
            lax.dynamic_slice_in_dim(query_key_value_weight, rep * qw, qw, 1),
            lax.dynamic_slice_in_dim(query_key_value_weight, q_all + rep * hw, hw, 1),
            lax.dynamic_slice_in_dim(query_key_value_weight, q_all + heads * hw + rep * hw, hw, 1),
        ],
        axis=1,
    )
    piece = own // 4
    gu_piece = lax.dynamic_slice_in_dim(w_gate_up, chip * piece, piece, 0)
    dn_piece = lax.dynamic_slice_in_dim(w_down, chip * piece, piece, 0)
    both = jnp.concatenate(
        [
            lax.dynamic_slice_in_dim(gu_piece, core * half, half, 2),
            lax.dynamic_slice_in_dim(gu_piece, HID + core * half, half, 2),
            lax.dynamic_slice_in_dim(dn_piece, core * half, half, 2),
        ],
        axis=2,
    )
    wpiece = both.transpose(1, 0, 2).reshape(4, 4, piece, 3 * half)
    chosen, kept = choices(expert_ids, priority)
    masks = jnp.stack([chosen, kept]).astype(F32)
    prefix = jnp.broadcast_to(prefix_len.astype(F32), (8, 128))
    cos, sin = rope_tables(seq)
    cos_t, sin_t = jnp.tile(cos, (1, 4)), jnp.tile(jnp.concatenate([-sin, sin], axis=1), (1, 2))
    (x_all, dy_all, ggu, hidden_w, act_plane, query, key, value, probs, attended, qkv_head, proj_head,
     smalls, residual, gates, gact, grad_gates, output) = front(
        tokens, cotangent, wpiece, qkv_cols, attn_proj, small, masks, prefix, cos_t, sin_t)
    grad_gu, grad_dn = expert_grads(x_all.reshape(1024, width), dy_all.reshape(1024, width), ggu, hidden_w)
    grad_gu = grad_gu.reshape(own, EXPERTS, 2 * HID)
    grad_dn = grad_dn.reshape(own, EXPERTS, HID)

    gain_one = smalls[:, 0].reshape(1, width).astype(F32)
    gain_two = smalls[:, 1].reshape(1, width).astype(F32)
    router_t = jnp.concatenate([smalls[i, 16:] for i in range(4)], axis=1)
    tokens_f = tokens.astype(F32)
    inverse_one = lax.rsqrt(jnp.mean(tokens_f * tokens_f, axis=1, keepdims=True) + EPS)
    normed_one = tokens_f * inverse_one
    inverse_two = lax.rsqrt(jnp.mean(residual * residual, axis=1, keepdims=True) + EPS)
    normed_two = residual * inverse_two
    act_two = (normed_two * gain_two).astype(BF)

    grad_gates = grad_gates * masks[1]
    grad_logits = (gates * (grad_gates - jnp.sum(gates * grad_gates, axis=1, keepdims=True))).astype(BF)
    gact = gact + dot(grad_logits, router_t)
    router_term = dot(act_two.T, grad_logits)
    gain_two_term = jnp.sum(gact * normed_two, axis=0)
    scaled = gact * gain_two
    dy = cotangent.astype(F32)
    grad_residual = dy + inverse_two * (
        scaled - normed_two * jnp.mean(scaled * normed_two, axis=1, keepdims=True)
    )
    gres_low = grad_residual.astype(BF)

    def by_core(v):
        return v.reshape(4, 2, *v.shape[1:]).swapaxes(0, 1)

    gres_plane = by_core(lax.all_gather(gres_low, "rep", axis=0)).reshape(1024, width)
    query = query.reshape(heads, QPK, seq, hw)
    key, value = key.reshape(heads, seq, hw), value.reshape(heads, seq, hw)
    probs = probs.reshape(heads, QPK, seq, seq)
    attended = attended.reshape(heads * seq, qw)
    proj_term = dot(attended.T, gres_plane)
    grad_att = dot(gres_plane, proj_head.T).astype(BF).reshape(heads, seq, QPK, hw)
    grad_value = jnp.einsum("bgst,bsgd->btd", probs.astype(BF), grad_att, preferred_element_type=F32)
    grad_probs = jnp.einsum("bsgd,btd->bgst", grad_att, value, preferred_element_type=F32)
    grad_scores = (
        probs * (grad_probs - jnp.sum(probs * grad_probs, axis=-1, keepdims=True))
    ).astype(BF)
    scale = HEAD_WIDTH ** (-0.5)
    grad_query = jnp.einsum("bgst,btd->bsgd", grad_scores, key, preferred_element_type=F32) * scale
    grad_key = jnp.einsum("bgst,bgsd->btd", grad_scores, query, preferred_element_type=F32) * scale
    turned_back = rotate(
        jnp.concatenate([grad_query, grad_key[:, :, None]], axis=2),
        cos[None, :, None, :],
        -sin[None, :, None, :],
    )
    gproj = jnp.concatenate([turned_back, grad_value[:, :, None]], axis=2).astype(BF)
    gproj = gproj.reshape(heads * seq, qw + 2 * hw)
    qkv_term = dot(act_plane.reshape(1024, width).T, gproj)
    gact_one = dot(gproj, qkv_head.T).astype(BF).reshape(2, 4, seq, width).swapaxes(0, 1)
    gact_one = lax.psum_scatter(
        gact_one.reshape(1024, width), "rep", scatter_dimension=0, tiled=True
    ).astype(F32)
    gain_one_term = jnp.sum(gact_one * normed_one, axis=0)
    scaled_one = gact_one * gain_one
    grad_tokens = grad_residual + inverse_one * (
        scaled_one - normed_one * jnp.mean(scaled_one * normed_one, axis=1, keepdims=True)
    )

    qkv_own = lax.psum_scatter(qkv_term.astype(BF), "grp", scatter_dimension=0, tiled=True)
    proj_sum = lax.psum(proj_term.astype(BF), "grp")
    qkv_own = lax.all_gather(qkv_own, "rep", axis=0, tiled=False).astype(F32)
    grad_qkv = jnp.concatenate(
        [
            qkv_own[:, :, lo:hi].transpose(1, 0, 2).reshape(own, -1)
            for lo, hi in ((0, qw), (qw, qw + hw), (qw + hw, qw + 2 * hw))
        ],
        axis=1,
    )
    proj_all = lax.all_gather(proj_sum, "rep", axis=0, tiled=True)
    grad_proj = lax.dynamic_slice_in_dim(proj_all, lax.axis_index("grp") * own, own, 0).astype(F32)
    terms = jnp.concatenate([gain_one_term[:, None], gain_two_term[:, None], router_term], axis=1)
    terms = lax.psum(lax.psum_scatter(terms, "grp", scatter_dimension=0, tiled=True), "rep")
    return (
        output,
        grad_tokens,
        terms[:, 0],
        grad_qkv,
        grad_proj,
        terms[:, 1],
        terms[:, 2:],
        grad_gu,
        grad_dn,
    )


def solution(mesh):
    tok, par = ("rep", "grp"), "grp"
    in_specs = (
        P(tok, None),
        P(par),
        P(par, None),
        P(par, None),
        P(par),
        P(par, None),
        P(par, None, None),
        P(par, None, None),
        P(tok),
        P(tok, None),
        P(tok, None),
        P(tok, None),
    )
    out_specs = (
        P(tok, None),
        P(tok, None),
        P(par),
        P(par, None),
        P(par, None),
        P(par),
        P(par, None),
        P(par, None, None),
        P(par, None, None),
    )
    reps, grps = mesh.shape["rep"], mesh.shape["grp"]

    def body(*args):
        if (reps, grps) == (8, 4):
            return shards(*args)
        return shards_general(reps, grps, *args)

    return jax.shard_map(body, mesh=mesh, in_specs=in_specs, out_specs=out_specs, check_vma=False)
```

```python
import jax
import jax.numpy as jnp
from jax import lax
from jax.experimental import pallas as pl
from jax.experimental.pallas import tpu as pltpu
from jax.sharding import PartitionSpec as P

QUERY_HEADS = 24
KEY_VALUE_HEADS = 8
HEAD_WIDTH = 64
HID = 512
EXPERTS = 16
CAP = 72
EPS = 1e-05
BF = jnp.bfloat16
F32 = jnp.float32
QPK = QUERY_HEADS // KEY_VALUE_HEADS
BIG = 1 << 20
MESH = pl.DeviceIdType.MESH


def dot(a, b):
    return jnp.dot(a, b, preferred_element_type=F32)


def rope_tables(length):
    half = HEAD_WIDTH // 2
    position = jnp.arange(length, dtype=F32)[:, None]
    inverse_freq = 10000.0 ** (-jnp.arange(half, dtype=F32) * 2.0 / HEAD_WIDTH)
    angles = position * inverse_freq[None, :]
    return jnp.cos(angles), jnp.sin(angles)


def rotate(v, cos, sin):
    half = HEAD_WIDTH // 2
    a, b = v[..., :half], v[..., half:]
    return jnp.concatenate([a * cos - b * sin, b * cos + a * sin], axis=-1)


def choices(expert_ids, priority):
    seq, top = expert_ids.shape
    choose = expert_ids[:, :, None] == jnp.arange(EXPERTS, dtype=jnp.int32)[None, None, :]
    chosen = jnp.any(choose, axis=1)
    rank_of = jnp.sum(jnp.where(choose, priority.reshape(seq, top)[:, :, None], 0), axis=1)
    rank_of = jnp.where(chosen, rank_of, BIG)
    slot = jnp.sum((rank_of[None, :, :] < rank_of[:, None, :]).astype(jnp.int32), axis=1)
    return chosen, chosen & (slot < CAP)


def routing(expert_ids, priority, logits):
    chosen, kept = choices(expert_ids, priority)
    top_logit = jnp.max(jnp.where(chosen, logits, -jnp.inf), axis=1, keepdims=True)
    gate_exp = jnp.where(chosen, jnp.exp(jnp.where(chosen, logits - top_logit, 0.0)), 0.0)
    gates = gate_exp / jnp.sum(gate_exp, axis=1, keepdims=True)
    return gates, kept


def place():
    r, z = lax.axis_index("rep"), lax.axis_index("grp")
    return r // 4, (r // 2) % 2, r % 2, z


def flip(bit, by):
    return bit + by * (1 - 2 * bit)


def grads_kernel(nq, x_ref, dy_ref, ggu_ref, hw_ref, gu_out, dn_out,
                 gw, recv1, send2, recv2, zs, zr, ag, sb, ib, st,
                 s1, r1, s2, r2, sz, rz, sa, ra, ss, rs, so):
    y, x, c, z = place()
    half = HID // 2
    wide = 3 * half

    def slot(a, b):
        return flip(y, a * c + b * (1 - c)) * 2 + flip(x, a * (1 - c) + b * c)

    def dev(p, core, zz):
        return (p * 2 + core, zz)

    p0 = slot(0, 0)
    d1, d2, dsib = dev(slot(1, 0), c, z), dev(slot(0, 1), c, z), dev(p0, 1 - c, z)
    zk = [lax.rem(z + k, 4) for k in range(4)]
    barrier = pltpu.get_barrier_semaphore()
    for to in (d1, d2, dsib, dev(p0, c, zk[1]), dev(p0, c, zk[2]), dev(p0, c, zk[3])):
        pl.semaphore_signal(barrier, 1, device_id=to, device_id_type=MESH)
    pl.semaphore_wait(barrier, 6)

    def copy1(q, b):
        return pltpu.make_async_remote_copy(
            gw.at[q // 2, slot(1, b), q % 2], recv1.at[q, b], s1.at[q, b], r1.at[q, b],
            device_id=d1, device_id_type=MESH)

    def copy2(q):
        return pltpu.make_async_remote_copy(
            send2.at[q % 2], recv2.at[q], s2.at[q], r2.at[q], device_id=d2, device_id_type=MESH)

    def copyz(q, k):
        return pltpu.make_async_remote_copy(
            zs.at[q % 2, zk[k]], zr.at[q, z], sz.at[q, k - 1], rz.at[q, k - 1],
            device_id=dev(p0, c, zk[k]), device_id_type=MESH)

    def copya(q, i):
        src, dst = ((0, 1), (0, 2), (1, 3))[i]
        return pltpu.make_async_remote_copy(
            ag.at[q, src], ag.at[q, dst], sa.at[q, i], ra.at[q, i],
            device_id=d1 if i == 0 else d2, device_id_type=MESH)

    def copys(q, i):
        return pltpu.make_async_remote_copy(
            ag.at[q, i], sb.at[q, i], ss.at[q, i], rs.at[q, i], device_id=dsib, device_id_type=MESH)

    def out_copies(q, k, p, core):
        rows = 256
        at = pl.multiple_of(((q // 2) * 128 + p * 32 + (q % 2) * 16) * EXPERTS, rows)
        lo = pl.multiple_of(core * half, half)
        hi = pl.multiple_of(HID + core * half, half)
        pairs = ((gu_out.at[pl.ds(at, rows), pl.ds(lo, half)], 0),
                 (gu_out.at[pl.ds(at, rows), pl.ds(hi, half)], half),
                 (dn_out.at[pl.ds(at, rows), pl.ds(lo, half)], 2 * half))
        return [pltpu.make_async_copy(st.at[k, :, pl.ds(off, half)], ref, so.at[k, i])
                for i, (ref, off) in enumerate(pairs)]

    def emit(q, k, first, p, core, ref):
        @pl.when(jnp.logical_not(first))
        def _():
            for one in out_copies(q, k, p, core):
                one.wait()
        st[k] = ref[...].astype(F32)
        for one in out_copies(q, k, p, core):
            one.start()

    def stage1(q):
        @pl.when(q % 2 == 0)
        def _():
            q3 = q // 2
            xs = jnp.concatenate(
                [x_ref[:, pl.ds(pl.multiple_of(zz * 384 + q3 * 128, 128), 128)] for zz in range(4)], axis=1)
            ds_ = jnp.concatenate(
                [dy_ref[:, pl.ds(pl.multiple_of(zz * 384 + q3 * 128, 128), 128)] for zz in range(4)], axis=1)

            def one(j, _):
                up = lax.dot_general(xs, ggu_ref[j], (((0,), (0,)), ((), ())),
                                     preferred_element_type=F32).astype(BF)
                dn = lax.dot_general(ds_, hw_ref[j], (((0,), (0,)), ((), ())),
                                     preferred_element_type=F32).astype(BF)
                for zz in range(4):
                    for p in range(4):
                        for h in range(2):
                            at = zz * 128 + p * 32 + h * 16
                            gw[q3, p, h, zz, j, :, : 2 * half] = up[at : at + 16]
                            gw[q3, p, h, zz, j, :, 2 * half :] = dn[at : at + 16]
                return 0
            lax.fori_loop(0, 4, one, 0)
        for b in range(2):
            copy1(q, b).start()

    def stage2(q):
        for b in range(2):
            copy1(q, b).wait_recv()

        def one(zz, _):
            send2[q % 2, zz] = (gw[q // 2, slot(0, 1), q % 2, zz].astype(F32)
                                + recv1[q, 1, zz].astype(F32)).astype(BF)
            return 0
        lax.fori_loop(0, 4, one, 0)
        copy2(q).start()

    def stage3(q):
        copy2(q).wait()

        def one(zz, _):
            zs[q % 2, zz] = (gw[q // 2, p0, q % 2, zz].astype(F32) + recv1[q, 0, zz].astype(F32)
                             + recv2[q, zz].astype(F32)).astype(BF)
            return 0
        lax.fori_loop(0, 4, one, 0)
        for k in range(1, 4):
            copyz(q, k).start()
        zr[q, z] = zs[q % 2, z]

    def stage4(q):
        for k in range(1, 4):
            copyz(q, k).wait()
        for zz in range(4):
            for j in range(4):
                for l in range(wide // 128):
                    ib[l, pl.ds(zz * 4 + j, 16, stride=EXPERTS), :] = (
                        zr[q, zz, j, :, l * 128 : (l + 1) * 128].astype(F32))
        for l in range(wide // 128):
            ag[q, 0, :, l * 128 : (l + 1) * 128] = ib[l].astype(BF)
        copya(q, 0).start()
        copys(q, 0).start()

    def stage5(q):
        copya(q, 0).wait_recv()
        copya(q, 1).start()
        copya(q, 2).start()
        copys(q, 1).start()
        emit(q, 0, q == 0, p0, c, ag.at[q, 0])
        emit(q, 1, q == 0, slot(1, 0), c, ag.at[q, 1])

    def stage6(q):
        copya(q, 1).wait_recv()
        copya(q, 2).wait_recv()
        copys(q, 2).start()
        copys(q, 3).start()
        emit(q, 2, q == 0, slot(0, 1), c, ag.at[q, 2])
        emit(q, 3, q == 0, slot(1, 1), c, ag.at[q, 3])

    def stage7(q):
        for i in range(4):
            copys(q, i).wait_recv()
        for i, p in enumerate((p0, slot(0, 1), slot(1, 0), slot(1, 1))):
            emit(q, i, False, p, 1 - c, sb.at[q, i])
        for i in range(4):
            copys(q, i).wait_send()
        for i in range(3):
            copya(q, i).wait_send()
        for b in range(2):
            copy1(q, b).wait_send()

    stages = (stage1, stage2, stage3, stage4, stage5, stage6, stage7)

    def step(t, _):
        for i, stage in enumerate(stages):
            q = t - i

            @pl.when((q >= 0) & (q < nq))
            def _(stage=stage, q=q):
                stage(q)
        return 0

    lax.fori_loop(0, nq + len(stages) - 1, step, 0)
    for k in range(4):
        for one in out_copies(0, k, p0, c):
            one.wait()


def expert_grads(xs, dys, ggu, hw):
    nq, half, wide = 6, HID // 2, 3 * HID // 2
    piece = (4, 4, 16, wide)
    sem = pltpu.SemaphoreType.DMA
    return pl.pallas_call(
        lambda *a: grads_kernel(nq, *a),
        out_shape=(jax.ShapeDtypeStruct((384 * 16, 2 * HID), F32), jax.ShapeDtypeStruct((384 * 16, HID), F32)),
        in_specs=[pl.BlockSpec(memory_space=pltpu.VMEM)] * 4,
        out_specs=[pl.BlockSpec(memory_space=pl.ANY)] * 2,
        scratch_shapes=[
            pltpu.VMEM((3, 4, 2) + piece, BF),
            pltpu.VMEM((nq, 2) + piece, BF),
            pltpu.VMEM((2,) + piece, BF),
            pltpu.VMEM((nq,) + piece, BF),
            pltpu.VMEM((2,) + piece, BF),
            pltpu.VMEM((nq,) + piece, BF),
            pltpu.VMEM((nq, 4, 256, wide), BF),
            pltpu.VMEM((nq, 4, 256, wide), BF),
            pltpu.VMEM((wide // 128, 256, 128), F32),
            pltpu.VMEM((4, 256, wide), F32),
            sem((nq, 2)), sem((nq, 2)), sem((nq,)), sem((nq,)), sem((nq, 3)), sem((nq, 3)),
            sem((nq, 3)), sem((nq, 3)), sem((nq, 4)), sem((nq, 4)), sem((4, 3)),
        ],
        compiler_params=pltpu.CompilerParams(
            collective_id=3, has_side_effects=True, vmem_limit_bytes=62 * 1024 * 1024),
        name="expert_grads",
    )(xs, dys, ggu, hw)


def turn(v, cos, sin):
    lane = lax.broadcasted_iota(jnp.int32, v.shape, 1)
    partner = jnp.where(lax.rem(lane, 64) < 32, pltpu.roll(v, 96, 1), pltpu.roll(v, 32, 1))
    return v * cos + partner * sin


def front_kernel(tok, dy, wpiece, qkv_cols, proj, small, masks, prefix, cos_t, sin_t,
                 o_x, o_dy, o_ggu, o_hw, o_act, o_q, o_k, o_v, o_probs, o_att, o_qkvw, o_projw,
                 o_small, o_res, o_gates, o_gact, o_gg, o_out,
                 smalls, qkvw, projw, projq, actp, pre, pr, qs, ks, vs, probs, att, part, sibr, sums, plr,
                 xall, dyall, wbuf, ggu, hw, gpart, opart, ggp, gsib, osib,
                 gsum, osum, grecv, orecv, res, gates, gact, ggt, outb,
                 s_small, r_small, s_qkv, r_qkv, s_pz, r_pz, s_pq, r_pq, s_wz, r_wz, s_wp, r_wp,
                 s_act, r_act, s_pre, r_pre, s_actc, r_actc, s_prec, r_prec, s_sib, r_sib, s_pl, r_pl,
                 s_x, r_x, s_xc, r_xc, s_y, r_y, s_yc, r_yc,
                 s_g, r_g, s_o, r_o, s_gc, r_gc, s_oc, r_oc, sl):
    y, x, c, z = place()
    half = HID // 2

    def slot(a, b):
        return flip(y, a * c + b * (1 - c)) * 2 + flip(x, a * (1 - c) + b * c)

    p0, p1, p2, p3 = slot(0, 0), slot(1, 0), slot(0, 1), slot(1, 1)
    peers = (p1, p2, p3)
    d1, d2, dsib = (p1 * 2 + c, z), (p2 * 2 + c, z), (p0 * 2 + 1 - c, z)
    dpl = [(p * 2 + c, z) for p in peers]
    zk = [lax.rem(z + k, 4) for k in range(4)]
    zf = [lax.rem(z + 4 - k, 4) for k in range(4)]
    dz = [(p0 * 2 + c, zz) for zz in zk]

    barrier = pltpu.get_barrier_semaphore()
    for to in dpl + dz[1:] + [dsib]:
        pl.semaphore_signal(barrier, 1, device_id=to, device_id_type=MESH)
    pl.semaphore_wait(barrier, 7)

    def remote(src, dst, s, r, to):
        return pltpu.make_async_remote_copy(src, dst, s, r, device_id=to, device_id_type=MESH)

    def c_small(k):
        return remote(small, smalls.at[z], s_small.at[k - 1], r_small.at[k - 1], dz[k])

    def rows(zz, pp):
        return pl.ds(pl.multiple_of(zz * 384 + pp * 96, 96), 96)

    def c_wz(k):
        return remote(wpiece.at[zk[k]], wbuf.at[:, rows(z, p0)], s_wz.at[k - 1], r_wz.at[k - 1], dz[k])

    def c_wp(k, i):
        zz = zf[k]
        who, pp = ((d1, p0), (d2, p0), (d2, p1))[i]
        src = wpiece.at[z] if (k == 0 and i < 2) else wbuf.at[:, rows(zz, pp)]
        return remote(src, wbuf.at[:, rows(zz, pp)], s_wp.at[k, i], r_wp.at[k, i], who)

    def quarter(p):
        return pl.ds(pl.multiple_of(p * 48, 48), 48)

    def c_pz(k):
        src = proj.at[pl.ds(pl.multiple_of(c * 192 + p0 * 48, 48), 48)]
        return remote(src, projq.at[k - 1], s_pz.at[k - 1], r_pz.at[k - 1], dz[k])

    def c_pq(k, owner):
        return remote(projq.at[k - 1], projw.at[quarter(p0)], s_pq.at[k - 1], r_pq.at[p0], (owner * 2 + c, z))

    def c_pq_in(i):
        return remote(projq.at[0], projw.at[quarter(peers[i])], s_pq.at[0], r_pq.at[peers[i]], dpl[i])

    def c_act(i):
        return remote(actp.at[c, p0], actp.at[c, p0], s_act.at[i], r_act.at[i], dpl[i])

    def c_pre(i):
        return remote(pre.at[c, p0], pre.at[c, p0], s_pre.at[i], r_pre.at[i], dpl[i])

    def c_actc(i):
        p = (p0, p1, p2, p3)[i]
        return remote(actp.at[c, p], actp.at[c, p], s_actc.at[i], r_actc.at[i], dsib)

    def c_prec(i):
        p = (p0, p1, p2, p3)[i]
        return remote(pre.at[c, p], pre.at[c, p], s_prec.at[i], r_prec.at[i], dsib)

    def c_sib():
        return remote(part, sibr, s_sib, r_sib, dsib)

    def c_pl(i):
        return remote(sums.at[i], plr.at[i], s_pl.at[i], r_pl.at[i], dpl[i])

    def chain(at, s, r, sc=None, rc=None):
        def hop(h, d, send):
            block = z - (h - 1) if d == 0 else z + (h - 1)
            if not send:
                block = z - h if d == 0 else z + h
            return remote(at(block), at(block), s.at[d, h - 1], r.at[d, h - 1],
                          (p0 * 2 + c, z + 1 if d == 0 else z - 1))

        def may(h, d, send):
            if send:
                return (z < 3) & (z >= h - 1) if d == 0 else (z > 0) & (z <= 4 - h)
            return z >= h if d == 0 else z <= 3 - h

        def across(h, d):
            block = z - h if d == 0 else z + h
            return remote(at(block), at(block), sc.at[d, h - 1], rc.at[d, h - 1], dsib)

        def over():
            return remote(at(z), at(z), sc.at[2, 0], rc.at[2, 0], dsib)

        def send(h):
            for d in range(2):
                @pl.when(may(h, d, True))
                def _(d=d):
                    hop(h, d, True).start()
            if h == 1 and sc is not None:
                over().start()

        def recv(h):
            for d in range(2):
                @pl.when(may(h, d, False))
                def _(d=d):
                    hop(h, d, False).wait_recv()
                    if sc is not None:
                        across(h, d).start()

        def finish():
            over().wait_recv()
            for h in (1, 2, 3):
                for d in range(2):
                    @pl.when(may(h, d, False))
                    def _(d=d, h=h):
                        across(h, d).wait_recv()

        def sent():
            if sc is not None:
                over().wait_send()
            for h in (1, 2, 3):
                for d in range(2):
                    @pl.when(may(h, d, True))
                    def _(d=d, h=h):
                        hop(h, d, True).wait_send()
                    if sc is not None:
                        @pl.when(may(h, d, False))
                        def _(d=d, h=h):
                            across(h, d).wait_send()
        return send, recv, finish, sent

    x_send, x_recv, x_finish, x_sent = chain(lambda b: xall.at[c, b], s_x, r_x, s_xc, r_xc)
    y_send, y_recv, y_finish, y_sent = chain(lambda b: dyall.at[c, b], s_y, r_y, s_yc, r_yc)
    q_send, q_recv, _, q_sent = chain(
        lambda b: qkvw.at[pl.ds(pl.multiple_of(b * 384, 384), 384)], s_qkv, r_qkv)

    def back(src, dst, s, r):
        return lambda k: remote(src.at[zk[k]], dst.at[k - 1], s.at[k - 1], r.at[k - 1], dz[k])

    g_z, o_z = back(gsum, grecv, s_g, r_g), back(osum, orecv, s_o, r_o)
    g_c = remote(gpart, gsib, s_gc, r_gc, dsib)
    o_c = remote(opart, osib, s_oc, r_oc, dsib)

    def weights_a(k):
        if k:
            c_wz(k).wait_recv()
        c_wp(k, 0).start()

    def weights_b(k):
        c_wp(k, 0).wait_recv()
        c_wp(k, 1).start()
        c_wp(k, 2).start()

    for k in (1, 2, 3):
        c_small(k).start()
    local = [pltpu.make_async_copy(small, smalls.at[z], sl.at[0]),
             pltpu.make_async_copy(qkv_cols, qkvw.at[pl.ds(pl.multiple_of(z * 384, 384), 384)], sl.at[1]),
             pltpu.make_async_copy(wpiece.at[z], wbuf.at[:, rows(z, p0)], sl.at[2]),
             pltpu.make_async_copy(dy, dyall.at[c, z], sl.at[3])]
    for one in local:
        one.start()
    own_proj = pltpu.make_async_copy(proj.at[pl.ds(pl.multiple_of(c * 192, 192), 192)], projw, sl.at[4])

    @pl.when(z == p0)
    def _():
        own_proj.start()
    tok_f = tok[...].astype(F32)
    inv1 = lax.rsqrt(jnp.mean(tok_f * tok_f, axis=1, keepdims=True) + EPS)
    for k in (1, 2, 3):
        c_small(k).wait_recv()
    local[1].wait()
    q_send(1)
    for k in (1, 2, 3):
        c_pz(k).start()
    local[0].wait()
    gain1 = jnp.concatenate([smalls[i, 0:1, :] for i in range(4)], axis=1).astype(F32)
    actp[c, p0] = (tok_f * inv1 * gain1).astype(BF)
    pre[c, p0] = prefix[...]
    for i in range(3):
        c_act(i).start()
        c_pre(i).start()
    c_actc(0).start()
    c_prec(0).start()
    q_recv(1)
    q_send(2)
    q_recv(2)
    q_send(3)
    for i in range(3):
        c_act(i).wait_recv()
        c_pre(i).wait_recv()
        c_actc(i + 1).start()
        c_prec(i + 1).start()
    weights_a(0)
    q_recv(3)
    local[3].wait()

    row = lax.broadcasted_iota(jnp.int32, (128, 128), 0)
    col = lax.broadcasted_iota(jnp.int32, (128, 128), 1)
    causal = col <= row
    col_f = col.astype(F32)

    def attention(cc):
        pr[...] = jnp.dot(actp[cc].reshape(512, 1536), qkvw[...], preferred_element_type=F32).reshape(4, 128, 320)

        def one(i, _):
            lo = turn(pr[i, :, 0:128], cos_t[...], sin_t[...]).astype(BF)
            hi = turn(pr[i, :, 128:256], cos_t[...], sin_t[...]).astype(BF)
            qs[cc, i, 0:128] = lo[:, 0:64]
            qs[cc, i, 128:256] = lo[:, 64:128]
            qs[cc, i, 256:384] = hi[:, 0:64]
            ks[cc, i] = hi[:, 64:128]
            vs[cc, i] = pr[i, :, 256:320].astype(BF)
            sc = lax.dot_general(qs[cc, i], ks[cc, i], (((1,), (1,)), ((), ())), preferred_element_type=F32)
            allowed = causal | (col_f < pre[cc, i, 0:1, :])
            sc = jnp.where(allowed[None], sc.reshape(3, 128, 128) * (64 ** -0.5), -1e30)
            ex = jnp.exp(sc - jnp.max(sc, axis=-1, keepdims=True))
            pb = (ex / jnp.sum(ex, axis=-1, keepdims=True)).reshape(384, 128)
            probs[cc, i] = pb
            at = jnp.dot(pb.astype(BF), vs[cc, i], preferred_element_type=F32).astype(BF)
            for h in range(3):
                att[cc, i, :, h * 64 : (h + 1) * 64] = at[h * 128 : (h + 1) * 128]
            return 0
        lax.fori_loop(0, 4, one, 0)

    attention(c)
    for i in range(4):
        c_actc(i).wait_recv()
        c_prec(i).wait_recv()
    attention(1 - c)
    for k in (1, 2, 3):
        c_pz(k).wait_recv()
        owner = zf[k]

        @pl.when(owner != p0)
        def _(k=k, owner=owner):
            c_pq(k, owner).start()

        @pl.when(owner == p0)
        def _(k=k):
            projw[quarter(p0)] = projq[k - 1]

    for k in (1, 3, 2):
        c_wz(k).start()

    @pl.when(z == p0)
    def _():
        own_proj.wait()

    @pl.when(z != p0)
    def _():
        for i in range(3):
            c_pq_in(i).wait_recv()

    weights_b(0)

    def to_sib(i, _):
        part[i] = jnp.dot(att[1 - c, i], projw[...], preferred_element_type=F32).astype(BF)
        return 0
    lax.fori_loop(0, 4, to_sib, 0)
    c_sib().start()
    c_sib().wait_recv()
    for i in range(3):
        sums[i] = (jnp.dot(att[c, peers[i]], projw[...], preferred_element_type=F32)
                   + sibr[peers[i]].astype(F32)).astype(BF)
        c_pl(i).start()
    residual = (tok_f + jnp.dot(att[c, p0], projw[...], preferred_element_type=F32) + sibr[p0].astype(F32))
    for i in range(3):
        c_pl(i).wait_recv()
        residual = residual + plr[i].astype(F32)
    res[...] = residual
    inv2 = lax.rsqrt(jnp.mean(residual * residual, axis=1, keepdims=True) + EPS)
    gain2 = jnp.concatenate([smalls[i, 1:2, :] for i in range(4)], axis=1).astype(F32)
    act2 = (residual * inv2 * gain2).astype(BF)
    router = jnp.concatenate([smalls[i, 16:32, :] for i in range(4)], axis=1)
    logits = lax.dot_general(act2, router, (((1,), (1,)), ((), ())), preferred_element_type=F32)
    chosen, kept = masks[0] > 0.0, masks[1]
    top = jnp.max(jnp.where(chosen, logits, -1e30), axis=1, keepdims=True)
    ge = jnp.where(chosen, jnp.exp(jnp.where(chosen, logits - top, 0.0)), 0.0)
    gt = ge / jnp.sum(ge, axis=1, keepdims=True)
    gates[...] = gt
    wide_gates = jnp.concatenate([gt * kept, jnp.zeros((128, 112), F32)], axis=1)
    gate_hi = wide_gates.astype(BF)
    xall[c, z, :, :1536] = act2
    xall[c, z, :, 1536:1664] = gate_hi
    xall[c, z, :, 1664:] = (wide_gates - gate_hi.astype(F32)).astype(BF)
    x_send(1)
    weights_a(1)
    weights_a(3)
    weights_b(1)
    x_recv(1)
    x_send(2)
    weights_b(3)
    weights_a(2)
    x_recv(2)
    x_send(3)
    y_send(1)
    weights_b(2)
    x_recv(3)
    y_recv(1)
    y_send(2)
    y_recv(2)
    y_send(3)
    y_recv(3)
    local[2].wait()
    for k in range(4):
        c_wp(k, 1).wait_recv()
        c_wp(k, 2).wait_recv()
    x_finish()
    y_finish()

    lane = lax.broadcasted_iota(jnp.int32, (512, 128), 1)
    ggp[...] = jnp.zeros_like(ggp)

    def expert(n, _):
        j, t = n // 2, lax.rem(n, 2)
        gu = jnp.dot(xall[t, :, :, :1536].reshape(512, 1536), wbuf[j, :, : 2 * half], preferred_element_type=F32)
        bk = jnp.dot(dyall[t].reshape(512, 1536), wbuf[j, :, 2 * half :], preferred_element_type=F32)
        mine = lane == z * 4 + j
        both = (xall[t, :, :, 1536:1664].astype(F32) + xall[t, :, :, 1664:].astype(F32)).reshape(512, 128)
        w = jnp.sum(jnp.where(mine, both, 0.0), axis=1, keepdims=True)
        g, u = gu[:, :half], gu[:, half:]
        sg = 1.0 / (1.0 + jnp.exp(-g))
        silu = g * sg
        hid = silu * u
        hw[j, pl.ds(pl.multiple_of(t * 512, 512), 512)] = (hid * w).astype(BF)
        ggp[t] = ggp[t] + jnp.where(mine, jnp.sum(bk * hid, axis=1, keepdims=True), 0.0).reshape(4, 128, 128)
        gh = bk * w
        at = pl.ds(pl.multiple_of(t * 512, 512), 512)
        ggu[j, at, :half] = (gh * u * sg * (1.0 + g * (1.0 - sg))).astype(BF)
        ggu[j, at, half:] = (gh * silu).astype(BF)
        return 0
    lax.fori_loop(0, 8, expert, 0)
    saves = []

    def save(src, dst):
        one = pltpu.make_async_copy(src, dst, sl.at[5 + len(saves)])
        one.start()
        saves.append(one)
    for src, dst in ((xall, o_x), (dyall, o_dy), (ggu, o_ggu), (hw, o_hw), (actp, o_act), (qs, o_q), (ks, o_k),
                     (vs, o_v), (probs, o_probs), (att, o_att), (qkvw, o_qkvw), (projw, o_projw),
                     (smalls, o_small), (res, o_res), (gates, o_gates)):
        save(src, dst)

    def block(grad, t, n):
        at = pl.ds(pl.multiple_of(t * 512, 512), 512)
        lanes = pl.ds(pl.multiple_of(n * 256, 256), 256)
        acc = jnp.zeros((512, 256), F32)
        for j in range(4):
            a = ggu[j, at] if grad else hw[j, at]
            b = wbuf[j, lanes, : 2 * half] if grad else wbuf[j, lanes, 2 * half :]
            acc = acc + lax.dot_general(a, b, (((1,), (1,)), ((), ())), preferred_element_type=F32)
        return acc.reshape(4, 128, 256), lanes

    def partial(grad, buf):
        def one(n, _):
            v, lanes = block(grad, 1 - c, n)
            buf[:, :, lanes] = v.astype(BF)
            return 0
        lax.fori_loop(0, 6, one, 0)

    def own(grad, sib, dst):
        def one(n, _):
            v, lanes = block(grad, c, n)
            dst[:, :, lanes] = (v + sib[:, :, lanes].astype(F32)).astype(BF)
            return 0
        lax.fori_loop(0, 6, one, 0)

    def put_gate_grads(dst, v):
        hi = v.astype(BF)
        dst[:, :, 1536:1664] = hi
        dst[:, :, 1664:] = (v - hi.astype(F32)).astype(BF)

    def gate_grads(v):
        return v[..., 1536:1664].astype(F32) + v[..., 1664:].astype(F32)

    put_gate_grads(gpart, ggp[1 - c])
    partial(True, gpart)
    g_c.start()
    partial(False, opart)
    o_c.start()
    g_c.wait_recv()
    put_gate_grads(gsum, ggp[c] + gate_grads(gsib))
    own(True, gsib, gsum)
    for k in (1, 2, 3):
        g_z(k).start()
    o_c.wait_recv()
    own(False, osib, osum)
    for k in (1, 2, 3):
        g_z(k).wait_recv()
    for k in (1, 2, 3):
        o_z(k).start()
    ggt[...] = (gate_grads(gsum[z]) + gate_grads(grecv[0]) + gate_grads(grecv[1])
                + gate_grads(grecv[2]))[:, :EXPERTS]
    save(ggt, o_gg)
    gact[...] = (gsum[z, :, :1536].astype(F32) + grecv[0, :, :1536].astype(F32)
                 + grecv[1, :, :1536].astype(F32) + grecv[2, :, :1536].astype(F32))
    save(gact, o_gact)
    for k in (1, 2, 3):
        o_z(k).wait_recv()
    outb[...] = (res[...] + osum[z].astype(F32) + orecv[0].astype(F32) + orecv[1].astype(F32)
                 + orecv[2].astype(F32)).astype(BF)
    save(outb, o_out)

    for k in (1, 2, 3):
        for one in (c_small(k), c_pz(k), c_wz(k), g_z(k), o_z(k)):
            one.wait_send()

        @pl.when(zf[k] != p0)
        def _(k=k):
            c_pq(k, zf[k]).wait_send()
    for k in range(4):
        for i in range(3):
            c_wp(k, i).wait_send()
        for one in (c_actc(k), c_prec(k)):
            one.wait_send()
    for i in range(3):
        for one in (c_act(i), c_pre(i), c_pl(i)):
            one.wait_send()
    for one in (c_sib(), g_c, o_c):
        one.wait_send()
    x_sent()
    y_sent()
    q_sent()
    for one in saves:
        one.wait()


def front(tok, dy, wpiece, qkv_cols, proj, small, masks, prefix, cos_t, sin_t):
    sem, vm = pltpu.SemaphoreType.DMA, pltpu.VMEM
    out = lambda shape, kind=BF: jax.ShapeDtypeStruct(shape, kind)
    outs = (
        out((2, 4, 128, 1792)), out((2, 4, 128, 1536)), out((4, 1024, 512)), out((4, 1024, 256)),
        out((2, 4, 128, 1536)), out((2, 4, 384, 64)), out((2, 4, 128, 64)), out((2, 4, 128, 64)),
        out((2, 4, 384, 128), F32), out((2, 4, 128, 192)), out((1536, 320)), out((192, 1536)),
        out((4, 32, 384)), out((128, 1536), F32), out((128, 16), F32), out((128, 1536), F32),
        out((128, 16), F32), out((128, 1536)),
    )
    block, quad = vm((2, 4, 128, 1536), BF), vm((4, 128, 1536), BF)
    three = vm((3, 128, 1536), BF)
    quad_g, three_g = vm((4, 128, 1792), BF), vm((3, 128, 1792), BF)
    scratch = [
        vm((4, 32, 384), BF), vm((1536, 320), BF), vm((192, 1536), BF), vm((3, 48, 1536), BF),
        block, vm((2, 4, 8, 128), F32),
        vm((4, 128, 320), F32), vm((2, 4, 384, 64), BF), vm((2, 4, 128, 64), BF), vm((2, 4, 128, 64), BF),
        vm((2, 4, 384, 128), F32), vm((2, 4, 128, 192), BF), quad, quad, three, three,
        vm((2, 4, 128, 1792), BF), block, vm((4, 1536, 768), BF), vm((4, 1024, 512), BF),
        vm((4, 1024, 256), BF), quad_g, quad, vm((2, 4, 128, 128), F32), quad_g, quad,
        quad_g, quad, three_g, three,
        vm((128, 1536), F32), vm((128, 16), F32), vm((128, 1536), F32), vm((128, 16), F32), vm((128, 1536), BF),
    ]
    n3, n4, one = sem((3,)), sem((4,)), sem(())
    hops = [sem((2, 3)), sem((2, 3)), sem((3, 3)), sem((3, 3))]
    sems = [
        n3, n3, sem((2, 3)), sem((2, 3)), n3, n3, n3, n4, n3, n3, sem((4, 3)), sem((4, 3)),
        n3, n3, n3, n3, n4, n4, n4, n4, one, one, n3, n3,
        *hops, *hops, n3, n3, n3, n3, one, one, one, one, sem((24,)),
    ]
    vmem, any_ = pl.BlockSpec(memory_space=pltpu.VMEM), pl.BlockSpec(memory_space=pl.ANY)
    return pl.pallas_call(
        front_kernel,
        out_shape=outs,
        in_specs=[vmem, any_, any_, any_, any_, any_, vmem, vmem, vmem, vmem],
        out_specs=[any_] * len(outs),
        scratch_shapes=scratch + sems,
        compiler_params=pltpu.CompilerParams(
            collective_id=1, has_side_effects=True, vmem_limit_bytes=62 * 1024 * 1024),
        name="front",
    )(tok, dy, wpiece, qkv_cols, proj, small, masks, prefix, cos_t, sin_t)


def expert_grads_general(reps, grps, xs, dys, ggu, hw):
    local, half, width = ggu.shape[0], HID // 2, xs.shape[1]
    own = width // grps
    chips = reps // 2
    piece = own // chips
    same_core = [[2 * i + c for i in range(chips)] for c in range(2)]
    pairs = [[2 * i, 2 * i + 1] for i in range(chips)]
    up = jnp.einsum("td,eth->edh", xs, ggu, preferred_element_type=F32).astype(BF)
    down = jnp.einsum("td,eth->edh", dys, hw, preferred_element_type=F32).astype(BF)
    gw = jnp.concatenate([up, down], axis=2)
    gw = gw.reshape(local, grps, chips, piece, 3 * half).transpose(2, 1, 3, 0, 4)
    gw = gw.reshape(chips * grps * piece, local * 3 * half)
    gw = lax.psum_scatter(gw, "rep", scatter_dimension=0, tiled=True, axis_index_groups=same_core)
    gw = lax.all_to_all(gw.reshape(grps, piece, local, 3 * half), "grp", 0, 0, tiled=True)
    gw = gw.transpose(1, 0, 2, 3).reshape(piece, EXPERTS, 3 * half)
    gw = lax.all_gather(gw, "rep", axis=0, tiled=True, axis_index_groups=same_core)
    gw = lax.all_gather(gw, "rep", axis=0, tiled=False, axis_index_groups=pairs).astype(F32)
    gw = gw.reshape(2, own * EXPERTS, 3, half)
    gw = jnp.moveaxis(gw, 0, 2).reshape(own * EXPERTS, 3 * HID)
    return gw[:, : 2 * HID], gw[:, 2 * HID :]


def shards_general(
    reps,
    grps,
    tokens,
    attn_gain,
    query_key_value_weight,
    attn_proj,
    mlp_gain,
    w_router,
    w_gate_up,
    w_down,
    prefix_len,
    expert_ids,
    priority,
    cotangent,
):
    seq, width = tokens.shape
    own = width // grps
    local_experts = EXPERTS // grps
    heads = KEY_VALUE_HEADS
    groups = None if reps == heads else [list(range(i, i + heads)) for i in range(0, reps, heads)]
    rep, grp = lax.axis_index("rep"), lax.axis_index("grp")
    head = lax.rem(rep, heads)
    qw, hw = QPK * HEAD_WIDTH, HEAD_WIDTH
    q_all = QUERY_HEADS * HEAD_WIDTH

    small = jnp.concatenate([attn_gain[:, None], mlp_gain[:, None], w_router], axis=1)
    small = lax.all_gather(small, "grp", axis=0, tiled=True)
    gain_one, gain_two = small[:, 0].astype(F32)[None, :], small[:, 1].astype(F32)[None, :]
    router = small[:, 2:]
    qkv_cols = jnp.concatenate(
        [
            lax.dynamic_slice_in_dim(query_key_value_weight, head * qw, qw, 1),
            lax.dynamic_slice_in_dim(query_key_value_weight, q_all + head * hw, hw, 1),
            lax.dynamic_slice_in_dim(query_key_value_weight, q_all + heads * hw + head * hw, hw, 1),
        ],
        axis=1,
    )
    qkv_head = lax.all_gather(qkv_cols, "grp", axis=0, tiled=True)
    row = head * qw + jnp.arange(qw)
    mine = (row // own) == grp
    proj_rows = jnp.where(mine[:, None], jnp.take(attn_proj, jnp.where(mine, row - grp * own, 0), axis=0), 0)
    proj_head = lax.psum(proj_rows, "grp")

    core, chip, chips, half = lax.rem(rep, 2), rep // 2, reps // 2, HID // 2
    pairs = [[2 * i, 2 * i + 1] for i in range(chips)]
    same_core = [[2 * i + c for i in range(chips)] for c in range(2)]
    piece = own // chips
    gu_piece = lax.dynamic_slice_in_dim(w_gate_up, chip * piece, piece, 0)
    dn_piece = lax.dynamic_slice_in_dim(w_down, chip * piece, piece, 0)
    both = jnp.concatenate(
        [
            lax.dynamic_slice_in_dim(gu_piece, core * half, half, 2),
            lax.dynamic_slice_in_dim(gu_piece, HID + core * half, half, 2),
            lax.dynamic_slice_in_dim(dn_piece, core * half, half, 2),
        ],
        axis=2,
    )
    both = both.reshape(piece, grps, local_experts, 3 * half).transpose(1, 2, 0, 3)
    both = lax.all_to_all(both, "grp", 0, 0, tiled=True)
    both = lax.all_gather(both, "rep", axis=0, tiled=False, axis_index_groups=same_core)
    both = both.transpose(2, 1, 0, 3, 4).reshape(local_experts, width, 3 * half)
    wgu, wdn = both[:, :, : 2 * half], both[:, :, 2 * half :]

    tokens_f = tokens.astype(F32)
    inverse_one = lax.rsqrt(jnp.mean(tokens_f * tokens_f, axis=1, keepdims=True) + EPS)
    normed_one = tokens_f * inverse_one
    act_one = (normed_one * gain_one).astype(BF)
    act_plane = lax.all_gather(act_one, "rep", axis=0, tiled=True, axis_index_groups=groups)
    prefix_plane = lax.all_gather(prefix_len, "rep", axis=0, tiled=True, axis_index_groups=groups)
    cos, sin = rope_tables(seq)
    projected = dot(act_plane, qkv_head).reshape(heads, seq, QPK + 2, HEAD_WIDTH)
    cos_b, sin_b = cos[None, :, None, :], sin[None, :, None, :]
    turned = rotate(projected[:, :, : QPK + 1], cos_b, sin_b).astype(BF)
    query = turned[:, :, :QPK]
    key = turned[:, :, QPK]
    value = projected[:, :, QPK + 1].astype(BF)
    scale = HEAD_WIDTH ** (-0.5)
    row_pos, col_pos = jnp.arange(seq)[:, None], jnp.arange(seq)[None, :]
    allowed = (col_pos <= row_pos)[None] | (col_pos[None] < prefix_plane[:, None, None])
    scores = jnp.einsum("bsgd,btd->bgst", query, key, preferred_element_type=F32) * scale
    scores = jnp.where(allowed[:, None], scores, -1e30)
    exps = jnp.exp(scores - jnp.max(scores, axis=-1, keepdims=True))
    probs = exps / jnp.sum(exps, axis=-1, keepdims=True)
    probs_low = probs.astype(BF)
    attended = jnp.einsum("bgst,btd->bsgd", probs_low, value, preferred_element_type=F32)
    attended = attended.astype(BF).reshape(heads * seq, qw)
    part = dot(attended, proj_head).astype(BF)
    part = lax.psum_scatter(part, "rep", scatter_dimension=0, tiled=True, axis_index_groups=groups)
    residual = tokens_f + part.astype(F32)
    inverse_two = lax.rsqrt(jnp.mean(residual * residual, axis=1, keepdims=True) + EPS)
    normed_two = residual * inverse_two
    act_two = (normed_two * gain_two).astype(BF)
    gates, kept = routing(expert_ids, priority, dot(act_two, router))

    def column(v):
        v = lax.all_gather(v, "grp", axis=0, tiled=True)
        return lax.all_gather(v, "rep", axis=0, tiled=True, axis_index_groups=pairs)

    def to_owners(v):
        v = lax.psum_scatter(v, "rep", scatter_dimension=0, tiled=True, axis_index_groups=pairs)
        return lax.psum_scatter(v, "grp", scatter_dimension=0, tiled=True).astype(F32)

    dy_all = column(cotangent)
    x_all = column(act_two)
    weight = column(jnp.where(kept, gates, 0.0))
    weight = lax.dynamic_slice_in_dim(weight, grp * local_experts, local_experts, 1).T[:, :, None]
    gate_up = jnp.einsum("td,edh->eth", x_all, wgu, preferred_element_type=F32)
    g, u = gate_up[..., :half], gate_up[..., half:]
    sig = jax.nn.sigmoid(g)
    silu = g * sig
    hidden = silu * u
    hidden_w = (hidden * weight).astype(BF)
    back = jnp.einsum("td,edh->eth", dy_all, wdn, preferred_element_type=F32)
    grad_gate_part = jnp.sum(back * hidden, axis=2)
    grad_hidden = back * weight
    ggu = jnp.concatenate(
        [grad_hidden * u * sig * (1.0 + g * (1.0 - sig)), grad_hidden * silu], axis=2
    ).astype(BF)
    out_part = jnp.einsum("eth,edh->td", hidden_w, wdn, preferred_element_type=F32).astype(BF)
    gact_part = jnp.einsum("eth,edh->td", ggu, wgu, preferred_element_type=F32).astype(BF)
    gact = to_owners(gact_part)
    grad_gates = lax.psum_scatter(
        grad_gate_part.T, "rep", scatter_dimension=0, tiled=True, axis_index_groups=pairs
    )
    grad_gates = lax.all_to_all(grad_gates, "grp", 0, 1, tiled=True)
    grad_gates = jnp.where(kept, grad_gates, 0.0)
    out = to_owners(out_part)
    output = (residual + out).astype(BF)
    grad_gu, grad_dn = expert_grads_general(reps, grps, x_all, dy_all, ggu, hidden_w)
    grad_gu = grad_gu.reshape(own, EXPERTS, 2 * HID)
    grad_dn = grad_dn.reshape(own, EXPERTS, HID)

    grad_logits = (gates * (grad_gates - jnp.sum(gates * grad_gates, axis=1, keepdims=True))).astype(BF)
    gact = gact + dot(grad_logits, router.T)
    router_term = dot(act_two.T, grad_logits)
    gain_two_term = jnp.sum(gact * normed_two, axis=0)
    scaled = gact * gain_two
    dy = cotangent.astype(F32)
    grad_residual = dy + inverse_two * (
        scaled - normed_two * jnp.mean(scaled * normed_two, axis=1, keepdims=True)
    )
    gres_low = grad_residual.astype(BF)

    gres_plane = lax.all_gather(gres_low, "rep", axis=0, tiled=True, axis_index_groups=groups)
    proj_term = dot(attended.T, gres_plane)
    grad_att = dot(gres_plane, proj_head.T).astype(BF).reshape(heads, seq, QPK, HEAD_WIDTH)
    grad_value = jnp.einsum("bgst,bsgd->btd", probs_low, grad_att, preferred_element_type=F32)
    grad_probs = jnp.einsum("bsgd,btd->bgst", grad_att, value, preferred_element_type=F32)
    grad_scores = (
        probs * (grad_probs - jnp.sum(probs * grad_probs, axis=-1, keepdims=True))
    ).astype(BF)
    grad_query = jnp.einsum("bgst,btd->bsgd", grad_scores, key, preferred_element_type=F32) * scale
    grad_key = jnp.einsum("bgst,bsgd->btd", grad_scores, query, preferred_element_type=F32) * scale
    turned_back = rotate(
        jnp.concatenate([grad_query, grad_key[:, :, None]], axis=2), cos_b, -sin_b
    )
    gproj = jnp.concatenate([turned_back, grad_value[:, :, None]], axis=2).astype(BF)
    gproj = gproj.reshape(heads * seq, qw + 2 * hw)
    qkv_term = dot(act_plane.T, gproj)
    gact_one = dot(gproj, qkv_head.T).astype(BF)
    gact_one = lax.psum_scatter(
        gact_one, "rep", scatter_dimension=0, tiled=True, axis_index_groups=groups
    ).astype(F32)
    gain_one_term = jnp.sum(gact_one * normed_one, axis=0)
    scaled_one = gact_one * gain_one
    grad_tokens = grad_residual + inverse_one * (
        scaled_one - normed_one * jnp.mean(scaled_one * normed_one, axis=1, keepdims=True)
    )

    qkv_own = lax.psum_scatter(qkv_term.astype(BF), "grp", scatter_dimension=0, tiled=True)
    proj_sum = lax.psum(proj_term.astype(BF), "grp")
    if groups is not None:
        across = [[i + heads * j for j in range(reps // heads)] for i in range(heads)]
        qkv_own = lax.psum(qkv_own, "rep", axis_index_groups=across)
        proj_sum = lax.psum(proj_sum, "rep", axis_index_groups=across)
    qkv_own = lax.all_gather(qkv_own, "rep", axis=0, tiled=False, axis_index_groups=groups)
    qkv_own = qkv_own.astype(F32)
    grad_qkv = jnp.concatenate(
        [
            qkv_own[:, :, lo:hi].transpose(1, 0, 2).reshape(own, -1)
            for lo, hi in ((0, qw), (qw, qw + hw), (qw + hw, qw + 2 * hw))
        ],
        axis=1,
    )
    proj_all = lax.all_gather(proj_sum, "rep", axis=0, tiled=True, axis_index_groups=groups)
    grad_proj = lax.dynamic_slice_in_dim(proj_all, grp * own, own, 0).astype(F32)
    terms = jnp.concatenate([gain_one_term[:, None], gain_two_term[:, None], router_term], axis=1)
    terms = lax.psum(lax.psum_scatter(terms, "grp", scatter_dimension=0, tiled=True), "rep")
    return (
        output,
        grad_tokens,
        terms[:, 0],
        grad_qkv,
        grad_proj,
        terms[:, 1],
        terms[:, 2:],
        grad_gu,
        grad_dn,
    )


def shards(
    tokens,
    attn_gain,
    query_key_value_weight,
    attn_proj,
    mlp_gain,
    w_router,
    w_gate_up,
    w_down,
    prefix_len,
    expert_ids,
    priority,
    cotangent,
):
    heads, half, own = KEY_VALUE_HEADS, HID // 2, attn_gain.shape[0]
    qw, hw, q_all = QPK * HEAD_WIDTH, HEAD_WIDTH, QUERY_HEADS * HEAD_WIDTH
    rep = lax.axis_index("rep")
    core, chip = lax.rem(rep, 2), rep // 2
    seq, width = tokens.shape
    small = jnp.concatenate(
        [attn_gain[None], mlp_gain[None], jnp.zeros((14, own), BF), w_router.T], axis=0
    )
    qkv_cols = jnp.concatenate(
        [
            lax.dynamic_slice_in_dim(query_key_value_weight, rep * qw, qw, 1),
            lax.dynamic_slice_in_dim(query_key_value_weight, q_all + rep * hw, hw, 1),
            lax.dynamic_slice_in_dim(query_key_value_weight, q_all + heads * hw + rep * hw, hw, 1),
        ],
        axis=1,
    )
    piece = own // 4
    gu_piece = lax.dynamic_slice_in_dim(w_gate_up, chip * piece, piece, 0)
    dn_piece = lax.dynamic_slice_in_dim(w_down, chip * piece, piece, 0)
    both = jnp.concatenate(
        [
            lax.dynamic_slice_in_dim(gu_piece, core * half, half, 2),
            lax.dynamic_slice_in_dim(gu_piece, HID + core * half, half, 2),
            lax.dynamic_slice_in_dim(dn_piece, core * half, half, 2),
        ],
        axis=2,
    )
    wpiece = both.transpose(1, 0, 2).reshape(4, 4, piece, 3 * half)
    chosen, kept = choices(expert_ids, priority)
    masks = jnp.stack([chosen, kept]).astype(F32)
    prefix = jnp.broadcast_to(prefix_len.astype(F32), (8, 128))
    cos, sin = rope_tables(seq)
    cos_t, sin_t = jnp.tile(cos, (1, 4)), jnp.tile(jnp.concatenate([-sin, sin], axis=1), (1, 2))
    (x_all, dy_all, ggu, hidden_w, act_plane, query, key, value, probs, attended, qkv_head, proj_head,
     smalls, residual, gates, gact, grad_gates, output) = front(
        tokens, cotangent, wpiece, qkv_cols, attn_proj, small, masks, prefix, cos_t, sin_t)
    grad_gu, grad_dn = expert_grads(x_all.reshape(1024, 1792), dy_all.reshape(1024, width), ggu, hidden_w)
    grad_gu = grad_gu.reshape(own, EXPERTS, 2 * HID)
    grad_dn = grad_dn.reshape(own, EXPERTS, HID)

    gain_one = smalls[:, 0].reshape(1, width).astype(F32)
    gain_two = smalls[:, 1].reshape(1, width).astype(F32)
    router_t = jnp.concatenate([smalls[i, 16:] for i in range(4)], axis=1)
    tokens_f = tokens.astype(F32)
    inverse_one = lax.rsqrt(jnp.mean(tokens_f * tokens_f, axis=1, keepdims=True) + EPS)
    normed_one = tokens_f * inverse_one
    inverse_two = lax.rsqrt(jnp.mean(residual * residual, axis=1, keepdims=True) + EPS)
    normed_two = residual * inverse_two
    act_two = (normed_two * gain_two).astype(BF)

    grad_gates = grad_gates * masks[1]
    grad_logits = (gates * (grad_gates - jnp.sum(gates * grad_gates, axis=1, keepdims=True))).astype(BF)
    gact = gact + dot(grad_logits, router_t)
    router_term = dot(act_two.T, grad_logits)
    gain_two_term = jnp.sum(gact * normed_two, axis=0)
    scaled = gact * gain_two
    dy = cotangent.astype(F32)
    grad_residual = dy + inverse_two * (
        scaled - normed_two * jnp.mean(scaled * normed_two, axis=1, keepdims=True)
    )
    gres_low = grad_residual.astype(BF)

    def by_core(v):
        return v.reshape(4, 2, *v.shape[1:]).swapaxes(0, 1)

    gres_plane = by_core(lax.all_gather(gres_low, "rep", axis=0)).reshape(1024, width)
    query = query.reshape(heads, QPK, seq, hw)
    key, value = key.reshape(heads, seq, hw), value.reshape(heads, seq, hw)
    probs = probs.reshape(heads, QPK, seq, seq)
    attended = attended.reshape(heads * seq, qw)
    proj_term = dot(attended.T, gres_plane)
    grad_att = dot(gres_plane, proj_head.T).astype(BF).reshape(heads, seq, QPK, hw)
    grad_value = jnp.einsum("bgst,bsgd->btd", probs.astype(BF), grad_att, preferred_element_type=F32)
    grad_probs = jnp.einsum("bsgd,btd->bgst", grad_att, value, preferred_element_type=F32)
    grad_scores = (
        probs * (grad_probs - jnp.sum(probs * grad_probs, axis=-1, keepdims=True))
    ).astype(BF)
    scale = HEAD_WIDTH ** (-0.5)
    grad_query = jnp.einsum("bgst,btd->bsgd", grad_scores, key, preferred_element_type=F32) * scale
    grad_key = jnp.einsum("bgst,bgsd->btd", grad_scores, query, preferred_element_type=F32) * scale
    turned_back = rotate(
        jnp.concatenate([grad_query, grad_key[:, :, None]], axis=2),
        cos[None, :, None, :],
        -sin[None, :, None, :],
    )
    gproj = jnp.concatenate([turned_back, grad_value[:, :, None]], axis=2).astype(BF)
    gproj = gproj.reshape(heads * seq, qw + 2 * hw)
    qkv_term = dot(act_plane.reshape(1024, width).T, gproj)
    gact_one = dot(gproj, qkv_head.T).astype(BF).reshape(2, 4, seq, width).swapaxes(0, 1)
    gact_one = lax.psum_scatter(
        gact_one.reshape(1024, width), "rep", scatter_dimension=0, tiled=True
    ).astype(F32)
    gain_one_term = jnp.sum(gact_one * normed_one, axis=0)
    scaled_one = gact_one * gain_one
    grad_tokens = grad_residual + inverse_one * (
        scaled_one - normed_one * jnp.mean(scaled_one * normed_one, axis=1, keepdims=True)
    )

    qkv_own = lax.psum_scatter(qkv_term.astype(BF), "grp", scatter_dimension=0, tiled=True)
    proj_sum = lax.psum(proj_term.astype(BF), "grp")
    qkv_own = lax.all_gather(qkv_own, "rep", axis=0, tiled=False).astype(F32)
    grad_qkv = jnp.concatenate(
        [
            qkv_own[:, :, lo:hi].transpose(1, 0, 2).reshape(own, -1)
            for lo, hi in ((0, qw), (qw, qw + hw), (qw + hw, qw + 2 * hw))
        ],
        axis=1,
    )
    proj_all = lax.all_gather(proj_sum, "rep", axis=0, tiled=True)
    grad_proj = lax.dynamic_slice_in_dim(proj_all, lax.axis_index("grp") * own, own, 0).astype(F32)
    terms = jnp.concatenate([gain_one_term[:, None], gain_two_term[:, None], router_term], axis=1)
    terms = lax.psum(lax.psum_scatter(terms, "grp", scatter_dimension=0, tiled=True), "rep")
    return (
        output,
        grad_tokens,
        terms[:, 0],
        grad_qkv,
        grad_proj,
        terms[:, 1],
        terms[:, 2:],
        grad_gu,
        grad_dn,
    )


def solution(mesh):
    tok, par = ("rep", "grp"), "grp"
    in_specs = (
        P(tok, None),
        P(par),
        P(par, None),
        P(par, None),
        P(par),
        P(par, None),
        P(par, None, None),
        P(par, None, None),
        P(tok),
        P(tok, None),
        P(tok, None),
        P(tok, None),
    )
    out_specs = (
        P(tok, None),
        P(tok, None),
        P(par),
        P(par, None),
        P(par, None),
        P(par),
        P(par, None),
        P(par, None, None),
        P(par, None, None),
    )
    reps, grps = mesh.shape["rep"], mesh.shape["grp"]

    def body(*args):
        if (reps, grps) == (8, 4):
            return shards(*args)
        return shards_general(reps, grps, *args)

    return jax.shard_map(body, mesh=mesh, in_specs=in_specs, out_specs=out_specs, check_vma=False)
```

```python
import jax
import jax.numpy as jnp
from jax import lax
from jax.experimental import pallas as pl
from jax.experimental.pallas import tpu as pltpu
from jax.sharding import PartitionSpec as P

QUERY_HEADS = 24
KEY_VALUE_HEADS = 8
HEAD_WIDTH = 64
HID = 512
EXPERTS = 16
CAP = 72
EPS = 1e-05
BF = jnp.bfloat16
F32 = jnp.float32
QPK = QUERY_HEADS // KEY_VALUE_HEADS
BIG = 1 << 20
MESH = pl.DeviceIdType.MESH


def dot(a, b):
    return jnp.dot(a, b, preferred_element_type=F32)


def rope_tables(length):
    half = HEAD_WIDTH // 2
    position = jnp.arange(length, dtype=F32)[:, None]
    inverse_freq = 10000.0 ** (-jnp.arange(half, dtype=F32) * 2.0 / HEAD_WIDTH)
    angles = position * inverse_freq[None, :]
    return jnp.cos(angles), jnp.sin(angles)


def rotate(v, cos, sin):
    half = HEAD_WIDTH // 2
    a, b = v[..., :half], v[..., half:]
    return jnp.concatenate([a * cos - b * sin, b * cos + a * sin], axis=-1)


def choices(expert_ids, priority):
    seq, top = expert_ids.shape
    choose = expert_ids[:, :, None] == jnp.arange(EXPERTS, dtype=jnp.int32)[None, None, :]
    chosen = jnp.any(choose, axis=1)
    rank_of = jnp.sum(jnp.where(choose, priority.reshape(seq, top)[:, :, None], 0), axis=1)
    rank_of = jnp.where(chosen, rank_of, BIG)
    slot = jnp.sum((rank_of[None, :, :] < rank_of[:, None, :]).astype(jnp.int32), axis=1)
    return chosen, chosen & (slot < CAP)


def routing(expert_ids, priority, logits):
    chosen, kept = choices(expert_ids, priority)
    top_logit = jnp.max(jnp.where(chosen, logits, -jnp.inf), axis=1, keepdims=True)
    gate_exp = jnp.where(chosen, jnp.exp(jnp.where(chosen, logits - top_logit, 0.0)), 0.0)
    gates = gate_exp / jnp.sum(gate_exp, axis=1, keepdims=True)
    return gates, kept


def place():
    r, z = lax.axis_index("rep"), lax.axis_index("grp")
    return r // 4, (r // 2) % 2, r % 2, z


def flip(bit, by):
    return bit + by * (1 - 2 * bit)


def turn(v, cos, sin):
    lane = lax.broadcasted_iota(jnp.int32, v.shape, 1)
    partner = jnp.where(lax.rem(lane, 64) < 32, pltpu.roll(v, 96, 1), pltpu.roll(v, 32, 1))
    return v * cos + partner * sin


def front_kernel(tok, dy, wpiece, qkv_cols, proj, small, masks, prefix, cos_t, sin_t,
                 o_x, o_dy, o_ggu, o_hw, o_act, o_q, o_k, o_v, o_probs, o_att, o_qkvw, o_projw,
                 o_small, o_res, o_gates, o_gsum, o_osum,
                 smalls, qkvw, projw, projq, actp, pre, pr, qs, ks, vs, probs, att, part, sibr, sums, plr,
                 xall, dyall, wbuf, ggu, hw, gpart, opart, ggp, gsib, osib,
                 gsum, osum, res, gates,
                 s_small, r_small, s_qkv, r_qkv, s_pz, r_pz, s_pq, r_pq, s_wz, r_wz, s_wp, r_wp,
                 s_act, r_act, s_pre, r_pre, s_actc, r_actc, s_prec, r_prec, s_sib, r_sib, s_pl, r_pl,
                 s_x, r_x, s_xc, r_xc, s_y, r_y, s_yc, r_yc,
                 s_gc, r_gc, s_oc, r_oc, sl):
    y, x, c, z = place()
    half = HID // 2

    def slot(a, b):
        return flip(y, a * c + b * (1 - c)) * 2 + flip(x, a * (1 - c) + b * c)

    p0, p1, p2, p3 = slot(0, 0), slot(1, 0), slot(0, 1), slot(1, 1)
    peers = (p1, p2, p3)
    d1, d2, dsib = (p1 * 2 + c, z), (p2 * 2 + c, z), (p0 * 2 + 1 - c, z)
    dpl = [(p * 2 + c, z) for p in peers]
    zk = [lax.rem(z + k, 4) for k in range(4)]
    zf = [lax.rem(z + 4 - k, 4) for k in range(4)]
    dz = [(p0 * 2 + c, zz) for zz in zk]

    barrier = pltpu.get_barrier_semaphore()
    for to in dpl + dz[1:] + [dsib]:
        pl.semaphore_signal(barrier, 1, device_id=to, device_id_type=MESH)
    pl.semaphore_wait(barrier, 7)

    def remote(src, dst, s, r, to):
        return pltpu.make_async_remote_copy(src, dst, s, r, device_id=to, device_id_type=MESH)

    def c_small(k):
        return remote(small, smalls.at[z], s_small.at[k - 1], r_small.at[k - 1], dz[k])

    def rows(zz, pp):
        return pl.ds(pl.multiple_of(zz * 384 + pp * 96, 96), 96)

    def c_wz(k):
        return remote(wpiece.at[zk[k]], wbuf.at[:, rows(z, p0)], s_wz.at[k - 1], r_wz.at[k - 1], dz[k])

    def c_wp(k, i):
        zz = zf[k]
        who, pp = ((d1, p0), (d2, p0), (d2, p1))[i]
        src = wpiece.at[z] if (k == 0 and i < 2) else wbuf.at[:, rows(zz, pp)]
        return remote(src, wbuf.at[:, rows(zz, pp)], s_wp.at[k, i], r_wp.at[k, i], who)

    def quarter(p):
        return pl.ds(pl.multiple_of(p * 48, 48), 48)

    def c_pz(k):
        src = proj.at[pl.ds(pl.multiple_of(c * 192 + p0 * 48, 48), 48)]
        return remote(src, projq.at[k - 1], s_pz.at[k - 1], r_pz.at[k - 1], dz[k])

    def c_pq(k, owner):
        return remote(projq.at[k - 1], projw.at[quarter(p0)], s_pq.at[k - 1], r_pq.at[p0], (owner * 2 + c, z))

    def c_pq_in(i):
        return remote(projq.at[0], projw.at[quarter(peers[i])], s_pq.at[0], r_pq.at[peers[i]], dpl[i])

    def c_act(i):
        return remote(actp.at[c, p0], actp.at[c, p0], s_act.at[i], r_act.at[i], dpl[i])

    def c_pre(i):
        return remote(pre.at[c, p0], pre.at[c, p0], s_pre.at[i], r_pre.at[i], dpl[i])

    def c_actc(i):
        p = (p0, p1, p2, p3)[i]
        return remote(actp.at[c, p], actp.at[c, p], s_actc.at[i], r_actc.at[i], dsib)

    def c_prec(i):
        p = (p0, p1, p2, p3)[i]
        return remote(pre.at[c, p], pre.at[c, p], s_prec.at[i], r_prec.at[i], dsib)

    def c_sib():
        return remote(part, sibr, s_sib, r_sib, dsib)

    def c_pl(i):
        return remote(sums.at[i], plr.at[i], s_pl.at[i], r_pl.at[i], dpl[i])

    def chain(at, s, r, sc=None, rc=None):
        def hop(h, d, send):
            block = z - (h - 1) if d == 0 else z + (h - 1)
            if not send:
                block = z - h if d == 0 else z + h
            return remote(at(block), at(block), s.at[d, h - 1], r.at[d, h - 1],
                          (p0 * 2 + c, z + 1 if d == 0 else z - 1))

        def may(h, d, send):
            if send:
                return (z < 3) & (z >= h - 1) if d == 0 else (z > 0) & (z <= 4 - h)
            return z >= h if d == 0 else z <= 3 - h

        def across(h, d):
            block = z - h if d == 0 else z + h
            return remote(at(block), at(block), sc.at[d, h - 1], rc.at[d, h - 1], dsib)

        def over():
            return remote(at(z), at(z), sc.at[2, 0], rc.at[2, 0], dsib)

        def send(h):
            for d in range(2):
                @pl.when(may(h, d, True))
                def _(d=d):
                    hop(h, d, True).start()
            if h == 1 and sc is not None:
                over().start()

        def recv(h):
            for d in range(2):
                @pl.when(may(h, d, False))
                def _(d=d):
                    hop(h, d, False).wait_recv()
                    if sc is not None:
                        across(h, d).start()

        def finish():
            over().wait_recv()
            for h in (1, 2, 3):
                for d in range(2):
                    @pl.when(may(h, d, False))
                    def _(d=d, h=h):
                        across(h, d).wait_recv()

        def sent():
            if sc is not None:
                over().wait_send()
            for h in (1, 2, 3):
                for d in range(2):
                    @pl.when(may(h, d, True))
                    def _(d=d, h=h):
                        hop(h, d, True).wait_send()
                    if sc is not None:
                        @pl.when(may(h, d, False))
                        def _(d=d, h=h):
                            across(h, d).wait_send()
        return send, recv, finish, sent

    x_send, x_recv, x_finish, x_sent = chain(lambda b: xall.at[c, b], s_x, r_x, s_xc, r_xc)
    y_send, y_recv, y_finish, y_sent = chain(lambda b: dyall.at[c, b], s_y, r_y, s_yc, r_yc)
    q_send, q_recv, _, q_sent = chain(
        lambda b: qkvw.at[pl.ds(pl.multiple_of(b * 384, 384), 384)], s_qkv, r_qkv)

    g_c = remote(gpart, gsib, s_gc, r_gc, dsib)
    o_c = remote(opart, osib, s_oc, r_oc, dsib)

    def weights_a(k):
        if k:
            c_wz(k).wait_recv()
        c_wp(k, 0).start()

    def weights_b(k):
        c_wp(k, 0).wait_recv()
        c_wp(k, 1).start()
        c_wp(k, 2).start()

    for k in (1, 2, 3):
        c_small(k).start()
    local = [pltpu.make_async_copy(small, smalls.at[z], sl.at[0]),
             pltpu.make_async_copy(qkv_cols, qkvw.at[pl.ds(pl.multiple_of(z * 384, 384), 384)], sl.at[1]),
             pltpu.make_async_copy(wpiece.at[z], wbuf.at[:, rows(z, p0)], sl.at[2]),
             pltpu.make_async_copy(dy, dyall.at[c, z], sl.at[3])]
    for one in local:
        one.start()
    own_proj = pltpu.make_async_copy(proj.at[pl.ds(pl.multiple_of(c * 192, 192), 192)], projw, sl.at[4])

    @pl.when(z == p0)
    def _():
        own_proj.start()
    tok_f = tok[...].astype(F32)
    inv1 = lax.rsqrt(jnp.mean(tok_f * tok_f, axis=1, keepdims=True) + EPS)
    for k in (1, 2, 3):
        c_small(k).wait_recv()
    local[1].wait()
    q_send(1)
    for k in (1, 2, 3):
        c_pz(k).start()
    local[0].wait()
    gain1 = jnp.concatenate([smalls[i, 0:1, :] for i in range(4)], axis=1).astype(F32)
    actp[c, p0] = (tok_f * inv1 * gain1).astype(BF)
    pre[c, p0] = prefix[...]
    for i in range(3):
        c_act(i).start()
        c_pre(i).start()
    c_actc(0).start()
    c_prec(0).start()
    q_recv(1)
    q_send(2)
    q_recv(2)
    q_send(3)
    for i in range(3):
        c_act(i).wait_recv()
        c_pre(i).wait_recv()
        c_actc(i + 1).start()
        c_prec(i + 1).start()
    weights_a(0)
    q_recv(3)
    local[3].wait()

    row = lax.broadcasted_iota(jnp.int32, (128, 128), 0)
    col = lax.broadcasted_iota(jnp.int32, (128, 128), 1)
    causal = col <= row
    col_f = col.astype(F32)

    def attention(cc):
        pr[...] = jnp.dot(actp[cc].reshape(512, 1536), qkvw[...], preferred_element_type=F32).reshape(4, 128, 320)

        def one(i, _):
            lo = turn(pr[i, :, 0:128], cos_t[...], sin_t[...]).astype(BF)
            hi = turn(pr[i, :, 128:256], cos_t[...], sin_t[...]).astype(BF)
            qs[cc, i, 0:128] = lo[:, 0:64]
            qs[cc, i, 128:256] = lo[:, 64:128]
            qs[cc, i, 256:384] = hi[:, 0:64]
            ks[cc, i] = hi[:, 64:128]
            vs[cc, i] = pr[i, :, 256:320].astype(BF)
            sc = lax.dot_general(qs[cc, i], ks[cc, i], (((1,), (1,)), ((), ())), preferred_element_type=F32)
            allowed = causal | (col_f < pre[cc, i, 0:1, :])
            sc = jnp.where(allowed[None], sc.reshape(3, 128, 128) * (64 ** -0.5), -1e30)
            ex = jnp.exp(sc - jnp.max(sc, axis=-1, keepdims=True))
            pb = (ex / jnp.sum(ex, axis=-1, keepdims=True)).reshape(384, 128)
            probs[cc, i] = pb
            at = jnp.dot(pb.astype(BF), vs[cc, i], preferred_element_type=F32).astype(BF)
            for h in range(3):
                att[cc, i, :, h * 64 : (h + 1) * 64] = at[h * 128 : (h + 1) * 128]
            return 0
        lax.fori_loop(0, 4, one, 0)

    attention(c)
    for i in range(4):
        c_actc(i).wait_recv()
        c_prec(i).wait_recv()
    attention(1 - c)
    for k in (1, 2, 3):
        c_pz(k).wait_recv()
        owner = zf[k]

        @pl.when(owner != p0)
        def _(k=k, owner=owner):
            c_pq(k, owner).start()

        @pl.when(owner == p0)
        def _(k=k):
            projw[quarter(p0)] = projq[k - 1]

    for k in (1, 3, 2):
        c_wz(k).start()

    @pl.when(z == p0)
    def _():
        own_proj.wait()

    @pl.when(z != p0)
    def _():
        for i in range(3):
            c_pq_in(i).wait_recv()

    weights_b(0)

    def to_sib(i, _):
        part[i] = jnp.dot(att[1 - c, i], projw[...], preferred_element_type=F32).astype(BF)
        return 0
    lax.fori_loop(0, 4, to_sib, 0)
    c_sib().start()
    c_sib().wait_recv()
    for i in range(3):
        sums[i] = (jnp.dot(att[c, peers[i]], projw[...], preferred_element_type=F32)
                   + sibr[peers[i]].astype(F32)).astype(BF)
        c_pl(i).start()
    residual = (tok_f + jnp.dot(att[c, p0], projw[...], preferred_element_type=F32) + sibr[p0].astype(F32))
    for i in range(3):
        c_pl(i).wait_recv()
        residual = residual + plr[i].astype(F32)
    res[...] = residual
    inv2 = lax.rsqrt(jnp.mean(residual * residual, axis=1, keepdims=True) + EPS)
    gain2 = jnp.concatenate([smalls[i, 1:2, :] for i in range(4)], axis=1).astype(F32)
    act2 = (residual * inv2 * gain2).astype(BF)
    router = jnp.concatenate([smalls[i, 16:32, :] for i in range(4)], axis=1)
    logits = lax.dot_general(act2, router, (((1,), (1,)), ((), ())), preferred_element_type=F32)
    chosen, kept = masks[0] > 0.0, masks[1]
    top = jnp.max(jnp.where(chosen, logits, -1e30), axis=1, keepdims=True)
    ge = jnp.where(chosen, jnp.exp(jnp.where(chosen, logits - top, 0.0)), 0.0)
    gt = ge / jnp.sum(ge, axis=1, keepdims=True)
    gates[...] = gt
    wide_gates = jnp.concatenate([gt * kept, jnp.zeros((128, 112), F32)], axis=1)
    gate_hi = wide_gates.astype(BF)
    xall[c, z, :, :1536] = act2
    xall[c, z, :, 1536:1664] = gate_hi
    xall[c, z, :, 1664:] = (wide_gates - gate_hi.astype(F32)).astype(BF)
    x_send(1)
    weights_a(1)
    weights_a(3)
    weights_b(1)
    x_recv(1)
    x_send(2)
    weights_b(3)
    weights_a(2)
    x_recv(2)
    x_send(3)
    y_send(1)
    weights_b(2)
    x_recv(3)
    y_recv(1)
    y_send(2)
    y_recv(2)
    y_send(3)
    y_recv(3)
    local[2].wait()
    for k in range(4):
        c_wp(k, 1).wait_recv()
        c_wp(k, 2).wait_recv()
    x_finish()
    y_finish()

    lane = lax.broadcasted_iota(jnp.int32, (512, 128), 1)
    ggp[...] = jnp.zeros_like(ggp)

    def expert(n, _):
        j, t = n // 2, lax.rem(n, 2)
        gu = jnp.dot(xall[t, :, :, :1536].reshape(512, 1536), wbuf[j, :, : 2 * half], preferred_element_type=F32)
        bk = jnp.dot(dyall[t].reshape(512, 1536), wbuf[j, :, 2 * half :], preferred_element_type=F32)
        mine = lane == z * 4 + j
        both = (xall[t, :, :, 1536:1664].astype(F32) + xall[t, :, :, 1664:].astype(F32)).reshape(512, 128)
        w = jnp.sum(jnp.where(mine, both, 0.0), axis=1, keepdims=True)
        g, u = gu[:, :half], gu[:, half:]
        sg = 1.0 / (1.0 + jnp.exp(-g))
        silu = g * sg
        hid = silu * u
        hw[j, pl.ds(pl.multiple_of(t * 512, 512), 512)] = (hid * w).astype(BF)
        ggp[t] = ggp[t] + jnp.where(mine, jnp.sum(bk * hid, axis=1, keepdims=True), 0.0).reshape(4, 128, 128)
        gh = bk * w
        at = pl.ds(pl.multiple_of(t * 512, 512), 512)
        ggu[j, at, :half] = (gh * u * sg * (1.0 + g * (1.0 - sg))).astype(BF)
        ggu[j, at, half:] = (gh * silu).astype(BF)
        return 0
    lax.fori_loop(0, 8, expert, 0)
    saves = []

    def save(src, dst):
        one = pltpu.make_async_copy(src, dst, sl.at[5 + len(saves)])
        one.start()
        saves.append(one)
    for src, dst in ((xall, o_x), (dyall, o_dy), (ggu, o_ggu), (hw, o_hw), (actp, o_act), (qs, o_q), (ks, o_k),
                     (vs, o_v), (probs, o_probs), (att, o_att), (qkvw, o_qkvw), (projw, o_projw),
                     (smalls, o_small), (res, o_res), (gates, o_gates)):
        save(src, dst)

    def block(grad, t, n):
        at = pl.ds(pl.multiple_of(t * 512, 512), 512)
        lanes = pl.ds(pl.multiple_of(n * 256, 256), 256)
        acc = jnp.zeros((512, 256), F32)
        for j in range(4):
            a = ggu[j, at] if grad else hw[j, at]
            b = wbuf[j, lanes, : 2 * half] if grad else wbuf[j, lanes, 2 * half :]
            acc = acc + lax.dot_general(a, b, (((1,), (1,)), ((), ())), preferred_element_type=F32)
        return acc.reshape(4, 128, 256), lanes

    def partial(grad, buf):
        def one(n, _):
            v, lanes = block(grad, 1 - c, n)
            buf[:, :, lanes] = v.astype(BF)
            return 0
        lax.fori_loop(0, 6, one, 0)

    def own(grad, sib, dst):
        def one(n, _):
            v, lanes = block(grad, c, n)
            dst[:, :, lanes] = (v + sib[:, :, lanes].astype(F32)).astype(BF)
            return 0
        lax.fori_loop(0, 6, one, 0)

    def put_gate_grads(dst, v):
        hi = v.astype(BF)
        dst[:, :, 1536:1664] = hi
        dst[:, :, 1664:] = (v - hi.astype(F32)).astype(BF)

    def gate_grads(v):
        return v[..., 1536:1664].astype(F32) + v[..., 1664:].astype(F32)

    put_gate_grads(gpart, ggp[1 - c])
    partial(True, gpart)
    g_c.start()
    partial(False, opart)
    o_c.start()
    g_c.wait_recv()
    put_gate_grads(gsum, ggp[c] + gate_grads(gsib))
    own(True, gsib, gsum)
    save(gsum, o_gsum)
    o_c.wait_recv()
    own(False, osib, osum)
    save(osum, o_osum)

    for k in (1, 2, 3):
        for one in (c_small(k), c_pz(k), c_wz(k)):
            one.wait_send()

        @pl.when(zf[k] != p0)
        def _(k=k):
            c_pq(k, zf[k]).wait_send()
    for k in range(4):
        for i in range(3):
            c_wp(k, i).wait_send()
        for one in (c_actc(k), c_prec(k)):
            one.wait_send()
    for i in range(3):
        for one in (c_act(i), c_pre(i), c_pl(i)):
            one.wait_send()
    for one in (c_sib(), g_c, o_c):
        one.wait_send()
    x_sent()
    y_sent()
    q_sent()
    for one in saves:
        one.wait()


def front(tok, dy, wpiece, qkv_cols, proj, small, masks, prefix, cos_t, sin_t):
    sem, vm = pltpu.SemaphoreType.DMA, pltpu.VMEM
    out = lambda shape, kind=BF: jax.ShapeDtypeStruct(shape, kind)
    outs = (
        out((2, 4, 128, 1792)), out((2, 4, 128, 1536)), out((4, 1024, 512)), out((4, 1024, 256)),
        out((2, 4, 128, 1536)), out((2, 4, 384, 64)), out((2, 4, 128, 64)), out((2, 4, 128, 64)),
        out((2, 4, 384, 128), F32), out((2, 4, 128, 192)), out((1536, 320)), out((192, 1536)),
        out((4, 32, 384)), out((128, 1536), F32), out((128, 16), F32), out((4, 128, 1792)),
        out((4, 128, 1536)),
    )
    block, quad = vm((2, 4, 128, 1536), BF), vm((4, 128, 1536), BF)
    three = vm((3, 128, 1536), BF)
    quad_g = vm((4, 128, 1792), BF)
    scratch = [
        vm((4, 32, 384), BF), vm((1536, 320), BF), vm((192, 1536), BF), vm((3, 48, 1536), BF),
        block, vm((2, 4, 8, 128), F32),
        vm((4, 128, 320), F32), vm((2, 4, 384, 64), BF), vm((2, 4, 128, 64), BF), vm((2, 4, 128, 64), BF),
        vm((2, 4, 384, 128), F32), vm((2, 4, 128, 192), BF), quad, quad, three, three,
        vm((2, 4, 128, 1792), BF), block, vm((4, 1536, 768), BF), vm((4, 1024, 512), BF),
        vm((4, 1024, 256), BF), quad_g, quad, vm((2, 4, 128, 128), F32), quad_g, quad,
        quad_g, quad, vm((128, 1536), F32), vm((128, 16), F32),
    ]
    n3, n4, one = sem((3,)), sem((4,)), sem(())
    hops = [sem((2, 3)), sem((2, 3)), sem((3, 3)), sem((3, 3))]
    sems = [
        n3, n3, sem((2, 3)), sem((2, 3)), n3, n3, n3, n4, n3, n3, sem((4, 3)), sem((4, 3)),
        n3, n3, n3, n3, n4, n4, n4, n4, one, one, n3, n3,
        *hops, *hops, one, one, one, one, sem((24,)),
    ]
    vmem, any_ = pl.BlockSpec(memory_space=pltpu.VMEM), pl.BlockSpec(memory_space=pl.ANY)
    return pl.pallas_call(
        front_kernel,
        out_shape=outs,
        in_specs=[vmem, any_, any_, any_, any_, any_, vmem, vmem, vmem, vmem],
        out_specs=[any_] * len(outs),
        scratch_shapes=scratch + sems,
        compiler_params=pltpu.CompilerParams(
            collective_id=1, has_side_effects=True, vmem_limit_bytes=62 * 1024 * 1024),
        name="front",
    )(tok, dy, wpiece, qkv_cols, proj, small, masks, prefix, cos_t, sin_t)


def back_kernel(i_x, i_dy, i_ggu, i_hw, i_act, i_q, i_k, i_v, i_probs, i_att, i_qkvw, i_projw, i_small,
                i_res, i_gates, i_gsum, i_osum, tok, kept, cos_t, sin_t,
                o_e, o_gtok, o_qg, o_pg, o_terms, o_op,
                xb, dyb, ggu, hw, qs, ks, vs, probs, att, qkvw, projw, smalls, res, gates, gown, grecv,
                gw, recv1, send2, recv2, zs, zr, ib, agv,
                gres, gresf, gproj, sibr, plr, qgp, qz, qgo, pgp, pgr, pq2, pgo, terms, tz, tsib, tpl, tout, gtok,
                s1, r1, s2, r2, sz, rz, sa, ra, ss, rs, la,
                s_g, r_g, s_gr, r_gr, s_grc, r_grc, s_sib, r_sib, s_pl, r_pl, s_qz, r_qz, s_qo, r_qo,
                s_qoc, r_qoc, s_p1, r_p1, s_p2, r_p2, s_po, r_po, s_poc, r_poc, s_tz, r_tz, s_ts, r_ts,
                s_tp, r_tp, s_o, r_o, ld, sv):
    y, x, c, z = place()
    half = HID // 2
    wide = 3 * half
    nq = 6

    def slot(a, b):
        return flip(y, a * c + b * (1 - c)) * 2 + flip(x, a * (1 - c) + b * c)

    p0, p1, p2, p3 = slot(0, 0), slot(1, 0), slot(0, 1), slot(1, 1)
    peers = (p1, p2, p3)
    d1, d2, dsib = (p1 * 2 + c, z), (p2 * 2 + c, z), (p0 * 2 + 1 - c, z)
    dpl = [(p * 2 + c, z) for p in peers]
    zk = [lax.rem(z + k, 4) for k in range(4)]
    dz = [(p0 * 2 + c, zz) for zz in zk]

    loads = {}

    def load(name, src, dst):
        loads[name] = pltpu.make_async_copy(src, dst, ld.at[len(loads)])
        loads[name].start()
    load("x", i_x.at[:, :, :, pl.ds(0, 1536)], xb)
    load("ggu", i_ggu, ggu)
    load("dy", i_dy, dyb)
    load("hw", i_hw, hw)
    load("gown", i_gsum.at[z], gown)
    for name, src, dst in (("res", i_res, res), ("gates", i_gates, gates), ("small", i_small, smalls),
                           ("projw", i_projw, projw), ("probs", i_probs, probs), ("q", i_q, qs), ("k", i_k, ks),
                           ("v", i_v, vs), ("att", i_att, att), ("qkvw", i_qkvw, qkvw)):
        load(name, src, dst)

    barrier = pltpu.get_barrier_semaphore()
    for to in dpl + dz[1:] + [dsib]:
        pl.semaphore_signal(barrier, 1, device_id=to, device_id_type=MESH)
    pl.semaphore_wait(barrier, 7)

    def remote(src, dst, s, r, to):
        return pltpu.make_async_remote_copy(src, dst, s, r, device_id=to, device_id_type=MESH)

    def copy1(q, b):
        return remote(gw.at[q // 2, slot(1, b), lax.rem(q, 2)], recv1.at[q, b], s1.at[q, b], r1.at[q, b], d1)

    def copy2(q):
        return remote(send2.at[lax.rem(q, 2)], recv2.at[q], s2.at[q], r2.at[q], d2)

    def copyz(q, k):
        return remote(zs.at[lax.rem(q, 2), zk[k]], zr.at[q, z], sz.at[q, k - 1], rz.at[q, k - 1], dz[k])

    def rows(q, p):
        return pl.ds(pl.multiple_of(((q // 2) * 8 + p * 2 + lax.rem(q, 2)) * 256, 256), 256)

    def copya(q, i):
        p, who = ((p0, d1), (p0, d2), (p1, d2))[i]
        src = agv.at[lax.rem(q, 2)] if i < 2 else o_e.at[c, rows(q, p)]
        return remote(src, o_e.at[c, rows(q, p)], sa.at[q, i], ra.at[q, i], who)

    def copys(q, i):
        p = (p0, p1, p2, p3)[i]
        src = agv.at[lax.rem(q, 2)] if i == 0 else o_e.at[c, rows(q, p)]
        return remote(src, o_e.at[c, rows(q, p)], ss.at[q, i], rs.at[q, i], dsib)

    def keep(q):
        return pltpu.make_async_copy(agv.at[lax.rem(q, 2)], o_e.at[c, rows(q, p0)], la.at[q])

    def c_g(k):
        return remote(i_gsum.at[zk[k]], grecv.at[k - 1], s_g.at[k - 1], r_g.at[k - 1], dz[k])

    def c_o(k):
        return remote(i_osum.at[zk[k]], o_op.at[k - 1], s_o.at[k - 1], r_o.at[k - 1], dz[k])

    def c_gr(i):
        return remote(gres.at[c, p0], gres.at[c, p0], s_gr.at[i], r_gr.at[i], dpl[i])

    def c_grc(i):
        p = (p0, p1, p2, p3)[i]
        return remote(gres.at[c, p], gres.at[c, p], s_grc.at[i], r_grc.at[i], dsib)

    def c_sib():
        return remote(dyb.at[0], sibr, s_sib, r_sib, dsib)

    def c_pl(i):
        return remote(dyb.at[1, i], plr.at[i], s_pl.at[i], r_pl.at[i], dpl[i])

    def c_qz(k):
        return remote(qgp.at[zk[k]], qz.at[k - 1], s_qz.at[k - 1], r_qz.at[k - 1], dz[k])

    def c_qo(i):
        return remote(qgo, o_qg.at[p0 * 2 + c], s_qo.at[i], r_qo.at[i], dpl[i])

    def c_qoc(i):
        r = (p0, p1, p2, p3)[i] * 2 + c
        return remote(qgo if i == 0 else o_qg.at[r], o_qg.at[r], s_qoc.at[i], r_qoc.at[i], dsib)

    def c_p1(i):
        return remote(pgp.at[peers[i]], pgr.at[p0], s_p1.at[i], r_p1.at[i], dpl[i])

    def c_p2(k):
        return remote(pgr.at[zk[k]], pq2.at[k - 1], s_p2.at[k - 1], r_p2.at[k - 1], dz[k])

    def c_po(i):
        return remote(pgo, o_pg.at[c, p0], s_po.at[i], r_po.at[i], dpl[i])

    def c_poc(i):
        p = (p0, p1, p2, p3)[i]
        return remote(pgo if i == 0 else o_pg.at[c, p], o_pg.at[c, p], s_poc.at[i], r_poc.at[i], dsib)

    def lanes_of(zz):
        return pl.ds(pl.multiple_of(zz * 384, 384), 384)

    def c_tz(k):
        return remote(terms.at[:, lanes_of(zk[k])], tz.at[k], s_tz.at[k - 1], r_tz.at[k - 1], dz[k])

    def c_ts():
        return remote(tz.at[0], tsib, s_ts, r_ts, dsib)

    def c_tp(i):
        return remote(tpl.at[p0], tpl.at[p0], s_tp.at[i], r_tp.at[i], dpl[i])

    saves = [pltpu.make_async_copy(gtok, o_gtok, sv.at[0]),
             pltpu.make_async_copy(qgo, o_qg.at[p0 * 2 + c], sv.at[1]),
             pltpu.make_async_copy(pgo, o_pg.at[c, p0], sv.at[2]),
             pltpu.make_async_copy(tout, o_terms, sv.at[3])]
    act_load = pltpu.make_async_copy(i_act, xb, sv.at[4])

    for k in (1, 2, 3):
        c_g(k).start()
    loads["x"].wait()
    loads["ggu"].wait()
    loads["dy"].wait()
    loads["hw"].wait()

    def stage1(q):
        @pl.when(lax.rem(q, 2) == 0)
        def _():
            q3 = q // 2

            def side(ref):
                return jnp.concatenate(
                    [ref[:, :, :, pl.ds(pl.multiple_of(zz * 384 + q3 * 128, 128), 128)].reshape(1024, 128)
                     for zz in range(4)], axis=1)
            xs, ds_ = side(xb), side(dyb)

            def one(j, _):
                up = lax.dot_general(xs, ggu[j], (((0,), (0,)), ((), ())), preferred_element_type=F32).astype(BF)
                dn = lax.dot_general(ds_, hw[j], (((0,), (0,)), ((), ())), preferred_element_type=F32).astype(BF)
                for zz in range(4):
                    for p in range(4):
                        for h in range(2):
                            at = zz * 128 + p * 32 + h * 16
                            gw[q3, p, h, zz, j, :, : 2 * half] = up[at : at + 16]
                            gw[q3, p, h, zz, j, :, 2 * half :] = dn[at : at + 16]
                return 0
            lax.fori_loop(0, 4, one, 0)
        for b in range(2):
            copy1(q, b).start()

    def stage2(q):
        for b in range(2):
            copy1(q, b).wait_recv()

        def one(zz, _):
            send2[lax.rem(q, 2), zz] = (gw[q // 2, p2, lax.rem(q, 2), zz].astype(F32)
                                        + recv1[q, 1, zz].astype(F32)).astype(BF)
            return 0
        lax.fori_loop(0, 4, one, 0)
        copy2(q).start()

    def stage3(q):
        copy2(q).wait()

        def one(zz, _):
            zs[lax.rem(q, 2), zz] = (gw[q // 2, p0, lax.rem(q, 2), zz].astype(F32) + recv1[q, 0, zz].astype(F32)
                                     + recv2[q, zz].astype(F32)).astype(BF)
            return 0
        lax.fori_loop(0, 4, one, 0)
        for k in range(1, 4):
            copyz(q, k).start()
        zr[q, z] = zs[lax.rem(q, 2), z]

    def stage4(q):
        for k in range(1, 4):
            copyz(q, k).wait()

        @pl.when(q >= 2)
        def _():
            copya(q - 2, 0).wait_send()
            copya(q - 2, 1).wait_send()
            copys(q - 2, 0).wait_send()
            keep(q - 2).wait()
        for zz in range(4):
            for j in range(4):
                for l in range(wide // 128):
                    ib[l, pl.ds(zz * 4 + j, 16, stride=EXPERTS), :] = (
                        zr[q, zz, j, :, l * 128 : (l + 1) * 128].astype(F32))
        for l in range(wide // 128):
            agv[lax.rem(q, 2), :, l * 128 : (l + 1) * 128] = ib[l].astype(BF)
        copya(q, 0).start()
        copys(q, 0).start()
        keep(q).start()

    def stage5(q):
        copya(q, 0).wait_recv()
        copya(q, 1).start()
        copya(q, 2).start()
        copys(q, 1).start()

    def stage6(q):
        copya(q, 1).wait_recv()
        copya(q, 2).wait_recv()
        copys(q, 2).start()
        copys(q, 3).start()

    def stage7(q):
        for i in range(4):
            copys(q, i).wait_recv()

    def norm_two():
        r = res[...]
        inv = lax.rsqrt(jnp.mean(r * r, axis=1, keepdims=True) + EPS)
        return inv, r * inv

    def norm_one():
        t = tok[...].astype(F32)
        inv = lax.rsqrt(jnp.mean(t * t, axis=1, keepdims=True) + EPS)
        return inv, t * inv

    def gain(row):
        return jnp.concatenate([smalls[i, row : row + 1, :] for i in range(4)], axis=1).astype(F32)

    def event_residual():
        for name in ("gown", "res", "gates", "small"):
            loads[name].wait()
        for k in (1, 2, 3):
            c_g(k).wait_recv()
        tail = slice(1536, 1664), slice(1664, 1792)

        def gate_part(v):
            return (v[:, tail[0]].astype(F32) + v[:, tail[1]].astype(F32))[:, :EXPERTS]
        gg = (gate_part(gown[...]) + gate_part(grecv[0]) + gate_part(grecv[1]) + gate_part(grecv[2])) * kept[...]
        gt = gates[...]
        gl = (gt * (gg - jnp.sum(gt * gg, axis=1, keepdims=True))).astype(BF)
        router_t = jnp.concatenate([smalls[i, 16:32, :] for i in range(4)], axis=1)
        ga = jnp.dot(gl, router_t, preferred_element_type=F32)
        ga = ga + gown[:, :1536].astype(F32)
        for k in range(3):
            ga = ga + grecv[k, :, :1536].astype(F32)
        inv, normed = norm_two()
        terms[8:24, :] = lax.dot_general(gl, xb[c, z], (((0,), (0,)), ((), ())), preferred_element_type=F32)
        terms[1:2, :] = jnp.sum(ga * normed, axis=0, keepdims=True)
        scaled = ga * gain(1)
        gr = dyb[c, z].astype(F32) + inv * (scaled - normed * jnp.mean(scaled * normed, axis=1, keepdims=True))
        gresf[...] = gr
        gres[c, p0] = gr.astype(BF)
        for i in range(3):
            c_gr(i).start()
        c_grc(0).start()

    def event_share():
        for i in range(3):
            c_gr(i).wait_recv()
            c_grc(i + 1).start()
        act_load.start()

    scale = 64 ** -0.5

    def event_attention():
        for name in ("projw", "probs", "q", "k", "v", "att", "qkvw"):
            loads[name].wait()
        for i in range(4):
            c_grc(i).wait_recv()

        def one(n, _):
            cc, i = n // 4, lax.rem(n, 4)
            gb = lax.dot_general(gres[cc, i], projw[...], (((1,), (1,)), ((), ())),
                                 preferred_element_type=F32).astype(BF)
            ga = jnp.concatenate([gb[:, h * 64 : (h + 1) * 64] for h in range(3)], axis=0)
            pb = probs[cc, i]
            gv = lax.dot_general(pb.astype(BF), ga, (((0,), (0,)), ((), ())), preferred_element_type=F32)
            gp = lax.dot_general(ga, vs[cc, i], (((1,), (1,)), ((), ())), preferred_element_type=F32)
            gs = (pb * (gp - jnp.sum(pb * gp, axis=-1, keepdims=True))).astype(BF)
            gq = jnp.dot(gs, ks[cc, i], preferred_element_type=F32) * scale
            gk = lax.dot_general(gs, qs[cc, i], (((0,), (0,)), ((), ())), preferred_element_type=F32) * scale
            lo = jnp.concatenate([gq[0:128], gq[128:256]], axis=1)
            hi = jnp.concatenate([gq[256:384], gk], axis=1)
            gproj[cc, i, :, 0:128] = turn(lo, cos_t[...], -sin_t[...]).astype(BF)
            gproj[cc, i, :, 128:256] = turn(hi, cos_t[...], -sin_t[...]).astype(BF)
            gproj[cc, i, :, 256:320] = gv.astype(BF)
            return 0
        lax.fori_loop(0, 8, one, 0)

        def to_sib(i, _):
            dyb[0, i] = lax.dot_general(gproj[1 - c, i], qkvw[...], (((1,), (1,)), ((), ())),
                                        preferred_element_type=F32).astype(BF)
            return 0
        lax.fori_loop(0, 4, to_sib, 0)
        c_sib().start()
        pg = lax.dot_general(att[...].reshape(1024, 192), gres[...].reshape(1024, 1536), (((0,), (0,)), ((), ())),
                             preferred_element_type=F32)
        pgp[...] = pg.astype(BF).reshape(4, 48, 1536)
        for i in range(3):
            c_p1(i).start()
        pgr[p0] = pgp[p0]

    def event_columns():
        act_load.wait()

        def one(zz, _):
            a = xb[:, :, :, lanes_of(zz)].reshape(1024, 384)
            qgp[zz] = lax.dot_general(a, gproj[...].reshape(1024, 320), (((0,), (0,)), ((), ())),
                                      preferred_element_type=F32).astype(BF)
            return 0
        lax.fori_loop(0, 4, one, 0)
        for k in (1, 2, 3):
            c_qz(k).start()
        c_sib().wait()

        def part(p):
            return lax.dot_general(gproj[c, p], qkvw[...], (((1,), (1,)), ((), ())),
                                   preferred_element_type=F32) + sibr[p].astype(F32)
        for i in range(3):
            dyb[1, i] = part(peers[i]).astype(BF)
            c_pl(i).start()
        gtok[...] = part(p0)
        for i in range(3):
            c_p1(i).wait_recv()
        for k in (1, 2, 3):
            c_p2(k).start()

    def event_tokens():
        ga = gtok[...]
        for i in range(3):
            c_pl(i).wait_recv()
            ga = ga + plr[i].astype(F32)
        inv, normed = norm_one()
        terms[0:1, :] = jnp.sum(ga * normed, axis=0, keepdims=True)
        scaled = ga * gain(0)
        gtok[...] = gresf[...] + inv * (scaled - normed * jnp.mean(scaled * normed, axis=1, keepdims=True))
        saves[0].start()
        for k in (1, 2, 3):
            c_tz(k).start()
        for k in (1, 2, 3):
            c_qz(k).wait_recv()
        qgo[...] = (qgp[z].astype(F32) + qz[0].astype(F32) + qz[1].astype(F32) + qz[2].astype(F32)).astype(BF)
        for i in range(3):
            c_qo(i).start()
        c_qoc(0).start()
        saves[1].start()
        for k in (1, 2, 3):
            c_p2(k).wait_recv()
        pgo[...] = (pgr[z].astype(F32) + pq2[0].astype(F32) + pq2[1].astype(F32) + pq2[2].astype(F32)).astype(BF)
        for i in range(3):
            c_po(i).start()
        c_poc(0).start()
        saves[2].start()
        for k in (1, 2, 3):
            c_o(k).start()

    def event_terms():
        for k in (1, 2, 3):
            c_tz(k).wait_recv()
        tz[0] = terms[:, lanes_of(z)] + tz[1] + tz[2] + tz[3]
        c_ts().start()
        for i in range(3):
            c_qo(i).wait_recv()
            c_qoc(i + 1).start()
            c_po(i).wait_recv()
            c_poc(i + 1).start()

    def event_sums():
        c_ts().wait()
        tpl[p0] = tz[0] + tsib[...]
        for i in range(3):
            c_tp(i).start()

    def event_last():
        for i in range(3):
            c_tp(i).wait_recv()
        tout[...] = tpl[0] + tpl[1] + tpl[2] + tpl[3]
        saves[3].start()
        for i in range(4):
            c_qoc(i).wait_recv()
            c_poc(i).wait_recv()
        for k in (1, 2, 3):
            c_o(k).wait_recv()

    stages = (stage1, stage2, stage3, stage4, stage5, stage6, stage7)
    events = {3: event_residual, 4: event_share, 5: event_attention, 6: event_columns, 8: event_tokens,
              9: event_terms, 10: event_sums, 11: event_last}

    def step(t, _):
        for i, stage in enumerate(stages):
            q = t - i

            @pl.when((q >= 0) & (q < nq))
            def _(stage=stage, q=q):
                stage(q)
        for at, event in events.items():
            @pl.when(t == at)
            def _(event=event):
                event()
        return 0

    lax.fori_loop(0, nq + len(stages) - 1, step, 0)

    def left(q, _):
        for b in range(2):
            copy1(q, b).wait_send()
        for i in range(1, 4):
            copys(q, i).wait_send()
        copya(q, 2).wait_send()

        @pl.when(q >= nq - 2)
        def _():
            copya(q, 0).wait_send()
            copya(q, 1).wait_send()
            copys(q, 0).wait_send()
            keep(q).wait()
        return 0
    lax.fori_loop(0, nq, left, 0)
    for k in (1, 2, 3):
        for one in (c_g(k), c_o(k), c_qz(k), c_p2(k), c_tz(k)):
            one.wait_send()
    for i in range(3):
        for one in (c_gr(i), c_pl(i), c_qo(i), c_p1(i), c_po(i), c_tp(i)):
            one.wait_send()
    for i in range(4):
        for one in (c_grc(i), c_qoc(i), c_poc(i)):
            one.wait_send()
    for one in saves:
        one.wait()


def back(front_outs, tok, kept, cos_t, sin_t):
    nq, wide = 6, 3 * HID // 2
    sem, vm = pltpu.SemaphoreType.DMA, pltpu.VMEM
    out = lambda shape, kind=BF: jax.ShapeDtypeStruct(shape, kind)
    piece = (4, 4, 16, wide)
    outs = (out((2, 6144, wide)), out((128, 1536), F32), out((8, 384, 320)), out((2, 4, 48, 1536)),
            out((24, 384), F32), out((3, 128, 1536)))
    block, quad, three = vm((2, 4, 128, 1536), BF), vm((4, 128, 1536), BF), vm((3, 128, 1536), BF)
    scratch = [
        block, block, vm((4, 1024, 512), BF), vm((4, 1024, 256), BF), vm((2, 4, 384, 64), BF),
        vm((2, 4, 128, 64), BF), vm((2, 4, 128, 64), BF), vm((2, 4, 384, 128), F32), vm((2, 4, 128, 192), BF),
        vm((1536, 320), BF), vm((192, 1536), BF), vm((4, 32, 384), BF), vm((128, 1536), F32), vm((128, 16), F32),
        vm((128, 1792), BF), vm((3, 128, 1792), BF),
        vm((3, 4, 2) + piece, BF), vm((nq, 2) + piece, BF), vm((2,) + piece, BF), vm((nq,) + piece, BF),
        vm((2,) + piece, BF), vm((nq,) + piece, BF), vm((wide // 128, 256, 128), F32), vm((2, 256, wide), BF),
        block, vm((128, 1536), F32), vm((2, 4, 128, 320), BF), quad, three, vm((4, 384, 320), BF),
        vm((3, 384, 320), BF), vm((384, 320), BF), vm((4, 48, 1536), BF), vm((4, 48, 1536), BF),
        vm((3, 48, 1536), BF), vm((48, 1536), BF), vm((24, 1536), F32), vm((4, 24, 384), F32),
        vm((24, 384), F32), vm((4, 24, 384), F32), vm((24, 384), F32), vm((128, 1536), F32),
    ]
    n3, n4, one = sem((3,)), sem((4,)), sem(())
    sems = [
        sem((nq, 2)), sem((nq, 2)), sem((nq,)), sem((nq,)), sem((nq, 3)), sem((nq, 3)), sem((nq, 3)), sem((nq, 3)),
        sem((nq, 4)), sem((nq, 4)), sem((nq,)),
        n3, n3, n3, n3, n4, n4, one, one, n3, n3, n3, n3, n3, n3,
        n4, n4, n3, n3, n3, n3, n3, n3, n4, n4, n3, n3, one, one,
        n3, n3, n3, n3, sem((16,)), sem((5,)),
    ]
    vmem, any_ = pl.BlockSpec(memory_space=pltpu.VMEM), pl.BlockSpec(memory_space=pl.ANY)
    return pl.pallas_call(
        back_kernel,
        out_shape=outs,
        in_specs=[any_] * 17 + [vmem] * 4,
        out_specs=[any_] * len(outs),
        scratch_shapes=scratch + sems,
        compiler_params=pltpu.CompilerParams(
            collective_id=2, has_side_effects=True, vmem_limit_bytes=62 * 1024 * 1024),
        name="back",
    )(*front_outs, tok, kept, cos_t, sin_t)


def widen_kernel(v, gu, dn):
    half = HID // 2
    for c in range(2):
        gu[:, c * half : (c + 1) * half] = v[c, :, :half].astype(F32)
        gu[:, HID + c * half : HID + (c + 1) * half] = v[c, :, half : 2 * half].astype(F32)
        dn[:, c * half : (c + 1) * half] = v[c, :, 2 * half :].astype(F32)


def widen(v):
    rows, step = v.shape[1], 512
    return pl.pallas_call(
        widen_kernel,
        out_shape=(jax.ShapeDtypeStruct((rows, 2 * HID), F32), jax.ShapeDtypeStruct((rows, HID), F32)),
        grid=(rows // step,),
        in_specs=[pl.BlockSpec((2, step, 3 * HID // 2), lambda i: (0, i, 0))],
        out_specs=[pl.BlockSpec((step, 2 * HID), lambda i: (i, 0)), pl.BlockSpec((step, HID), lambda i: (i, 0))],
        compiler_params=pltpu.CompilerParams(vmem_limit_bytes=40 * 1024 * 1024),
        name="widen",
    )(v)


def expert_grads_general(reps, grps, xs, dys, ggu, hw):
    local, half, width = ggu.shape[0], HID // 2, xs.shape[1]
    own = width // grps
    chips = reps // 2
    piece = own // chips
    same_core = [[2 * i + c for i in range(chips)] for c in range(2)]
    pairs = [[2 * i, 2 * i + 1] for i in range(chips)]
    up = jnp.einsum("td,eth->edh", xs, ggu, preferred_element_type=F32).astype(BF)
    down = jnp.einsum("td,eth->edh", dys, hw, preferred_element_type=F32).astype(BF)
    gw = jnp.concatenate([up, down], axis=2)
    gw = gw.reshape(local, grps, chips, piece, 3 * half).transpose(2, 1, 3, 0, 4)
    gw = gw.reshape(chips * grps * piece, local * 3 * half)
    gw = lax.psum_scatter(gw, "rep", scatter_dimension=0, tiled=True, axis_index_groups=same_core)
    gw = lax.all_to_all(gw.reshape(grps, piece, local, 3 * half), "grp", 0, 0, tiled=True)
    gw = gw.transpose(1, 0, 2, 3).reshape(piece, EXPERTS, 3 * half)
    gw = lax.all_gather(gw, "rep", axis=0, tiled=True, axis_index_groups=same_core)
    gw = lax.all_gather(gw, "rep", axis=0, tiled=False, axis_index_groups=pairs).astype(F32)
    gw = gw.reshape(2, own * EXPERTS, 3, half)
    gw = jnp.moveaxis(gw, 0, 2).reshape(own * EXPERTS, 3 * HID)
    return gw[:, : 2 * HID], gw[:, 2 * HID :]


def shards_general(
    reps,
    grps,
    tokens,
    attn_gain,
    query_key_value_weight,
    attn_proj,
    mlp_gain,
    w_router,
    w_gate_up,
    w_down,
    prefix_len,
    expert_ids,
    priority,
    cotangent,
):
    seq, width = tokens.shape
    own = width // grps
    local_experts = EXPERTS // grps
    heads = KEY_VALUE_HEADS
    groups = None if reps == heads else [list(range(i, i + heads)) for i in range(0, reps, heads)]
    rep, grp = lax.axis_index("rep"), lax.axis_index("grp")
    head = lax.rem(rep, heads)
    qw, hw = QPK * HEAD_WIDTH, HEAD_WIDTH
    q_all = QUERY_HEADS * HEAD_WIDTH

    small = jnp.concatenate([attn_gain[:, None], mlp_gain[:, None], w_router], axis=1)
    small = lax.all_gather(small, "grp", axis=0, tiled=True)
    gain_one, gain_two = small[:, 0].astype(F32)[None, :], small[:, 1].astype(F32)[None, :]
    router = small[:, 2:]
    qkv_cols = jnp.concatenate(
        [
            lax.dynamic_slice_in_dim(query_key_value_weight, head * qw, qw, 1),
            lax.dynamic_slice_in_dim(query_key_value_weight, q_all + head * hw, hw, 1),
            lax.dynamic_slice_in_dim(query_key_value_weight, q_all + heads * hw + head * hw, hw, 1),
        ],
        axis=1,
    )
    qkv_head = lax.all_gather(qkv_cols, "grp", axis=0, tiled=True)
    row = head * qw + jnp.arange(qw)
    mine = (row // own) == grp
    proj_rows = jnp.where(mine[:, None], jnp.take(attn_proj, jnp.where(mine, row - grp * own, 0), axis=0), 0)
    proj_head = lax.psum(proj_rows, "grp")

    core, chip, chips, half = lax.rem(rep, 2), rep // 2, reps // 2, HID // 2
    pairs = [[2 * i, 2 * i + 1] for i in range(chips)]
    same_core = [[2 * i + c for i in range(chips)] for c in range(2)]
    piece = own // chips
    gu_piece = lax.dynamic_slice_in_dim(w_gate_up, chip * piece, piece, 0)
    dn_piece = lax.dynamic_slice_in_dim(w_down, chip * piece, piece, 0)
    both = jnp.concatenate(
        [
            lax.dynamic_slice_in_dim(gu_piece, core * half, half, 2),
            lax.dynamic_slice_in_dim(gu_piece, HID + core * half, half, 2),
            lax.dynamic_slice_in_dim(dn_piece, core * half, half, 2),
        ],
        axis=2,
    )
    both = both.reshape(piece, grps, local_experts, 3 * half).transpose(1, 2, 0, 3)
    both = lax.all_to_all(both, "grp", 0, 0, tiled=True)
    both = lax.all_gather(both, "rep", axis=0, tiled=False, axis_index_groups=same_core)
    both = both.transpose(2, 1, 0, 3, 4).reshape(local_experts, width, 3 * half)
    wgu, wdn = both[:, :, : 2 * half], both[:, :, 2 * half :]

    tokens_f = tokens.astype(F32)
    inverse_one = lax.rsqrt(jnp.mean(tokens_f * tokens_f, axis=1, keepdims=True) + EPS)
    normed_one = tokens_f * inverse_one
    act_one = (normed_one * gain_one).astype(BF)
    act_plane = lax.all_gather(act_one, "rep", axis=0, tiled=True, axis_index_groups=groups)
    prefix_plane = lax.all_gather(prefix_len, "rep", axis=0, tiled=True, axis_index_groups=groups)
    cos, sin = rope_tables(seq)
    projected = dot(act_plane, qkv_head).reshape(heads, seq, QPK + 2, HEAD_WIDTH)
    cos_b, sin_b = cos[None, :, None, :], sin[None, :, None, :]
    turned = rotate(projected[:, :, : QPK + 1], cos_b, sin_b).astype(BF)
    query = turned[:, :, :QPK]
    key = turned[:, :, QPK]
    value = projected[:, :, QPK + 1].astype(BF)
    scale = HEAD_WIDTH ** (-0.5)
    row_pos, col_pos = jnp.arange(seq)[:, None], jnp.arange(seq)[None, :]
    allowed = (col_pos <= row_pos)[None] | (col_pos[None] < prefix_plane[:, None, None])
    scores = jnp.einsum("bsgd,btd->bgst", query, key, preferred_element_type=F32) * scale
    scores = jnp.where(allowed[:, None], scores, -1e30)
    exps = jnp.exp(scores - jnp.max(scores, axis=-1, keepdims=True))
    probs = exps / jnp.sum(exps, axis=-1, keepdims=True)
    probs_low = probs.astype(BF)
    attended = jnp.einsum("bgst,btd->bsgd", probs_low, value, preferred_element_type=F32)
    attended = attended.astype(BF).reshape(heads * seq, qw)
    part = dot(attended, proj_head).astype(BF)
    part = lax.psum_scatter(part, "rep", scatter_dimension=0, tiled=True, axis_index_groups=groups)
    residual = tokens_f + part.astype(F32)
    inverse_two = lax.rsqrt(jnp.mean(residual * residual, axis=1, keepdims=True) + EPS)
    normed_two = residual * inverse_two
    act_two = (normed_two * gain_two).astype(BF)
    gates, kept = routing(expert_ids, priority, dot(act_two, router))

    def column(v):
        v = lax.all_gather(v, "grp", axis=0, tiled=True)
        return lax.all_gather(v, "rep", axis=0, tiled=True, axis_index_groups=pairs)

    def to_owners(v):
        v = lax.psum_scatter(v, "rep", scatter_dimension=0, tiled=True, axis_index_groups=pairs)
        return lax.psum_scatter(v, "grp", scatter_dimension=0, tiled=True).astype(F32)

    dy_all = column(cotangent)
    x_all = column(act_two)
    weight = column(jnp.where(kept, gates, 0.0))
    weight = lax.dynamic_slice_in_dim(weight, grp * local_experts, local_experts, 1).T[:, :, None]
    gate_up = jnp.einsum("td,edh->eth", x_all, wgu, preferred_element_type=F32)
    g, u = gate_up[..., :half], gate_up[..., half:]
    sig = jax.nn.sigmoid(g)
    silu = g * sig
    hidden = silu * u
    hidden_w = (hidden * weight).astype(BF)
    back = jnp.einsum("td,edh->eth", dy_all, wdn, preferred_element_type=F32)
    grad_gate_part = jnp.sum(back * hidden, axis=2)
    grad_hidden = back * weight
    ggu = jnp.concatenate(
        [grad_hidden * u * sig * (1.0 + g * (1.0 - sig)), grad_hidden * silu], axis=2
    ).astype(BF)
    out_part = jnp.einsum("eth,edh->td", hidden_w, wdn, preferred_element_type=F32).astype(BF)
    gact_part = jnp.einsum("eth,edh->td", ggu, wgu, preferred_element_type=F32).astype(BF)
    gact = to_owners(gact_part)
    grad_gates = lax.psum_scatter(
        grad_gate_part.T, "rep", scatter_dimension=0, tiled=True, axis_index_groups=pairs
    )
    grad_gates = lax.all_to_all(grad_gates, "grp", 0, 1, tiled=True)
    grad_gates = jnp.where(kept, grad_gates, 0.0)
    out = to_owners(out_part)
    output = (residual + out).astype(BF)
    grad_gu, grad_dn = expert_grads_general(reps, grps, x_all, dy_all, ggu, hidden_w)
    grad_gu = grad_gu.reshape(own, EXPERTS, 2 * HID)
    grad_dn = grad_dn.reshape(own, EXPERTS, HID)

    grad_logits = (gates * (grad_gates - jnp.sum(gates * grad_gates, axis=1, keepdims=True))).astype(BF)
    gact = gact + dot(grad_logits, router.T)
    router_term = dot(act_two.T, grad_logits)
    gain_two_term = jnp.sum(gact * normed_two, axis=0)
    scaled = gact * gain_two
    dy = cotangent.astype(F32)
    grad_residual = dy + inverse_two * (
        scaled - normed_two * jnp.mean(scaled * normed_two, axis=1, keepdims=True)
    )
    gres_low = grad_residual.astype(BF)

    gres_plane = lax.all_gather(gres_low, "rep", axis=0, tiled=True, axis_index_groups=groups)
    proj_term = dot(attended.T, gres_plane)
    grad_att = dot(gres_plane, proj_head.T).astype(BF).reshape(heads, seq, QPK, HEAD_WIDTH)
    grad_value = jnp.einsum("bgst,bsgd->btd", probs_low, grad_att, preferred_element_type=F32)
    grad_probs = jnp.einsum("bsgd,btd->bgst", grad_att, value, preferred_element_type=F32)
    grad_scores = (
        probs * (grad_probs - jnp.sum(probs * grad_probs, axis=-1, keepdims=True))
    ).astype(BF)
    grad_query = jnp.einsum("bgst,btd->bsgd", grad_scores, key, preferred_element_type=F32) * scale
    grad_key = jnp.einsum("bgst,bsgd->btd", grad_scores, query, preferred_element_type=F32) * scale
    turned_back = rotate(
        jnp.concatenate([grad_query, grad_key[:, :, None]], axis=2), cos_b, -sin_b
    )
    gproj = jnp.concatenate([turned_back, grad_value[:, :, None]], axis=2).astype(BF)
    gproj = gproj.reshape(heads * seq, qw + 2 * hw)
    qkv_term = dot(act_plane.T, gproj)
    gact_one = dot(gproj, qkv_head.T).astype(BF)
    gact_one = lax.psum_scatter(
        gact_one, "rep", scatter_dimension=0, tiled=True, axis_index_groups=groups
    ).astype(F32)
    gain_one_term = jnp.sum(gact_one * normed_one, axis=0)
    scaled_one = gact_one * gain_one
    grad_tokens = grad_residual + inverse_one * (
        scaled_one - normed_one * jnp.mean(scaled_one * normed_one, axis=1, keepdims=True)
    )

    qkv_own = lax.psum_scatter(qkv_term.astype(BF), "grp", scatter_dimension=0, tiled=True)
    proj_sum = lax.psum(proj_term.astype(BF), "grp")
    if groups is not None:
        across = [[i + heads * j for j in range(reps // heads)] for i in range(heads)]
        qkv_own = lax.psum(qkv_own, "rep", axis_index_groups=across)
        proj_sum = lax.psum(proj_sum, "rep", axis_index_groups=across)
    qkv_own = lax.all_gather(qkv_own, "rep", axis=0, tiled=False, axis_index_groups=groups)
    qkv_own = qkv_own.astype(F32)
    grad_qkv = jnp.concatenate(
        [
            qkv_own[:, :, lo:hi].transpose(1, 0, 2).reshape(own, -1)
            for lo, hi in ((0, qw), (qw, qw + hw), (qw + hw, qw + 2 * hw))
        ],
        axis=1,
    )
    proj_all = lax.all_gather(proj_sum, "rep", axis=0, tiled=True, axis_index_groups=groups)
    grad_proj = lax.dynamic_slice_in_dim(proj_all, grp * own, own, 0).astype(F32)
    terms = jnp.concatenate([gain_one_term[:, None], gain_two_term[:, None], router_term], axis=1)
    terms = lax.psum(lax.psum_scatter(terms, "grp", scatter_dimension=0, tiled=True), "rep")
    return (
        output,
        grad_tokens,
        terms[:, 0],
        grad_qkv,
        grad_proj,
        terms[:, 1],
        terms[:, 2:],
        grad_gu,
        grad_dn,
    )


def shards(
    tokens,
    attn_gain,
    query_key_value_weight,
    attn_proj,
    mlp_gain,
    w_router,
    w_gate_up,
    w_down,
    prefix_len,
    expert_ids,
    priority,
    cotangent,
):
    heads, half, own = KEY_VALUE_HEADS, HID // 2, attn_gain.shape[0]
    qw, hw, q_all = QPK * HEAD_WIDTH, HEAD_WIDTH, QUERY_HEADS * HEAD_WIDTH
    rep = lax.axis_index("rep")
    core, chip = lax.rem(rep, 2), rep // 2
    seq, width = tokens.shape
    small = jnp.concatenate(
        [attn_gain[None], mlp_gain[None], jnp.zeros((14, own), BF), w_router.T], axis=0
    )
    qkv_cols = jnp.concatenate(
        [
            lax.dynamic_slice_in_dim(query_key_value_weight, rep * qw, qw, 1),
            lax.dynamic_slice_in_dim(query_key_value_weight, q_all + rep * hw, hw, 1),
            lax.dynamic_slice_in_dim(query_key_value_weight, q_all + heads * hw + rep * hw, hw, 1),
        ],
        axis=1,
    )
    piece = own // 4
    gu_piece = lax.dynamic_slice_in_dim(w_gate_up, chip * piece, piece, 0)
    dn_piece = lax.dynamic_slice_in_dim(w_down, chip * piece, piece, 0)
    both = jnp.concatenate(
        [
            lax.dynamic_slice_in_dim(gu_piece, core * half, half, 2),
            lax.dynamic_slice_in_dim(gu_piece, HID + core * half, half, 2),
            lax.dynamic_slice_in_dim(dn_piece, core * half, half, 2),
        ],
        axis=2,
    )
    wpiece = both.transpose(1, 0, 2).reshape(4, 4, piece, 3 * half)
    chosen, kept = choices(expert_ids, priority)
    masks = jnp.stack([chosen, kept]).astype(F32)
    prefix = jnp.broadcast_to(prefix_len.astype(F32), (8, 128))
    cos, sin = rope_tables(seq)
    cos_t, sin_t = jnp.tile(cos, (1, 4)), jnp.tile(jnp.concatenate([-sin, sin], axis=1), (1, 2))
    parts = front(tokens, cotangent, wpiece, qkv_cols, attn_proj, small, masks, prefix, cos_t, sin_t)
    residual, out_sum = parts[13], parts[16]
    wide, grad_tokens, qkv_own, proj_own, terms, out_parts = back(parts, tokens, masks[1], cos_t, sin_t)
    grad_gu, grad_dn = widen(wide)
    out = lax.dynamic_index_in_dim(out_sum, lax.axis_index("grp"), 0, False).astype(F32)
    output = (residual + out + jnp.sum(out_parts.astype(F32), axis=0)).astype(BF)
    grad_qkv = jnp.concatenate(
        [
            jnp.concatenate([qkv_own[h, :, lo:hi] for h in range(heads)], axis=1)
            for lo, hi in ((0, qw), (qw, qw + hw), (qw + hw, qw + 2 * hw))
        ],
        axis=1,
    ).astype(F32)
    grad_proj = proj_own.reshape(own, width).astype(F32)
    return (
        output,
        grad_tokens,
        terms[0],
        grad_qkv,
        grad_proj,
        terms[1],
        terms[8:].T,
        grad_gu.reshape(own, EXPERTS, 2 * HID),
        grad_dn.reshape(own, EXPERTS, HID),
    )


def solution(mesh):
    tok, par = ("rep", "grp"), "grp"
    in_specs = (
        P(tok, None),
        P(par),
        P(par, None),
        P(par, None),
        P(par),
        P(par, None),
        P(par, None, None),
        P(par, None, None),
        P(tok),
        P(tok, None),
        P(tok, None),
        P(tok, None),
    )
    out_specs = (
        P(tok, None),
        P(tok, None),
        P(par),
        P(par, None),
        P(par, None),
        P(par),
        P(par, None),
        P(par, None, None),
        P(par, None, None),
    )
    reps, grps = mesh.shape["rep"], mesh.shape["grp"]

    def body(*args):
        if (reps, grps) == (8, 4):
            return shards(*args)
        return shards_general(reps, grps, *args)

    return jax.shard_map(body, mesh=mesh, in_specs=in_specs, out_specs=out_specs, check_vma=False)
```

```python
import jax
import jax.numpy as jnp
import numpy as np
from jax import lax
from jax.experimental import pallas as pl
from jax.experimental.pallas import tpu as pltpu
from jax.sharding import PartitionSpec as P

QUERY_HEADS = 24
KEY_VALUE_HEADS = 8
HEAD_WIDTH = 64
HID = 512
EXPERTS = 16
CAP = 72
EPS = 1e-05
BF = jnp.bfloat16
F32 = jnp.float32
QPK = QUERY_HEADS // KEY_VALUE_HEADS
BIG = 1 << 20
MESH = pl.DeviceIdType.MESH


def dot(a, b):
    return jnp.dot(a, b, preferred_element_type=F32)


def rope_tables(length):
    half = HEAD_WIDTH // 2
    position = jnp.arange(length, dtype=F32)[:, None]
    inverse_freq = 10000.0 ** (-jnp.arange(half, dtype=F32) * 2.0 / HEAD_WIDTH)
    angles = position * inverse_freq[None, :]
    return jnp.cos(angles), jnp.sin(angles)


def rotate(v, cos, sin):
    half = HEAD_WIDTH // 2
    a, b = v[..., :half], v[..., half:]
    return jnp.concatenate([a * cos - b * sin, b * cos + a * sin], axis=-1)


def choices(expert_ids, priority):
    seq, top = expert_ids.shape
    choose = expert_ids[:, :, None] == jnp.arange(EXPERTS, dtype=jnp.int32)[None, None, :]
    chosen = jnp.any(choose, axis=1)
    rank_of = jnp.sum(jnp.where(choose, priority.reshape(seq, top)[:, :, None], 0), axis=1)
    rank_of = jnp.where(chosen, rank_of, BIG)
    slot = jnp.sum((rank_of[None, :, :] < rank_of[:, None, :]).astype(jnp.int32), axis=1)
    return chosen, chosen & (slot < CAP)


def routing(expert_ids, priority, logits):
    chosen, kept = choices(expert_ids, priority)
    top_logit = jnp.max(jnp.where(chosen, logits, -jnp.inf), axis=1, keepdims=True)
    gate_exp = jnp.where(chosen, jnp.exp(jnp.where(chosen, logits - top_logit, 0.0)), 0.0)
    gates = gate_exp / jnp.sum(gate_exp, axis=1, keepdims=True)
    return gates, kept


def place():
    r, z = lax.axis_index("rep"), lax.axis_index("grp")
    return r // 4, (r // 2) % 2, r % 2, z


def flip(bit, by):
    return bit + by * (1 - 2 * bit)


def turn(v, cos, sin):
    lane = lax.broadcasted_iota(jnp.int32, v.shape, 1)
    partner = jnp.where(lax.rem(lane, 64) < 32, pltpu.roll(v, 96, 1), pltpu.roll(v, 32, 1))
    return v * cos + partner * sin


def front_kernel(tok, dy, w_gu, w_dn, qkv, proj, small, ids, prio, prefix, cos_t, sin_t,
                 o_x, o_dy, o_ggu, o_hw, o_act, o_q, o_k, o_v, o_probs, o_att, o_qkvw, o_projw,
                 o_small, o_res, o_gates, o_kept, o_gsum, o_osum,
                 smalls, qkvw, projw, projq, actp, pre, pr, qs, ks, vs, probs, att, part, sibr, sums, plr,
                 xall, dyall, wbuf, ggu, hw, gpart, ggp, gsib,
                 gsum, res, gates, kept, qwin, wst, wcol, wpiece,
                 s_small, r_small, s_qkv, r_qkv, s_pz, r_pz, s_pq, r_pq, s_wz, r_wz, s_wp, r_wp,
                 s_act, r_act, s_pre, r_pre, s_actc, r_actc, s_prec, r_prec, s_sib, r_sib, s_pl, r_pl,
                 s_x, r_x, s_xc, r_xc, s_y, r_y, s_yc, r_yc,
                 s_gc, r_gc, s_oc, r_oc, sl):
    y, x, c, z = place()
    half = HID // 2

    def slot(a, b):
        return flip(y, a * c + b * (1 - c)) * 2 + flip(x, a * (1 - c) + b * c)

    p0, p1, p2, p3 = slot(0, 0), slot(1, 0), slot(0, 1), slot(1, 1)
    peers = (p1, p2, p3)
    d1, d2, dsib = (p1 * 2 + c, z), (p2 * 2 + c, z), (p0 * 2 + 1 - c, z)
    dpl = [(p * 2 + c, z) for p in peers]
    zk = [lax.rem(z + k, 4) for k in range(4)]
    zf = [lax.rem(z + 4 - k, 4) for k in range(4)]
    dz = [(p0 * 2 + c, zz) for zz in zk]

    barrier = pltpu.get_barrier_semaphore()
    for to in dpl + dz[1:] + [dsib]:
        pl.semaphore_signal(barrier, 1, device_id=to, device_id_type=MESH)
    pl.semaphore_wait(barrier, 7)

    def remote(src, dst, s, r, to):
        return pltpu.make_async_remote_copy(src, dst, s, r, device_id=to, device_id_type=MESH)

    def c_small(k):
        return remote(small, smalls.at[z], s_small.at[k - 1], r_small.at[k - 1], dz[k])

    def rows(zz, pp):
        return pl.ds(pl.multiple_of(zz * 384 + pp * 96, 96), 96)

    def c_wz(k):
        return remote(wpiece.at[zk[k]], wbuf.at[:, rows(z, p0)], s_wz.at[k - 1], r_wz.at[k - 1], dz[k])

    def c_wp(k, i):
        zz = zf[k]
        who, pp = ((d1, p0), (d2, p0), (d2, p1))[i]
        src = wpiece.at[z] if (k == 0 and i < 2) else wbuf.at[:, rows(zz, pp)]
        return remote(src, wbuf.at[:, rows(zz, pp)], s_wp.at[k, i], r_wp.at[k, i], who)

    def quarter(p):
        return pl.ds(pl.multiple_of(p * 48, 48), 48)

    def c_pz(k):
        src = proj.at[pl.ds(pl.multiple_of(c * 192 + p0 * 48, 48), 48)]
        return remote(src, projq.at[k - 1], s_pz.at[k - 1], r_pz.at[k - 1], dz[k])

    def c_pq(k, owner):
        return remote(projq.at[k - 1], projw.at[quarter(p0)], s_pq.at[k - 1], r_pq.at[p0], (owner * 2 + c, z))

    def c_pq_in(i):
        return remote(projq.at[0], projw.at[quarter(peers[i])], s_pq.at[0], r_pq.at[peers[i]], dpl[i])

    def c_act(i):
        return remote(actp.at[c, p0], actp.at[c, p0], s_act.at[i], r_act.at[i], dpl[i])

    def c_pre(i):
        return remote(pre.at[c, p0], pre.at[c, p0], s_pre.at[i], r_pre.at[i], dpl[i])

    def c_actc(i):
        p = (p0, p1, p2, p3)[i]
        return remote(actp.at[c, p], actp.at[c, p], s_actc.at[i], r_actc.at[i], dsib)

    def c_prec(i):
        p = (p0, p1, p2, p3)[i]
        return remote(pre.at[c, p], pre.at[c, p], s_prec.at[i], r_prec.at[i], dsib)

    def c_sib():
        return remote(part, sibr, s_sib, r_sib, dsib)

    def c_pl(i):
        return remote(sums.at[i], plr.at[i], s_pl.at[i], r_pl.at[i], dpl[i])

    def chain(at, s, r, sc=None, rc=None):
        def hop(h, d, send):
            block = z - (h - 1) if d == 0 else z + (h - 1)
            if not send:
                block = z - h if d == 0 else z + h
            return remote(at(block), at(block), s.at[d, h - 1], r.at[d, h - 1],
                          (p0 * 2 + c, z + 1 if d == 0 else z - 1))

        def may(h, d, send):
            if send:
                return (z < 3) & (z >= h - 1) if d == 0 else (z > 0) & (z <= 4 - h)
            return z >= h if d == 0 else z <= 3 - h

        def across(h, d):
            block = z - h if d == 0 else z + h
            return remote(at(block), at(block), sc.at[d, h - 1], rc.at[d, h - 1], dsib)

        def over():
            return remote(at(z), at(z), sc.at[2, 0], rc.at[2, 0], dsib)

        def send(h):
            for d in range(2):
                @pl.when(may(h, d, True))
                def _(d=d):
                    hop(h, d, True).start()
            if h == 1 and sc is not None:
                over().start()

        def recv(h):
            for d in range(2):
                @pl.when(may(h, d, False))
                def _(d=d):
                    hop(h, d, False).wait_recv()
                    if sc is not None:
                        across(h, d).start()

        def finish():
            over().wait_recv()
            for h in (1, 2, 3):
                for d in range(2):
                    @pl.when(may(h, d, False))
                    def _(d=d, h=h):
                        across(h, d).wait_recv()

        def sent():
            if sc is not None:
                over().wait_send()
            for h in (1, 2, 3):
                for d in range(2):
                    @pl.when(may(h, d, True))
                    def _(d=d, h=h):
                        hop(h, d, True).wait_send()
                    if sc is not None:
                        @pl.when(may(h, d, False))
                        def _(d=d, h=h):
                            across(h, d).wait_send()
        return send, recv, finish, sent

    x_send, x_recv, x_finish, x_sent = chain(lambda b: xall.at[c, b], s_x, r_x, s_xc, r_xc)
    y_send, y_recv, y_finish, y_sent = chain(lambda b: dyall.at[c, b], s_y, r_y, s_yc, r_yc)
    q_send, q_recv, _, q_sent = chain(
        lambda b: qkvw.at[pl.ds(pl.multiple_of(b * 384, 384), 384)], s_qkv, r_qkv)

    opart, osib, osum = part, sibr, sums
    g_c = remote(gpart, gsib, s_gc, r_gc, dsib)
    o_c = remote(opart, osib, s_oc, r_oc, dsib)

    def weights_a(k):
        if k:
            c_wz(k).wait_recv()
        c_wp(k, 0).start()

    def weights_b(k):
        c_wp(k, 0).wait_recv()
        c_wp(k, 1).start()
        c_wp(k, 2).start()

    for k in (1, 2, 3):
        c_small(k).start()
    local = [pltpu.make_async_copy(small, smalls.at[z], sl.at[0]),
             pltpu.make_async_copy(dy, dyall.at[c, z], sl.at[3])]

    def window(off, width, at, n):
        src = qkv.at[:, pl.ds(pl.multiple_of(off, 128), width)]
        return pltpu.make_async_copy(src, qwin.at[:, pl.ds(at, width)], sl.at[n])
    mine = p0 * 96
    windows = [window(384 * p0 + 128 * c, 256, 0, 1), window(1536 + 128 * p0, 128, 256, 2),
               window(2048 + 128 * p0, 128, 384, 24)]
    pieces = [pltpu.make_async_copy(
        ref.at[pl.ds(pl.multiple_of(mine, 96), 96), :, pl.ds(pl.multiple_of(off, half), half)],
        wst.at[:, :, pl.ds(i * half, half)], sl.at[25 + i])
        for i, (ref, off) in enumerate(((w_gu, c * half), (w_gu, HID + c * half), (w_dn, c * half)))]
    for one in local + windows + pieces:
        one.start()
    own_proj = pltpu.make_async_copy(proj.at[pl.ds(pl.multiple_of(c * 192, 192), 192)], projw, sl.at[4])

    @pl.when(z == p0)
    def _():
        own_proj.start()
    for one in windows:
        one.wait()
    cols = qwin[...].astype(F32)
    own_rows = pl.ds(pl.multiple_of(z * 384, 384), 384)
    for at, lo, width in ((0, 0, 256), (192, 256, 128), (256, 384, 128)):
        part_ = cols[:, lo : lo + width]
        part_ = jnp.where(c == 0, part_, pltpu.roll(part_, width - 64, 1)).astype(BF)
        qkvw[own_rows, at : at + (192 if at == 0 else 64)] = part_[:, : 192 if at == 0 else 64]

    tok_f = tok[...].astype(F32)
    inv1 = lax.rsqrt(jnp.mean(tok_f * tok_f, axis=1, keepdims=True) + EPS)
    for k in (1, 2, 3):
        c_small(k).wait_recv()
    q_send(1)
    for k in (1, 2, 3):
        c_pz(k).start()
    local[0].wait()
    gain1 = jnp.concatenate([smalls[i, 0:1, :] for i in range(4)], axis=1).astype(F32)
    actp[c, p0] = (tok_f * inv1 * gain1).astype(BF)
    pre[c, p0] = prefix[...]
    for i in range(3):
        c_act(i).start()
        c_pre(i).start()
    c_actc(0).start()
    c_prec(0).start()
    chosen_f = jnp.zeros((128, 128), F32)
    rank_of = jnp.zeros((128, 128), F32)
    lane_e = lax.broadcasted_iota(jnp.int32, (128, 128), 1)
    for k in range(8):
        hit = ids[:, k : k + 1] == lane_e
        chosen_f = jnp.where(hit, 1.0, chosen_f)
        rank_of = jnp.where(hit, prio[:, k : k + 1].astype(F32), rank_of)
    rank_of = jnp.where(chosen_f > 0.0, rank_of, 65536.0)
    rank_t = rank_of.T
    slots = jnp.zeros((128, 128), F32)
    for e in range(EXPERTS):
        before = jnp.sum((rank_t[e : e + 1, :] < rank_of[:, e : e + 1]).astype(F32), axis=1, keepdims=True)
        slots = jnp.where(lane_e == e, before, slots)
    kept_f = jnp.where(slots < CAP, chosen_f, 0.0)
    kept[...] = kept_f[:, :EXPERTS]
    q_recv(1)
    q_send(2)

    for one in pieces:
        one.wait()

    def expert_rows(l, _):
        wcol[...] = wst[:, :, pl.ds(pl.multiple_of(l * 128, 128), 128)].astype(F32).reshape(1536, 128)
        for e in range(EXPERTS):
            wpiece[e // 4, e % 4, :, pl.ds(pl.multiple_of(l * 128, 128), 128)] = (
                wcol[pl.ds(e, 96, stride=EXPERTS), :].astype(BF))
        return 0
    lax.fori_loop(0, 6, expert_rows, 0)
    own_piece = pltpu.make_async_copy(wpiece.at[z], wbuf.at[:, rows(z, p0)], sl.at[28])
    own_piece.start()
    weights_a(0)
    q_recv(2)
    q_send(3)
    for i in range(3):
        c_act(i).wait_recv()
        c_pre(i).wait_recv()
        c_actc(i + 1).start()
        c_prec(i + 1).start()
    q_recv(3)
    local[1].wait()

    row = lax.broadcasted_iota(jnp.int32, (128, 128), 0)
    col = lax.broadcasted_iota(jnp.int32, (128, 128), 1)
    causal = col <= row
    col_f = col.astype(F32)

    def attention(cc):
        pr[...] = jnp.dot(actp[cc].reshape(512, 1536), qkvw[...], preferred_element_type=F32).reshape(4, 128, 320)

        def one(i, _):
            lo = turn(pr[i, :, 0:128], cos_t[...], sin_t[...]).astype(BF)
            hi = turn(pr[i, :, 128:256], cos_t[...], sin_t[...]).astype(BF)
            qs[cc, i, 0:128] = lo[:, 0:64]
            qs[cc, i, 128:256] = lo[:, 64:128]
            qs[cc, i, 256:384] = hi[:, 0:64]
            ks[cc, i] = hi[:, 64:128]
            vs[cc, i] = pr[i, :, 256:320].astype(BF)
            sc = lax.dot_general(qs[cc, i], ks[cc, i], (((1,), (1,)), ((), ())), preferred_element_type=F32)
            allowed = causal | (col_f < pre[cc, i, 0:1, :])
            sc = jnp.where(allowed[None], sc.reshape(3, 128, 128) * (64 ** -0.5), -1e30)
            ex = jnp.exp(sc - jnp.max(sc, axis=-1, keepdims=True))
            pb = (ex / jnp.sum(ex, axis=-1, keepdims=True)).reshape(384, 128)
            probs[cc, i] = pb
            at = jnp.dot(pb.astype(BF), vs[cc, i], preferred_element_type=F32).astype(BF)
            for h in range(3):
                att[cc, i, :, h * 64 : (h + 1) * 64] = at[h * 128 : (h + 1) * 128]
            return 0
        lax.fori_loop(0, 4, one, 0)

    attention(c)
    for i in range(4):
        c_actc(i).wait_recv()
        c_prec(i).wait_recv()
    attention(1 - c)
    for k in (1, 2, 3):
        c_pz(k).wait_recv()
        owner = zf[k]

        @pl.when(owner != p0)
        def _(k=k, owner=owner):
            c_pq(k, owner).start()

        @pl.when(owner == p0)
        def _(k=k):
            projw[quarter(p0)] = projq[k - 1]

    for k in (1, 3, 2):
        c_wz(k).start()

    @pl.when(z == p0)
    def _():
        own_proj.wait()

    @pl.when(z != p0)
    def _():
        for i in range(3):
            c_pq_in(i).wait_recv()

    weights_b(0)

    def to_sib(i, _):
        part[i] = jnp.dot(att[1 - c, i], projw[...], preferred_element_type=F32).astype(BF)
        return 0
    lax.fori_loop(0, 4, to_sib, 0)
    c_sib().start()
    c_sib().wait_recv()
    for i in range(3):
        sums[i] = (jnp.dot(att[c, peers[i]], projw[...], preferred_element_type=F32)
                   + sibr[peers[i]].astype(F32)).astype(BF)
        c_pl(i).start()
    residual = (tok_f + jnp.dot(att[c, p0], projw[...], preferred_element_type=F32) + sibr[p0].astype(F32))
    for i in range(3):
        c_pl(i).wait_recv()
        residual = residual + plr[i].astype(F32)
    res[...] = residual
    inv2 = lax.rsqrt(jnp.mean(residual * residual, axis=1, keepdims=True) + EPS)
    gain2 = jnp.concatenate([smalls[i, 1:2, :] for i in range(4)], axis=1).astype(F32)
    act2 = (residual * inv2 * gain2).astype(BF)
    router = jnp.concatenate([smalls[i, 16:32, :] for i in range(4)], axis=1)
    logits = lax.dot_general(act2, router, (((1,), (1,)), ((), ())), preferred_element_type=F32)
    chosen = chosen_f[:, :EXPERTS] > 0.0
    top = jnp.max(jnp.where(chosen, logits, -1e30), axis=1, keepdims=True)
    ge = jnp.where(chosen, jnp.exp(jnp.where(chosen, logits - top, 0.0)), 0.0)
    gt = ge / jnp.sum(ge, axis=1, keepdims=True)
    gates[...] = gt
    wide_gates = jnp.concatenate([gt * kept[...], jnp.zeros((128, 112), F32)], axis=1)
    gate_hi = wide_gates.astype(BF)
    xall[c, z, :, :1536] = act2
    xall[c, z, :, 1536:1664] = gate_hi
    xall[c, z, :, 1664:] = (wide_gates - gate_hi.astype(F32)).astype(BF)
    x_send(1)
    weights_a(1)
    weights_a(3)
    weights_b(1)
    x_recv(1)
    x_send(2)
    weights_b(3)
    weights_a(2)
    x_recv(2)
    x_send(3)
    y_send(1)
    weights_b(2)
    x_recv(3)
    y_recv(1)
    y_send(2)
    y_recv(2)
    y_send(3)
    y_recv(3)
    own_piece.wait()
    for k in range(4):
        c_wp(k, 1).wait_recv()
        c_wp(k, 2).wait_recv()
    x_finish()
    y_finish()

    lane = lax.broadcasted_iota(jnp.int32, (512, 128), 1)
    ggp[...] = jnp.zeros_like(ggp)

    def expert(n, _):
        j, t = n // 2, lax.rem(n, 2)
        gu = jnp.dot(xall[t, :, :, :1536].reshape(512, 1536), wbuf[j, :, : 2 * half], preferred_element_type=F32)
        bk = jnp.dot(dyall[t].reshape(512, 1536), wbuf[j, :, 2 * half :], preferred_element_type=F32)
        mine = lane == z * 4 + j
        both = (xall[t, :, :, 1536:1664].astype(F32) + xall[t, :, :, 1664:].astype(F32)).reshape(512, 128)
        w = jnp.sum(jnp.where(mine, both, 0.0), axis=1, keepdims=True)
        g, u = gu[:, :half], gu[:, half:]
        sg = 1.0 / (1.0 + jnp.exp(-g))
        silu = g * sg
        hid = silu * u
        hw[j, pl.ds(pl.multiple_of(t * 512, 512), 512)] = (hid * w).astype(BF)
        ggp[t] = ggp[t] + jnp.where(mine, jnp.sum(bk * hid, axis=1, keepdims=True), 0.0).reshape(4, 128, 128)
        gh = bk * w
        at = pl.ds(pl.multiple_of(t * 512, 512), 512)
        ggu[j, at, :half] = (gh * u * sg * (1.0 + g * (1.0 - sg))).astype(BF)
        ggu[j, at, half:] = (gh * silu).astype(BF)
        return 0
    lax.fori_loop(0, 8, expert, 0)
    saves = []

    def save(src, dst):
        one = pltpu.make_async_copy(src, dst, sl.at[5 + len(saves)])
        one.start()
        saves.append(one)
    for src, dst in ((xall, o_x), (dyall, o_dy), (ggu, o_ggu), (hw, o_hw), (actp, o_act), (qs, o_q), (ks, o_k),
                     (vs, o_v), (probs, o_probs), (att, o_att), (qkvw, o_qkvw), (projw, o_projw),
                     (smalls, o_small), (res, o_res), (gates, o_gates), (kept, o_kept)):
        save(src, dst)

    def block(grad, t, n):
        at = pl.ds(pl.multiple_of(t * 512, 512), 512)
        lanes = pl.ds(pl.multiple_of(n * 256, 256), 256)
        acc = jnp.zeros((512, 256), F32)
        for j in range(4):
            a = ggu[j, at] if grad else hw[j, at]
            b = wbuf[j, lanes, : 2 * half] if grad else wbuf[j, lanes, 2 * half :]
            acc = acc + lax.dot_general(a, b, (((1,), (1,)), ((), ())), preferred_element_type=F32)
        return acc.reshape(4, 128, 256), lanes

    def partial(grad, buf):
        def one(n, _):
            v, lanes = block(grad, 1 - c, n)
            buf[:, :, lanes] = v.astype(BF)
            return 0
        lax.fori_loop(0, 6, one, 0)

    def own(grad, sib, dst):
        def one(n, _):
            v, lanes = block(grad, c, n)
            dst[:, :, lanes] = (v + sib[:, :, lanes].astype(F32)).astype(BF)
            return 0
        lax.fori_loop(0, 6, one, 0)

    def put_gate_grads(dst, v):
        hi = v.astype(BF)
        dst[:, :, 1536:1664] = hi
        dst[:, :, 1664:] = (v - hi.astype(F32)).astype(BF)

    def gate_grads(v):
        return v[..., 1536:1664].astype(F32) + v[..., 1664:].astype(F32)

    c_sib().wait_send()
    for i in range(3):
        c_pl(i).wait_send()
    put_gate_grads(gpart, ggp[1 - c])
    partial(True, gpart)
    g_c.start()
    partial(False, opart)
    o_c.start()
    g_c.wait_recv()
    put_gate_grads(gsum, ggp[c] + gate_grads(gsib))
    own(True, gsib, gsum)
    save(gsum, o_gsum)
    o_c.wait_recv()
    own(False, osib, osum)
    save(osum, o_osum)

    for k in (1, 2, 3):
        for one in (c_small(k), c_pz(k), c_wz(k)):
            one.wait_send()

        @pl.when(zf[k] != p0)
        def _(k=k):
            c_pq(k, zf[k]).wait_send()
    for k in range(4):
        for i in range(3):
            c_wp(k, i).wait_send()
        for one in (c_actc(k), c_prec(k)):
            one.wait_send()
    for i in range(3):
        for one in (c_act(i), c_pre(i)):
            one.wait_send()
    for one in (g_c, o_c):
        one.wait_send()
    x_sent()
    y_sent()
    q_sent()
    for one in saves:
        one.wait()


def front(*args):
    sem, vm = pltpu.SemaphoreType.DMA, pltpu.VMEM
    out = lambda shape, kind=BF: jax.ShapeDtypeStruct(shape, kind)
    outs = (
        out((2, 4, 128, 1792)), out((2, 4, 128, 1536)), out((4, 1024, 512)), out((4, 1024, 256)),
        out((2, 4, 128, 1536)), out((2, 4, 384, 64)), out((2, 4, 128, 64)), out((2, 4, 128, 64)),
        out((2, 4, 384, 128), F32), out((2, 4, 128, 192)), out((1536, 320)), out((192, 1536)),
        out((4, 32, 384)), out((128, 1536), F32), out((128, 16), F32), out((128, 16), F32), out((4, 128, 1792)),
        out((4, 128, 1536)),
    )
    block, quad = vm((2, 4, 128, 1536), BF), vm((4, 128, 1536), BF)
    three = vm((3, 128, 1536), BF)
    quad_g = vm((4, 128, 1792), BF)
    scratch = [
        vm((4, 32, 384), BF), vm((1536, 320), BF), vm((192, 1536), BF), vm((3, 48, 1536), BF),
        block, vm((2, 4, 8, 128), F32),
        vm((4, 128, 320), F32), vm((2, 4, 384, 64), BF), vm((2, 4, 128, 64), BF), vm((2, 4, 128, 64), BF),
        vm((2, 4, 384, 128), F32), vm((2, 4, 128, 192), BF), quad, quad, quad, three,
        vm((2, 4, 128, 1792), BF), block, vm((4, 1536, 768), BF), vm((4, 1024, 512), BF),
        vm((4, 1024, 256), BF), quad_g, vm((2, 4, 128, 128), F32), quad_g,
        quad_g, vm((128, 1536), F32), vm((128, 16), F32), vm((128, 16), F32),
        vm((384, 512), BF), vm((96, 16, 768), BF), vm((1536, 128), F32), vm((4, 4, 96, 768), BF),
    ]
    n3, n4, one = sem((3,)), sem((4,)), sem(())
    hops = [sem((2, 3)), sem((2, 3)), sem((3, 3)), sem((3, 3))]
    sems = [
        n3, n3, sem((2, 3)), sem((2, 3)), n3, n3, n3, n4, n3, n3, sem((4, 3)), sem((4, 3)),
        n3, n3, n3, n3, n4, n4, n4, n4, one, one, n3, n3,
        *hops, *hops, one, one, one, one, sem((29,)),
    ]
    vmem, any_ = pl.BlockSpec(memory_space=pltpu.VMEM), pl.BlockSpec(memory_space=pl.ANY)
    return pl.pallas_call(
        front_kernel,
        out_shape=outs,
        in_specs=[vmem, any_, any_, any_, any_, any_, any_, vmem, vmem, vmem, vmem, vmem],
        out_specs=[any_] * len(outs),
        scratch_shapes=scratch + sems,
        compiler_params=pltpu.CompilerParams(
            collective_id=1, has_side_effects=True, vmem_limit_bytes=62 * 1024 * 1024),
        name="front",
    )(*args)


def back_kernel(i_x, i_dy, i_ggu, i_hw, i_act, i_q, i_k, i_v, i_probs, i_att, i_qkvw, i_projw, i_small,
                i_res, i_gates, i_kept, i_gsum, i_osum, tok, cos_t, sin_t,
                o_e, o_gtok, o_qg, o_pg, o_terms, o_op,
                xb, dyb, ggu, hw, qs, ks, vs, probs, att, qkvw, projw, smalls, res, gates, kept, gown, grecv,
                gw, recv1, send2, recv2, zs, zr, ib, agv,
                gres, gresf, gproj, sibr, plr, qgp, qz, qgo, pgp, pgr, pq2, pgo, terms, tz, tsib, tpl, tout, gtok,
                s1, r1, s2, r2, sz, rz, sa, ra, ss, rs, la,
                s_g, r_g, s_gr, r_gr, s_grc, r_grc, s_sib, r_sib, s_pl, r_pl, s_qz, r_qz, s_qo, r_qo,
                s_qoc, r_qoc, s_p1, r_p1, s_p2, r_p2, s_po, r_po, s_poc, r_poc, s_tz, r_tz, s_ts, r_ts,
                s_tp, r_tp, s_o, r_o, ld, sv):
    y, x, c, z = place()
    half = HID // 2
    wide = 3 * half
    nq = 6

    def slot(a, b):
        return flip(y, a * c + b * (1 - c)) * 2 + flip(x, a * (1 - c) + b * c)

    p0, p1, p2, p3 = slot(0, 0), slot(1, 0), slot(0, 1), slot(1, 1)
    peers = (p1, p2, p3)
    d1, d2, dsib = (p1 * 2 + c, z), (p2 * 2 + c, z), (p0 * 2 + 1 - c, z)
    dpl = [(p * 2 + c, z) for p in peers]
    zk = [lax.rem(z + k, 4) for k in range(4)]
    dz = [(p0 * 2 + c, zz) for zz in zk]

    loads = {}

    def load(name, src, dst):
        loads[name] = pltpu.make_async_copy(src, dst, ld.at[len(loads)])
        loads[name].start()
    load("x", i_x.at[:, :, :, pl.ds(0, 1536)], xb)
    load("ggu", i_ggu, ggu)
    load("dy", i_dy, dyb)
    load("hw", i_hw, hw)
    load("gown", i_gsum.at[z], gown)
    for name, src, dst in (("res", i_res, res), ("gates", i_gates, gates), ("kept", i_kept, kept),
                           ("small", i_small, smalls),
                           ("projw", i_projw, projw), ("probs", i_probs, probs), ("q", i_q, qs), ("k", i_k, ks),
                           ("v", i_v, vs), ("att", i_att, att), ("qkvw", i_qkvw, qkvw)):
        load(name, src, dst)

    barrier = pltpu.get_barrier_semaphore()
    for to in dpl + dz[1:] + [dsib]:
        pl.semaphore_signal(barrier, 1, device_id=to, device_id_type=MESH)
    pl.semaphore_wait(barrier, 7)

    def remote(src, dst, s, r, to):
        return pltpu.make_async_remote_copy(src, dst, s, r, device_id=to, device_id_type=MESH)

    def copy1(q, b):
        return remote(gw.at[q // 2, slot(1, b), lax.rem(q, 2)], recv1.at[q, b], s1.at[q, b], r1.at[q, b], d1)

    def copy2(q):
        return remote(send2.at[lax.rem(q, 2)], recv2.at[q], s2.at[q], r2.at[q], d2)

    def copyz(q, k):
        return remote(zs.at[lax.rem(q, 2), zk[k]], zr.at[q, z], sz.at[q, k - 1], rz.at[q, k - 1], dz[k])

    def rows(q, p):
        return pl.ds(pl.multiple_of(((q // 2) * 8 + p * 2 + lax.rem(q, 2)) * 256, 256), 256)

    def copya(q, i):
        p, who = ((p0, d1), (p0, d2), (p1, d2))[i]
        src = agv.at[lax.rem(q, 2)] if i < 2 else o_e.at[c, rows(q, p)]
        return remote(src, o_e.at[c, rows(q, p)], sa.at[q, i], ra.at[q, i], who)

    def copys(q, i):
        p = (p0, p1, p2, p3)[i]
        src = agv.at[lax.rem(q, 2)] if i == 0 else o_e.at[c, rows(q, p)]
        return remote(src, o_e.at[c, rows(q, p)], ss.at[q, i], rs.at[q, i], dsib)

    def keep(q):
        return pltpu.make_async_copy(agv.at[lax.rem(q, 2)], o_e.at[c, rows(q, p0)], la.at[q])

    def c_g(k):
        return remote(i_gsum.at[zk[k]], grecv.at[k - 1], s_g.at[k - 1], r_g.at[k - 1], dz[k])

    def c_o(k):
        return remote(i_osum.at[zk[k]], o_op.at[k], s_o.at[k - 1], r_o.at[k - 1], dz[k])

    def c_gr(i):
        return remote(gres.at[c, p0], gres.at[c, p0], s_gr.at[i], r_gr.at[i], dpl[i])

    def c_grc(i):
        p = (p0, p1, p2, p3)[i]
        return remote(gres.at[c, p], gres.at[c, p], s_grc.at[i], r_grc.at[i], dsib)

    def c_sib():
        return remote(dyb.at[0], sibr, s_sib, r_sib, dsib)

    def c_pl(i):
        return remote(dyb.at[1, i], plr.at[i], s_pl.at[i], r_pl.at[i], dpl[i])

    def c_qz(k):
        return remote(qgp.at[zk[k]], qz.at[k - 1], s_qz.at[k - 1], r_qz.at[k - 1], dz[k])

    def c_qo(i):
        return remote(qgo, o_qg.at[p0 * 2 + c], s_qo.at[i], r_qo.at[i], dpl[i])

    def c_qoc(i):
        r = (p0, p1, p2, p3)[i] * 2 + c
        return remote(qgo if i == 0 else o_qg.at[r], o_qg.at[r], s_qoc.at[i], r_qoc.at[i], dsib)

    def c_p1(i):
        return remote(pgp.at[peers[i]], pgr.at[p0], s_p1.at[i], r_p1.at[i], dpl[i])

    def c_p2(k):
        return remote(pgr.at[zk[k]], pq2.at[k - 1], s_p2.at[k - 1], r_p2.at[k - 1], dz[k])

    def c_po(i):
        return remote(pgo, o_pg.at[c, p0], s_po.at[i], r_po.at[i], dpl[i])

    def c_poc(i):
        p = (p0, p1, p2, p3)[i]
        return remote(pgo if i == 0 else o_pg.at[c, p], o_pg.at[c, p], s_poc.at[i], r_poc.at[i], dsib)

    def lanes_of(zz):
        return pl.ds(pl.multiple_of(zz * 384, 384), 384)

    def c_tz(k):
        return remote(terms.at[:, lanes_of(zk[k])], tz.at[k], s_tz.at[k - 1], r_tz.at[k - 1], dz[k])

    def c_ts():
        return remote(tz.at[0], tsib, s_ts, r_ts, dsib)

    def c_tp(i):
        return remote(tpl.at[p0], tpl.at[p0], s_tp.at[i], r_tp.at[i], dpl[i])

    saves = [pltpu.make_async_copy(gtok, o_gtok, sv.at[0]),
             pltpu.make_async_copy(qgo, o_qg.at[p0 * 2 + c], sv.at[1]),
             pltpu.make_async_copy(pgo, o_pg.at[c, p0], sv.at[2]),
             pltpu.make_async_copy(tout, o_terms, sv.at[3])]
    own_out = pltpu.make_async_copy(i_osum.at[z], o_op.at[0], sv.at[5])
    own_out.start()
    act_load = pltpu.make_async_copy(i_act, xb, sv.at[4])

    for k in (1, 2, 3):
        c_g(k).start()
    loads["x"].wait()
    loads["ggu"].wait()
    loads["dy"].wait()
    loads["hw"].wait()

    def stage1(q):
        def multiply():
            q3 = q // 2

            def side(ref):
                return jnp.concatenate(
                    [ref[:, :, :, pl.ds(pl.multiple_of(zz * 384 + q3 * 128, 128), 128)].reshape(1024, 128)
                     for zz in range(4)], axis=1)
            xs, ds_ = side(xb), side(dyb)

            def one(j, _):
                up = lax.dot_general(xs, ggu[j], (((0,), (0,)), ((), ())), preferred_element_type=F32).astype(BF)
                dn = lax.dot_general(ds_, hw[j], (((0,), (0,)), ((), ())), preferred_element_type=F32).astype(BF)
                for zz in range(4):
                    for p in range(4):
                        for h in range(2):
                            at = zz * 128 + p * 32 + h * 16
                            gw[q3, p, h, zz, j, :, : 2 * half] = up[at : at + 16]
                            gw[q3, p, h, zz, j, :, 2 * half :] = dn[at : at + 16]
                return 0
            lax.fori_loop(0, 4, one, 0)
        if isinstance(q, int):
            if q % 2 == 0:
                multiply()
        else:
            pl.when(lax.rem(q, 2) == 0)(multiply)
        for b in range(2):
            copy1(q, b).start()

    def stage2(q):
        for b in range(2):
            copy1(q, b).wait_recv()

        def one(zz, _):
            send2[lax.rem(q, 2), zz] = (gw[q // 2, p2, lax.rem(q, 2), zz].astype(F32)
                                        + recv1[q, 1, zz].astype(F32)).astype(BF)
            return 0
        lax.fori_loop(0, 4, one, 0)
        copy2(q).start()

    def stage3(q):
        copy2(q).wait()

        def one(zz, _):
            zs[lax.rem(q, 2), zz] = (gw[q // 2, p0, lax.rem(q, 2), zz].astype(F32) + recv1[q, 0, zz].astype(F32)
                                     + recv2[q, zz].astype(F32)).astype(BF)
            return 0
        lax.fori_loop(0, 4, one, 0)
        for k in range(1, 4):
            copyz(q, k).start()
        zr[q, z] = zs[lax.rem(q, 2), z]

    def stage4(q):
        for k in range(1, 4):
            copyz(q, k).wait()

        @pl.when(q >= 2)
        def _():
            copya(q - 2, 0).wait_send()
            copya(q - 2, 1).wait_send()
            copys(q - 2, 0).wait_send()
            keep(q - 2).wait()
        for zz in range(4):
            for j in range(4):
                for l in range(wide // 128):
                    ib[l, pl.ds(zz * 4 + j, 16, stride=EXPERTS), :] = (
                        zr[q, zz, j, :, l * 128 : (l + 1) * 128].astype(F32))
        for l in range(wide // 128):
            agv[lax.rem(q, 2), :, l * 128 : (l + 1) * 128] = ib[l].astype(BF)
        copya(q, 0).start()
        copys(q, 0).start()
        keep(q).start()

    def stage5(q):
        copya(q, 0).wait_recv()
        copya(q, 1).start()
        copya(q, 2).start()
        copys(q, 1).start()

    def stage6(q):
        copya(q, 1).wait_recv()
        copya(q, 2).wait_recv()
        copys(q, 2).start()
        copys(q, 3).start()

    def stage7(q):
        for i in range(4):
            copys(q, i).wait_recv()

    def norm_two():
        r = res[...]
        inv = lax.rsqrt(jnp.mean(r * r, axis=1, keepdims=True) + EPS)
        return inv, r * inv

    def norm_one():
        t = tok[...].astype(F32)
        inv = lax.rsqrt(jnp.mean(t * t, axis=1, keepdims=True) + EPS)
        return inv, t * inv

    def gain(row):
        return jnp.concatenate([smalls[i, row : row + 1, :] for i in range(4)], axis=1).astype(F32)

    def event_residual():
        for name in ("gown", "res", "gates", "kept", "small"):
            loads[name].wait()
        for k in (1, 2, 3):
            c_g(k).wait_recv()
        tail = slice(1536, 1664), slice(1664, 1792)

        def gate_part(v):
            return (v[:, tail[0]].astype(F32) + v[:, tail[1]].astype(F32))[:, :EXPERTS]
        gg = (gate_part(gown[...]) + gate_part(grecv[0]) + gate_part(grecv[1]) + gate_part(grecv[2])) * kept[...]
        gt = gates[...]
        gl = (gt * (gg - jnp.sum(gt * gg, axis=1, keepdims=True))).astype(BF)
        router_t = jnp.concatenate([smalls[i, 16:32, :] for i in range(4)], axis=1)
        ga = jnp.dot(gl, router_t, preferred_element_type=F32)
        ga = ga + gown[:, :1536].astype(F32)
        for k in range(3):
            ga = ga + grecv[k, :, :1536].astype(F32)
        inv, normed = norm_two()
        terms[8:24, :] = lax.dot_general(gl, xb[c, z], (((0,), (0,)), ((), ())), preferred_element_type=F32)
        terms[1:2, :] = jnp.sum(ga * normed, axis=0, keepdims=True)
        scaled = ga * gain(1)
        gr = dyb[c, z].astype(F32) + inv * (scaled - normed * jnp.mean(scaled * normed, axis=1, keepdims=True))
        gresf[...] = gr
        gres[c, p0] = gr.astype(BF)
        for i in range(3):
            c_gr(i).start()
        c_grc(0).start()

    def event_share():
        for i in range(3):
            c_gr(i).wait_recv()
            c_grc(i + 1).start()
        act_load.start()

    scale = 64 ** -0.5

    def event_attention():
        for name in ("projw", "probs", "q", "k", "v", "att", "qkvw"):
            loads[name].wait()
        for i in range(4):
            c_grc(i).wait_recv()

        def one(n, _):
            cc, i = n // 4, lax.rem(n, 4)
            gb = lax.dot_general(gres[cc, i], projw[...], (((1,), (1,)), ((), ())),
                                 preferred_element_type=F32).astype(BF)
            ga = jnp.concatenate([gb[:, h * 64 : (h + 1) * 64] for h in range(3)], axis=0)
            pb = probs[cc, i]
            gv = lax.dot_general(pb.astype(BF), ga, (((0,), (0,)), ((), ())), preferred_element_type=F32)
            gp = lax.dot_general(ga, vs[cc, i], (((1,), (1,)), ((), ())), preferred_element_type=F32)
            gs = (pb * (gp - jnp.sum(pb * gp, axis=-1, keepdims=True))).astype(BF)
            gq = jnp.dot(gs, ks[cc, i], preferred_element_type=F32) * scale
            gk = lax.dot_general(gs, qs[cc, i], (((0,), (0,)), ((), ())), preferred_element_type=F32) * scale
            lo = jnp.concatenate([gq[0:128], gq[128:256]], axis=1)
            hi = jnp.concatenate([gq[256:384], gk], axis=1)
            gproj[cc, i, :, 0:128] = turn(lo, cos_t[...], -sin_t[...]).astype(BF)
            gproj[cc, i, :, 128:256] = turn(hi, cos_t[...], -sin_t[...]).astype(BF)
            gproj[cc, i, :, 256:320] = gv.astype(BF)
            return 0
        lax.fori_loop(0, 8, one, 0)

        def to_sib(i, _):
            dyb[0, i] = lax.dot_general(gproj[1 - c, i], qkvw[...], (((1,), (1,)), ((), ())),
                                        preferred_element_type=F32).astype(BF)
            return 0
        lax.fori_loop(0, 4, to_sib, 0)
        c_sib().start()
        pg = lax.dot_general(att[...].reshape(1024, 192), gres[...].reshape(1024, 1536), (((0,), (0,)), ((), ())),
                             preferred_element_type=F32)
        pgp[...] = pg.astype(BF).reshape(4, 48, 1536)
        for i in range(3):
            c_p1(i).start()
        pgr[p0] = pgp[p0]

    def event_columns():
        act_load.wait()

        def one(zz, _):
            a = xb[:, :, :, lanes_of(zz)].reshape(1024, 384)
            qgp[zz] = lax.dot_general(a, gproj[...].reshape(1024, 320), (((0,), (0,)), ((), ())),
                                      preferred_element_type=F32).astype(BF)
            return 0
        lax.fori_loop(0, 4, one, 0)
        for k in (1, 2, 3):
            c_qz(k).start()
        c_sib().wait()

        def part(p):
            return lax.dot_general(gproj[c, p], qkvw[...], (((1,), (1,)), ((), ())),
                                   preferred_element_type=F32) + sibr[p].astype(F32)
        for i in range(3):
            dyb[1, i] = part(peers[i]).astype(BF)
            c_pl(i).start()
        gtok[...] = part(p0)
        for i in range(3):
            c_p1(i).wait_recv()
        for k in (1, 2, 3):
            c_p2(k).start()

    def event_tokens():
        ga = gtok[...]
        for i in range(3):
            c_pl(i).wait_recv()
            ga = ga + plr[i].astype(F32)
        inv, normed = norm_one()
        terms[0:1, :] = jnp.sum(ga * normed, axis=0, keepdims=True)
        scaled = ga * gain(0)
        gtok[...] = gresf[...] + inv * (scaled - normed * jnp.mean(scaled * normed, axis=1, keepdims=True))
        saves[0].start()
        for k in (1, 2, 3):
            c_tz(k).start()
        for k in (1, 2, 3):
            c_qz(k).wait_recv()
        qgo[...] = (qgp[z].astype(F32) + qz[0].astype(F32) + qz[1].astype(F32) + qz[2].astype(F32)).astype(BF)
        for i in range(3):
            c_qo(i).start()
        c_qoc(0).start()
        saves[1].start()
        for k in (1, 2, 3):
            c_p2(k).wait_recv()
        pgo[...] = (pgr[z].astype(F32) + pq2[0].astype(F32) + pq2[1].astype(F32) + pq2[2].astype(F32)).astype(BF)
        for i in range(3):
            c_po(i).start()
        c_poc(0).start()
        saves[2].start()
        for k in (1, 2, 3):
            c_o(k).start()

    def event_terms():
        for k in (1, 2, 3):
            c_tz(k).wait_recv()
        tz[0] = terms[:, lanes_of(z)] + tz[1] + tz[2] + tz[3]
        c_ts().start()
        for i in range(3):
            c_qo(i).wait_recv()
            c_qoc(i + 1).start()
            c_po(i).wait_recv()
            c_poc(i + 1).start()

    def event_sums():
        c_ts().wait()
        tpl[p0] = tz[0] + tsib[...]
        for i in range(3):
            c_tp(i).start()

    def event_last():
        for i in range(3):
            c_tp(i).wait_recv()
        tout[...] = tpl[0] + tpl[1] + tpl[2] + tpl[3]
        saves[3].start()
        for i in range(4):
            c_qoc(i).wait_recv()
            c_poc(i).wait_recv()
        for k in (1, 2, 3):
            c_o(k).wait_recv()

    stages = (stage1, stage2, stage3, stage4, stage5, stage6, stage7)
    lead = 1
    events = {2: event_residual, 3: event_share, 4: event_attention, 5: event_columns, 7: event_tokens,
              8: event_terms, 9: event_sums, 10: event_last}

    for q in range(lead):
        stage1(q)

    def step(t, _):
        for i, stage in enumerate(stages):
            q = t + lead if i == 0 else t + 1 - i

            @pl.when((q >= 0) & (q < nq))
            def _(stage=stage, q=q):
                stage(q)
        for at, event in events.items():
            @pl.when(t == at)
            def _(event=event):
                event()
        return 0

    lax.fori_loop(0, nq + len(stages) - 2, step, 0)

    def left(q, _):
        for b in range(2):
            copy1(q, b).wait_send()
        for i in range(1, 4):
            copys(q, i).wait_send()
        copya(q, 2).wait_send()

        @pl.when(q >= nq - 2)
        def _():
            copya(q, 0).wait_send()
            copya(q, 1).wait_send()
            copys(q, 0).wait_send()
            keep(q).wait()
        return 0
    lax.fori_loop(0, nq, left, 0)
    for k in (1, 2, 3):
        for one in (c_g(k), c_o(k), c_qz(k), c_p2(k), c_tz(k)):
            one.wait_send()
    for i in range(3):
        for one in (c_gr(i), c_pl(i), c_qo(i), c_p1(i), c_po(i), c_tp(i)):
            one.wait_send()
    for i in range(4):
        for one in (c_grc(i), c_qoc(i), c_poc(i)):
            one.wait_send()
    for one in saves + [own_out]:
        one.wait()


def back(front_outs, tok, cos_t, sin_t):
    nq, wide = 6, 3 * HID // 2
    sem, vm = pltpu.SemaphoreType.DMA, pltpu.VMEM
    out = lambda shape, kind=BF: jax.ShapeDtypeStruct(shape, kind)
    piece = (4, 4, 16, wide)
    outs = (out((2, 6144, wide)), out((128, 1536), F32), out((8, 384, 320)), out((2, 4, 48, 1536)),
            out((24, 384), F32), out((4, 128, 1536)))
    block, quad, three = vm((2, 4, 128, 1536), BF), vm((4, 128, 1536), BF), vm((3, 128, 1536), BF)
    scratch = [
        block, block, vm((4, 1024, 512), BF), vm((4, 1024, 256), BF), vm((2, 4, 384, 64), BF),
        vm((2, 4, 128, 64), BF), vm((2, 4, 128, 64), BF), vm((2, 4, 384, 128), F32), vm((2, 4, 128, 192), BF),
        vm((1536, 320), BF), vm((192, 1536), BF), vm((4, 32, 384), BF), vm((128, 1536), F32), vm((128, 16), F32), vm((128, 16), F32),
        vm((128, 1792), BF), vm((3, 128, 1792), BF),
        vm((3, 4, 2) + piece, BF), vm((nq, 2) + piece, BF), vm((2,) + piece, BF), vm((nq,) + piece, BF),
        vm((2,) + piece, BF), vm((nq,) + piece, BF), vm((wide // 128, 256, 128), F32), vm((2, 256, wide), BF),
        block, vm((128, 1536), F32), vm((2, 4, 128, 320), BF), quad, three, vm((4, 384, 320), BF),
        vm((3, 384, 320), BF), vm((384, 320), BF), vm((4, 48, 1536), BF), vm((4, 48, 1536), BF),
        vm((3, 48, 1536), BF), vm((48, 1536), BF), vm((24, 1536), F32), vm((4, 24, 384), F32),
        vm((24, 384), F32), vm((4, 24, 384), F32), vm((24, 384), F32), vm((128, 1536), F32),
    ]
    n3, n4, one = sem((3,)), sem((4,)), sem(())
    sems = [
        sem((nq, 2)), sem((nq, 2)), sem((nq,)), sem((nq,)), sem((nq, 3)), sem((nq, 3)), sem((nq, 3)), sem((nq, 3)),
        sem((nq, 4)), sem((nq, 4)), sem((nq,)),
        n3, n3, n3, n3, n4, n4, one, one, n3, n3, n3, n3, n3, n3,
        n4, n4, n3, n3, n3, n3, n3, n3, n4, n4, n3, n3, one, one,
        n3, n3, n3, n3, sem((16,)), sem((6,)),
    ]
    vmem, any_ = pl.BlockSpec(memory_space=pltpu.VMEM), pl.BlockSpec(memory_space=pl.ANY)
    return pl.pallas_call(
        back_kernel,
        out_shape=outs,
        in_specs=[any_] * 18 + [vmem] * 3,
        out_specs=[any_] * len(outs),
        scratch_shapes=scratch + sems,
        compiler_params=pltpu.CompilerParams(
            collective_id=2, has_side_effects=True, vmem_limit_bytes=62 * 1024 * 1024),
        name="back",
    )(*front_outs, tok, cos_t, sin_t)


def finish_kernel(v, qkv, proj, res, parts, gu, dn, g_qkv, g_proj, out):
    half = HID // 2
    for c in range(2):
        gu[:, c * half : (c + 1) * half] = v[c, :, :half].astype(F32)
        gu[:, HID + c * half : HID + (c + 1) * half] = v[c, :, half : 2 * half].astype(F32)
        dn[:, c * half : (c + 1) * half] = v[c, :, 2 * half :].astype(F32)
    heads = range(qkv.shape[0])
    g_qkv[...] = jnp.concatenate(
        [qkv[h, :, lo:hi].astype(F32) for lo, hi in ((0, 192), (192, 256), (256, 320)) for h in heads], axis=1)
    g_proj[...] = proj[...].astype(F32)

    @pl.when(pl.program_id(0) == 0)
    def _():
        total = res[...]
        for k in range(4):
            total = total + parts[k].astype(F32)
        out[...] = total.astype(BF)


def finish(v, qkv, proj, res, parts):
    steps, own, width = 24, proj.shape[0], proj.shape[1]
    row, some = v.shape[1] // steps, own // steps
    once = lambda n: (lambda i: (0,) * n)
    return pl.pallas_call(
        finish_kernel,
        grid=(steps,),
        out_shape=(
            jax.ShapeDtypeStruct((v.shape[1], 2 * HID), F32), jax.ShapeDtypeStruct((v.shape[1], HID), F32),
            jax.ShapeDtypeStruct((own, 2560), F32), jax.ShapeDtypeStruct((own, width), F32),
            jax.ShapeDtypeStruct(res.shape, BF)),
        in_specs=[
            pl.BlockSpec((2, row, v.shape[2]), lambda i: (0, i, 0)),
            pl.BlockSpec((8, some, 320), lambda i: (0, i, 0)), pl.BlockSpec((some, width), lambda i: (i, 0)),
            pl.BlockSpec(res.shape, once(2)), pl.BlockSpec(parts.shape, once(3))],
        out_specs=[
            pl.BlockSpec((row, 2 * HID), lambda i: (i, 0)), pl.BlockSpec((row, HID), lambda i: (i, 0)),
            pl.BlockSpec((some, 2560), lambda i: (i, 0)), pl.BlockSpec((some, width), lambda i: (i, 0)),
            pl.BlockSpec(res.shape, once(2))],
        compiler_params=pltpu.CompilerParams(vmem_limit_bytes=40 * 1024 * 1024),
        name="finish",
    )(v, qkv, proj, res, parts)


def expert_grads_general(reps, grps, xs, dys, ggu, hw):
    local, half, width = ggu.shape[0], HID // 2, xs.shape[1]
    own = width // grps
    chips = reps // 2
    piece = own // chips
    same_core = [[2 * i + c for i in range(chips)] for c in range(2)]
    pairs = [[2 * i, 2 * i + 1] for i in range(chips)]
    up = jnp.einsum("td,eth->edh", xs, ggu, preferred_element_type=F32).astype(BF)
    down = jnp.einsum("td,eth->edh", dys, hw, preferred_element_type=F32).astype(BF)
    gw = jnp.concatenate([up, down], axis=2)
    gw = gw.reshape(local, grps, chips, piece, 3 * half).transpose(2, 1, 3, 0, 4)
    gw = gw.reshape(chips * grps * piece, local * 3 * half)
    gw = lax.psum_scatter(gw, "rep", scatter_dimension=0, tiled=True, axis_index_groups=same_core)
    gw = lax.all_to_all(gw.reshape(grps, piece, local, 3 * half), "grp", 0, 0, tiled=True)
    gw = gw.transpose(1, 0, 2, 3).reshape(piece, EXPERTS, 3 * half)
    gw = lax.all_gather(gw, "rep", axis=0, tiled=True, axis_index_groups=same_core)
    gw = lax.all_gather(gw, "rep", axis=0, tiled=False, axis_index_groups=pairs).astype(F32)
    gw = gw.reshape(2, own * EXPERTS, 3, half)
    gw = jnp.moveaxis(gw, 0, 2).reshape(own * EXPERTS, 3 * HID)
    return gw[:, : 2 * HID], gw[:, 2 * HID :]


def shards_general(
    reps,
    grps,
    tokens,
    attn_gain,
    query_key_value_weight,
    attn_proj,
    mlp_gain,
    w_router,
    w_gate_up,
    w_down,
    prefix_len,
    expert_ids,
    priority,
    cotangent,
):
    seq, width = tokens.shape
    own = width // grps
    local_experts = EXPERTS // grps
    heads = KEY_VALUE_HEADS
    groups = None if reps == heads else [list(range(i, i + heads)) for i in range(0, reps, heads)]
    rep, grp = lax.axis_index("rep"), lax.axis_index("grp")
    head = lax.rem(rep, heads)
    qw, hw = QPK * HEAD_WIDTH, HEAD_WIDTH
    q_all = QUERY_HEADS * HEAD_WIDTH

    small = jnp.concatenate([attn_gain[:, None], mlp_gain[:, None], w_router], axis=1)
    small = lax.all_gather(small, "grp", axis=0, tiled=True)
    gain_one, gain_two = small[:, 0].astype(F32)[None, :], small[:, 1].astype(F32)[None, :]
    router = small[:, 2:]
    qkv_cols = jnp.concatenate(
        [
            lax.dynamic_slice_in_dim(query_key_value_weight, head * qw, qw, 1),
            lax.dynamic_slice_in_dim(query_key_value_weight, q_all + head * hw, hw, 1),
            lax.dynamic_slice_in_dim(query_key_value_weight, q_all + heads * hw + head * hw, hw, 1),
        ],
        axis=1,
    )
    qkv_head = lax.all_gather(qkv_cols, "grp", axis=0, tiled=True)
    row = head * qw + jnp.arange(qw)
    mine = (row // own) == grp
    proj_rows = jnp.where(mine[:, None], jnp.take(attn_proj, jnp.where(mine, row - grp * own, 0), axis=0), 0)
    proj_head = lax.psum(proj_rows, "grp")

    core, chip, chips, half = lax.rem(rep, 2), rep // 2, reps // 2, HID // 2
    pairs = [[2 * i, 2 * i + 1] for i in range(chips)]
    same_core = [[2 * i + c for i in range(chips)] for c in range(2)]
    piece = own // chips
    gu_piece = lax.dynamic_slice_in_dim(w_gate_up, chip * piece, piece, 0)
    dn_piece = lax.dynamic_slice_in_dim(w_down, chip * piece, piece, 0)
    both = jnp.concatenate(
        [
            lax.dynamic_slice_in_dim(gu_piece, core * half, half, 2),
            lax.dynamic_slice_in_dim(gu_piece, HID + core * half, half, 2),
            lax.dynamic_slice_in_dim(dn_piece, core * half, half, 2),
        ],
        axis=2,
    )
    both = both.reshape(piece, grps, local_experts, 3 * half).transpose(1, 2, 0, 3)
    both = lax.all_to_all(both, "grp", 0, 0, tiled=True)
    both = lax.all_gather(both, "rep", axis=0, tiled=False, axis_index_groups=same_core)
    both = both.transpose(2, 1, 0, 3, 4).reshape(local_experts, width, 3 * half)
    wgu, wdn = both[:, :, : 2 * half], both[:, :, 2 * half :]

    tokens_f = tokens.astype(F32)
    inverse_one = lax.rsqrt(jnp.mean(tokens_f * tokens_f, axis=1, keepdims=True) + EPS)
    normed_one = tokens_f * inverse_one
    act_one = (normed_one * gain_one).astype(BF)
    act_plane = lax.all_gather(act_one, "rep", axis=0, tiled=True, axis_index_groups=groups)
    prefix_plane = lax.all_gather(prefix_len, "rep", axis=0, tiled=True, axis_index_groups=groups)
    cos, sin = rope_tables(seq)
    projected = dot(act_plane, qkv_head).reshape(heads, seq, QPK + 2, HEAD_WIDTH)
    cos_b, sin_b = cos[None, :, None, :], sin[None, :, None, :]
    turned = rotate(projected[:, :, : QPK + 1], cos_b, sin_b).astype(BF)
    query = turned[:, :, :QPK]
    key = turned[:, :, QPK]
    value = projected[:, :, QPK + 1].astype(BF)
    scale = HEAD_WIDTH ** (-0.5)
    row_pos, col_pos = jnp.arange(seq)[:, None], jnp.arange(seq)[None, :]
    allowed = (col_pos <= row_pos)[None] | (col_pos[None] < prefix_plane[:, None, None])
    scores = jnp.einsum("bsgd,btd->bgst", query, key, preferred_element_type=F32) * scale
    scores = jnp.where(allowed[:, None], scores, -1e30)
    exps = jnp.exp(scores - jnp.max(scores, axis=-1, keepdims=True))
    probs = exps / jnp.sum(exps, axis=-1, keepdims=True)
    probs_low = probs.astype(BF)
    attended = jnp.einsum("bgst,btd->bsgd", probs_low, value, preferred_element_type=F32)
    attended = attended.astype(BF).reshape(heads * seq, qw)
    part = dot(attended, proj_head).astype(BF)
    part = lax.psum_scatter(part, "rep", scatter_dimension=0, tiled=True, axis_index_groups=groups)
    residual = tokens_f + part.astype(F32)
    inverse_two = lax.rsqrt(jnp.mean(residual * residual, axis=1, keepdims=True) + EPS)
    normed_two = residual * inverse_two
    act_two = (normed_two * gain_two).astype(BF)
    gates, kept = routing(expert_ids, priority, dot(act_two, router))

    def column(v):
        v = lax.all_gather(v, "grp", axis=0, tiled=True)
        return lax.all_gather(v, "rep", axis=0, tiled=True, axis_index_groups=pairs)

    def to_owners(v):
        v = lax.psum_scatter(v, "rep", scatter_dimension=0, tiled=True, axis_index_groups=pairs)
        return lax.psum_scatter(v, "grp", scatter_dimension=0, tiled=True).astype(F32)

    dy_all = column(cotangent)
    x_all = column(act_two)
    weight = column(jnp.where(kept, gates, 0.0))
    weight = lax.dynamic_slice_in_dim(weight, grp * local_experts, local_experts, 1).T[:, :, None]
    gate_up = jnp.einsum("td,edh->eth", x_all, wgu, preferred_element_type=F32)
    g, u = gate_up[..., :half], gate_up[..., half:]
    sig = jax.nn.sigmoid(g)
    silu = g * sig
    hidden = silu * u
    hidden_w = (hidden * weight).astype(BF)
    back = jnp.einsum("td,edh->eth", dy_all, wdn, preferred_element_type=F32)
    grad_gate_part = jnp.sum(back * hidden, axis=2)
    grad_hidden = back * weight
    ggu = jnp.concatenate(
        [grad_hidden * u * sig * (1.0 + g * (1.0 - sig)), grad_hidden * silu], axis=2
    ).astype(BF)
    out_part = jnp.einsum("eth,edh->td", hidden_w, wdn, preferred_element_type=F32).astype(BF)
    gact_part = jnp.einsum("eth,edh->td", ggu, wgu, preferred_element_type=F32).astype(BF)
    gact = to_owners(gact_part)
    grad_gates = lax.psum_scatter(
        grad_gate_part.T, "rep", scatter_dimension=0, tiled=True, axis_index_groups=pairs
    )
    grad_gates = lax.all_to_all(grad_gates, "grp", 0, 1, tiled=True)
    grad_gates = jnp.where(kept, grad_gates, 0.0)
    out = to_owners(out_part)
    output = (residual + out).astype(BF)
    grad_gu, grad_dn = expert_grads_general(reps, grps, x_all, dy_all, ggu, hidden_w)
    grad_gu = grad_gu.reshape(own, EXPERTS, 2 * HID)
    grad_dn = grad_dn.reshape(own, EXPERTS, HID)

    grad_logits = (gates * (grad_gates - jnp.sum(gates * grad_gates, axis=1, keepdims=True))).astype(BF)
    gact = gact + dot(grad_logits, router.T)
    router_term = dot(act_two.T, grad_logits)
    gain_two_term = jnp.sum(gact * normed_two, axis=0)
    scaled = gact * gain_two
    dy = cotangent.astype(F32)
    grad_residual = dy + inverse_two * (
        scaled - normed_two * jnp.mean(scaled * normed_two, axis=1, keepdims=True)
    )
    gres_low = grad_residual.astype(BF)

    gres_plane = lax.all_gather(gres_low, "rep", axis=0, tiled=True, axis_index_groups=groups)
    proj_term = dot(attended.T, gres_plane)
    grad_att = dot(gres_plane, proj_head.T).astype(BF).reshape(heads, seq, QPK, HEAD_WIDTH)
    grad_value = jnp.einsum("bgst,bsgd->btd", probs_low, grad_att, preferred_element_type=F32)
    grad_probs = jnp.einsum("bsgd,btd->bgst", grad_att, value, preferred_element_type=F32)
    grad_scores = (
        probs * (grad_probs - jnp.sum(probs * grad_probs, axis=-1, keepdims=True))
    ).astype(BF)
    grad_query = jnp.einsum("bgst,btd->bsgd", grad_scores, key, preferred_element_type=F32) * scale
    grad_key = jnp.einsum("bgst,bsgd->btd", grad_scores, query, preferred_element_type=F32) * scale
    turned_back = rotate(
        jnp.concatenate([grad_query, grad_key[:, :, None]], axis=2), cos_b, -sin_b
    )
    gproj = jnp.concatenate([turned_back, grad_value[:, :, None]], axis=2).astype(BF)
    gproj = gproj.reshape(heads * seq, qw + 2 * hw)
    qkv_term = dot(act_plane.T, gproj)
    gact_one = dot(gproj, qkv_head.T).astype(BF)
    gact_one = lax.psum_scatter(
        gact_one, "rep", scatter_dimension=0, tiled=True, axis_index_groups=groups
    ).astype(F32)
    gain_one_term = jnp.sum(gact_one * normed_one, axis=0)
    scaled_one = gact_one * gain_one
    grad_tokens = grad_residual + inverse_one * (
        scaled_one - normed_one * jnp.mean(scaled_one * normed_one, axis=1, keepdims=True)
    )

    qkv_own = lax.psum_scatter(qkv_term.astype(BF), "grp", scatter_dimension=0, tiled=True)
    proj_sum = lax.psum(proj_term.astype(BF), "grp")
    if groups is not None:
        across = [[i + heads * j for j in range(reps // heads)] for i in range(heads)]
        qkv_own = lax.psum(qkv_own, "rep", axis_index_groups=across)
        proj_sum = lax.psum(proj_sum, "rep", axis_index_groups=across)
    qkv_own = lax.all_gather(qkv_own, "rep", axis=0, tiled=False, axis_index_groups=groups)
    qkv_own = qkv_own.astype(F32)
    grad_qkv = jnp.concatenate(
        [
            qkv_own[:, :, lo:hi].transpose(1, 0, 2).reshape(own, -1)
            for lo, hi in ((0, qw), (qw, qw + hw), (qw + hw, qw + 2 * hw))
        ],
        axis=1,
    )
    proj_all = lax.all_gather(proj_sum, "rep", axis=0, tiled=True, axis_index_groups=groups)
    grad_proj = lax.dynamic_slice_in_dim(proj_all, grp * own, own, 0).astype(F32)
    terms = jnp.concatenate([gain_one_term[:, None], gain_two_term[:, None], router_term], axis=1)
    terms = lax.psum(lax.psum_scatter(terms, "grp", scatter_dimension=0, tiled=True), "rep")
    return (
        output,
        grad_tokens,
        terms[:, 0],
        grad_qkv,
        grad_proj,
        terms[:, 1],
        terms[:, 2:],
        grad_gu,
        grad_dn,
    )


def shards(
    tokens,
    attn_gain,
    query_key_value_weight,
    attn_proj,
    mlp_gain,
    w_router,
    w_gate_up,
    w_down,
    prefix_len,
    expert_ids,
    priority,
    cotangent,
):
    own, width = attn_gain.shape[0], tokens.shape[1]
    small = jnp.concatenate(
        [attn_gain[None], mlp_gain[None], jnp.zeros((14, own), BF), w_router.T], axis=0
    )
    prefix = jnp.broadcast_to(prefix_len.astype(F32), (8, 128))
    half = HEAD_WIDTH // 2
    inverse_freq = np.float32(10000.0) ** (-np.arange(half, dtype=np.float32) * np.float32(2.0 / HEAD_WIDTH))
    angles = np.arange(tokens.shape[0], dtype=np.float32)[:, None] * inverse_freq[None, :]
    cos_t = jnp.asarray(np.tile(np.cos(angles), (1, 4)), F32)
    sin = np.sin(angles)
    sin_t = jnp.asarray(np.tile(np.concatenate([-sin, sin], axis=1), (1, 2)), F32)
    parts = front(
        tokens, cotangent, w_gate_up, w_down, query_key_value_weight, attn_proj, small, expert_ids,
        priority.reshape(expert_ids.shape), prefix, cos_t, sin_t)
    wide, grad_tokens, qkv_own, proj_own, terms, out_parts = back(parts, tokens, cos_t, sin_t)
    grad_gu, grad_dn, grad_qkv, grad_proj, output = finish(
        wide, qkv_own, proj_own.reshape(own, width), parts[13], out_parts)
    return (
        output,
        grad_tokens,
        terms[0],
        grad_qkv,
        grad_proj,
        terms[1],
        terms[8:].T,
        grad_gu.reshape(own, EXPERTS, 2 * HID),
        grad_dn.reshape(own, EXPERTS, HID),
    )


def solution(mesh):
    tok, par = ("rep", "grp"), "grp"
    in_specs = (
        P(tok, None),
        P(par),
        P(par, None),
        P(par, None),
        P(par),
        P(par, None),
        P(par, None, None),
        P(par, None, None),
        P(tok),
        P(tok, None),
        P(tok, None),
        P(tok, None),
    )
    out_specs = (
        P(tok, None),
        P(tok, None),
        P(par),
        P(par, None),
        P(par, None),
        P(par),
        P(par, None),
        P(par, None, None),
        P(par, None, None),
    )
    reps, grps = mesh.shape["rep"], mesh.shape["grp"]

    def body(*args):
        if (reps, grps) == (8, 4):
            return shards(*args)
        return shards_general(reps, grps, *args)

    return jax.shard_map(body, mesh=mesh, in_specs=in_specs, out_specs=out_specs, check_vma=False)
```

```python
import jax
import jax.numpy as jnp
import numpy as np
from jax import lax
from jax.experimental import pallas as pl
from jax.experimental.pallas import tpu as pltpu
from jax.sharding import PartitionSpec as P

QUERY_HEADS = 24
KEY_VALUE_HEADS = 8
HEAD_WIDTH = 64
HID = 512
EXPERTS = 16
CAP = 72
EPS = 1e-05
BF = jnp.bfloat16
F32 = jnp.float32
QPK = QUERY_HEADS // KEY_VALUE_HEADS
BIG = 1 << 20
MESH = pl.DeviceIdType.MESH


def dot(a, b):
    return jnp.dot(a, b, preferred_element_type=F32)


def rope_tables(length):
    half = HEAD_WIDTH // 2
    position = jnp.arange(length, dtype=F32)[:, None]
    inverse_freq = 10000.0 ** (-jnp.arange(half, dtype=F32) * 2.0 / HEAD_WIDTH)
    angles = position * inverse_freq[None, :]
    return jnp.cos(angles), jnp.sin(angles)


def rotate(v, cos, sin):
    half = HEAD_WIDTH // 2
    a, b = v[..., :half], v[..., half:]
    return jnp.concatenate([a * cos - b * sin, b * cos + a * sin], axis=-1)


def choices(expert_ids, priority):
    seq, top = expert_ids.shape
    choose = expert_ids[:, :, None] == jnp.arange(EXPERTS, dtype=jnp.int32)[None, None, :]
    chosen = jnp.any(choose, axis=1)
    rank_of = jnp.sum(jnp.where(choose, priority.reshape(seq, top)[:, :, None], 0), axis=1)
    rank_of = jnp.where(chosen, rank_of, BIG)
    slot = jnp.sum((rank_of[None, :, :] < rank_of[:, None, :]).astype(jnp.int32), axis=1)
    return chosen, chosen & (slot < CAP)


def routing(expert_ids, priority, logits):
    chosen, kept = choices(expert_ids, priority)
    top_logit = jnp.max(jnp.where(chosen, logits, -jnp.inf), axis=1, keepdims=True)
    gate_exp = jnp.where(chosen, jnp.exp(jnp.where(chosen, logits - top_logit, 0.0)), 0.0)
    gates = gate_exp / jnp.sum(gate_exp, axis=1, keepdims=True)
    return gates, kept


def place():
    r, z = lax.axis_index("rep"), lax.axis_index("grp")
    return r // 4, (r // 2) % 2, r % 2, z


def flip(bit, by):
    return bit + by * (1 - 2 * bit)


def turn(v, cos, sin):
    lane = lax.broadcasted_iota(jnp.int32, v.shape, 1)
    partner = jnp.where(lax.rem(lane, 64) < 32, pltpu.roll(v, 96, 1), pltpu.roll(v, 32, 1))
    return v * cos + partner * sin


def gradient_rows(q3, x, dy, ggu, hw, gw):
    half = HID // 2

    def side(ref):
        return jnp.concatenate(
            [ref[:, :, :, pl.ds(pl.multiple_of(zz * 384 + q3 * 128, 128), 128)].reshape(1024, 128)
             for zz in range(4)], axis=1)
    xs, ds = side(x), side(dy)

    def one(j, _):
        up = lax.dot_general(xs, ggu[j], (((0,), (0,)), ((), ())), preferred_element_type=F32).astype(BF)
        dn = lax.dot_general(ds, hw[j], (((0,), (0,)), ((), ())), preferred_element_type=F32).astype(BF)
        for zz in range(4):
            for p in range(4):
                for h in range(2):
                    at = zz * 128 + p * 32 + h * 16
                    gw[p, h, zz, j, :, : 2 * half] = up[at : at + 16]
                    gw[p, h, zz, j, :, 2 * half :] = dn[at : at + 16]
        return 0
    lax.fori_loop(0, 4, one, 0)


def front_kernel(tok, dy, w_gu, w_dn, qkv, proj, small, ids, prio, prefix, cos_t, sin_t,
                 o_x, o_dy, o_ggu, o_hw, o_act, o_q, o_k, o_v, o_probs, o_att, o_qkvw, o_projw,
                 o_small, o_res, o_gates, o_kept, o_gsum, o_osum, o_gw, o_r1,
                 smalls, qkvw, projw, projq, actp, pre, pr, qs, ks, vs, probs, att, part, sibr, sums, plr,
                 xall, dyall, wbuf, ggu, hw, gpart, ggp, gsib,
                 gsum, res, gates, kept, qwin, wst, wcol, wpiece, gw, recv1,
                 s_small, r_small, s_qkv, r_qkv, s_pz, r_pz, s_pq, r_pq, s_wz, r_wz, s_wp, r_wp,
                 s_act, r_act, s_pre, r_pre, s_actc, r_actc, s_prec, r_prec, s_sib, r_sib, s_pl, r_pl,
                 s_x, r_x, s_xc, r_xc, s_y, r_y, s_yc, r_yc,
                 s_gc, r_gc, s_oc, r_oc, s1, r1, sl):
    y, x, c, z = place()
    half = HID // 2

    def slot(a, b):
        return flip(y, a * c + b * (1 - c)) * 2 + flip(x, a * (1 - c) + b * c)

    p0, p1, p2, p3 = slot(0, 0), slot(1, 0), slot(0, 1), slot(1, 1)
    peers = (p1, p2, p3)
    d1, d2, dsib = (p1 * 2 + c, z), (p2 * 2 + c, z), (p0 * 2 + 1 - c, z)
    dpl = [(p * 2 + c, z) for p in peers]
    zk = [lax.rem(z + k, 4) for k in range(4)]
    zf = [lax.rem(z + 4 - k, 4) for k in range(4)]
    dz = [(p0 * 2 + c, zz) for zz in zk]

    barrier = pltpu.get_barrier_semaphore()
    for to in dpl + dz[1:] + [dsib]:
        pl.semaphore_signal(barrier, 1, device_id=to, device_id_type=MESH)
    pl.semaphore_wait(barrier, 7)

    def remote(src, dst, s, r, to):
        return pltpu.make_async_remote_copy(src, dst, s, r, device_id=to, device_id_type=MESH)

    def c_small(k):
        return remote(small, smalls.at[z], s_small.at[k - 1], r_small.at[k - 1], dz[k])

    def rows(zz, pp):
        return pl.ds(pl.multiple_of(zz * 384 + pp * 96, 96), 96)

    def c_wz(k):
        return remote(wpiece.at[zk[k]], wbuf.at[:, rows(z, p0)], s_wz.at[k - 1], r_wz.at[k - 1], dz[k])

    def c_wp(k, i):
        zz = zf[k]
        who, pp = ((d1, p0), (d2, p0), (d2, p1))[i]
        src = wpiece.at[z] if (k == 0 and i < 2) else wbuf.at[:, rows(zz, pp)]
        return remote(src, wbuf.at[:, rows(zz, pp)], s_wp.at[k, i], r_wp.at[k, i], who)

    def quarter(p):
        return pl.ds(pl.multiple_of(p * 48, 48), 48)

    def c_pz(k):
        src = proj.at[pl.ds(pl.multiple_of(c * 192 + p0 * 48, 48), 48)]
        return remote(src, projq.at[k - 1], s_pz.at[k - 1], r_pz.at[k - 1], dz[k])

    def c_pq(k, owner):
        return remote(projq.at[k - 1], projw.at[quarter(p0)], s_pq.at[k - 1], r_pq.at[p0], (owner * 2 + c, z))

    def c_pq_in(i):
        return remote(projq.at[0], projw.at[quarter(peers[i])], s_pq.at[0], r_pq.at[peers[i]], dpl[i])

    def c_act(i):
        blk = actp.at[c, p1 if i == 2 else p0]
        return remote(blk, blk, s_act.at[i], r_act.at[i], d1 if i == 0 else d2)

    def c_pre(i):
        blk = pre.at[c, p1 if i == 2 else p0]
        return remote(blk, blk, s_pre.at[i], r_pre.at[i], d1 if i == 0 else d2)

    def c_actc(i):
        p = (p0, p1, p2, p3)[i]
        return remote(actp.at[c, p], actp.at[c, p], s_actc.at[i], r_actc.at[i], dsib)

    def c_prec(i):
        p = (p0, p1, p2, p3)[i]
        return remote(pre.at[c, p], pre.at[c, p], s_prec.at[i], r_prec.at[i], dsib)

    def c_sib():
        return remote(part, sibr, s_sib, r_sib, dsib)

    def c_pl(i):
        return remote(sums.at[i], plr.at[i], s_pl.at[i], r_pl.at[i], d2 if i == 1 else d1)

    def chain(at, s, r, sc=None, rc=None):
        def hop(h, d, send):
            block = z - (h - 1) if d == 0 else z + (h - 1)
            if not send:
                block = z - h if d == 0 else z + h
            return remote(at(block), at(block), s.at[d, h - 1], r.at[d, h - 1],
                          (p0 * 2 + c, z + 1 if d == 0 else z - 1))

        def may(h, d, send):
            if send:
                return (z < 3) & (z >= h - 1) if d == 0 else (z > 0) & (z <= 4 - h)
            return z >= h if d == 0 else z <= 3 - h

        def across(h, d):
            block = z - h if d == 0 else z + h
            return remote(at(block), at(block), sc.at[d, h - 1], rc.at[d, h - 1], dsib)

        def over():
            return remote(at(z), at(z), sc.at[2, 0], rc.at[2, 0], dsib)

        def send(h):
            for d in range(2):
                @pl.when(may(h, d, True))
                def _(d=d):
                    hop(h, d, True).start()
            if h == 1 and sc is not None:
                over().start()

        def recv(h):
            for d in range(2):
                @pl.when(may(h, d, False))
                def _(d=d):
                    hop(h, d, False).wait_recv()
                    if sc is not None:
                        across(h, d).start()

        def finish():
            over().wait_recv()
            for h in (1, 2, 3):
                for d in range(2):
                    @pl.when(may(h, d, False))
                    def _(d=d, h=h):
                        across(h, d).wait_recv()

        def sent():
            if sc is not None:
                over().wait_send()
            for h in (1, 2, 3):
                for d in range(2):
                    @pl.when(may(h, d, True))
                    def _(d=d, h=h):
                        hop(h, d, True).wait_send()
                    if sc is not None:
                        @pl.when(may(h, d, False))
                        def _(d=d, h=h):
                            across(h, d).wait_send()
        return send, recv, finish, sent

    x_send, x_recv, x_finish, x_sent = chain(lambda b: xall.at[c, b], s_x, r_x, s_xc, r_xc)
    y_send, y_recv, y_finish, y_sent = chain(lambda b: dyall.at[c, b], s_y, r_y, s_yc, r_yc)
    q_send, q_recv, _, q_sent = chain(
        lambda b: qkvw.at[pl.ds(pl.multiple_of(b * 384, 384), 384)], s_qkv, r_qkv)

    opart, osib, osum = part, sibr, sums

    def copy1(h, b):
        return remote(gw.at[slot(1, b), h], recv1.at[h, b], s1.at[h, b], r1.at[h, b], d1)
    g_c = remote(gpart, gsib, s_gc, r_gc, dsib)
    o_c = remote(opart, osib, s_oc, r_oc, dsib)

    def weights_a(k):
        if k:
            c_wz(k).wait_recv()
        c_wp(k, 0).start()

    def weights_b(k):
        c_wp(k, 0).wait_recv()
        c_wp(k, 1).start()
        c_wp(k, 2).start()

    for k in (1, 2, 3):
        c_small(k).start()
    local = [pltpu.make_async_copy(small, smalls.at[z], sl.at[0]),
             pltpu.make_async_copy(dy, dyall.at[c, z], sl.at[3])]

    def window(off, width, at, n):
        src = qkv.at[:, pl.ds(pl.multiple_of(off, 128), width)]
        return pltpu.make_async_copy(src, qwin.at[:, pl.ds(at, width)], sl.at[n])
    mine = p0 * 96
    windows = [window(384 * p0 + 128 * c, 256, 0, 1), window(1536 + 128 * p0, 128, 256, 2),
               window(2048 + 128 * p0, 128, 384, 5)]
    pieces = [pltpu.make_async_copy(
        ref.at[pl.ds(pl.multiple_of(mine, 96), 96), :, pl.ds(pl.multiple_of(off, half), half)],
        wst.at[:, :, pl.ds(i * half, half)], sl.at[6 + i])
        for i, (ref, off) in enumerate(((w_gu, c * half), (w_gu, HID + c * half), (w_dn, c * half)))]
    for one in local + windows + pieces:
        one.start()
    own_proj = pltpu.make_async_copy(proj.at[pl.ds(pl.multiple_of(c * 192, 192), 192)], projw, sl.at[4])

    @pl.when(z == p0)
    def _():
        own_proj.start()
    for one in windows:
        one.wait()
    cols = qwin[...].astype(F32)
    own_rows = pl.ds(pl.multiple_of(z * 384, 384), 384)
    for at, lo, width in ((0, 0, 256), (192, 256, 128), (256, 384, 128)):
        part_ = cols[:, lo : lo + width]
        part_ = jnp.where(c == 0, part_, pltpu.roll(part_, width - 64, 1)).astype(BF)
        qkvw[own_rows, at : at + (192 if at == 0 else 64)] = part_[:, : 192 if at == 0 else 64]

    tok_f = tok[...].astype(F32)
    inv1 = lax.rsqrt(jnp.mean(tok_f * tok_f, axis=1, keepdims=True) + EPS)
    for k in (1, 2, 3):
        c_small(k).wait_recv()
    q_send(1)
    for k in (1, 2, 3):
        c_pz(k).start()
    local[0].wait()
    gain1 = jnp.concatenate([smalls[i, 0:1, :] for i in range(4)], axis=1).astype(F32)
    actp[c, p0] = (tok_f * inv1 * gain1).astype(BF)
    pre[c, p0] = prefix[...]
    for i in range(2):
        c_act(i).start()
        c_pre(i).start()
    c_actc(0).start()
    c_prec(0).start()
    chosen_f = jnp.zeros((128, 128), F32)
    rank_of = jnp.zeros((128, 128), F32)
    lane_e = lax.broadcasted_iota(jnp.int32, (128, 128), 1)
    for k in range(8):
        hit = ids[:, k : k + 1] == lane_e
        chosen_f = jnp.where(hit, 1.0, chosen_f)
        rank_of = jnp.where(hit, prio[:, k : k + 1].astype(F32), rank_of)
    rank_of = jnp.where(chosen_f > 0.0, rank_of, 65536.0)
    rank_t = rank_of.T
    slots = jnp.zeros((128, 128), F32)
    for e in range(EXPERTS):
        before = jnp.sum((rank_t[e : e + 1, :] < rank_of[:, e : e + 1]).astype(F32), axis=1, keepdims=True)
        slots = jnp.where(lane_e == e, before, slots)
    kept_f = jnp.where(slots < CAP, chosen_f, 0.0)
    kept[...] = kept_f[:, :EXPERTS]
    q_recv(1)
    q_send(2)

    for one in pieces:
        one.wait()

    def expert_rows(l, _):
        wcol[...] = wst[:, :, pl.ds(pl.multiple_of(l * 128, 128), 128)].astype(F32).reshape(1536, 128)
        for e in range(EXPERTS):
            wpiece[e // 4, e % 4, :, pl.ds(pl.multiple_of(l * 128, 128), 128)] = (
                wcol[pl.ds(e, 96, stride=EXPERTS), :].astype(BF))
        return 0
    lax.fori_loop(0, 6, expert_rows, 0)
    own_piece = pltpu.make_async_copy(wpiece.at[z], wbuf.at[:, rows(z, p0)], sl.at[30])
    own_piece.start()
    weights_a(0)
    q_recv(2)
    q_send(3)
    for i in range(3):
        c_act(i).wait_recv()
        c_pre(i).wait_recv()
        if i == 0:
            c_act(2).start()
            c_pre(2).start()
        c_actc(i + 1).start()
        c_prec(i + 1).start()
    q_recv(3)
    for k in (1, 3, 2):
        c_wz(k).start()
    local[1].wait()

    row = lax.broadcasted_iota(jnp.int32, (128, 128), 0)
    col = lax.broadcasted_iota(jnp.int32, (128, 128), 1)
    causal = col <= row
    col_f = col.astype(F32)

    def attention(cc):
        pr[...] = jnp.dot(actp[cc].reshape(512, 1536), qkvw[...], preferred_element_type=F32).reshape(4, 128, 320)

        def one(i, _):
            lo = turn(pr[i, :, 0:128], cos_t[...], sin_t[...]).astype(BF)
            hi = turn(pr[i, :, 128:256], cos_t[...], sin_t[...]).astype(BF)
            qs[cc, i, 0:128] = lo[:, 0:64]
            qs[cc, i, 128:256] = lo[:, 64:128]
            qs[cc, i, 256:384] = hi[:, 0:64]
            ks[cc, i] = hi[:, 64:128]
            vs[cc, i] = pr[i, :, 256:320].astype(BF)
            sc = lax.dot_general(qs[cc, i], ks[cc, i], (((1,), (1,)), ((), ())), preferred_element_type=F32)
            allowed = causal | (col_f < pre[cc, i, 0:1, :])
            sc = jnp.where(allowed[None], sc.reshape(3, 128, 128) * (64 ** -0.5), -1e30)
            ex = jnp.exp(sc - jnp.max(sc, axis=-1, keepdims=True))
            pb = (ex / jnp.sum(ex, axis=-1, keepdims=True)).reshape(384, 128)
            probs[cc, i] = pb
            at = jnp.dot(pb.astype(BF), vs[cc, i], preferred_element_type=F32).astype(BF)
            for h in range(3):
                att[cc, i, :, h * 64 : (h + 1) * 64] = at[h * 128 : (h + 1) * 128]
            return 0
        lax.fori_loop(0, 4, one, 0)

    attention(c)
    for i in range(4):
        c_actc(i).wait_recv()
        c_prec(i).wait_recv()
    attention(1 - c)
    for k in (1, 2, 3):
        c_pz(k).wait_recv()
        owner = zf[k]

        @pl.when(owner != p0)
        def _(k=k, owner=owner):
            c_pq(k, owner).start()

        @pl.when(owner == p0)
        def _(k=k):
            projw[quarter(p0)] = projq[k - 1]

    @pl.when(z == p0)
    def _():
        own_proj.wait()

    @pl.when(z != p0)
    def _():
        for i in range(3):
            c_pq_in(i).wait_recv()

    def to_sib(i, _):
        part[i] = jnp.dot(att[1 - c, i], projw[...], preferred_element_type=F32).astype(BF)
        return 0
    lax.fori_loop(0, 4, to_sib, 0)
    c_sib().start()
    c_sib().wait_recv()
    def mixed(p):
        return jnp.dot(att[c, p], projw[...], preferred_element_type=F32) + sibr[p].astype(F32)

    for i in (2, 0):
        sums[i] = mixed(peers[i]).astype(BF)
        c_pl(i).start()
    to_second = mixed(p2)
    residual = tok_f + mixed(p0)
    c_pl(2).wait_recv()
    sums[1] = (to_second + plr[2].astype(F32)).astype(BF)
    c_pl(1).start()
    for i in range(2):
        c_pl(i).wait_recv()
        residual = residual + plr[i].astype(F32)
    res[...] = residual
    inv2 = lax.rsqrt(jnp.mean(residual * residual, axis=1, keepdims=True) + EPS)
    gain2 = jnp.concatenate([smalls[i, 1:2, :] for i in range(4)], axis=1).astype(F32)
    act2 = (residual * inv2 * gain2).astype(BF)
    router = jnp.concatenate([smalls[i, 16:32, :] for i in range(4)], axis=1)
    logits = lax.dot_general(act2, router, (((1,), (1,)), ((), ())), preferred_element_type=F32)
    chosen = chosen_f[:, :EXPERTS] > 0.0
    top = jnp.max(jnp.where(chosen, logits, -1e30), axis=1, keepdims=True)
    ge = jnp.where(chosen, jnp.exp(jnp.where(chosen, logits - top, 0.0)), 0.0)
    gt = ge / jnp.sum(ge, axis=1, keepdims=True)
    gates[...] = gt
    wide_gates = jnp.concatenate([gt * kept[...], jnp.zeros((128, 112), F32)], axis=1)
    gate_hi = wide_gates.astype(BF)
    xall[c, z, :, :1536] = act2
    xall[c, z, :, 1536:1664] = gate_hi
    xall[c, z, :, 1664:] = (wide_gates - gate_hi.astype(F32)).astype(BF)
    x_send(1)
    weights_b(0)
    weights_a(1)
    weights_a(3)
    weights_b(1)
    x_recv(1)
    x_send(2)
    weights_b(3)
    weights_a(2)
    x_recv(2)
    x_send(3)
    y_send(1)
    weights_b(2)
    x_recv(3)
    y_recv(1)
    y_send(2)
    y_recv(2)
    y_send(3)
    y_recv(3)
    own_piece.wait()
    for k in range(4):
        c_wp(k, 1).wait_recv()
        c_wp(k, 2).wait_recv()
    x_finish()
    y_finish()

    lane = lax.broadcasted_iota(jnp.int32, (512, 128), 1)
    ggp[...] = jnp.zeros_like(ggp)

    def expert(n, _):
        j, t = n // 2, lax.rem(n, 2)
        gu = jnp.dot(xall[t, :, :, :1536].reshape(512, 1536), wbuf[j, :, : 2 * half], preferred_element_type=F32)
        bk = jnp.dot(dyall[t].reshape(512, 1536), wbuf[j, :, 2 * half :], preferred_element_type=F32)
        mine = lane == z * 4 + j
        both = (xall[t, :, :, 1536:1664].astype(F32) + xall[t, :, :, 1664:].astype(F32)).reshape(512, 128)
        w = jnp.sum(jnp.where(mine, both, 0.0), axis=1, keepdims=True)
        g, u = gu[:, :half], gu[:, half:]
        sg = 1.0 / (1.0 + jnp.exp(-g))
        silu = g * sg
        hid = silu * u
        hw[j, pl.ds(pl.multiple_of(t * 512, 512), 512)] = (hid * w).astype(BF)
        ggp[t] = ggp[t] + jnp.where(mine, jnp.sum(bk * hid, axis=1, keepdims=True), 0.0).reshape(4, 128, 128)
        gh = bk * w
        at = pl.ds(pl.multiple_of(t * 512, 512), 512)
        ggu[j, at, :half] = (gh * u * sg * (1.0 + g * (1.0 - sg))).astype(BF)
        ggu[j, at, half:] = (gh * silu).astype(BF)
        return 0
    lax.fori_loop(0, 8, expert, 0)

    gradient_rows(0, xall, dyall, ggu, hw, gw)
    for h in range(2):
        for b in range(2):
            copy1(h, b).start()
    saves = []

    def save(src, dst):
        one = pltpu.make_async_copy(src, dst, sl.at[9 + len(saves)])
        one.start()
        saves.append(one)
    for src, dst in ((xall, o_x), (dyall, o_dy), (ggu, o_ggu), (hw, o_hw), (actp, o_act), (qs, o_q), (ks, o_k),
                     (vs, o_v), (probs, o_probs), (att, o_att), (qkvw, o_qkvw), (projw, o_projw),
                     (smalls, o_small), (res, o_res), (gates, o_gates), (kept, o_kept)):
        save(src, dst)

    def block(grad, t, n):
        at = pl.ds(pl.multiple_of(t * 512, 512), 512)
        lanes = pl.ds(pl.multiple_of(n * 256, 256), 256)
        acc = jnp.zeros((512, 256), F32)
        for j in range(4):
            a = ggu[j, at] if grad else hw[j, at]
            b = wbuf[j, lanes, : 2 * half] if grad else wbuf[j, lanes, 2 * half :]
            acc = acc + lax.dot_general(a, b, (((1,), (1,)), ((), ())), preferred_element_type=F32)
        return acc.reshape(4, 128, 256), lanes

    def partial(grad, buf):
        def one(n, _):
            v, lanes = block(grad, 1 - c, n)
            buf[:, :, lanes] = v.astype(BF)
            return 0
        lax.fori_loop(0, 6, one, 0)

    def own(grad, sib, dst):
        def one(n, _):
            v, lanes = block(grad, c, n)
            dst[:, :, lanes] = (v + sib[:, :, lanes].astype(F32)).astype(BF)
            return 0
        lax.fori_loop(0, 6, one, 0)

    def put_gate_grads(dst, v):
        hi = v.astype(BF)
        dst[:, :, 1536:1664] = hi
        dst[:, :, 1664:] = (v - hi.astype(F32)).astype(BF)

    def gate_grads(v):
        return v[..., 1536:1664].astype(F32) + v[..., 1664:].astype(F32)

    c_sib().wait_send()
    for i in range(3):
        c_pl(i).wait_send()
    put_gate_grads(gpart, ggp[1 - c])
    partial(True, gpart)
    g_c.start()
    partial(False, opart)
    o_c.start()
    g_c.wait_recv()
    put_gate_grads(gsum, ggp[c] + gate_grads(gsib))
    own(True, gsib, gsum)
    save(gsum, o_gsum)
    o_c.wait_recv()
    own(False, osib, osum)
    save(osum, o_osum)
    save(gw, o_gw)
    for h in range(2):
        for b in range(2):
            copy1(h, b).wait()
    save(recv1, o_r1)

    for k in (1, 2, 3):
        for one in (c_small(k), c_pz(k), c_wz(k)):
            one.wait_send()

        @pl.when(zf[k] != p0)
        def _(k=k):
            c_pq(k, zf[k]).wait_send()
    for k in range(4):
        for i in range(3):
            c_wp(k, i).wait_send()
        for one in (c_actc(k), c_prec(k)):
            one.wait_send()
    for i in range(3):
        for one in (c_act(i), c_pre(i)):
            one.wait_send()
    for one in (g_c, o_c):
        one.wait_send()
    x_sent()
    y_sent()
    q_sent()
    for one in saves:
        one.wait()


def front(*args):
    sem, vm = pltpu.SemaphoreType.DMA, pltpu.VMEM
    out = lambda shape, kind=BF: jax.ShapeDtypeStruct(shape, kind)
    outs = (
        out((2, 4, 128, 1792)), out((2, 4, 128, 1536)), out((4, 1024, 512)), out((4, 1024, 256)),
        out((2, 4, 128, 1536)), out((2, 4, 384, 64)), out((2, 4, 128, 64)), out((2, 4, 128, 64)),
        out((2, 4, 384, 128), F32), out((2, 4, 128, 192)), out((1536, 320)), out((192, 1536)),
        out((4, 32, 384)), out((128, 1536), F32), out((128, 16), F32), out((128, 16), F32), out((4, 128, 1792)),
        out((4, 128, 1536)), out((4, 2, 4, 4, 16, 768)), out((2, 2, 4, 4, 16, 768)),
    )
    block, quad = vm((2, 4, 128, 1536), BF), vm((4, 128, 1536), BF)
    three = vm((3, 128, 1536), BF)
    quad_g = vm((4, 128, 1792), BF)
    scratch = [
        vm((4, 32, 384), BF), vm((1536, 320), BF), vm((192, 1536), BF), vm((3, 48, 1536), BF),
        block, vm((2, 4, 8, 128), F32),
        vm((4, 128, 320), F32), vm((2, 4, 384, 64), BF), vm((2, 4, 128, 64), BF), vm((2, 4, 128, 64), BF),
        vm((2, 4, 384, 128), F32), vm((2, 4, 128, 192), BF), quad, quad, quad, three,
        vm((2, 4, 128, 1792), BF), block, vm((4, 1536, 768), BF), vm((4, 1024, 512), BF),
        vm((4, 1024, 256), BF), quad_g, vm((2, 4, 128, 128), F32), quad_g,
        quad_g, vm((128, 1536), F32), vm((128, 16), F32), vm((128, 16), F32),
        vm((384, 512), BF), vm((96, 16, 768), BF), vm((1536, 128), F32), vm((4, 4, 96, 768), BF),
        vm((4, 2, 4, 4, 16, 768), BF), vm((2, 2, 4, 4, 16, 768), BF),
    ]
    n3, n4, one = sem((3,)), sem((4,)), sem(())
    hops = [sem((2, 3)), sem((2, 3)), sem((3, 3)), sem((3, 3))]
    sems = [
        n3, n3, sem((2, 3)), sem((2, 3)), n3, n3, n3, n4, n3, n3, sem((4, 3)), sem((4, 3)),
        n3, n3, n3, n3, n4, n4, n4, n4, one, one, n3, n3,
        *hops, *hops, one, one, one, one, sem((2, 2)), sem((2, 2)), sem((31,)),
    ]
    vmem, any_ = pl.BlockSpec(memory_space=pltpu.VMEM), pl.BlockSpec(memory_space=pl.ANY)
    return pl.pallas_call(
        front_kernel,
        out_shape=outs,
        in_specs=[vmem, any_, any_, any_, any_, any_, any_, vmem, vmem, vmem, vmem, vmem],
        out_specs=[any_] * len(outs),
        scratch_shapes=scratch + sems,
        compiler_params=pltpu.CompilerParams(
            collective_id=1, has_side_effects=True, vmem_limit_bytes=62 * 1024 * 1024),
        name="front",
    )(*args)


def back_kernel(i_x, i_dy, i_ggu, i_hw, i_act, i_q, i_k, i_v, i_probs, i_att, i_qkvw, i_projw, i_small,
                i_res, i_gates, i_kept, i_gsum, i_osum, i_gw, i_r1, tok, cos_t, sin_t,
                o_e, o_gtok, o_qg, o_pg, o_terms, o_op,
                xb, dyb, ggu, hw, qs, ks, vs, probs, att, qkvw, projw, smalls, res, gates, kept, gown, grecv,
                gw, recv1, send2, recv2, zs, zr, ib, agv,
                gres, gresf, gproj, sibr, plr, qgp, qz, qgo, pgp, pgr, pq2, pgo, terms, tz, tsib, tpl, tout, gtok,
                s1, r1, s2, r2, sz, rz, sa, ra, ss, rs, la,
                s_g, r_g, s_gr, r_gr, s_grc, r_grc, s_sib, r_sib, s_pl, r_pl, s_qz, r_qz, s_qo, r_qo,
                s_qoc, r_qoc, s_p1, r_p1, s_p2, r_p2, s_po, r_po, s_poc, r_poc, s_tz, r_tz, s_ts, r_ts,
                s_tp, r_tp, s_o, r_o, ld, sv):
    y, x, c, z = place()
    half = HID // 2
    wide = 3 * half
    nq = 6

    def slot(a, b):
        return flip(y, a * c + b * (1 - c)) * 2 + flip(x, a * (1 - c) + b * c)

    p0, p1, p2, p3 = slot(0, 0), slot(1, 0), slot(0, 1), slot(1, 1)
    peers = (p1, p2, p3)
    d1, d2, dsib = (p1 * 2 + c, z), (p2 * 2 + c, z), (p0 * 2 + 1 - c, z)
    dpl = [(p * 2 + c, z) for p in peers]
    zk = [lax.rem(z + k, 4) for k in range(4)]
    dz = [(p0 * 2 + c, zz) for zz in zk]

    loads = {}

    def load(name, src, dst):
        loads[name] = pltpu.make_async_copy(src, dst, ld.at[len(loads)])
        loads[name].start()
    load("gw", i_gw, gw.at[0])
    load("r1", i_r1, recv1.at[pl.ds(0, 2)])
    load("x", i_x.at[:, :, :, pl.ds(0, 1536)], xb)
    load("ggu", i_ggu, ggu)
    load("dy", i_dy, dyb)
    load("hw", i_hw, hw)
    load("gown", i_gsum.at[z], gown)
    for name, src, dst in (("res", i_res, res), ("gates", i_gates, gates), ("kept", i_kept, kept),
                           ("small", i_small, smalls),
                           ("projw", i_projw, projw), ("probs", i_probs, probs), ("q", i_q, qs), ("k", i_k, ks),
                           ("v", i_v, vs), ("att", i_att, att), ("qkvw", i_qkvw, qkvw)):
        load(name, src, dst)

    barrier = pltpu.get_barrier_semaphore()
    for to in dpl + dz[1:] + [dsib]:
        pl.semaphore_signal(barrier, 1, device_id=to, device_id_type=MESH)
    pl.semaphore_wait(barrier, 7)

    def remote(src, dst, s, r, to):
        return pltpu.make_async_remote_copy(src, dst, s, r, device_id=to, device_id_type=MESH)

    def copy1(q, b):
        return remote(gw.at[q // 2, slot(1, b), lax.rem(q, 2)], recv1.at[q, b], s1.at[q, b], r1.at[q, b], d1)

    def copy2(q):
        return remote(send2.at[lax.rem(q, 2)], recv2.at[q], s2.at[q], r2.at[q], d2)

    def copyz(q, k):
        return remote(zs.at[lax.rem(q, 2), zk[k]], zr.at[q, z], sz.at[q, k - 1], rz.at[q, k - 1], dz[k])

    def rows(q, p):
        return pl.ds(pl.multiple_of(((q // 2) * 8 + p * 2 + lax.rem(q, 2)) * 256, 256), 256)

    def copya(q, i):
        p, who = ((p0, d1), (p0, d2), (p1, d2))[i]
        src = agv.at[lax.rem(q, 2)] if i < 2 else o_e.at[c, rows(q, p)]
        return remote(src, o_e.at[c, rows(q, p)], sa.at[q, i], ra.at[q, i], who)

    def copys(q, i):
        p = (p0, p1, p2, p3)[i]
        src = agv.at[lax.rem(q, 2)] if i == 0 else o_e.at[c, rows(q, p)]
        return remote(src, o_e.at[c, rows(q, p)], ss.at[q, i], rs.at[q, i], dsib)

    def keep(q):
        return pltpu.make_async_copy(agv.at[lax.rem(q, 2)], o_e.at[c, rows(q, p0)], la.at[q])

    def c_g(k):
        return remote(i_gsum.at[zk[k]], grecv.at[k - 1], s_g.at[k - 1], r_g.at[k - 1], dz[k])

    def c_o(k):
        return remote(i_osum.at[zk[k]], o_op.at[k], s_o.at[k - 1], r_o.at[k - 1], dz[k])

    def c_gr(i):
        blk = gres.at[c, p1 if i == 2 else p0]
        return remote(blk, blk, s_gr.at[i], r_gr.at[i], d1 if i == 0 else d2)

    def c_grc(i):
        p = (p0, p1, p2, p3)[i]
        return remote(gres.at[c, p], gres.at[c, p], s_grc.at[i], r_grc.at[i], dsib)

    def c_sib():
        return remote(dyb.at[0], sibr, s_sib, r_sib, dsib)

    def c_pl(i):
        return remote(dyb.at[1, i], plr.at[i], s_pl.at[i], r_pl.at[i], d2 if i == 1 else d1)

    def c_qz(k):
        return remote(qgp.at[zk[k]], qz.at[k - 1], s_qz.at[k - 1], r_qz.at[k - 1], dz[k])

    def c_qo(i):
        dst = o_qg.at[(p1 if i == 2 else p0) * 2 + c]
        return remote(dst if i == 2 else qgo, dst, s_qo.at[i], r_qo.at[i], d1 if i == 0 else d2)

    def c_qoc(i):
        r = (p0, p1, p2, p3)[i] * 2 + c
        return remote(qgo if i == 0 else o_qg.at[r], o_qg.at[r], s_qoc.at[i], r_qoc.at[i], dsib)

    def c_p1(i):
        return remote(pgp.at[peers[i]], pgr.at[p0], s_p1.at[i], r_p1.at[i], dpl[i])

    def c_p2(k):
        return remote(pgr.at[zk[k]], pq2.at[k - 1], s_p2.at[k - 1], r_p2.at[k - 1], dz[k])

    def c_po(i):
        dst = o_pg.at[c, p1 if i == 2 else p0]
        return remote(dst if i == 2 else pgo, dst, s_po.at[i], r_po.at[i], d1 if i == 0 else d2)

    def c_poc(i):
        p = (p0, p1, p2, p3)[i]
        return remote(pgo if i == 0 else o_pg.at[c, p], o_pg.at[c, p], s_poc.at[i], r_poc.at[i], dsib)

    def lanes_of(zz):
        return pl.ds(pl.multiple_of(zz * 384, 384), 384)

    def c_tz(k):
        return remote(terms.at[:, lanes_of(zk[k])], tz.at[k], s_tz.at[k - 1], r_tz.at[k - 1], dz[k])

    def c_ts():
        return remote(tz.at[0], tsib, s_ts, r_ts, dsib)

    def c_tp(i):
        return remote(tpl.at[p0], tpl.at[p0], s_tp.at[i], r_tp.at[i], dpl[i])

    saves = [pltpu.make_async_copy(gtok, o_gtok, sv.at[0]),
             pltpu.make_async_copy(qgo, o_qg.at[p0 * 2 + c], sv.at[1]),
             pltpu.make_async_copy(pgo, o_pg.at[c, p0], sv.at[2]),
             pltpu.make_async_copy(tout, o_terms, sv.at[3])]
    own_out = pltpu.make_async_copy(i_osum.at[z], o_op.at[0], sv.at[5])
    own_out.start()
    act_load = pltpu.make_async_copy(i_act, xb, sv.at[4])

    for k in (1, 2, 3):
        c_g(k).start()
    loads["gw"].wait()
    loads["r1"].wait()
    loads["x"].wait()
    loads["ggu"].wait()
    loads["dy"].wait()
    loads["hw"].wait()

    def stage1(q):
        @pl.when(lax.rem(q, 2) == 0)
        def _():
            gradient_rows(q // 2, xb, dyb, ggu, hw, gw.at[q // 2])
        for b in range(2):
            copy1(q, b).start()

    def stage2(q):
        @pl.when(q >= 2)
        def _():
            for b in range(2):
                copy1(q, b).wait_recv()

        def one(zz, _):
            send2[lax.rem(q, 2), zz] = (gw[q // 2, p2, lax.rem(q, 2), zz].astype(F32)
                                        + recv1[q, 1, zz].astype(F32)).astype(BF)
            return 0
        lax.fori_loop(0, 4, one, 0)
        copy2(q).start()

    def stage3(q):
        copy2(q).wait()

        def one(zz, _):
            zs[lax.rem(q, 2), zz] = (gw[q // 2, p0, lax.rem(q, 2), zz].astype(F32) + recv1[q, 0, zz].astype(F32)
                                     + recv2[q, zz].astype(F32)).astype(BF)
            return 0
        lax.fori_loop(0, 4, one, 0)
        for k in range(1, 4):
            copyz(q, k).start()
        zr[q, z] = zs[lax.rem(q, 2), z]

    def stage4(q):
        for k in range(1, 4):
            copyz(q, k).wait()

        @pl.when(q >= 2)
        def _():
            copya(q - 2, 0).wait_send()
            copya(q - 2, 1).wait_send()
            copys(q - 2, 0).wait_send()
            keep(q - 2).wait()
        for zz in range(4):
            for j in range(4):
                for l in range(wide // 128):
                    ib[l, pl.ds(zz * 4 + j, 16, stride=EXPERTS), :] = (
                        zr[q, zz, j, :, l * 128 : (l + 1) * 128].astype(F32))
        for l in range(wide // 128):
            agv[lax.rem(q, 2), :, l * 128 : (l + 1) * 128] = ib[l].astype(BF)
        copya(q, 0).start()
        copys(q, 0).start()
        keep(q).start()

    def stage5(q):
        copya(q, 0).wait_recv()
        copya(q, 1).start()
        copya(q, 2).start()
        copys(q, 1).start()

    def stage6(q):
        copya(q, 1).wait_recv()
        copya(q, 2).wait_recv()
        copys(q, 2).start()
        copys(q, 3).start()

    def stage7(q):
        for i in range(4):
            copys(q, i).wait_recv()

    def norm_two():
        r = res[...]
        inv = lax.rsqrt(jnp.mean(r * r, axis=1, keepdims=True) + EPS)
        return inv, r * inv

    def norm_one():
        t = tok[...].astype(F32)
        inv = lax.rsqrt(jnp.mean(t * t, axis=1, keepdims=True) + EPS)
        return inv, t * inv

    def gain(row):
        return jnp.concatenate([smalls[i, row : row + 1, :] for i in range(4)], axis=1).astype(F32)

    def event_residual():
        for name in ("gown", "res", "gates", "kept", "small"):
            loads[name].wait()
        for k in (1, 2, 3):
            c_g(k).wait_recv()
        tail = slice(1536, 1664), slice(1664, 1792)

        def gate_part(v):
            return (v[:, tail[0]].astype(F32) + v[:, tail[1]].astype(F32))[:, :EXPERTS]
        gg = (gate_part(gown[...]) + gate_part(grecv[0]) + gate_part(grecv[1]) + gate_part(grecv[2])) * kept[...]
        gt = gates[...]
        gl = (gt * (gg - jnp.sum(gt * gg, axis=1, keepdims=True))).astype(BF)
        router_t = jnp.concatenate([smalls[i, 16:32, :] for i in range(4)], axis=1)
        ga = jnp.dot(gl, router_t, preferred_element_type=F32)
        ga = ga + gown[:, :1536].astype(F32)
        for k in range(3):
            ga = ga + grecv[k, :, :1536].astype(F32)
        inv, normed = norm_two()
        terms[8:24, :] = lax.dot_general(gl, xb[c, z], (((0,), (0,)), ((), ())), preferred_element_type=F32)
        terms[1:2, :] = jnp.sum(ga * normed, axis=0, keepdims=True)
        scaled = ga * gain(1)
        gr = dyb[c, z].astype(F32) + inv * (scaled - normed * jnp.mean(scaled * normed, axis=1, keepdims=True))
        gresf[...] = gr
        gres[c, p0] = gr.astype(BF)
        for i in range(2):
            c_gr(i).start()
        c_grc(0).start()

    def event_share():
        for i in range(3):
            c_gr(i).wait_recv()
            if i == 0:
                c_gr(2).start()
            c_grc(i + 1).start()
        act_load.start()

    scale = 64 ** -0.5

    def event_attention():
        for name in ("projw", "probs", "q", "k", "v", "att", "qkvw"):
            loads[name].wait()
        for i in range(4):
            c_grc(i).wait_recv()

        def one(n, _):
            cc, i = n // 4, lax.rem(n, 4)
            gb = lax.dot_general(gres[cc, i], projw[...], (((1,), (1,)), ((), ())),
                                 preferred_element_type=F32).astype(BF)
            ga = jnp.concatenate([gb[:, h * 64 : (h + 1) * 64] for h in range(3)], axis=0)
            pb = probs[cc, i]
            gv = lax.dot_general(pb.astype(BF), ga, (((0,), (0,)), ((), ())), preferred_element_type=F32)
            gp = lax.dot_general(ga, vs[cc, i], (((1,), (1,)), ((), ())), preferred_element_type=F32)
            gs = (pb * (gp - jnp.sum(pb * gp, axis=-1, keepdims=True))).astype(BF)
            gq = jnp.dot(gs, ks[cc, i], preferred_element_type=F32) * scale
            gk = lax.dot_general(gs, qs[cc, i], (((0,), (0,)), ((), ())), preferred_element_type=F32) * scale
            lo = jnp.concatenate([gq[0:128], gq[128:256]], axis=1)
            hi = jnp.concatenate([gq[256:384], gk], axis=1)
            gproj[cc, i, :, 0:128] = turn(lo, cos_t[...], -sin_t[...]).astype(BF)
            gproj[cc, i, :, 128:256] = turn(hi, cos_t[...], -sin_t[...]).astype(BF)
            gproj[cc, i, :, 256:320] = gv.astype(BF)
            return 0
        lax.fori_loop(0, 8, one, 0)

        def to_sib(i, _):
            dyb[0, i] = lax.dot_general(gproj[1 - c, i], qkvw[...], (((1,), (1,)), ((), ())),
                                        preferred_element_type=F32).astype(BF)
            return 0
        lax.fori_loop(0, 4, to_sib, 0)
        c_sib().start()
        pg = lax.dot_general(att[...].reshape(1024, 192), gres[...].reshape(1024, 1536), (((0,), (0,)), ((), ())),
                             preferred_element_type=F32)
        pgp[...] = pg.astype(BF).reshape(4, 48, 1536)
        for i in range(3):
            c_p1(i).start()
        pgr[p0] = pgp[p0]

    def event_columns():
        act_load.wait()

        def one(zz, _):
            a = xb[:, :, :, lanes_of(zz)].reshape(1024, 384)
            qgp[zz] = lax.dot_general(a, gproj[...].reshape(1024, 320), (((0,), (0,)), ((), ())),
                                      preferred_element_type=F32).astype(BF)
            return 0
        lax.fori_loop(0, 4, one, 0)
        for k in (1, 2, 3):
            c_qz(k).start()
        c_sib().wait()

        def part(p):
            return lax.dot_general(gproj[c, p], qkvw[...], (((1,), (1,)), ((), ())),
                                   preferred_element_type=F32) + sibr[p].astype(F32)
        for i in (2, 0):
            dyb[1, i] = part(peers[i]).astype(BF)
            c_pl(i).start()
        dyb[1, 1] = part(p2).astype(BF)
        gtok[...] = part(p0)
        for i in range(3):
            c_p1(i).wait_recv()
        for k in (1, 2, 3):
            c_p2(k).start()

    def event_second():
        c_pl(2).wait_recv()
        dyb[1, 1] = (dyb[1, 1].astype(F32) + plr[2].astype(F32)).astype(BF)
        c_pl(1).start()

    def event_tokens():
        ga = gtok[...]
        for i in range(2):
            c_pl(i).wait_recv()
            ga = ga + plr[i].astype(F32)
        inv, normed = norm_one()
        terms[0:1, :] = jnp.sum(ga * normed, axis=0, keepdims=True)
        scaled = ga * gain(0)
        gtok[...] = gresf[...] + inv * (scaled - normed * jnp.mean(scaled * normed, axis=1, keepdims=True))
        saves[0].start()
        for k in (1, 2, 3):
            c_tz(k).start()
        for k in (1, 2, 3):
            c_qz(k).wait_recv()
        qgo[...] = (qgp[z].astype(F32) + qz[0].astype(F32) + qz[1].astype(F32) + qz[2].astype(F32)).astype(BF)
        for i in range(2):
            c_qo(i).start()
        c_qoc(0).start()
        saves[1].start()
        for k in (1, 2, 3):
            c_p2(k).wait_recv()
        pgo[...] = (pgr[z].astype(F32) + pq2[0].astype(F32) + pq2[1].astype(F32) + pq2[2].astype(F32)).astype(BF)
        for i in range(2):
            c_po(i).start()
        c_poc(0).start()
        saves[2].start()
        for k in (1, 2, 3):
            c_o(k).start()

    def event_terms():
        for k in (1, 2, 3):
            c_tz(k).wait_recv()
        tz[0] = terms[:, lanes_of(z)] + tz[1] + tz[2] + tz[3]
        c_ts().start()
        for i in range(3):
            c_qo(i).wait_recv()
            if i == 0:
                c_qo(2).start()
            c_qoc(i + 1).start()
            c_po(i).wait_recv()
            if i == 0:
                c_po(2).start()
            c_poc(i + 1).start()

    def event_sums():
        c_ts().wait()
        tpl[p0] = tz[0] + tsib[...]
        for i in range(3):
            c_tp(i).start()

    def event_last():
        for i in range(3):
            c_tp(i).wait_recv()
        tout[...] = tpl[0] + tpl[1] + tpl[2] + tpl[3]
        saves[3].start()
        for i in range(4):
            c_qoc(i).wait_recv()
            c_poc(i).wait_recv()
        for k in (1, 2, 3):
            c_o(k).wait_recv()

    stages = (stage1, stage2, stage3, stage4, stage5, stage6, stage7)
    lead = 4
    for q in (2, 3):
        stage1(jnp.int32(q))
    events = {2: event_residual, 3: event_share, 4: event_attention, 5: event_columns, 6: event_second,
              7: event_tokens, 8: event_terms, 9: event_sums, 10: event_last}

    def step(t, _):
        for i, stage in enumerate(stages):
            q = t + lead if i == 0 else t + 1 - i

            @pl.when((q >= 0) & (q < nq))
            def _(stage=stage, q=q):
                stage(q)
        for at, event in events.items():
            @pl.when(t == at)
            def _(event=event):
                event()
        return 0

    lax.fori_loop(0, nq + len(stages) - 2, step, 0)

    def left(q, _):
        @pl.when(q >= 2)
        def _():
            for b in range(2):
                copy1(q, b).wait_send()
        for i in range(1, 4):
            copys(q, i).wait_send()
        copya(q, 2).wait_send()

        @pl.when(q >= nq - 2)
        def _():
            copya(q, 0).wait_send()
            copya(q, 1).wait_send()
            copys(q, 0).wait_send()
            keep(q).wait()
        return 0
    lax.fori_loop(0, nq, left, 0)
    for k in (1, 2, 3):
        for one in (c_g(k), c_o(k), c_qz(k), c_p2(k), c_tz(k)):
            one.wait_send()
    for i in range(3):
        for one in (c_gr(i), c_pl(i), c_qo(i), c_p1(i), c_po(i), c_tp(i)):
            one.wait_send()
    for i in range(4):
        for one in (c_grc(i), c_qoc(i), c_poc(i)):
            one.wait_send()
    for one in saves + [own_out]:
        one.wait()


def back(front_outs, tok, cos_t, sin_t):
    nq, wide = 6, 3 * HID // 2
    sem, vm = pltpu.SemaphoreType.DMA, pltpu.VMEM
    out = lambda shape, kind=BF: jax.ShapeDtypeStruct(shape, kind)
    piece = (4, 4, 16, wide)
    outs = (out((2, 6144, wide)), out((128, 1536), F32), out((8, 384, 320)), out((2, 4, 48, 1536)),
            out((24, 384), F32), out((4, 128, 1536)))
    block, quad, three = vm((2, 4, 128, 1536), BF), vm((4, 128, 1536), BF), vm((3, 128, 1536), BF)
    scratch = [
        block, block, vm((4, 1024, 512), BF), vm((4, 1024, 256), BF), vm((2, 4, 384, 64), BF),
        vm((2, 4, 128, 64), BF), vm((2, 4, 128, 64), BF), vm((2, 4, 384, 128), F32), vm((2, 4, 128, 192), BF),
        vm((1536, 320), BF), vm((192, 1536), BF), vm((4, 32, 384), BF), vm((128, 1536), F32), vm((128, 16), F32), vm((128, 16), F32),
        vm((128, 1792), BF), vm((3, 128, 1792), BF),
        vm((3, 4, 2) + piece, BF), vm((nq, 2) + piece, BF), vm((2,) + piece, BF), vm((nq,) + piece, BF),
        vm((2,) + piece, BF), vm((nq,) + piece, BF), vm((wide // 128, 256, 128), F32), vm((2, 256, wide), BF),
        block, vm((128, 1536), F32), vm((2, 4, 128, 320), BF), quad, three, vm((4, 384, 320), BF),
        vm((3, 384, 320), BF), vm((384, 320), BF), vm((4, 48, 1536), BF), vm((4, 48, 1536), BF),
        vm((3, 48, 1536), BF), vm((48, 1536), BF), vm((24, 1536), F32), vm((4, 24, 384), F32),
        vm((24, 384), F32), vm((4, 24, 384), F32), vm((24, 384), F32), vm((128, 1536), F32),
    ]
    n3, n4, one = sem((3,)), sem((4,)), sem(())
    sems = [
        sem((nq, 2)), sem((nq, 2)), sem((nq,)), sem((nq,)), sem((nq, 3)), sem((nq, 3)), sem((nq, 3)), sem((nq, 3)),
        sem((nq, 4)), sem((nq, 4)), sem((nq,)),
        n3, n3, n3, n3, n4, n4, one, one, n3, n3, n3, n3, n3, n3,
        n4, n4, n3, n3, n3, n3, n3, n3, n4, n4, n3, n3, one, one,
        n3, n3, n3, n3, sem((18,)), sem((6,)),
    ]
    vmem, any_ = pl.BlockSpec(memory_space=pltpu.VMEM), pl.BlockSpec(memory_space=pl.ANY)
    return pl.pallas_call(
        back_kernel,
        out_shape=outs,
        in_specs=[any_] * 20 + [vmem] * 3,
        out_specs=[any_] * len(outs),
        scratch_shapes=scratch + sems,
        compiler_params=pltpu.CompilerParams(
            collective_id=2, has_side_effects=True, vmem_limit_bytes=62 * 1024 * 1024),
        name="back",
    )(*front_outs, tok, cos_t, sin_t)


def finish_kernel(v, qkv, proj, res, parts, terms, gu, dn, g_qkv, g_proj, out, g_router):
    half = HID // 2
    for c in range(2):
        gu[:, c * half : (c + 1) * half] = v[c, :, :half].astype(F32)
        gu[:, HID + c * half : HID + (c + 1) * half] = v[c, :, half : 2 * half].astype(F32)
        dn[:, c * half : (c + 1) * half] = v[c, :, 2 * half :].astype(F32)
    heads = range(qkv.shape[0])
    g_qkv[...] = jnp.concatenate(
        [qkv[h, :, lo:hi].astype(F32) for lo, hi in ((0, 192), (192, 256), (256, 320)) for h in heads], axis=1)
    g_proj[...] = proj[...].astype(F32)

    @pl.when(pl.program_id(0) == 0)
    def _():
        total = res[...]
        for k in range(4):
            total = total + parts[k].astype(F32)
        out[...] = total.astype(BF)
        g_router[...] = terms[8:, :]


def finish(v, qkv, proj, res, parts, terms):
    steps, own, width = 8, proj.shape[0], proj.shape[1]
    row, some = v.shape[1] // steps, own // steps
    once = lambda n: (lambda i: (0,) * n)
    return pl.pallas_call(
        finish_kernel,
        grid=(steps,),
        out_shape=(
            jax.ShapeDtypeStruct((v.shape[1], 2 * HID), F32), jax.ShapeDtypeStruct((v.shape[1], HID), F32),
            jax.ShapeDtypeStruct((own, 2560), F32), jax.ShapeDtypeStruct((own, width), F32),
            jax.ShapeDtypeStruct(res.shape, BF), jax.ShapeDtypeStruct((EXPERTS, own), F32)),
        in_specs=[
            pl.BlockSpec((2, row, v.shape[2]), lambda i: (0, i, 0)),
            pl.BlockSpec((8, some, 320), lambda i: (0, i, 0)), pl.BlockSpec((some, width), lambda i: (i, 0)),
            pl.BlockSpec(res.shape, once(2)), pl.BlockSpec(parts.shape, once(3)),
            pl.BlockSpec(terms.shape, once(2))],
        out_specs=[
            pl.BlockSpec((row, 2 * HID), lambda i: (i, 0)), pl.BlockSpec((row, HID), lambda i: (i, 0)),
            pl.BlockSpec((some, 2560), lambda i: (i, 0)), pl.BlockSpec((some, width), lambda i: (i, 0)),
            pl.BlockSpec(res.shape, once(2)), pl.BlockSpec((EXPERTS, own), once(2))],
        compiler_params=pltpu.CompilerParams(vmem_limit_bytes=62 * 1024 * 1024),
        name="finish",
    )(v, qkv, proj, res, parts, terms)


def expert_grads_general(reps, grps, xs, dys, ggu, hw):
    local, half, width = ggu.shape[0], HID // 2, xs.shape[1]
    own = width // grps
    chips = reps // 2
    piece = own // chips
    same_core = [[2 * i + c for i in range(chips)] for c in range(2)]
    pairs = [[2 * i, 2 * i + 1] for i in range(chips)]
    up = jnp.einsum("td,eth->edh", xs, ggu, preferred_element_type=F32).astype(BF)
    down = jnp.einsum("td,eth->edh", dys, hw, preferred_element_type=F32).astype(BF)
    gw = jnp.concatenate([up, down], axis=2)
    gw = gw.reshape(local, grps, chips, piece, 3 * half).transpose(2, 1, 3, 0, 4)
    gw = gw.reshape(chips * grps * piece, local * 3 * half)
    gw = lax.psum_scatter(gw, "rep", scatter_dimension=0, tiled=True, axis_index_groups=same_core)
    gw = lax.all_to_all(gw.reshape(grps, piece, local, 3 * half), "grp", 0, 0, tiled=True)
    gw = gw.transpose(1, 0, 2, 3).reshape(piece, EXPERTS, 3 * half)
    gw = lax.all_gather(gw, "rep", axis=0, tiled=True, axis_index_groups=same_core)
    gw = lax.all_gather(gw, "rep", axis=0, tiled=False, axis_index_groups=pairs).astype(F32)
    gw = gw.reshape(2, own * EXPERTS, 3, half)
    gw = jnp.moveaxis(gw, 0, 2).reshape(own * EXPERTS, 3 * HID)
    return gw[:, : 2 * HID], gw[:, 2 * HID :]


def shards_general(
    reps,
    grps,
    tokens,
    attn_gain,
    query_key_value_weight,
    attn_proj,
    mlp_gain,
    w_router,
    w_gate_up,
    w_down,
    prefix_len,
    expert_ids,
    priority,
    cotangent,
):
    seq, width = tokens.shape
    own = width // grps
    local_experts = EXPERTS // grps
    heads = KEY_VALUE_HEADS
    groups = None if reps == heads else [list(range(i, i + heads)) for i in range(0, reps, heads)]
    rep, grp = lax.axis_index("rep"), lax.axis_index("grp")
    head = lax.rem(rep, heads)
    qw, hw = QPK * HEAD_WIDTH, HEAD_WIDTH
    q_all = QUERY_HEADS * HEAD_WIDTH

    small = jnp.concatenate([attn_gain[:, None], mlp_gain[:, None], w_router], axis=1)
    small = lax.all_gather(small, "grp", axis=0, tiled=True)
    gain_one, gain_two = small[:, 0].astype(F32)[None, :], small[:, 1].astype(F32)[None, :]
    router = small[:, 2:]
    qkv_cols = jnp.concatenate(
        [
            lax.dynamic_slice_in_dim(query_key_value_weight, head * qw, qw, 1),
            lax.dynamic_slice_in_dim(query_key_value_weight, q_all + head * hw, hw, 1),
            lax.dynamic_slice_in_dim(query_key_value_weight, q_all + heads * hw + head * hw, hw, 1),
        ],
        axis=1,
    )
    qkv_head = lax.all_gather(qkv_cols, "grp", axis=0, tiled=True)
    row = head * qw + jnp.arange(qw)
    mine = (row // own) == grp
    proj_rows = jnp.where(mine[:, None], jnp.take(attn_proj, jnp.where(mine, row - grp * own, 0), axis=0), 0)
    proj_head = lax.psum(proj_rows, "grp")

    core, chip, chips, half = lax.rem(rep, 2), rep // 2, reps // 2, HID // 2
    pairs = [[2 * i, 2 * i + 1] for i in range(chips)]
    same_core = [[2 * i + c for i in range(chips)] for c in range(2)]
    piece = own // chips
    gu_piece = lax.dynamic_slice_in_dim(w_gate_up, chip * piece, piece, 0)
    dn_piece = lax.dynamic_slice_in_dim(w_down, chip * piece, piece, 0)
    both = jnp.concatenate(
        [
            lax.dynamic_slice_in_dim(gu_piece, core * half, half, 2),
            lax.dynamic_slice_in_dim(gu_piece, HID + core * half, half, 2),
            lax.dynamic_slice_in_dim(dn_piece, core * half, half, 2),
        ],
        axis=2,
    )
    both = both.reshape(piece, grps, local_experts, 3 * half).transpose(1, 2, 0, 3)
    both = lax.all_to_all(both, "grp", 0, 0, tiled=True)
    both = lax.all_gather(both, "rep", axis=0, tiled=False, axis_index_groups=same_core)
    both = both.transpose(2, 1, 0, 3, 4).reshape(local_experts, width, 3 * half)
    wgu, wdn = both[:, :, : 2 * half], both[:, :, 2 * half :]

    tokens_f = tokens.astype(F32)
    inverse_one = lax.rsqrt(jnp.mean(tokens_f * tokens_f, axis=1, keepdims=True) + EPS)
    normed_one = tokens_f * inverse_one
    act_one = (normed_one * gain_one).astype(BF)
    act_plane = lax.all_gather(act_one, "rep", axis=0, tiled=True, axis_index_groups=groups)
    prefix_plane = lax.all_gather(prefix_len, "rep", axis=0, tiled=True, axis_index_groups=groups)
    cos, sin = rope_tables(seq)
    projected = dot(act_plane, qkv_head).reshape(heads, seq, QPK + 2, HEAD_WIDTH)
    cos_b, sin_b = cos[None, :, None, :], sin[None, :, None, :]
    turned = rotate(projected[:, :, : QPK + 1], cos_b, sin_b).astype(BF)
    query = turned[:, :, :QPK]
    key = turned[:, :, QPK]
    value = projected[:, :, QPK + 1].astype(BF)
    scale = HEAD_WIDTH ** (-0.5)
    row_pos, col_pos = jnp.arange(seq)[:, None], jnp.arange(seq)[None, :]
    allowed = (col_pos <= row_pos)[None] | (col_pos[None] < prefix_plane[:, None, None])
    scores = jnp.einsum("bsgd,btd->bgst", query, key, preferred_element_type=F32) * scale
    scores = jnp.where(allowed[:, None], scores, -1e30)
    exps = jnp.exp(scores - jnp.max(scores, axis=-1, keepdims=True))
    probs = exps / jnp.sum(exps, axis=-1, keepdims=True)
    probs_low = probs.astype(BF)
    attended = jnp.einsum("bgst,btd->bsgd", probs_low, value, preferred_element_type=F32)
    attended = attended.astype(BF).reshape(heads * seq, qw)
    part = dot(attended, proj_head).astype(BF)
    part = lax.psum_scatter(part, "rep", scatter_dimension=0, tiled=True, axis_index_groups=groups)
    residual = tokens_f + part.astype(F32)
    inverse_two = lax.rsqrt(jnp.mean(residual * residual, axis=1, keepdims=True) + EPS)
    normed_two = residual * inverse_two
    act_two = (normed_two * gain_two).astype(BF)
    gates, kept = routing(expert_ids, priority, dot(act_two, router))

    def column(v):
        v = lax.all_gather(v, "grp", axis=0, tiled=True)
        return lax.all_gather(v, "rep", axis=0, tiled=True, axis_index_groups=pairs)

    def to_owners(v):
        v = lax.psum_scatter(v, "rep", scatter_dimension=0, tiled=True, axis_index_groups=pairs)
        return lax.psum_scatter(v, "grp", scatter_dimension=0, tiled=True).astype(F32)

    dy_all = column(cotangent)
    x_all = column(act_two)
    weight = column(jnp.where(kept, gates, 0.0))
    weight = lax.dynamic_slice_in_dim(weight, grp * local_experts, local_experts, 1).T[:, :, None]
    gate_up = jnp.einsum("td,edh->eth", x_all, wgu, preferred_element_type=F32)
    g, u = gate_up[..., :half], gate_up[..., half:]
    sig = jax.nn.sigmoid(g)
    silu = g * sig
    hidden = silu * u
    hidden_w = (hidden * weight).astype(BF)
    back = jnp.einsum("td,edh->eth", dy_all, wdn, preferred_element_type=F32)
    grad_gate_part = jnp.sum(back * hidden, axis=2)
    grad_hidden = back * weight
    ggu = jnp.concatenate(
        [grad_hidden * u * sig * (1.0 + g * (1.0 - sig)), grad_hidden * silu], axis=2
    ).astype(BF)
    out_part = jnp.einsum("eth,edh->td", hidden_w, wdn, preferred_element_type=F32).astype(BF)
    gact_part = jnp.einsum("eth,edh->td", ggu, wgu, preferred_element_type=F32).astype(BF)
    gact = to_owners(gact_part)
    grad_gates = lax.psum_scatter(
        grad_gate_part.T, "rep", scatter_dimension=0, tiled=True, axis_index_groups=pairs
    )
    grad_gates = lax.all_to_all(grad_gates, "grp", 0, 1, tiled=True)
    grad_gates = jnp.where(kept, grad_gates, 0.0)
    out = to_owners(out_part)
    output = (residual + out).astype(BF)
    grad_gu, grad_dn = expert_grads_general(reps, grps, x_all, dy_all, ggu, hidden_w)
    grad_gu = grad_gu.reshape(own, EXPERTS, 2 * HID)
    grad_dn = grad_dn.reshape(own, EXPERTS, HID)

    grad_logits = (gates * (grad_gates - jnp.sum(gates * grad_gates, axis=1, keepdims=True))).astype(BF)
    gact = gact + dot(grad_logits, router.T)
    router_term = dot(act_two.T, grad_logits)
    gain_two_term = jnp.sum(gact * normed_two, axis=0)
    scaled = gact * gain_two
    dy = cotangent.astype(F32)
    grad_residual = dy + inverse_two * (
        scaled - normed_two * jnp.mean(scaled * normed_two, axis=1, keepdims=True)
    )
    gres_low = grad_residual.astype(BF)

    gres_plane = lax.all_gather(gres_low, "rep", axis=0, tiled=True, axis_index_groups=groups)
    proj_term = dot(attended.T, gres_plane)
    grad_att = dot(gres_plane, proj_head.T).astype(BF).reshape(heads, seq, QPK, HEAD_WIDTH)
    grad_value = jnp.einsum("bgst,bsgd->btd", probs_low, grad_att, preferred_element_type=F32)
    grad_probs = jnp.einsum("bsgd,btd->bgst", grad_att, value, preferred_element_type=F32)
    grad_scores = (
        probs * (grad_probs - jnp.sum(probs * grad_probs, axis=-1, keepdims=True))
    ).astype(BF)
    grad_query = jnp.einsum("bgst,btd->bsgd", grad_scores, key, preferred_element_type=F32) * scale
    grad_key = jnp.einsum("bgst,bsgd->btd", grad_scores, query, preferred_element_type=F32) * scale
    turned_back = rotate(
        jnp.concatenate([grad_query, grad_key[:, :, None]], axis=2), cos_b, -sin_b
    )
    gproj = jnp.concatenate([turned_back, grad_value[:, :, None]], axis=2).astype(BF)
    gproj = gproj.reshape(heads * seq, qw + 2 * hw)
    qkv_term = dot(act_plane.T, gproj)
    gact_one = dot(gproj, qkv_head.T).astype(BF)
    gact_one = lax.psum_scatter(
        gact_one, "rep", scatter_dimension=0, tiled=True, axis_index_groups=groups
    ).astype(F32)
    gain_one_term = jnp.sum(gact_one * normed_one, axis=0)
    scaled_one = gact_one * gain_one
    grad_tokens = grad_residual + inverse_one * (
        scaled_one - normed_one * jnp.mean(scaled_one * normed_one, axis=1, keepdims=True)
    )

    qkv_own = lax.psum_scatter(qkv_term.astype(BF), "grp", scatter_dimension=0, tiled=True)
    proj_sum = lax.psum(proj_term.astype(BF), "grp")
    if groups is not None:
        across = [[i + heads * j for j in range(reps // heads)] for i in range(heads)]
        qkv_own = lax.psum(qkv_own, "rep", axis_index_groups=across)
        proj_sum = lax.psum(proj_sum, "rep", axis_index_groups=across)
    qkv_own = lax.all_gather(qkv_own, "rep", axis=0, tiled=False, axis_index_groups=groups)
    qkv_own = qkv_own.astype(F32)
    grad_qkv = jnp.concatenate(
        [
            qkv_own[:, :, lo:hi].transpose(1, 0, 2).reshape(own, -1)
            for lo, hi in ((0, qw), (qw, qw + hw), (qw + hw, qw + 2 * hw))
        ],
        axis=1,
    )
    proj_all = lax.all_gather(proj_sum, "rep", axis=0, tiled=True, axis_index_groups=groups)
    grad_proj = lax.dynamic_slice_in_dim(proj_all, grp * own, own, 0).astype(F32)
    terms = jnp.concatenate([gain_one_term[:, None], gain_two_term[:, None], router_term], axis=1)
    terms = lax.psum(lax.psum_scatter(terms, "grp", scatter_dimension=0, tiled=True), "rep")
    return (
        output,
        grad_tokens,
        terms[:, 0],
        grad_qkv,
        grad_proj,
        terms[:, 1],
        terms[:, 2:],
        grad_gu,
        grad_dn,
    )


def shards(
    tokens,
    attn_gain,
    query_key_value_weight,
    attn_proj,
    mlp_gain,
    w_router,
    w_gate_up,
    w_down,
    prefix_len,
    expert_ids,
    priority,
    cotangent,
):
    own, width = attn_gain.shape[0], tokens.shape[1]
    small = jnp.concatenate(
        [attn_gain[None], mlp_gain[None], jnp.zeros((14, own), BF), w_router.T], axis=0
    )
    prefix = jnp.broadcast_to(prefix_len.astype(F32), (8, 128))
    half = HEAD_WIDTH // 2
    inverse_freq = np.float32(10000.0) ** (-np.arange(half, dtype=np.float32) * np.float32(2.0 / HEAD_WIDTH))
    angles = np.arange(tokens.shape[0], dtype=np.float32)[:, None] * inverse_freq[None, :]
    cos_t = jnp.asarray(np.tile(np.cos(angles), (1, 4)), F32)
    sin = np.sin(angles)
    sin_t = jnp.asarray(np.tile(np.concatenate([-sin, sin], axis=1), (1, 2)), F32)
    parts = front(
        tokens, cotangent, w_gate_up, w_down, query_key_value_weight, attn_proj, small, expert_ids,
        priority.reshape(expert_ids.shape), prefix, cos_t, sin_t)
    wide, grad_tokens, qkv_own, proj_own, terms, out_parts = back(parts, tokens, cos_t, sin_t)
    grad_gu, grad_dn, grad_qkv, grad_proj, output, grad_router = finish(
        wide, qkv_own, proj_own.reshape(own, width), parts[13], out_parts, terms)
    return (
        output,
        grad_tokens,
        terms[0],
        grad_qkv,
        grad_proj,
        terms[1],
        grad_router.T,
        grad_gu.reshape(own, EXPERTS, 2 * HID),
        grad_dn.reshape(own, EXPERTS, HID),
    )


def solution(mesh):
    tok, par = ("rep", "grp"), "grp"
    in_specs = (
        P(tok, None),
        P(par),
        P(par, None),
        P(par, None),
        P(par),
        P(par, None),
        P(par, None, None),
        P(par, None, None),
        P(tok),
        P(tok, None),
        P(tok, None),
        P(tok, None),
    )
    out_specs = (
        P(tok, None),
        P(tok, None),
        P(par),
        P(par, None),
        P(par, None),
        P(par),
        P(par, None),
        P(par, None, None),
        P(par, None, None),
    )
    reps, grps = mesh.shape["rep"], mesh.shape["grp"]

    def body(*args):
        if (reps, grps) == (8, 4):
            return shards(*args)
        return shards_general(reps, grps, *args)

    return jax.shard_map(body, mesh=mesh, in_specs=in_specs, out_specs=out_specs, check_vma=False)
```

```python
import jax
import jax.numpy as jnp
import numpy as np
from jax import lax
from jax.experimental import pallas as pl
from jax.experimental.pallas import tpu as pltpu
from jax.sharding import PartitionSpec as P

QUERY_HEADS = 24
KEY_VALUE_HEADS = 8
HEAD_WIDTH = 64
HID = 512
EXPERTS = 16
CAP = 72
EPS = 1e-05
BF = jnp.bfloat16
F32 = jnp.float32
QPK = QUERY_HEADS // KEY_VALUE_HEADS
BIG = 1 << 20
MESH = pl.DeviceIdType.MESH


def dot(a, b):
    return jnp.dot(a, b, preferred_element_type=F32)


def rope_tables(length):
    half = HEAD_WIDTH // 2
    position = jnp.arange(length, dtype=F32)[:, None]
    inverse_freq = 10000.0 ** (-jnp.arange(half, dtype=F32) * 2.0 / HEAD_WIDTH)
    angles = position * inverse_freq[None, :]
    return jnp.cos(angles), jnp.sin(angles)


def rotate(v, cos, sin):
    half = HEAD_WIDTH // 2
    a, b = v[..., :half], v[..., half:]
    return jnp.concatenate([a * cos - b * sin, b * cos + a * sin], axis=-1)


def choices(expert_ids, priority):
    seq, top = expert_ids.shape
    choose = expert_ids[:, :, None] == jnp.arange(EXPERTS, dtype=jnp.int32)[None, None, :]
    chosen = jnp.any(choose, axis=1)
    rank_of = jnp.sum(jnp.where(choose, priority.reshape(seq, top)[:, :, None], 0), axis=1)
    rank_of = jnp.where(chosen, rank_of, BIG)
    slot = jnp.sum((rank_of[None, :, :] < rank_of[:, None, :]).astype(jnp.int32), axis=1)
    return chosen, chosen & (slot < CAP)


def routing(expert_ids, priority, logits):
    chosen, kept = choices(expert_ids, priority)
    top_logit = jnp.max(jnp.where(chosen, logits, -jnp.inf), axis=1, keepdims=True)
    gate_exp = jnp.where(chosen, jnp.exp(jnp.where(chosen, logits - top_logit, 0.0)), 0.0)
    gates = gate_exp / jnp.sum(gate_exp, axis=1, keepdims=True)
    return gates, kept


def place():
    r, z = lax.axis_index("rep"), lax.axis_index("grp")
    return r // 4, (r // 2) % 2, r % 2, z


def flip(bit, by):
    return bit + by * (1 - 2 * bit)


def turn(v, cos, sin):
    lane = lax.broadcasted_iota(jnp.int32, v.shape, 1)
    partner = jnp.where(lax.rem(lane, 64) < 32, pltpu.roll(v, 96, 1), pltpu.roll(v, 32, 1))
    return v * cos + partner * sin


def gradient_rows(q3, x, dy, ggu, hw, gw):
    half = HID // 2

    def side(ref):
        return jnp.concatenate(
            [ref[:, :, :, pl.ds(pl.multiple_of(zz * 384 + q3 * 128, 128), 128)].reshape(1024, 128)
             for zz in range(4)], axis=1)
    xs, ds = side(x), side(dy)

    def one(j, _):
        up = lax.dot_general(xs, ggu[j], (((0,), (0,)), ((), ())), preferred_element_type=F32).astype(BF)
        dn = lax.dot_general(ds, hw[j], (((0,), (0,)), ((), ())), preferred_element_type=F32).astype(BF)
        for zz in range(4):
            for p in range(4):
                for h in range(2):
                    at = zz * 128 + p * 32 + h * 16
                    gw[p, h, zz, j, :, : 2 * half] = up[at : at + 16]
                    gw[p, h, zz, j, :, 2 * half :] = dn[at : at + 16]
        return 0
    lax.fori_loop(0, 4, one, 0)


def front_kernel(tok, dy, w_gu, w_dn, qkv, proj, small, ids, prio, prefix, cos_t, sin_t,
                 o_x, o_dy, o_ggu, o_hw, o_act, o_q, o_k, o_v, o_probs, o_att, o_qkvw, o_projw,
                 o_small, o_res, o_gates, o_kept, o_gsum, o_osum, o_gw, o_r1,
                 smalls, qkvw, projw, projq, actp, pre, pr, qs, ks, vs, probs, att, part, sibr, sums, plr,
                 xall, dyall, wbuf, ggu, hw, gpart, ggp, gsib,
                 gsum, res, gates, kept, qwin, wst, wcol, wpiece, gw, recv1,
                 s_small, r_small, s_qkv, r_qkv, s_pz, r_pz, s_pq, r_pq, s_wz, r_wz, s_wp, r_wp,
                 s_act, r_act, s_pre, r_pre, s_actc, r_actc, s_prec, r_prec, s_sib, r_sib, s_pl, r_pl,
                 s_x, r_x, s_xc, r_xc, s_y, r_y, s_yc, r_yc,
                 s_gc, r_gc, s_oc, r_oc, s1, r1, sl):
    y, x, c, z = place()
    half = HID // 2

    def slot(a, b):
        return flip(y, a * c + b * (1 - c)) * 2 + flip(x, a * (1 - c) + b * c)

    p0, p1, p2, p3 = slot(0, 0), slot(1, 0), slot(0, 1), slot(1, 1)
    peers = (p1, p2, p3)
    d1, d2, dsib = (p1 * 2 + c, z), (p2 * 2 + c, z), (p0 * 2 + 1 - c, z)
    dpl = [(p * 2 + c, z) for p in peers]
    zk = [lax.rem(z + k, 4) for k in range(4)]
    zf = [lax.rem(z + 4 - k, 4) for k in range(4)]
    dz = [(p0 * 2 + c, zz) for zz in zk]

    barrier = pltpu.get_barrier_semaphore()
    for to in dpl + dz[1:] + [dsib]:
        pl.semaphore_signal(barrier, 1, device_id=to, device_id_type=MESH)
    pl.semaphore_wait(barrier, 7)

    def remote(src, dst, s, r, to):
        return pltpu.make_async_remote_copy(src, dst, s, r, device_id=to, device_id_type=MESH)

    def c_small(k):
        return remote(small, smalls.at[z], s_small.at[k - 1], r_small.at[k - 1], dz[k])

    def rows(zz, pp):
        return pl.ds(pl.multiple_of(zz * 384 + pp * 96, 96), 96)

    def c_wz(k):
        return remote(wpiece.at[zk[k]], wbuf.at[:, rows(z, p0)], s_wz.at[k - 1], r_wz.at[k - 1], dz[k])

    def c_wp(k, i):
        zz = zf[k]
        who, pp = ((d1, p0), (d2, p0), (d2, p1))[i]
        src = wpiece.at[z] if (k == 0 and i < 2) else wbuf.at[:, rows(zz, pp)]
        return remote(src, wbuf.at[:, rows(zz, pp)], s_wp.at[k, i], r_wp.at[k, i], who)

    def quarter(p):
        return pl.ds(pl.multiple_of(p * 48, 48), 48)

    def c_pz(k):
        src = proj.at[pl.ds(pl.multiple_of(c * 192 + p0 * 48, 48), 48)]
        return remote(src, projq.at[k - 1], s_pz.at[k - 1], r_pz.at[k - 1], dz[k])

    def c_pq(k, owner):
        return remote(projq.at[k - 1], projw.at[quarter(p0)], s_pq.at[k - 1], r_pq.at[p0], (owner * 2 + c, z))

    def c_pq_in(i):
        return remote(projq.at[0], projw.at[quarter(peers[i])], s_pq.at[0], r_pq.at[peers[i]], dpl[i])

    def c_act(i):
        blk = actp.at[c, p1 if i == 2 else p0]
        return remote(blk, blk, s_act.at[i], r_act.at[i], d1 if i == 0 else d2)

    def c_pre(i):
        blk = pre.at[c, p1 if i == 2 else p0]
        return remote(blk, blk, s_pre.at[i], r_pre.at[i], d1 if i == 0 else d2)

    def c_actc(i):
        p = (p0, p1, p2, p3)[i]
        return remote(actp.at[c, p], actp.at[c, p], s_actc.at[i], r_actc.at[i], dsib)

    def c_prec(i):
        p = (p0, p1, p2, p3)[i]
        return remote(pre.at[c, p], pre.at[c, p], s_prec.at[i], r_prec.at[i], dsib)

    def c_sib():
        return remote(part, sibr, s_sib, r_sib, dsib)

    def c_pl(i):
        return remote(sums.at[i], plr.at[i], s_pl.at[i], r_pl.at[i], d2 if i == 1 else d1)

    def chain(at, s, r, sc=None, rc=None):
        def hop(h, d, send):
            block = z - (h - 1) if d == 0 else z + (h - 1)
            if not send:
                block = z - h if d == 0 else z + h
            return remote(at(block), at(block), s.at[d, h - 1], r.at[d, h - 1],
                          (p0 * 2 + c, z + 1 if d == 0 else z - 1))

        def may(h, d, send):
            if send:
                return (z < 3) & (z >= h - 1) if d == 0 else (z > 0) & (z <= 4 - h)
            return z >= h if d == 0 else z <= 3 - h

        def across(h, d):
            block = z - h if d == 0 else z + h
            return remote(at(block), at(block), sc.at[d, h - 1], rc.at[d, h - 1], dsib)

        def over():
            return remote(at(z), at(z), sc.at[2, 0], rc.at[2, 0], dsib)

        def send(h):
            for d in range(2):
                @pl.when(may(h, d, True))
                def _(d=d):
                    hop(h, d, True).start()
            if h == 1 and sc is not None:
                over().start()

        def recv(h):
            for d in range(2):
                @pl.when(may(h, d, False))
                def _(d=d):
                    hop(h, d, False).wait_recv()
                    if sc is not None:
                        across(h, d).start()

        def finish():
            over().wait_recv()
            for h in (1, 2, 3):
                for d in range(2):
                    @pl.when(may(h, d, False))
                    def _(d=d, h=h):
                        across(h, d).wait_recv()

        def sent():
            if sc is not None:
                over().wait_send()
            for h in (1, 2, 3):
                for d in range(2):
                    @pl.when(may(h, d, True))
                    def _(d=d, h=h):
                        hop(h, d, True).wait_send()
                    if sc is not None:
                        @pl.when(may(h, d, False))
                        def _(d=d, h=h):
                            across(h, d).wait_send()
        return send, recv, finish, sent

    x_send, x_recv, x_finish, x_sent = chain(lambda b: xall.at[c, b], s_x, r_x, s_xc, r_xc)
    y_send, y_recv, y_finish, y_sent = chain(lambda b: dyall.at[c, b], s_y, r_y, s_yc, r_yc)
    q_send, q_recv, _, q_sent = chain(
        lambda b: qkvw.at[pl.ds(pl.multiple_of(b * 384, 384), 384)], s_qkv, r_qkv)

    opart, osib, osum = part, sibr, sums

    def copy1(h, b):
        return remote(gw.at[slot(1, b), h], recv1.at[h, b], s1.at[h, b], r1.at[h, b], d1)
    g_c = remote(gpart, gsib, s_gc, r_gc, dsib)
    o_c = remote(opart, osib, s_oc, r_oc, dsib)

    def weights_a(k):
        if k:
            c_wz(k).wait_recv()
        c_wp(k, 0).start()

    def weights_b(k):
        c_wp(k, 0).wait_recv()
        c_wp(k, 1).start()
        c_wp(k, 2).start()

    for k in (1, 2, 3):
        c_small(k).start()
    local = [pltpu.make_async_copy(small, smalls.at[z], sl.at[0]),
             pltpu.make_async_copy(dy, dyall.at[c, z], sl.at[3])]

    def window(off, width, at, n):
        src = qkv.at[:, pl.ds(pl.multiple_of(off, 128), width)]
        return pltpu.make_async_copy(src, qwin.at[:, pl.ds(at, width)], sl.at[n])
    mine = p0 * 96
    windows = [window(384 * p0 + 128 * c, 256, 0, 1), window(1536 + 128 * p0, 128, 256, 2),
               window(2048 + 128 * p0, 128, 384, 5)]
    pieces = [pltpu.make_async_copy(
        ref.at[pl.ds(pl.multiple_of(mine, 96), 96), :, pl.ds(pl.multiple_of(off, half), half)],
        wst.at[:, :, pl.ds(i * half, half)], sl.at[6 + i])
        for i, (ref, off) in enumerate(((w_gu, c * half), (w_gu, HID + c * half), (w_dn, c * half)))]
    for one in local + windows + pieces:
        one.start()
    own_proj = pltpu.make_async_copy(proj.at[pl.ds(pl.multiple_of(c * 192, 192), 192)], projw, sl.at[4])

    @pl.when(z == p0)
    def _():
        own_proj.start()
    for one in windows:
        one.wait()
    cols = qwin[...].astype(F32)
    own_rows = pl.ds(pl.multiple_of(z * 384, 384), 384)
    for at, lo, width in ((0, 0, 256), (192, 256, 128), (256, 384, 128)):
        part_ = cols[:, lo : lo + width]
        part_ = jnp.where(c == 0, part_, pltpu.roll(part_, width - 64, 1)).astype(BF)
        qkvw[own_rows, at : at + (192 if at == 0 else 64)] = part_[:, : 192 if at == 0 else 64]

    tok_f = tok[...].astype(F32)
    inv1 = lax.rsqrt(jnp.mean(tok_f * tok_f, axis=1, keepdims=True) + EPS)
    for k in (1, 2, 3):
        c_small(k).wait_recv()
    q_send(1)
    local[0].wait()
    gain1 = jnp.concatenate([smalls[i, 0:1, :] for i in range(4)], axis=1).astype(F32)
    actp[c, p0] = (tok_f * inv1 * gain1).astype(BF)
    pre[c, p0] = prefix[...]
    for i in range(2):
        c_act(i).start()
        c_pre(i).start()
    c_actc(0).start()
    c_prec(0).start()
    chosen_f = jnp.zeros((128, 128), F32)
    rank_of = jnp.zeros((128, 128), F32)
    lane_e = lax.broadcasted_iota(jnp.int32, (128, 128), 1)
    for k in range(8):
        hit = ids[:, k : k + 1] == lane_e
        chosen_f = jnp.where(hit, 1.0, chosen_f)
        rank_of = jnp.where(hit, prio[:, k : k + 1].astype(F32), rank_of)
    rank_of = jnp.where(chosen_f > 0.0, rank_of, 65536.0)
    rank_t = rank_of.T
    slots = jnp.zeros((128, 128), F32)
    for e in range(EXPERTS):
        before = jnp.sum((rank_t[e : e + 1, :] < rank_of[:, e : e + 1]).astype(F32), axis=1, keepdims=True)
        slots = jnp.where(lane_e == e, before, slots)
    kept_f = jnp.where(slots < CAP, chosen_f, 0.0)
    kept[...] = kept_f[:, :EXPERTS]
    q_recv(1)
    q_send(2)

    for one in pieces:
        one.wait()

    def expert_rows(l, _):
        wcol[...] = wst[:, :, pl.ds(pl.multiple_of(l * 128, 128), 128)].astype(F32).reshape(1536, 128)
        for e in range(EXPERTS):
            wpiece[e // 4, e % 4, :, pl.ds(pl.multiple_of(l * 128, 128), 128)] = (
                wcol[pl.ds(e, 96, stride=EXPERTS), :].astype(BF))
        return 0
    lax.fori_loop(0, 6, expert_rows, 0)
    own_piece = pltpu.make_async_copy(wpiece.at[z], wbuf.at[:, rows(z, p0)], sl.at[30])
    own_piece.start()
    weights_a(0)
    q_recv(2)
    q_send(3)
    for k in (1, 2, 3):
        c_pz(k).start()
    for i in range(3):
        c_act(i).wait_recv()
        c_pre(i).wait_recv()
        if i == 0:
            c_act(2).start()
            c_pre(2).start()
        c_actc(i + 1).start()
        c_prec(i + 1).start()
    q_recv(3)
    local[1].wait()

    row = lax.broadcasted_iota(jnp.int32, (128, 128), 0)
    col = lax.broadcasted_iota(jnp.int32, (128, 128), 1)
    causal = col <= row
    col_f = col.astype(F32)

    def attention(cc):
        pr[...] = jnp.dot(actp[cc].reshape(512, 1536), qkvw[...], preferred_element_type=F32).reshape(4, 128, 320)

        def one(i, _):
            lo = turn(pr[i, :, 0:128], cos_t[...], sin_t[...]).astype(BF)
            hi = turn(pr[i, :, 128:256], cos_t[...], sin_t[...]).astype(BF)
            qs[cc, i, 0:128] = lo[:, 0:64]
            qs[cc, i, 128:256] = lo[:, 64:128]
            qs[cc, i, 256:384] = hi[:, 0:64]
            ks[cc, i] = hi[:, 64:128]
            vs[cc, i] = pr[i, :, 256:320].astype(BF)
            sc = lax.dot_general(qs[cc, i], ks[cc, i], (((1,), (1,)), ((), ())), preferred_element_type=F32)
            allowed = causal | (col_f < pre[cc, i, 0:1, :])
            sc = jnp.where(allowed[None], sc.reshape(3, 128, 128) * (64 ** -0.5), -1e30)
            ex = jnp.exp(sc - jnp.max(sc, axis=-1, keepdims=True))
            pb = (ex / jnp.sum(ex, axis=-1, keepdims=True)).reshape(384, 128)
            probs[cc, i] = pb
            at = jnp.dot(pb.astype(BF), vs[cc, i], preferred_element_type=F32).astype(BF)
            for h in range(3):
                att[cc, i, :, h * 64 : (h + 1) * 64] = at[h * 128 : (h + 1) * 128]
            return 0
        lax.fori_loop(0, 4, one, 0)

    attention(c)
    for k in (1, 3, 2):
        c_wz(k).start()
    for i in range(4):
        c_actc(i).wait_recv()
        c_prec(i).wait_recv()
    attention(1 - c)
    for k in (1, 2, 3):
        c_pz(k).wait_recv()
        owner = zf[k]

        @pl.when(owner != p0)
        def _(k=k, owner=owner):
            c_pq(k, owner).start()

        @pl.when(owner == p0)
        def _(k=k):
            projw[quarter(p0)] = projq[k - 1]

    @pl.when(z == p0)
    def _():
        own_proj.wait()

    @pl.when(z != p0)
    def _():
        for i in range(3):
            c_pq_in(i).wait_recv()

    def to_sib(i, _):
        part[i] = jnp.dot(att[1 - c, i], projw[...], preferred_element_type=F32).astype(BF)
        return 0
    lax.fori_loop(0, 4, to_sib, 0)
    c_sib().start()
    c_sib().wait_recv()
    def mixed(p):
        return jnp.dot(att[c, p], projw[...], preferred_element_type=F32) + sibr[p].astype(F32)

    for i in (2, 0):
        sums[i] = mixed(peers[i]).astype(BF)
        c_pl(i).start()
    to_second = mixed(p2)
    residual = tok_f + mixed(p0)
    c_pl(2).wait_recv()
    sums[1] = (to_second + plr[2].astype(F32)).astype(BF)
    c_pl(1).start()
    for i in range(2):
        c_pl(i).wait_recv()
        residual = residual + plr[i].astype(F32)
    res[...] = residual
    inv2 = lax.rsqrt(jnp.mean(residual * residual, axis=1, keepdims=True) + EPS)
    gain2 = jnp.concatenate([smalls[i, 1:2, :] for i in range(4)], axis=1).astype(F32)
    act2 = (residual * inv2 * gain2).astype(BF)
    router = jnp.concatenate([smalls[i, 16:32, :] for i in range(4)], axis=1)
    logits = lax.dot_general(act2, router, (((1,), (1,)), ((), ())), preferred_element_type=F32)
    chosen = chosen_f[:, :EXPERTS] > 0.0
    top = jnp.max(jnp.where(chosen, logits, -1e30), axis=1, keepdims=True)
    ge = jnp.where(chosen, jnp.exp(jnp.where(chosen, logits - top, 0.0)), 0.0)
    gt = ge / jnp.sum(ge, axis=1, keepdims=True)
    gates[...] = gt
    wide_gates = jnp.concatenate([gt * kept[...], jnp.zeros((128, 112), F32)], axis=1)
    gate_hi = wide_gates.astype(BF)
    xall[c, z, :, :1536] = act2
    xall[c, z, :, 1536:1664] = gate_hi
    xall[c, z, :, 1664:] = (wide_gates - gate_hi.astype(F32)).astype(BF)
    x_send(1)
    y_send(1)
    weights_b(0)
    weights_a(1)
    weights_a(3)
    weights_b(1)
    x_recv(1)
    x_send(2)
    y_recv(1)
    y_send(2)
    weights_b(3)
    weights_a(2)
    x_recv(2)
    x_send(3)
    y_recv(2)
    y_send(3)
    weights_b(2)
    x_recv(3)
    y_recv(3)
    own_piece.wait()
    for k in range(4):
        c_wp(k, 1).wait_recv()
        c_wp(k, 2).wait_recv()
    x_finish()
    y_finish()

    lane = lax.broadcasted_iota(jnp.int32, (512, 128), 1)
    ggp[...] = jnp.zeros_like(ggp)

    def expert(n, _):
        j, t = n // 2, lax.rem(n, 2)
        gu = jnp.dot(xall[t, :, :, :1536].reshape(512, 1536), wbuf[j, :, : 2 * half], preferred_element_type=F32)
        bk = jnp.dot(dyall[t].reshape(512, 1536), wbuf[j, :, 2 * half :], preferred_element_type=F32)
        mine = lane == z * 4 + j
        both = (xall[t, :, :, 1536:1664].astype(F32) + xall[t, :, :, 1664:].astype(F32)).reshape(512, 128)
        w = jnp.sum(jnp.where(mine, both, 0.0), axis=1, keepdims=True)
        g, u = gu[:, :half], gu[:, half:]
        sg = 1.0 / (1.0 + jnp.exp(-g))
        silu = g * sg
        hid = silu * u
        hw[j, pl.ds(pl.multiple_of(t * 512, 512), 512)] = (hid * w).astype(BF)
        ggp[t] = ggp[t] + jnp.where(mine, jnp.sum(bk * hid, axis=1, keepdims=True), 0.0).reshape(4, 128, 128)
        gh = bk * w
        at = pl.ds(pl.multiple_of(t * 512, 512), 512)
        ggu[j, at, :half] = (gh * u * sg * (1.0 + g * (1.0 - sg))).astype(BF)
        ggu[j, at, half:] = (gh * silu).astype(BF)
        return 0
    lax.fori_loop(0, 8, expert, 0)

    gradient_rows(0, xall, dyall, ggu, hw, gw)
    for h in range(2):
        for b in range(2):
            copy1(h, b).start()
    saves = []

    def save(src, dst):
        one = pltpu.make_async_copy(src, dst, sl.at[9 + len(saves)])
        one.start()
        saves.append(one)
    for src, dst in ((xall, o_x), (dyall, o_dy), (ggu, o_ggu), (hw, o_hw), (actp, o_act), (qs, o_q), (ks, o_k),
                     (vs, o_v), (probs, o_probs), (att, o_att), (qkvw, o_qkvw), (projw, o_projw),
                     (smalls, o_small), (res, o_res), (gates, o_gates), (kept, o_kept)):
        save(src, dst)

    def block(grad, t, n):
        at = pl.ds(pl.multiple_of(t * 512, 512), 512)
        lanes = pl.ds(pl.multiple_of(n * 256, 256), 256)
        acc = jnp.zeros((512, 256), F32)
        for j in range(4):
            a = ggu[j, at] if grad else hw[j, at]
            b = wbuf[j, lanes, : 2 * half] if grad else wbuf[j, lanes, 2 * half :]
            acc = acc + lax.dot_general(a, b, (((1,), (1,)), ((), ())), preferred_element_type=F32)
        return acc.reshape(4, 128, 256), lanes

    def partial(grad, buf):
        def one(n, _):
            v, lanes = block(grad, 1 - c, n)
            buf[:, :, lanes] = v.astype(BF)
            return 0
        lax.fori_loop(0, 6, one, 0)

    def own(grad, sib, dst):
        def one(n, _):
            v, lanes = block(grad, c, n)
            dst[:, :, lanes] = (v + sib[:, :, lanes].astype(F32)).astype(BF)
            return 0
        lax.fori_loop(0, 6, one, 0)

    def put_gate_grads(dst, v):
        hi = v.astype(BF)
        dst[:, :, 1536:1664] = hi
        dst[:, :, 1664:] = (v - hi.astype(F32)).astype(BF)

    def gate_grads(v):
        return v[..., 1536:1664].astype(F32) + v[..., 1664:].astype(F32)

    c_sib().wait_send()
    for i in range(3):
        c_pl(i).wait_send()
    put_gate_grads(gpart, ggp[1 - c])
    partial(True, gpart)
    g_c.start()
    partial(False, opart)
    o_c.start()
    g_c.wait_recv()
    put_gate_grads(gsum, ggp[c] + gate_grads(gsib))
    own(True, gsib, gsum)
    save(gsum, o_gsum)
    o_c.wait_recv()
    own(False, osib, osum)
    save(osum, o_osum)
    save(gw, o_gw)
    for h in range(2):
        for b in range(2):
            copy1(h, b).wait()
    save(recv1, o_r1)

    for k in (1, 2, 3):
        for one in (c_small(k), c_pz(k), c_wz(k)):
            one.wait_send()

        @pl.when(zf[k] != p0)
        def _(k=k):
            c_pq(k, zf[k]).wait_send()
    for k in range(4):
        for i in range(3):
            c_wp(k, i).wait_send()
        for one in (c_actc(k), c_prec(k)):
            one.wait_send()
    for i in range(3):
        for one in (c_act(i), c_pre(i)):
            one.wait_send()
    for one in (g_c, o_c):
        one.wait_send()
    x_sent()
    y_sent()
    q_sent()
    for one in saves:
        one.wait()


def front(*args):
    sem, vm = pltpu.SemaphoreType.DMA, pltpu.VMEM
    out = lambda shape, kind=BF: jax.ShapeDtypeStruct(shape, kind)
    outs = (
        out((2, 4, 128, 1792)), out((2, 4, 128, 1536)), out((4, 1024, 512)), out((4, 1024, 256)),
        out((2, 4, 128, 1536)), out((2, 4, 384, 64)), out((2, 4, 128, 64)), out((2, 4, 128, 64)),
        out((2, 4, 384, 128), F32), out((2, 4, 128, 192)), out((1536, 320)), out((192, 1536)),
        out((4, 32, 384)), out((128, 1536), F32), out((128, 16), F32), out((128, 16), F32), out((4, 128, 1792)),
        out((4, 128, 1536)), out((4, 2, 4, 4, 16, 768)), out((2, 2, 4, 4, 16, 768)),
    )
    block, quad = vm((2, 4, 128, 1536), BF), vm((4, 128, 1536), BF)
    three = vm((3, 128, 1536), BF)
    quad_g = vm((4, 128, 1792), BF)
    scratch = [
        vm((4, 32, 384), BF), vm((1536, 320), BF), vm((192, 1536), BF), vm((3, 48, 1536), BF),
        block, vm((2, 4, 8, 128), F32),
        vm((4, 128, 320), F32), vm((2, 4, 384, 64), BF), vm((2, 4, 128, 64), BF), vm((2, 4, 128, 64), BF),
        vm((2, 4, 384, 128), F32), vm((2, 4, 128, 192), BF), quad, quad, quad, three,
        vm((2, 4, 128, 1792), BF), block, vm((4, 1536, 768), BF), vm((4, 1024, 512), BF),
        vm((4, 1024, 256), BF), quad_g, vm((2, 4, 128, 128), F32), quad_g,
        quad_g, vm((128, 1536), F32), vm((128, 16), F32), vm((128, 16), F32),
        vm((384, 512), BF), vm((96, 16, 768), BF), vm((1536, 128), F32), vm((4, 4, 96, 768), BF),
        vm((4, 2, 4, 4, 16, 768), BF), vm((2, 2, 4, 4, 16, 768), BF),
    ]
    n3, n4, one = sem((3,)), sem((4,)), sem(())
    hops = [sem((2, 3)), sem((2, 3)), sem((3, 3)), sem((3, 3))]
    sems = [
        n3, n3, sem((2, 3)), sem((2, 3)), n3, n3, n3, n4, n3, n3, sem((4, 3)), sem((4, 3)),
        n3, n3, n3, n3, n4, n4, n4, n4, one, one, n3, n3,
        *hops, *hops, one, one, one, one, sem((2, 2)), sem((2, 2)), sem((31,)),
    ]
    vmem, any_ = pl.BlockSpec(memory_space=pltpu.VMEM), pl.BlockSpec(memory_space=pl.ANY)
    return pl.pallas_call(
        front_kernel,
        out_shape=outs,
        in_specs=[vmem, any_, any_, any_, any_, any_, any_, vmem, vmem, vmem, vmem, vmem],
        out_specs=[any_] * len(outs),
        scratch_shapes=scratch + sems,
        compiler_params=pltpu.CompilerParams(
            collective_id=1, has_side_effects=True, vmem_limit_bytes=62 * 1024 * 1024),
        name="front",
    )(*args)


def back_kernel(i_x, i_dy, i_ggu, i_hw, i_act, i_q, i_k, i_v, i_probs, i_att, i_qkvw, i_projw, i_small,
                i_res, i_gates, i_kept, i_gsum, i_osum, i_gw, i_r1, tok, cos_t, sin_t,
                o_e, o_gtok, o_qg, o_pg, o_terms, o_op,
                xb, dyb, ggu, hw, qs, ks, vs, probs, att, qkvw, projw, smalls, res, gates, kept, gown, grecv,
                gw, recv1, send2, recv2, zs, zr, ib, agv,
                gres, gresf, gproj, sibr, plr, qgp, qz, qgo, pgp, pgr, pq2, pgo, terms, tz, tsib, tpl, tout, gtok,
                s1, r1, s2, r2, sz, rz, sa, ra, ss, rs, la,
                s_g, r_g, s_gr, r_gr, s_grc, r_grc, s_sib, r_sib, s_pl, r_pl, s_qz, r_qz, s_qo, r_qo,
                s_qoc, r_qoc, s_p1, r_p1, s_p2, r_p2, s_po, r_po, s_poc, r_poc, s_tz, r_tz, s_ts, r_ts,
                s_tp, r_tp, s_o, r_o, ld, sv):
    y, x, c, z = place()
    half = HID // 2
    wide = 3 * half
    nq = 6

    def slot(a, b):
        return flip(y, a * c + b * (1 - c)) * 2 + flip(x, a * (1 - c) + b * c)

    p0, p1, p2, p3 = slot(0, 0), slot(1, 0), slot(0, 1), slot(1, 1)
    peers = (p1, p2, p3)
    d1, d2, dsib = (p1 * 2 + c, z), (p2 * 2 + c, z), (p0 * 2 + 1 - c, z)
    dpl = [(p * 2 + c, z) for p in peers]
    zk = [lax.rem(z + k, 4) for k in range(4)]
    dz = [(p0 * 2 + c, zz) for zz in zk]

    loads = {}

    def load(name, src, dst):
        loads[name] = pltpu.make_async_copy(src, dst, ld.at[len(loads)])
        loads[name].start()
    load("gw", i_gw, gw.at[0])
    load("r1", i_r1, recv1.at[pl.ds(0, 2)])
    load("x", i_x.at[:, :, :, pl.ds(0, 1536)], xb)
    load("ggu", i_ggu, ggu)
    load("dy", i_dy, dyb)
    load("hw", i_hw, hw)
    load("gown", i_gsum.at[z], gown)
    for name, src, dst in (("res", i_res, res), ("gates", i_gates, gates), ("kept", i_kept, kept),
                           ("small", i_small, smalls),
                           ("projw", i_projw, projw), ("probs", i_probs, probs), ("q", i_q, qs), ("k", i_k, ks),
                           ("v", i_v, vs), ("att", i_att, att), ("qkvw", i_qkvw, qkvw)):
        load(name, src, dst)

    barrier = pltpu.get_barrier_semaphore()
    for to in dpl + dz[1:] + [dsib]:
        pl.semaphore_signal(barrier, 1, device_id=to, device_id_type=MESH)
    pl.semaphore_wait(barrier, 7)

    def remote(src, dst, s, r, to):
        return pltpu.make_async_remote_copy(src, dst, s, r, device_id=to, device_id_type=MESH)

    def copy1(q, b):
        return remote(gw.at[q // 2, slot(1, b), lax.rem(q, 2)], recv1.at[q, b], s1.at[q, b], r1.at[q, b], d1)

    def copy2(q):
        return remote(send2.at[lax.rem(q, 2)], recv2.at[q], s2.at[q], r2.at[q], d2)

    def copyz(q, k):
        return remote(zs.at[lax.rem(q, 2), zk[k]], zr.at[q, z], sz.at[q, k - 1], rz.at[q, k - 1], dz[k])

    def rows(q, p):
        return pl.ds(pl.multiple_of(((q // 2) * 8 + p * 2 + lax.rem(q, 2)) * 256, 256), 256)

    def copya(q, i):
        p, who = ((p0, d1), (p0, d2), (p1, d2))[i]
        src = agv.at[lax.rem(q, 2)] if i < 2 else o_e.at[c, rows(q, p)]
        return remote(src, o_e.at[c, rows(q, p)], sa.at[q, i], ra.at[q, i], who)

    def copys(q, i):
        p = (p0, p1, p2, p3)[i]
        src = agv.at[lax.rem(q, 2)] if i == 0 else o_e.at[c, rows(q, p)]
        return remote(src, o_e.at[c, rows(q, p)], ss.at[q, i], rs.at[q, i], dsib)

    def keep(q):
        return pltpu.make_async_copy(agv.at[lax.rem(q, 2)], o_e.at[c, rows(q, p0)], la.at[q])

    def c_g(k):
        return remote(i_gsum.at[zk[k]], grecv.at[k - 1], s_g.at[k - 1], r_g.at[k - 1], dz[k])

    def c_o(k):
        return remote(i_osum.at[zk[k]], o_op.at[k], s_o.at[k - 1], r_o.at[k - 1], dz[k])

    def c_gr(i):
        blk = gres.at[c, p1 if i == 2 else p0]
        return remote(blk, blk, s_gr.at[i], r_gr.at[i], d1 if i == 0 else d2)

    def c_grc(i):
        p = (p0, p1, p2, p3)[i]
        return remote(gres.at[c, p], gres.at[c, p], s_grc.at[i], r_grc.at[i], dsib)

    def c_sib():
        return remote(dyb.at[0], sibr, s_sib, r_sib, dsib)

    def c_pl(i):
        return remote(dyb.at[1, i], plr.at[i], s_pl.at[i], r_pl.at[i], d2 if i == 1 else d1)

    def c_qz(k):
        return remote(qgp.at[zk[k]], qz.at[k - 1], s_qz.at[k - 1], r_qz.at[k - 1], dz[k])

    def c_qo(i):
        dst = o_qg.at[(p1 if i == 2 else p0) * 2 + c]
        return remote(dst if i == 2 else qgo, dst, s_qo.at[i], r_qo.at[i], d1 if i == 0 else d2)

    def c_qoc(i):
        r = (p0, p1, p2, p3)[i] * 2 + c
        return remote(qgo if i == 0 else o_qg.at[r], o_qg.at[r], s_qoc.at[i], r_qoc.at[i], dsib)

    def c_p1(i):
        return remote(pgp.at[peers[i]], pgr.at[p0], s_p1.at[i], r_p1.at[i], dpl[i])

    def c_p2(k):
        return remote(pgr.at[zk[k]], pq2.at[k - 1], s_p2.at[k - 1], r_p2.at[k - 1], dz[k])

    def c_po(i):
        dst = o_pg.at[c, p1 if i == 2 else p0]
        return remote(dst if i == 2 else pgo, dst, s_po.at[i], r_po.at[i], d1 if i == 0 else d2)

    def c_poc(i):
        p = (p0, p1, p2, p3)[i]
        return remote(pgo if i == 0 else o_pg.at[c, p], o_pg.at[c, p], s_poc.at[i], r_poc.at[i], dsib)

    def lanes_of(zz):
        return pl.ds(pl.multiple_of(zz * 384, 384), 384)

    def c_tz(k):
        return remote(terms.at[:, lanes_of(zk[k])], tz.at[k], s_tz.at[k - 1], r_tz.at[k - 1], dz[k])

    def c_ts():
        return remote(tz.at[0], tsib, s_ts, r_ts, dsib)

    def c_tp(i):
        return remote(tpl.at[p0], tpl.at[p0], s_tp.at[i], r_tp.at[i], dpl[i])

    saves = [pltpu.make_async_copy(gtok, o_gtok, sv.at[0]),
             pltpu.make_async_copy(qgo, o_qg.at[p0 * 2 + c], sv.at[1]),
             pltpu.make_async_copy(pgo, o_pg.at[c, p0], sv.at[2]),
             pltpu.make_async_copy(tout, o_terms, sv.at[3])]
    own_out = pltpu.make_async_copy(i_osum.at[z], o_op.at[0], sv.at[5])
    own_out.start()
    act_load = pltpu.make_async_copy(i_act, xb, sv.at[4])

    for k in (1, 2, 3):
        c_g(k).start()
    loads["gw"].wait()
    loads["r1"].wait()
    loads["x"].wait()
    loads["ggu"].wait()
    loads["dy"].wait()
    loads["hw"].wait()

    def stage1(q):
        @pl.when(lax.rem(q, 2) == 0)
        def _():
            gradient_rows(q // 2, xb, dyb, ggu, hw, gw.at[q // 2])
        for b in range(2):
            copy1(q, b).start()

    def stage2(q):
        @pl.when(q >= 2)
        def _():
            for b in range(2):
                copy1(q, b).wait_recv()

        def one(zz, _):
            send2[lax.rem(q, 2), zz] = (gw[q // 2, p2, lax.rem(q, 2), zz].astype(F32)
                                        + recv1[q, 1, zz].astype(F32)).astype(BF)
            return 0
        lax.fori_loop(0, 4, one, 0)
        copy2(q).start()

    def stage3(q):
        copy2(q).wait()

        def one(zz, _):
            zs[lax.rem(q, 2), zz] = (gw[q // 2, p0, lax.rem(q, 2), zz].astype(F32) + recv1[q, 0, zz].astype(F32)
                                     + recv2[q, zz].astype(F32)).astype(BF)
            return 0
        lax.fori_loop(0, 4, one, 0)
        for k in range(1, 4):
            copyz(q, k).start()
        zr[q, z] = zs[lax.rem(q, 2), z]

    def stage4(q):
        for k in range(1, 4):
            copyz(q, k).wait()

        @pl.when(q >= 2)
        def _():
            copya(q - 2, 0).wait_send()
            copya(q - 2, 1).wait_send()
            copys(q - 2, 0).wait_send()
            keep(q - 2).wait()
        for zz in range(4):
            for j in range(4):
                for l in range(wide // 128):
                    ib[l, pl.ds(zz * 4 + j, 16, stride=EXPERTS), :] = (
                        zr[q, zz, j, :, l * 128 : (l + 1) * 128].astype(F32))
        for l in range(wide // 128):
            agv[lax.rem(q, 2), :, l * 128 : (l + 1) * 128] = ib[l].astype(BF)
        copya(q, 0).start()
        copys(q, 0).start()
        keep(q).start()

    def stage5(q):
        copya(q, 0).wait_recv()
        copya(q, 1).start()
        copya(q, 2).start()
        copys(q, 1).start()

    def stage6(q):
        copya(q, 1).wait_recv()
        copya(q, 2).wait_recv()
        copys(q, 2).start()
        copys(q, 3).start()

    def stage7(q):
        for i in range(4):
            copys(q, i).wait_recv()

    def norm_two():
        r = res[...]
        inv = lax.rsqrt(jnp.mean(r * r, axis=1, keepdims=True) + EPS)
        return inv, r * inv

    def norm_one():
        t = tok[...].astype(F32)
        inv = lax.rsqrt(jnp.mean(t * t, axis=1, keepdims=True) + EPS)
        return inv, t * inv

    def gain(row):
        return jnp.concatenate([smalls[i, row : row + 1, :] for i in range(4)], axis=1).astype(F32)

    def event_residual():
        for name in ("gown", "res", "gates", "kept", "small"):
            loads[name].wait()
        for k in (1, 2, 3):
            c_g(k).wait_recv()
        tail = slice(1536, 1664), slice(1664, 1792)

        def gate_part(v):
            return (v[:, tail[0]].astype(F32) + v[:, tail[1]].astype(F32))[:, :EXPERTS]
        gg = (gate_part(gown[...]) + gate_part(grecv[0]) + gate_part(grecv[1]) + gate_part(grecv[2])) * kept[...]
        gt = gates[...]
        gl = (gt * (gg - jnp.sum(gt * gg, axis=1, keepdims=True))).astype(BF)
        router_t = jnp.concatenate([smalls[i, 16:32, :] for i in range(4)], axis=1)
        ga = jnp.dot(gl, router_t, preferred_element_type=F32)
        ga = ga + gown[:, :1536].astype(F32)
        for k in range(3):
            ga = ga + grecv[k, :, :1536].astype(F32)
        inv, normed = norm_two()
        terms[8:24, :] = lax.dot_general(gl, xb[c, z], (((0,), (0,)), ((), ())), preferred_element_type=F32)
        terms[1:2, :] = jnp.sum(ga * normed, axis=0, keepdims=True)
        scaled = ga * gain(1)
        gr = dyb[c, z].astype(F32) + inv * (scaled - normed * jnp.mean(scaled * normed, axis=1, keepdims=True))
        gresf[...] = gr
        gres[c, p0] = gr.astype(BF)
        for i in range(2):
            c_gr(i).start()
        c_grc(0).start()

    def event_share():
        for k in (1, 2, 3):
            c_o(k).start()
        for i in range(3):
            c_gr(i).wait_recv()
            if i == 0:
                c_gr(2).start()
            c_grc(i + 1).start()
        act_load.start()

    scale = 64 ** -0.5

    def event_attention():
        for name in ("projw", "probs", "q", "k", "v", "att", "qkvw"):
            loads[name].wait()
        for i in range(4):
            c_grc(i).wait_recv()

        def one(n, _):
            cc, i = n // 4, lax.rem(n, 4)
            gb = lax.dot_general(gres[cc, i], projw[...], (((1,), (1,)), ((), ())),
                                 preferred_element_type=F32).astype(BF)
            ga = jnp.concatenate([gb[:, h * 64 : (h + 1) * 64] for h in range(3)], axis=0)
            pb = probs[cc, i]
            gv = lax.dot_general(pb.astype(BF), ga, (((0,), (0,)), ((), ())), preferred_element_type=F32)
            gp = lax.dot_general(ga, vs[cc, i], (((1,), (1,)), ((), ())), preferred_element_type=F32)
            gs = (pb * (gp - jnp.sum(pb * gp, axis=-1, keepdims=True))).astype(BF)
            gq = jnp.dot(gs, ks[cc, i], preferred_element_type=F32) * scale
            gk = lax.dot_general(gs, qs[cc, i], (((0,), (0,)), ((), ())), preferred_element_type=F32) * scale
            lo = jnp.concatenate([gq[0:128], gq[128:256]], axis=1)
            hi = jnp.concatenate([gq[256:384], gk], axis=1)
            gproj[cc, i, :, 0:128] = turn(lo, cos_t[...], -sin_t[...]).astype(BF)
            gproj[cc, i, :, 128:256] = turn(hi, cos_t[...], -sin_t[...]).astype(BF)
            gproj[cc, i, :, 256:320] = gv.astype(BF)
            return 0
        lax.fori_loop(0, 8, one, 0)

        def to_sib(i, _):
            dyb[0, i] = lax.dot_general(gproj[1 - c, i], qkvw[...], (((1,), (1,)), ((), ())),
                                        preferred_element_type=F32).astype(BF)
            return 0
        lax.fori_loop(0, 4, to_sib, 0)
        c_sib().start()
        pg = lax.dot_general(att[...].reshape(1024, 192), gres[...].reshape(1024, 1536), (((0,), (0,)), ((), ())),
                             preferred_element_type=F32)
        pgp[...] = pg.astype(BF).reshape(4, 48, 1536)
        for i in range(3):
            c_p1(i).start()
        pgr[p0] = pgp[p0]

    def event_columns():
        act_load.wait()

        def one(zz, _):
            a = xb[:, :, :, lanes_of(zz)].reshape(1024, 384)
            qgp[zz] = lax.dot_general(a, gproj[...].reshape(1024, 320), (((0,), (0,)), ((), ())),
                                      preferred_element_type=F32).astype(BF)
            return 0
        lax.fori_loop(0, 4, one, 0)
        for k in (1, 2, 3):
            c_qz(k).start()
        c_sib().wait()

        def part(p):
            return lax.dot_general(gproj[c, p], qkvw[...], (((1,), (1,)), ((), ())),
                                   preferred_element_type=F32) + sibr[p].astype(F32)
        for i in (2, 0):
            dyb[1, i] = part(peers[i]).astype(BF)
            c_pl(i).start()
        dyb[1, 1] = part(p2).astype(BF)
        gtok[...] = part(p0)
        for i in range(3):
            c_p1(i).wait_recv()
        for k in (1, 2, 3):
            c_p2(k).start()

    def event_second():
        c_pl(2).wait_recv()
        dyb[1, 1] = (dyb[1, 1].astype(F32) + plr[2].astype(F32)).astype(BF)
        c_pl(1).start()

    def event_tokens():
        ga = gtok[...]
        for i in range(2):
            c_pl(i).wait_recv()
            ga = ga + plr[i].astype(F32)
        inv, normed = norm_one()
        terms[0:1, :] = jnp.sum(ga * normed, axis=0, keepdims=True)
        scaled = ga * gain(0)
        gtok[...] = gresf[...] + inv * (scaled - normed * jnp.mean(scaled * normed, axis=1, keepdims=True))
        saves[0].start()
        for k in (1, 2, 3):
            c_tz(k).start()
        for k in (1, 2, 3):
            c_qz(k).wait_recv()
        qgo[...] = (qgp[z].astype(F32) + qz[0].astype(F32) + qz[1].astype(F32) + qz[2].astype(F32)).astype(BF)
        for i in range(2):
            c_qo(i).start()
        c_qoc(0).start()
        saves[1].start()
        for k in (1, 2, 3):
            c_p2(k).wait_recv()
        pgo[...] = (pgr[z].astype(F32) + pq2[0].astype(F32) + pq2[1].astype(F32) + pq2[2].astype(F32)).astype(BF)
        for i in range(2):
            c_po(i).start()
        c_poc(0).start()
        saves[2].start()

    def event_terms():
        for k in (1, 2, 3):
            c_tz(k).wait_recv()
        tz[0] = terms[:, lanes_of(z)] + tz[1] + tz[2] + tz[3]
        c_ts().start()
        for i in range(3):
            c_qo(i).wait_recv()
            if i == 0:
                c_qo(2).start()
            c_qoc(i + 1).start()
            c_po(i).wait_recv()
            if i == 0:
                c_po(2).start()
            c_poc(i + 1).start()

    def event_sums():
        c_ts().wait()
        tpl[p0] = tz[0] + tsib[...]
        for i in range(3):
            c_tp(i).start()

    def event_last():
        for i in range(3):
            c_tp(i).wait_recv()
        tout[...] = tpl[0] + tpl[1] + tpl[2] + tpl[3]
        saves[3].start()
        for i in range(4):
            c_qoc(i).wait_recv()
            c_poc(i).wait_recv()
        for k in (1, 2, 3):
            c_o(k).wait_recv()

    stages = (stage1, stage2, stage3, stage4, stage5, stage6, stage7)
    lead = 4
    for q in (2, 3):
        stage1(jnp.int32(q))
    for q in range(1):
        stage2(jnp.int32(q))
    events = {2: event_residual, 3: event_share, 4: event_attention, 5: event_columns, 6: event_second,
              7: event_tokens, 8: event_terms, 9: event_sums, 10: event_last}

    def step(t, _):
        for i, stage in enumerate(stages):
            q = t + lead if i == 0 else t + 2 - i

            @pl.when((q >= 0) & (q < nq))
            def _(stage=stage, q=q):
                stage(q)
        for at, event in events.items():
            @pl.when(t == at)
            def _(event=event):
                event()
        return 0

    lax.fori_loop(0, nq + len(stages) - 2, step, 0)

    def left(q, _):
        @pl.when(q >= 2)
        def _():
            for b in range(2):
                copy1(q, b).wait_send()
        for i in range(1, 4):
            copys(q, i).wait_send()
        copya(q, 2).wait_send()

        @pl.when(q >= nq - 2)
        def _():
            copya(q, 0).wait_send()
            copya(q, 1).wait_send()
            copys(q, 0).wait_send()
            keep(q).wait()
        return 0
    lax.fori_loop(0, nq, left, 0)
    for k in (1, 2, 3):
        for one in (c_g(k), c_o(k), c_qz(k), c_p2(k), c_tz(k)):
            one.wait_send()
    for i in range(3):
        for one in (c_gr(i), c_pl(i), c_qo(i), c_p1(i), c_po(i), c_tp(i)):
            one.wait_send()
    for i in range(4):
        for one in (c_grc(i), c_qoc(i), c_poc(i)):
            one.wait_send()
    for one in saves + [own_out]:
        one.wait()


def back(front_outs, tok, cos_t, sin_t):
    nq, wide = 6, 3 * HID // 2
    sem, vm = pltpu.SemaphoreType.DMA, pltpu.VMEM
    out = lambda shape, kind=BF: jax.ShapeDtypeStruct(shape, kind)
    piece = (4, 4, 16, wide)
    outs = (out((2, 6144, wide)), out((128, 1536), F32), out((8, 384, 320)), out((2, 4, 48, 1536)),
            out((24, 384), F32), out((4, 128, 1536)))
    block, quad, three = vm((2, 4, 128, 1536), BF), vm((4, 128, 1536), BF), vm((3, 128, 1536), BF)
    scratch = [
        block, block, vm((4, 1024, 512), BF), vm((4, 1024, 256), BF), vm((2, 4, 384, 64), BF),
        vm((2, 4, 128, 64), BF), vm((2, 4, 128, 64), BF), vm((2, 4, 384, 128), F32), vm((2, 4, 128, 192), BF),
        vm((1536, 320), BF), vm((192, 1536), BF), vm((4, 32, 384), BF), vm((128, 1536), F32), vm((128, 16), F32), vm((128, 16), F32),
        vm((128, 1792), BF), vm((3, 128, 1792), BF),
        vm((3, 4, 2) + piece, BF), vm((nq, 2) + piece, BF), vm((2,) + piece, BF), vm((nq,) + piece, BF),
        vm((2,) + piece, BF), vm((nq,) + piece, BF), vm((wide // 128, 256, 128), F32), vm((2, 256, wide), BF),
        block, vm((128, 1536), F32), vm((2, 4, 128, 320), BF), quad, three, vm((4, 384, 320), BF),
        vm((3, 384, 320), BF), vm((384, 320), BF), vm((4, 48, 1536), BF), vm((4, 48, 1536), BF),
        vm((3, 48, 1536), BF), vm((48, 1536), BF), vm((24, 1536), F32), vm((4, 24, 384), F32),
        vm((24, 384), F32), vm((4, 24, 384), F32), vm((24, 384), F32), vm((128, 1536), F32),
    ]
    n3, n4, one = sem((3,)), sem((4,)), sem(())
    sems = [
        sem((nq, 2)), sem((nq, 2)), sem((nq,)), sem((nq,)), sem((nq, 3)), sem((nq, 3)), sem((nq, 3)), sem((nq, 3)),
        sem((nq, 4)), sem((nq, 4)), sem((nq,)),
        n3, n3, n3, n3, n4, n4, one, one, n3, n3, n3, n3, n3, n3,
        n4, n4, n3, n3, n3, n3, n3, n3, n4, n4, n3, n3, one, one,
        n3, n3, n3, n3, sem((18,)), sem((6,)),
    ]
    vmem, any_ = pl.BlockSpec(memory_space=pltpu.VMEM), pl.BlockSpec(memory_space=pl.ANY)
    return pl.pallas_call(
        back_kernel,
        out_shape=outs,
        in_specs=[any_] * 20 + [vmem] * 3,
        out_specs=[any_] * len(outs),
        scratch_shapes=scratch + sems,
        compiler_params=pltpu.CompilerParams(
            collective_id=2, has_side_effects=True, vmem_limit_bytes=62 * 1024 * 1024),
        name="back",
    )(*front_outs, tok, cos_t, sin_t)


def finish_kernel(v, qkv, proj, res, parts, terms, gu, dn, g_qkv, g_proj, out, g_router):
    half = HID // 2
    for c in range(2):
        gu[:, c * half : (c + 1) * half] = v[c, :, :half].astype(F32)
        gu[:, HID + c * half : HID + (c + 1) * half] = v[c, :, half : 2 * half].astype(F32)
        dn[:, c * half : (c + 1) * half] = v[c, :, 2 * half :].astype(F32)
    heads = range(qkv.shape[0])
    g_qkv[...] = jnp.concatenate(
        [qkv[h, :, lo:hi].astype(F32) for lo, hi in ((0, 192), (192, 256), (256, 320)) for h in heads], axis=1)
    g_proj[...] = proj[...].astype(F32)

    @pl.when(pl.program_id(0) == 0)
    def _():
        total = res[...]
        for k in range(4):
            total = total + parts[k].astype(F32)
        out[...] = total.astype(BF)
        g_router[...] = terms[8:, :]


def finish(v, qkv, proj, res, parts, terms):
    steps, own, width = 8, proj.shape[0], proj.shape[1]
    row, some = v.shape[1] // steps, own // steps
    once = lambda n: (lambda i: (0,) * n)
    return pl.pallas_call(
        finish_kernel,
        grid=(steps,),
        out_shape=(
            jax.ShapeDtypeStruct((v.shape[1], 2 * HID), F32), jax.ShapeDtypeStruct((v.shape[1], HID), F32),
            jax.ShapeDtypeStruct((own, 2560), F32), jax.ShapeDtypeStruct((own, width), F32),
            jax.ShapeDtypeStruct(res.shape, BF), jax.ShapeDtypeStruct((EXPERTS, own), F32)),
        in_specs=[
            pl.BlockSpec((2, row, v.shape[2]), lambda i: (0, i, 0)),
            pl.BlockSpec((8, some, 320), lambda i: (0, i, 0)), pl.BlockSpec((some, width), lambda i: (i, 0)),
            pl.BlockSpec(res.shape, once(2)), pl.BlockSpec(parts.shape, once(3)),
            pl.BlockSpec(terms.shape, once(2))],
        out_specs=[
            pl.BlockSpec((row, 2 * HID), lambda i: (i, 0)), pl.BlockSpec((row, HID), lambda i: (i, 0)),
            pl.BlockSpec((some, 2560), lambda i: (i, 0)), pl.BlockSpec((some, width), lambda i: (i, 0)),
            pl.BlockSpec(res.shape, once(2)), pl.BlockSpec((EXPERTS, own), once(2))],
        compiler_params=pltpu.CompilerParams(vmem_limit_bytes=62 * 1024 * 1024),
        name="finish",
    )(v, qkv, proj, res, parts, terms)


def expert_grads_general(reps, grps, xs, dys, ggu, hw):
    local, half, width = ggu.shape[0], HID // 2, xs.shape[1]
    own = width // grps
    chips = reps // 2
    piece = own // chips
    same_core = [[2 * i + c for i in range(chips)] for c in range(2)]
    pairs = [[2 * i, 2 * i + 1] for i in range(chips)]
    up = jnp.einsum("td,eth->edh", xs, ggu, preferred_element_type=F32).astype(BF)
    down = jnp.einsum("td,eth->edh", dys, hw, preferred_element_type=F32).astype(BF)
    gw = jnp.concatenate([up, down], axis=2)
    gw = gw.reshape(local, grps, chips, piece, 3 * half).transpose(2, 1, 3, 0, 4)
    gw = gw.reshape(chips * grps * piece, local * 3 * half)
    gw = lax.psum_scatter(gw, "rep", scatter_dimension=0, tiled=True, axis_index_groups=same_core)
    gw = lax.all_to_all(gw.reshape(grps, piece, local, 3 * half), "grp", 0, 0, tiled=True)
    gw = gw.transpose(1, 0, 2, 3).reshape(piece, EXPERTS, 3 * half)
    gw = lax.all_gather(gw, "rep", axis=0, tiled=True, axis_index_groups=same_core)
    gw = lax.all_gather(gw, "rep", axis=0, tiled=False, axis_index_groups=pairs).astype(F32)
    gw = gw.reshape(2, own * EXPERTS, 3, half)
    gw = jnp.moveaxis(gw, 0, 2).reshape(own * EXPERTS, 3 * HID)
    return gw[:, : 2 * HID], gw[:, 2 * HID :]


def shards_general(
    reps,
    grps,
    tokens,
    attn_gain,
    query_key_value_weight,
    attn_proj,
    mlp_gain,
    w_router,
    w_gate_up,
    w_down,
    prefix_len,
    expert_ids,
    priority,
    cotangent,
):
    seq, width = tokens.shape
    own = width // grps
    local_experts = EXPERTS // grps
    heads = KEY_VALUE_HEADS
    groups = None if reps == heads else [list(range(i, i + heads)) for i in range(0, reps, heads)]
    rep, grp = lax.axis_index("rep"), lax.axis_index("grp")
    head = lax.rem(rep, heads)
    qw, hw = QPK * HEAD_WIDTH, HEAD_WIDTH
    q_all = QUERY_HEADS * HEAD_WIDTH

    small = jnp.concatenate([attn_gain[:, None], mlp_gain[:, None], w_router], axis=1)
    small = lax.all_gather(small, "grp", axis=0, tiled=True)
    gain_one, gain_two = small[:, 0].astype(F32)[None, :], small[:, 1].astype(F32)[None, :]
    router = small[:, 2:]
    qkv_cols = jnp.concatenate(
        [
            lax.dynamic_slice_in_dim(query_key_value_weight, head * qw, qw, 1),
            lax.dynamic_slice_in_dim(query_key_value_weight, q_all + head * hw, hw, 1),
            lax.dynamic_slice_in_dim(query_key_value_weight, q_all + heads * hw + head * hw, hw, 1),
        ],
        axis=1,
    )
    qkv_head = lax.all_gather(qkv_cols, "grp", axis=0, tiled=True)
    row = head * qw + jnp.arange(qw)
    mine = (row // own) == grp
    proj_rows = jnp.where(mine[:, None], jnp.take(attn_proj, jnp.where(mine, row - grp * own, 0), axis=0), 0)
    proj_head = lax.psum(proj_rows, "grp")

    core, chip, chips, half = lax.rem(rep, 2), rep // 2, reps // 2, HID // 2
    pairs = [[2 * i, 2 * i + 1] for i in range(chips)]
    same_core = [[2 * i + c for i in range(chips)] for c in range(2)]
    piece = own // chips
    gu_piece = lax.dynamic_slice_in_dim(w_gate_up, chip * piece, piece, 0)
    dn_piece = lax.dynamic_slice_in_dim(w_down, chip * piece, piece, 0)
    both = jnp.concatenate(
        [
            lax.dynamic_slice_in_dim(gu_piece, core * half, half, 2),
            lax.dynamic_slice_in_dim(gu_piece, HID + core * half, half, 2),
            lax.dynamic_slice_in_dim(dn_piece, core * half, half, 2),
        ],
        axis=2,
    )
    both = both.reshape(piece, grps, local_experts, 3 * half).transpose(1, 2, 0, 3)
    both = lax.all_to_all(both, "grp", 0, 0, tiled=True)
    both = lax.all_gather(both, "rep", axis=0, tiled=False, axis_index_groups=same_core)
    both = both.transpose(2, 1, 0, 3, 4).reshape(local_experts, width, 3 * half)
    wgu, wdn = both[:, :, : 2 * half], both[:, :, 2 * half :]

    tokens_f = tokens.astype(F32)
    inverse_one = lax.rsqrt(jnp.mean(tokens_f * tokens_f, axis=1, keepdims=True) + EPS)
    normed_one = tokens_f * inverse_one
    act_one = (normed_one * gain_one).astype(BF)
    act_plane = lax.all_gather(act_one, "rep", axis=0, tiled=True, axis_index_groups=groups)
    prefix_plane = lax.all_gather(prefix_len, "rep", axis=0, tiled=True, axis_index_groups=groups)
    cos, sin = rope_tables(seq)
    projected = dot(act_plane, qkv_head).reshape(heads, seq, QPK + 2, HEAD_WIDTH)
    cos_b, sin_b = cos[None, :, None, :], sin[None, :, None, :]
    turned = rotate(projected[:, :, : QPK + 1], cos_b, sin_b).astype(BF)
    query = turned[:, :, :QPK]
    key = turned[:, :, QPK]
    value = projected[:, :, QPK + 1].astype(BF)
    scale = HEAD_WIDTH ** (-0.5)
    row_pos, col_pos = jnp.arange(seq)[:, None], jnp.arange(seq)[None, :]
    allowed = (col_pos <= row_pos)[None] | (col_pos[None] < prefix_plane[:, None, None])
    scores = jnp.einsum("bsgd,btd->bgst", query, key, preferred_element_type=F32) * scale
    scores = jnp.where(allowed[:, None], scores, -1e30)
    exps = jnp.exp(scores - jnp.max(scores, axis=-1, keepdims=True))
    probs = exps / jnp.sum(exps, axis=-1, keepdims=True)
    probs_low = probs.astype(BF)
    attended = jnp.einsum("bgst,btd->bsgd", probs_low, value, preferred_element_type=F32)
    attended = attended.astype(BF).reshape(heads * seq, qw)
    part = dot(attended, proj_head).astype(BF)
    part = lax.psum_scatter(part, "rep", scatter_dimension=0, tiled=True, axis_index_groups=groups)
    residual = tokens_f + part.astype(F32)
    inverse_two = lax.rsqrt(jnp.mean(residual * residual, axis=1, keepdims=True) + EPS)
    normed_two = residual * inverse_two
    act_two = (normed_two * gain_two).astype(BF)
    gates, kept = routing(expert_ids, priority, dot(act_two, router))

    def column(v):
        v = lax.all_gather(v, "grp", axis=0, tiled=True)
        return lax.all_gather(v, "rep", axis=0, tiled=True, axis_index_groups=pairs)

    def to_owners(v):
        v = lax.psum_scatter(v, "rep", scatter_dimension=0, tiled=True, axis_index_groups=pairs)
        return lax.psum_scatter(v, "grp", scatter_dimension=0, tiled=True).astype(F32)

    dy_all = column(cotangent)
    x_all = column(act_two)
    weight = column(jnp.where(kept, gates, 0.0))
    weight = lax.dynamic_slice_in_dim(weight, grp * local_experts, local_experts, 1).T[:, :, None]
    gate_up = jnp.einsum("td,edh->eth", x_all, wgu, preferred_element_type=F32)
    g, u = gate_up[..., :half], gate_up[..., half:]
    sig = jax.nn.sigmoid(g)
    silu = g * sig
    hidden = silu * u
    hidden_w = (hidden * weight).astype(BF)
    back = jnp.einsum("td,edh->eth", dy_all, wdn, preferred_element_type=F32)
    grad_gate_part = jnp.sum(back * hidden, axis=2)
    grad_hidden = back * weight
    ggu = jnp.concatenate(
        [grad_hidden * u * sig * (1.0 + g * (1.0 - sig)), grad_hidden * silu], axis=2
    ).astype(BF)
    out_part = jnp.einsum("eth,edh->td", hidden_w, wdn, preferred_element_type=F32).astype(BF)
    gact_part = jnp.einsum("eth,edh->td", ggu, wgu, preferred_element_type=F32).astype(BF)
    gact = to_owners(gact_part)
    grad_gates = lax.psum_scatter(
        grad_gate_part.T, "rep", scatter_dimension=0, tiled=True, axis_index_groups=pairs
    )
    grad_gates = lax.all_to_all(grad_gates, "grp", 0, 1, tiled=True)
    grad_gates = jnp.where(kept, grad_gates, 0.0)
    out = to_owners(out_part)
    output = (residual + out).astype(BF)
    grad_gu, grad_dn = expert_grads_general(reps, grps, x_all, dy_all, ggu, hidden_w)
    grad_gu = grad_gu.reshape(own, EXPERTS, 2 * HID)
    grad_dn = grad_dn.reshape(own, EXPERTS, HID)

    grad_logits = (gates * (grad_gates - jnp.sum(gates * grad_gates, axis=1, keepdims=True))).astype(BF)
    gact = gact + dot(grad_logits, router.T)
    router_term = dot(act_two.T, grad_logits)
    gain_two_term = jnp.sum(gact * normed_two, axis=0)
    scaled = gact * gain_two
    dy = cotangent.astype(F32)
    grad_residual = dy + inverse_two * (
        scaled - normed_two * jnp.mean(scaled * normed_two, axis=1, keepdims=True)
    )
    gres_low = grad_residual.astype(BF)

    gres_plane = lax.all_gather(gres_low, "rep", axis=0, tiled=True, axis_index_groups=groups)
    proj_term = dot(attended.T, gres_plane)
    grad_att = dot(gres_plane, proj_head.T).astype(BF).reshape(heads, seq, QPK, HEAD_WIDTH)
    grad_value = jnp.einsum("bgst,bsgd->btd", probs_low, grad_att, preferred_element_type=F32)
    grad_probs = jnp.einsum("bsgd,btd->bgst", grad_att, value, preferred_element_type=F32)
    grad_scores = (
        probs * (grad_probs - jnp.sum(probs * grad_probs, axis=-1, keepdims=True))
    ).astype(BF)
    grad_query = jnp.einsum("bgst,btd->bsgd", grad_scores, key, preferred_element_type=F32) * scale
    grad_key = jnp.einsum("bgst,bsgd->btd", grad_scores, query, preferred_element_type=F32) * scale
    turned_back = rotate(
        jnp.concatenate([grad_query, grad_key[:, :, None]], axis=2), cos_b, -sin_b
    )
    gproj = jnp.concatenate([turned_back, grad_value[:, :, None]], axis=2).astype(BF)
    gproj = gproj.reshape(heads * seq, qw + 2 * hw)
    qkv_term = dot(act_plane.T, gproj)
    gact_one = dot(gproj, qkv_head.T).astype(BF)
    gact_one = lax.psum_scatter(
        gact_one, "rep", scatter_dimension=0, tiled=True, axis_index_groups=groups
    ).astype(F32)
    gain_one_term = jnp.sum(gact_one * normed_one, axis=0)
    scaled_one = gact_one * gain_one
    grad_tokens = grad_residual + inverse_one * (
        scaled_one - normed_one * jnp.mean(scaled_one * normed_one, axis=1, keepdims=True)
    )

    qkv_own = lax.psum_scatter(qkv_term.astype(BF), "grp", scatter_dimension=0, tiled=True)
    proj_sum = lax.psum(proj_term.astype(BF), "grp")
    if groups is not None:
        across = [[i + heads * j for j in range(reps // heads)] for i in range(heads)]
        qkv_own = lax.psum(qkv_own, "rep", axis_index_groups=across)
        proj_sum = lax.psum(proj_sum, "rep", axis_index_groups=across)
    qkv_own = lax.all_gather(qkv_own, "rep", axis=0, tiled=False, axis_index_groups=groups)
    qkv_own = qkv_own.astype(F32)
    grad_qkv = jnp.concatenate(
        [
            qkv_own[:, :, lo:hi].transpose(1, 0, 2).reshape(own, -1)
            for lo, hi in ((0, qw), (qw, qw + hw), (qw + hw, qw + 2 * hw))
        ],
        axis=1,
    )
    proj_all = lax.all_gather(proj_sum, "rep", axis=0, tiled=True, axis_index_groups=groups)
    grad_proj = lax.dynamic_slice_in_dim(proj_all, grp * own, own, 0).astype(F32)
    terms = jnp.concatenate([gain_one_term[:, None], gain_two_term[:, None], router_term], axis=1)
    terms = lax.psum(lax.psum_scatter(terms, "grp", scatter_dimension=0, tiled=True), "rep")
    return (
        output,
        grad_tokens,
        terms[:, 0],
        grad_qkv,
        grad_proj,
        terms[:, 1],
        terms[:, 2:],
        grad_gu,
        grad_dn,
    )


def shards(
    tokens,
    attn_gain,
    query_key_value_weight,
    attn_proj,
    mlp_gain,
    w_router,
    w_gate_up,
    w_down,
    prefix_len,
    expert_ids,
    priority,
    cotangent,
):
    own, width = attn_gain.shape[0], tokens.shape[1]
    small = jnp.concatenate(
        [attn_gain[None], mlp_gain[None], jnp.zeros((14, own), BF), w_router.T], axis=0
    )
    prefix = jnp.broadcast_to(prefix_len.astype(F32), (8, 128))
    half = HEAD_WIDTH // 2
    inverse_freq = np.float32(10000.0) ** (-np.arange(half, dtype=np.float32) * np.float32(2.0 / HEAD_WIDTH))
    angles = np.arange(tokens.shape[0], dtype=np.float32)[:, None] * inverse_freq[None, :]
    cos_t = jnp.asarray(np.tile(np.cos(angles), (1, 4)), F32)
    sin = np.sin(angles)
    sin_t = jnp.asarray(np.tile(np.concatenate([-sin, sin], axis=1), (1, 2)), F32)
    parts = front(
        tokens, cotangent, w_gate_up, w_down, query_key_value_weight, attn_proj, small, expert_ids,
        priority.reshape(expert_ids.shape), prefix, cos_t, sin_t)
    wide, grad_tokens, qkv_own, proj_own, terms, out_parts = back(parts, tokens, cos_t, sin_t)
    grad_gu, grad_dn, grad_qkv, grad_proj, output, grad_router = finish(
        wide, qkv_own, proj_own.reshape(own, width), parts[13], out_parts, terms)
    return (
        output,
        grad_tokens,
        terms[0],
        grad_qkv,
        grad_proj,
        terms[1],
        grad_router.T,
        grad_gu.reshape(own, EXPERTS, 2 * HID),
        grad_dn.reshape(own, EXPERTS, HID),
    )


def solution(mesh):
    tok, par = ("rep", "grp"), "grp"
    in_specs = (
        P(tok, None),
        P(par),
        P(par, None),
        P(par, None),
        P(par),
        P(par, None),
        P(par, None, None),
        P(par, None, None),
        P(tok),
        P(tok, None),
        P(tok, None),
        P(tok, None),
    )
    out_specs = (
        P(tok, None),
        P(tok, None),
        P(par),
        P(par, None),
        P(par, None),
        P(par),
        P(par, None),
        P(par, None, None),
        P(par, None, None),
    )
    reps, grps = mesh.shape["rep"], mesh.shape["grp"]

    def body(*args):
        if (reps, grps) == (8, 4):
            return shards(*args)
        return shards_general(reps, grps, *args)

    return jax.shard_map(body, mesh=mesh, in_specs=in_specs, out_specs=out_specs, check_vma=False)
```

```python
import jax
import jax.numpy as jnp
import numpy as np
from jax import lax
from jax.experimental import pallas as pl
from jax.experimental.pallas import tpu as pltpu
from jax.sharding import PartitionSpec as P

QUERY_HEADS = 24
KEY_VALUE_HEADS = 8
HEAD_WIDTH = 64
HID = 512
EXPERTS = 16
CAP = 72
EPS = 1e-05
BF = jnp.bfloat16
F32 = jnp.float32
QPK = QUERY_HEADS // KEY_VALUE_HEADS
BIG = 1 << 20
MESH = pl.DeviceIdType.MESH


def dot(a, b):
    return jnp.dot(a, b, preferred_element_type=F32)


def rope_tables(length):
    half = HEAD_WIDTH // 2
    position = jnp.arange(length, dtype=F32)[:, None]
    inverse_freq = 10000.0 ** (-jnp.arange(half, dtype=F32) * 2.0 / HEAD_WIDTH)
    angles = position * inverse_freq[None, :]
    return jnp.cos(angles), jnp.sin(angles)


def rotate(v, cos, sin):
    half = HEAD_WIDTH // 2
    a, b = v[..., :half], v[..., half:]
    return jnp.concatenate([a * cos - b * sin, b * cos + a * sin], axis=-1)


def choices(expert_ids, priority):
    seq, top = expert_ids.shape
    choose = expert_ids[:, :, None] == jnp.arange(EXPERTS, dtype=jnp.int32)[None, None, :]
    chosen = jnp.any(choose, axis=1)
    rank_of = jnp.sum(jnp.where(choose, priority.reshape(seq, top)[:, :, None], 0), axis=1)
    rank_of = jnp.where(chosen, rank_of, BIG)
    slot = jnp.sum((rank_of[None, :, :] < rank_of[:, None, :]).astype(jnp.int32), axis=1)
    return chosen, chosen & (slot < CAP)


def routing(expert_ids, priority, logits):
    chosen, kept = choices(expert_ids, priority)
    top_logit = jnp.max(jnp.where(chosen, logits, -jnp.inf), axis=1, keepdims=True)
    gate_exp = jnp.where(chosen, jnp.exp(jnp.where(chosen, logits - top_logit, 0.0)), 0.0)
    gates = gate_exp / jnp.sum(gate_exp, axis=1, keepdims=True)
    return gates, kept


def place():
    r, z = lax.axis_index("rep"), lax.axis_index("grp")
    return r // 4, (r // 2) % 2, r % 2, z


def flip(bit, by):
    return bit + by * (1 - 2 * bit)


def turn(v, cos, sin):
    lane = lax.broadcasted_iota(jnp.int32, v.shape, 1)
    partner = jnp.where(lax.rem(lane, 64) < 32, pltpu.roll(v, 96, 1), pltpu.roll(v, 32, 1))
    return v * cos + partner * sin


def gradient_rows(q3, x, dy, ggu, hw, gw):
    half = HID // 2

    def side(ref):
        return jnp.concatenate(
            [ref[:, :, :, pl.ds(pl.multiple_of(zz * 384 + q3 * 128, 128), 128)].reshape(1024, 128)
             for zz in range(4)], axis=1)
    xs, ds = side(x), side(dy)

    def one(j, _):
        up = lax.dot_general(xs, ggu[j], (((0,), (0,)), ((), ())), preferred_element_type=F32).astype(BF)
        dn = lax.dot_general(ds, hw[j], (((0,), (0,)), ((), ())), preferred_element_type=F32).astype(BF)
        for zz in range(4):
            for p in range(4):
                for h in range(2):
                    at = zz * 128 + p * 32 + h * 16
                    gw[p, h, zz, j, :, : 2 * half] = up[at : at + 16]
                    gw[p, h, zz, j, :, 2 * half :] = dn[at : at + 16]
        return 0
    lax.fori_loop(0, 4, one, 0)


def front_kernel(tok, dy, w_gu, w_dn, qkv, proj, small, ids_t, prio, prefix, cos_t, sin_t,
                 o_x, o_dy, o_ggu, o_hw, o_act, o_q, o_k, o_v, o_probs, o_att, o_qkvw, o_projw,
                 o_small, o_res, o_gates, o_kept, o_gsum, o_osum, o_gw, o_r1,
                 smalls, qkvw, projw, projq, actp, pre, pr, qs, ks, vs, probs, att, part, sibr, sums, plr,
                 xall, dyall, wbuf, ggu, hw, gpart, ggp, gsib,
                 gsum, res, gates, kept, qwin, wst, wcol, wpiece, gw,
                 s_small, r_small, s_qkv, r_qkv, s_pz, r_pz, s_pq, r_pq, s_wz, r_wz, s_wp, r_wp,
                 s_act, r_act, s_pre, r_pre, s_actc, r_actc, s_prec, r_prec, s_sib, r_sib, s_pl, r_pl,
                 s_x, r_x, s_xc, r_xc, s_y, r_y, s_yc, r_yc,
                 s_gc, r_gc, s_oc, r_oc, s1, r1, sl):
    y, x, c, z = place()
    half = HID // 2

    def slot(a, b):
        return flip(y, a * c + b * (1 - c)) * 2 + flip(x, a * (1 - c) + b * c)

    p0, p1, p2, p3 = slot(0, 0), slot(1, 0), slot(0, 1), slot(1, 1)
    peers = (p1, p2, p3)
    d1, d2, dsib = (p1 * 2 + c, z), (p2 * 2 + c, z), (p0 * 2 + 1 - c, z)
    dpl = [(p * 2 + c, z) for p in peers]
    zk = [lax.rem(z + k, 4) for k in range(4)]
    zf = [lax.rem(z + 4 - k, 4) for k in range(4)]
    dz = [(p0 * 2 + c, zz) for zz in zk]

    barrier = pltpu.get_barrier_semaphore()
    for to in dpl + dz[1:] + [dsib]:
        pl.semaphore_signal(barrier, 1, device_id=to, device_id_type=MESH)
    pl.semaphore_wait(barrier, 7)

    def remote(src, dst, s, r, to):
        return pltpu.make_async_remote_copy(src, dst, s, r, device_id=to, device_id_type=MESH)

    def c_small(k):
        return remote(small, smalls.at[z], s_small.at[k - 1], r_small.at[k - 1], dz[k])

    def rows(zz, pp):
        return pl.ds(pl.multiple_of(zz * 384 + pp * 96, 96), 96)

    def c_wz(k):
        return remote(wpiece.at[zk[k]], wbuf.at[:, rows(z, p0)], s_wz.at[k - 1], r_wz.at[k - 1], dz[k])

    def c_wp(k, i):
        zz = zf[k]
        who, pp = ((d1, p0), (d2, p0), (d2, p1))[i]
        src = wpiece.at[z] if (k == 0 and i < 2) else wbuf.at[:, rows(zz, pp)]
        return remote(src, wbuf.at[:, rows(zz, pp)], s_wp.at[k, i], r_wp.at[k, i], who)

    def quarter(p):
        return pl.ds(pl.multiple_of(p * 48, 48), 48)

    def c_pz(k):
        src = proj.at[pl.ds(pl.multiple_of(c * 192 + p0 * 48, 48), 48)]
        return remote(src, projq.at[k - 1], s_pz.at[k - 1], r_pz.at[k - 1], dz[k])

    def c_pq(k, owner):
        return remote(projq.at[k - 1], projw.at[quarter(p0)], s_pq.at[k - 1], r_pq.at[p0], (owner * 2 + c, z))

    def c_pq_in(i):
        return remote(projq.at[0], projw.at[quarter(peers[i])], s_pq.at[0], r_pq.at[peers[i]], dpl[i])

    def c_act(i):
        blk = actp.at[c, p1 if i == 2 else p0]
        return remote(blk, blk, s_act.at[i], r_act.at[i], d1 if i == 0 else d2)

    def c_pre(i):
        blk = pre.at[c, p1 if i == 2 else p0]
        return remote(blk, blk, s_pre.at[i], r_pre.at[i], d1 if i == 0 else d2)

    def c_actc(i):
        p = (p0, p1, p2, p3)[i]
        return remote(actp.at[c, p], actp.at[c, p], s_actc.at[i], r_actc.at[i], dsib)

    def c_prec(i):
        p = (p0, p1, p2, p3)[i]
        return remote(pre.at[c, p], pre.at[c, p], s_prec.at[i], r_prec.at[i], dsib)

    def c_sib():
        return remote(part, sibr, s_sib, r_sib, dsib)

    def c_pl(i):
        return remote(sums.at[i], plr.at[i], s_pl.at[i], r_pl.at[i], d2 if i == 1 else d1)

    def chain(at, s, r, sc=None, rc=None):
        def hop(h, d, send):
            block = z - (h - 1) if d == 0 else z + (h - 1)
            if not send:
                block = z - h if d == 0 else z + h
            return remote(at(block), at(block), s.at[d, h - 1], r.at[d, h - 1],
                          (p0 * 2 + c, z + 1 if d == 0 else z - 1))

        def may(h, d, send):
            if send:
                return (z < 3) & (z >= h - 1) if d == 0 else (z > 0) & (z <= 4 - h)
            return z >= h if d == 0 else z <= 3 - h

        def across(h, d):
            block = z - h if d == 0 else z + h
            return remote(at(block), at(block), sc.at[d, h - 1], rc.at[d, h - 1], dsib)

        def over():
            return remote(at(z), at(z), sc.at[2, 0], rc.at[2, 0], dsib)

        def send(h):
            for d in range(2):
                @pl.when(may(h, d, True))
                def _(d=d):
                    hop(h, d, True).start()
            if h == 1 and sc is not None:
                over().start()

        def recv(h):
            for d in range(2):
                @pl.when(may(h, d, False))
                def _(d=d):
                    hop(h, d, False).wait_recv()
                    if sc is not None:
                        across(h, d).start()

        def finish():
            over().wait_recv()
            for h in (1, 2, 3):
                for d in range(2):
                    @pl.when(may(h, d, False))
                    def _(d=d, h=h):
                        across(h, d).wait_recv()

        def sent():
            if sc is not None:
                over().wait_send()
            for h in (1, 2, 3):
                for d in range(2):
                    @pl.when(may(h, d, True))
                    def _(d=d, h=h):
                        hop(h, d, True).wait_send()
                    if sc is not None:
                        @pl.when(may(h, d, False))
                        def _(d=d, h=h):
                            across(h, d).wait_send()
        return send, recv, finish, sent

    x_send, x_recv, x_finish, x_sent = chain(lambda b: xall.at[c, b], s_x, r_x, s_xc, r_xc)
    y_send, y_recv, y_finish, y_sent = chain(lambda b: dyall.at[c, b], s_y, r_y, s_yc, r_yc)
    q_send, q_recv, _, q_sent = chain(
        lambda b: qkvw.at[pl.ds(pl.multiple_of(b * 384, 384), 384)], s_qkv, r_qkv)

    opart, osib, osum = part, sibr, sums

    def copy1(h, b):
        return remote(gw.at[slot(1, b), h], o_r1.at[h, b], s1.at[h, b], r1.at[h, b], d1)
    g_c = remote(gpart, gsib, s_gc, r_gc, dsib)
    o_c = remote(opart, osib, s_oc, r_oc, dsib)

    def weights_a(k):
        if k:
            c_wz(k).wait_recv()
        c_wp(k, 0).start()
        if k == 0:
            c_wp(0, 1).start()

    def weights_b(k):
        c_wp(k, 0).wait_recv()
        if k:
            c_wp(k, 1).start()
        c_wp(k, 2).start()

    for k in (1, 2, 3):
        c_small(k).start()
    local = [pltpu.make_async_copy(small, smalls.at[z], sl.at[0]),
             pltpu.make_async_copy(dy, dyall.at[c, z], sl.at[3])]

    def window(off, width, at, n):
        src = qkv.at[:, pl.ds(pl.multiple_of(off, 128), width)]
        return pltpu.make_async_copy(src, qwin.at[:, pl.ds(at, width)], sl.at[n])
    mine = p0 * 96
    windows = [window(384 * p0 + 128 * c, 256, 0, 1), window(1536 + 128 * p0, 128, 256, 2),
               window(2048 + 128 * p0, 128, 384, 5)]
    pieces = [pltpu.make_async_copy(
        ref.at[pl.ds(pl.multiple_of(mine, 96), 96), :, pl.ds(pl.multiple_of(off, half), half)],
        wst.at[:, :, pl.ds(i * half, half)], sl.at[6 + i])
        for i, (ref, off) in enumerate(((w_gu, c * half), (w_gu, HID + c * half), (w_dn, c * half)))]
    for one in local + windows + pieces:
        one.start()
    own_proj = pltpu.make_async_copy(proj.at[pl.ds(pl.multiple_of(c * 192, 192), 192)], projw, sl.at[4])

    @pl.when(z == p0)
    def _():
        own_proj.start()
    for one in windows:
        one.wait()
    cols = qwin[...].astype(F32)
    own_rows = pl.ds(pl.multiple_of(z * 384, 384), 384)
    for at, lo, width in ((0, 0, 256), (192, 256, 128), (256, 384, 128)):
        part_ = cols[:, lo : lo + width]
        part_ = jnp.where(c == 0, part_, pltpu.roll(part_, width - 64, 1)).astype(BF)
        qkvw[own_rows, at : at + (192 if at == 0 else 64)] = part_[:, : 192 if at == 0 else 64]

    tok_f = tok[...].astype(F32)
    inv1 = lax.rsqrt(jnp.mean(tok_f * tok_f, axis=1, keepdims=True) + EPS)
    for k in (1, 2, 3):
        c_small(k).wait_recv()
    q_send(1)
    local[0].wait()
    gain1 = jnp.concatenate([smalls[i, 0:1, :] for i in range(4)], axis=1).astype(F32)
    actp[c, p0] = (tok_f * inv1 * gain1).astype(BF)
    pre[c, p0] = prefix[...]
    for i in range(2):
        c_act(i).start()
        c_pre(i).start()
    c_actc(0).start()
    c_prec(0).start()
    chosen_f = jnp.zeros((128, 128), F32)
    rank_of = jnp.zeros((128, 128), F32)
    lane_e = lax.broadcasted_iota(jnp.int32, (128, 128), 1)
    ids = ids_t[...].astype(F32).T
    for k in range(8):
        hit = ids[:, k : k + 1] == lane_e.astype(F32)
        chosen_f = jnp.where(hit, 1.0, chosen_f)
        rank_of = jnp.where(hit, prio[:, k : k + 1].astype(F32), rank_of)
    rank_of = jnp.where(chosen_f > 0.0, rank_of, 65536.0)
    rank_t = rank_of.T
    slots = jnp.zeros((128, 128), F32)
    for e in range(EXPERTS):
        before = jnp.sum((rank_t[e : e + 1, :] < rank_of[:, e : e + 1]).astype(F32), axis=1, keepdims=True)
        slots = jnp.where(lane_e == e, before, slots)
    kept_f = jnp.where(slots < CAP, chosen_f, 0.0)
    kept[...] = kept_f[:, :EXPERTS]
    q_recv(1)
    q_send(2)

    for one in pieces:
        one.wait()

    def expert_rows(l, _):
        wcol[...] = wst[:, :, pl.ds(pl.multiple_of(l * 128, 128), 128)].astype(F32).reshape(1536, 128)
        for e in range(EXPERTS):
            wpiece[e // 4, e % 4, :, pl.ds(pl.multiple_of(l * 128, 128), 128)] = (
                wcol[pl.ds(e, 96, stride=EXPERTS), :].astype(BF))
        return 0
    lax.fori_loop(0, 6, expert_rows, 0)
    own_piece = pltpu.make_async_copy(wpiece.at[z], wbuf.at[:, rows(z, p0)], sl.at[30])
    own_piece.start()
    weights_a(0)
    q_recv(2)
    q_send(3)
    for k in (1, 2, 3):
        c_pz(k).start()
    for i in range(3):
        c_act(i).wait_recv()
        c_pre(i).wait_recv()
        if i == 0:
            c_act(2).start()
            c_pre(2).start()
        c_actc(i + 1).start()
        c_prec(i + 1).start()
    q_recv(3)
    weights_b(0)
    local[1].wait()

    row = lax.broadcasted_iota(jnp.int32, (128, 128), 0)
    col = lax.broadcasted_iota(jnp.int32, (128, 128), 1)
    causal = col <= row
    col_f = col.astype(F32)

    def attention(cc):
        pr[...] = jnp.dot(actp[cc].reshape(512, 1536), qkvw[...], preferred_element_type=F32).reshape(4, 128, 320)

        def one(i, _):
            lo = turn(pr[i, :, 0:128], cos_t[...], sin_t[...]).astype(BF)
            hi = turn(pr[i, :, 128:256], cos_t[...], sin_t[...]).astype(BF)
            qs[cc, i, 0:128] = lo[:, 0:64]
            qs[cc, i, 128:256] = lo[:, 64:128]
            qs[cc, i, 256:384] = hi[:, 0:64]
            ks[cc, i] = hi[:, 64:128]
            vs[cc, i] = pr[i, :, 256:320].astype(BF)
            sc = lax.dot_general(qs[cc, i], ks[cc, i], (((1,), (1,)), ((), ())), preferred_element_type=F32)
            allowed = causal | (col_f < pre[cc, i, 0:1, :])
            sc = jnp.where(allowed[None], sc.reshape(3, 128, 128) * (64 ** -0.5), -1e30)
            ex = jnp.exp(sc - jnp.max(sc, axis=-1, keepdims=True))
            pb = (ex / jnp.sum(ex, axis=-1, keepdims=True)).reshape(384, 128)
            probs[cc, i] = pb
            at = jnp.dot(pb.astype(BF), vs[cc, i], preferred_element_type=F32).astype(BF)
            for h in range(3):
                att[cc, i, :, h * 64 : (h + 1) * 64] = at[h * 128 : (h + 1) * 128]
            return 0
        lax.fori_loop(0, 4, one, 0)

    attention(c)
    for k in (1, 3, 2):
        c_wz(k).start()
    for i in range(4):
        c_actc(i).wait_recv()
        c_prec(i).wait_recv()
    attention(1 - c)
    for k in (1, 2, 3):
        c_pz(k).wait_recv()
        owner = zf[k]

        @pl.when(owner != p0)
        def _(k=k, owner=owner):
            c_pq(k, owner).start()

        @pl.when(owner == p0)
        def _(k=k):
            projw[quarter(p0)] = projq[k - 1]

    @pl.when(z == p0)
    def _():
        own_proj.wait()

    @pl.when(z != p0)
    def _():
        for i in range(3):
            c_pq_in(i).wait_recv()

    def to_sib(i, _):
        part[i] = jnp.dot(att[1 - c, i], projw[...], preferred_element_type=F32).astype(BF)
        return 0
    lax.fori_loop(0, 4, to_sib, 0)
    c_sib().start()
    c_sib().wait_recv()
    def mixed(p):
        return jnp.dot(att[c, p], projw[...], preferred_element_type=F32) + sibr[p].astype(F32)

    for i in (2, 0):
        sums[i] = mixed(peers[i]).astype(BF)
        c_pl(i).start()
    to_second = mixed(p2)
    residual = tok_f + mixed(p0)
    c_pl(2).wait_recv()
    sums[1] = (to_second + plr[2].astype(F32)).astype(BF)
    c_pl(1).start()
    for i in range(2):
        c_pl(i).wait_recv()
        residual = residual + plr[i].astype(F32)
    res[...] = residual
    inv2 = lax.rsqrt(jnp.mean(residual * residual, axis=1, keepdims=True) + EPS)
    gain2 = jnp.concatenate([smalls[i, 1:2, :] for i in range(4)], axis=1).astype(F32)
    act2 = (residual * inv2 * gain2).astype(BF)
    router = jnp.concatenate([smalls[i, 16:32, :] for i in range(4)], axis=1)
    logits = lax.dot_general(act2, router, (((1,), (1,)), ((), ())), preferred_element_type=F32)
    chosen = chosen_f[:, :EXPERTS] > 0.0
    top = jnp.max(jnp.where(chosen, logits, -1e30), axis=1, keepdims=True)
    ge = jnp.where(chosen, jnp.exp(jnp.where(chosen, logits - top, 0.0)), 0.0)
    gt = ge / jnp.sum(ge, axis=1, keepdims=True)
    gates[...] = gt
    kept_gates = gt * kept[...]
    gate_hi = kept_gates.astype(BF)
    gate_lo = (kept_gates - gate_hi.astype(F32)).astype(BF)
    xall[c, z, :, :1536] = act2
    xall[c, z, :, 1536:] = jnp.concatenate([gate_hi, gate_lo, jnp.zeros((128, 96), BF)], axis=1)
    x_send(1)
    y_send(1)
    weights_a(1)
    weights_a(3)
    weights_b(1)
    weights_b(3)
    x_recv(1)
    x_send(2)
    weights_a(2)
    y_recv(1)
    y_send(2)
    x_recv(2)
    x_send(3)
    weights_b(2)
    y_recv(2)
    y_send(3)
    x_recv(3)
    y_recv(3)
    own_piece.wait()
    for k in range(4):
        c_wp(k, 1).wait_recv()
        c_wp(k, 2).wait_recv()
    x_finish()
    y_finish()

    lane = lax.broadcasted_iota(jnp.int32, (512, 128), 1)
    ggp[...] = jnp.zeros_like(ggp)

    def expert(n, _):
        j, t = n // 2, lax.rem(n, 2)
        gu = jnp.dot(xall[t, :, :, :1536].reshape(512, 1536), wbuf[j, :, : 2 * half], preferred_element_type=F32)
        bk = jnp.dot(dyall[t].reshape(512, 1536), wbuf[j, :, 2 * half :], preferred_element_type=F32)
        mine = lane == z * 4 + j
        both = xall[t, :, :, 1536:].astype(F32).reshape(512, 128)
        w = jnp.sum(jnp.where(mine | (lane == EXPERTS + z * 4 + j), both, 0.0), axis=1, keepdims=True)
        g, u = gu[:, :half], gu[:, half:]
        sg = 1.0 / (1.0 + jnp.exp(-g))
        silu = g * sg
        hid = silu * u
        hw[j, pl.ds(pl.multiple_of(t * 512, 512), 512)] = (hid * w).astype(BF)
        ggp[t] = ggp[t] + jnp.where(mine, jnp.sum(bk * hid, axis=1, keepdims=True), 0.0).reshape(4, 128, 128)
        gh = bk * w
        at = pl.ds(pl.multiple_of(t * 512, 512), 512)
        ggu[j, at, :half] = (gh * u * sg * (1.0 + g * (1.0 - sg))).astype(BF)
        ggu[j, at, half:] = (gh * silu).astype(BF)
        return 0
    lax.fori_loop(0, 8, expert, 0)

    gradient_rows(0, xall, dyall, ggu, hw, gw)
    for h in range(2):
        for b in range(2):
            copy1(h, b).start()
    saves = []

    def save(src, dst):
        one = pltpu.make_async_copy(src, dst, sl.at[9 + len(saves)])
        one.start()
        saves.append(one)
    for src, dst in ((xall, o_x), (dyall, o_dy), (ggu, o_ggu), (hw, o_hw), (actp, o_act), (qs, o_q), (ks, o_k),
                     (vs, o_v), (probs, o_probs), (att, o_att), (qkvw, o_qkvw), (projw, o_projw),
                     (smalls, o_small), (res, o_res), (gates, o_gates), (kept, o_kept)):
        save(src, dst)

    def block(grad, t, n):
        at = pl.ds(pl.multiple_of(t * 512, 512), 512)
        lanes = pl.ds(pl.multiple_of(n * 256, 256), 256)
        acc = jnp.zeros((512, 256), F32)
        for j in range(4):
            a = ggu[j, at] if grad else hw[j, at]
            b = wbuf[j, lanes, : 2 * half] if grad else wbuf[j, lanes, 2 * half :]
            acc = acc + lax.dot_general(a, b, (((1,), (1,)), ((), ())), preferred_element_type=F32)
        return acc.reshape(4, 128, 256), lanes

    def partial(grad, buf):
        def one(n, _):
            v, lanes = block(grad, 1 - c, n)
            buf[:, :, lanes] = v.astype(BF)
            return 0
        lax.fori_loop(0, 6, one, 0)

    def own(grad, sib, dst):
        def one(n, _):
            v, lanes = block(grad, c, n)
            dst[:, :, lanes] = (v + sib[:, :, lanes].astype(F32)).astype(BF)
            return 0
        lax.fori_loop(0, 6, one, 0)

    def put_gate_grads(dst, v):
        hi = v.astype(BF).astype(F32)
        lo = pltpu.roll((v - hi).reshape(512, 128), EXPERTS, 1)
        dst[:, :, 1536:] = jnp.where(lane < EXPERTS, hi.reshape(512, 128), lo).astype(BF).reshape(4, 128, 128)

    def gate_grads(v):
        both = v[..., 1536:].astype(F32).reshape(512, 128)
        return jnp.where(lane < EXPERTS, both + pltpu.roll(both, 128 - EXPERTS, 1), 0.0).reshape(4, 128, 128)

    c_sib().wait_send()
    for i in range(3):
        c_pl(i).wait_send()
    put_gate_grads(gpart, ggp[1 - c])
    partial(True, gpart)
    g_c.start()
    partial(False, opart)
    o_c.start()
    g_c.wait_recv()
    put_gate_grads(gsum, ggp[c] + gate_grads(gsib))
    own(True, gsib, gsum)
    save(gsum, o_gsum)
    o_c.wait_recv()
    own(False, osib, osum)
    save(osum, o_osum)
    save(gw, o_gw)
    for h in range(2):
        for b in range(2):
            copy1(h, b).wait()

    for k in (1, 2, 3):
        for one in (c_small(k), c_pz(k), c_wz(k)):
            one.wait_send()

        @pl.when(zf[k] != p0)
        def _(k=k):
            c_pq(k, zf[k]).wait_send()
    for k in range(4):
        for i in range(3):
            c_wp(k, i).wait_send()
        for one in (c_actc(k), c_prec(k)):
            one.wait_send()
    for i in range(3):
        for one in (c_act(i), c_pre(i)):
            one.wait_send()
    for one in (g_c, o_c):
        one.wait_send()
    x_sent()
    y_sent()
    q_sent()
    for one in saves:
        one.wait()


def front(*args):
    sem, vm = pltpu.SemaphoreType.DMA, pltpu.VMEM
    out = lambda shape, kind=BF: jax.ShapeDtypeStruct(shape, kind)
    outs = (
        out((2, 4, 128, 1664)), out((2, 4, 128, 1536)), out((4, 1024, 512)), out((4, 1024, 256)),
        out((2, 4, 128, 1536)), out((2, 4, 384, 64)), out((2, 4, 128, 64)), out((2, 4, 128, 64)),
        out((2, 4, 384, 128), F32), out((2, 4, 128, 192)), out((1536, 320)), out((192, 1536)),
        out((4, 32, 384)), out((128, 1536), F32), out((128, 16), F32), out((128, 16), F32), out((4, 128, 1664)),
        out((4, 128, 1536)), out((4, 2, 4, 4, 16, 768)), out((2, 2, 4, 4, 16, 768)),
    )
    block, quad = vm((2, 4, 128, 1536), BF), vm((4, 128, 1536), BF)
    three = vm((3, 128, 1536), BF)
    quad_g = vm((4, 128, 1664), BF)
    scratch = [
        vm((4, 32, 384), BF), vm((1536, 320), BF), vm((192, 1536), BF), vm((3, 48, 1536), BF),
        block, vm((2, 4, 8, 128), F32),
        vm((4, 128, 320), F32), vm((2, 4, 384, 64), BF), vm((2, 4, 128, 64), BF), vm((2, 4, 128, 64), BF),
        vm((2, 4, 384, 128), F32), vm((2, 4, 128, 192), BF), quad, quad, quad, three,
        vm((2, 4, 128, 1664), BF), block, vm((4, 1536, 768), BF), vm((4, 1024, 512), BF),
        vm((4, 1024, 256), BF), quad_g, vm((2, 4, 128, 128), F32), quad_g,
        quad_g, vm((128, 1536), F32), vm((128, 16), F32), vm((128, 16), F32),
        vm((384, 512), BF), vm((96, 16, 768), BF), vm((1536, 128), F32), vm((4, 4, 96, 768), BF),
        vm((4, 2, 4, 4, 16, 768), BF),
    ]
    n3, n4, one = sem((3,)), sem((4,)), sem(())
    hops = [sem((2, 3)), sem((2, 3)), sem((3, 3)), sem((3, 3))]
    sems = [
        n3, n3, sem((2, 3)), sem((2, 3)), n3, n3, n3, n4, n3, n3, sem((4, 3)), sem((4, 3)),
        n3, n3, n3, n3, n4, n4, n4, n4, one, one, n3, n3,
        *hops, *hops, one, one, one, one, sem((2, 2)), sem((2, 2)), sem((31,)),
    ]
    vmem, any_ = pl.BlockSpec(memory_space=pltpu.VMEM), pl.BlockSpec(memory_space=pl.ANY)
    return pl.pallas_call(
        front_kernel,
        out_shape=outs,
        in_specs=[vmem, any_, any_, any_, any_, any_, any_, vmem, vmem, vmem, vmem, vmem],
        out_specs=[any_] * len(outs),
        scratch_shapes=scratch + sems,
        compiler_params=pltpu.CompilerParams(
            collective_id=1, has_side_effects=True, vmem_limit_bytes=62 * 1024 * 1024),
        name="front",
    )(*args)


def back_kernel(i_x, i_dy, i_ggu, i_hw, i_act, i_q, i_k, i_v, i_probs, i_att, i_qkvw, i_projw, i_small,
                i_res, i_gates, i_kept, i_gsum, i_osum, i_gw, i_r1, tok, cos_t, sin_t,
                o_e, o_gtok, o_qg, o_pg, o_terms, o_op,
                xb, dyb, ggu, hw, qs, ks, vs, probs, att, qkvw, projw, smalls, res, gates, kept, gown, grecv,
                gw, recv1, send2, recv2, zs, zr, ib, agv,
                gres, gresf, gproj, sibr, plr, qgp, qz, qgo, pgp, pgr, pq2, pgo, terms, tz, tsib, tpl, tout, gtok,
                s1, r1, s2, r2, sz, rz, sa, ra, ss, rs, la,
                s_g, r_g, s_gr, r_gr, s_grc, r_grc, s_sib, r_sib, s_pl, r_pl, s_qz, r_qz, s_qo, r_qo,
                s_qoc, r_qoc, s_p1, r_p1, s_p2, r_p2, s_po, r_po, s_poc, r_poc, s_tz, r_tz, s_ts, r_ts,
                s_tp, r_tp, s_o, r_o, ld, sv):
    y, x, c, z = place()
    half = HID // 2
    wide = 3 * half
    nq = 6

    def slot(a, b):
        return flip(y, a * c + b * (1 - c)) * 2 + flip(x, a * (1 - c) + b * c)

    p0, p1, p2, p3 = slot(0, 0), slot(1, 0), slot(0, 1), slot(1, 1)
    peers = (p1, p2, p3)
    d1, d2, dsib = (p1 * 2 + c, z), (p2 * 2 + c, z), (p0 * 2 + 1 - c, z)
    dpl = [(p * 2 + c, z) for p in peers]
    zk = [lax.rem(z + k, 4) for k in range(4)]
    dz = [(p0 * 2 + c, zz) for zz in zk]

    loads = {}

    def load(name, src, dst):
        loads[name] = pltpu.make_async_copy(src, dst, ld.at[len(loads)])
        loads[name].start()
    load("gw", i_gw, gw.at[0])
    load("r1", i_r1, recv1.at[pl.ds(0, 2)])
    load("x", i_x.at[:, :, :, pl.ds(0, 1536)], xb)
    load("ggu", i_ggu, ggu)
    load("dy", i_dy, dyb)
    load("hw", i_hw, hw)
    load("gown", i_gsum.at[z], gown)
    for name, src, dst in (("res", i_res, res), ("gates", i_gates, gates), ("kept", i_kept, kept),
                           ("small", i_small, smalls),
                           ("projw", i_projw, projw), ("probs", i_probs, probs), ("q", i_q, qs), ("k", i_k, ks),
                           ("v", i_v, vs), ("att", i_att, att), ("qkvw", i_qkvw, qkvw)):
        load(name, src, dst)

    barrier = pltpu.get_barrier_semaphore()
    for to in dpl + dz[1:] + [dsib]:
        pl.semaphore_signal(barrier, 1, device_id=to, device_id_type=MESH)
    pl.semaphore_wait(barrier, 7)

    def remote(src, dst, s, r, to):
        return pltpu.make_async_remote_copy(src, dst, s, r, device_id=to, device_id_type=MESH)

    def copy1(q, b):
        return remote(gw.at[q // 2, slot(1, b), lax.rem(q, 2)], recv1.at[q, b], s1.at[q, b], r1.at[q, b], d1)

    def copy2(q):
        return remote(send2.at[lax.rem(q, 2)], recv2.at[q], s2.at[q], r2.at[q], d2)

    def copyz(q, k):
        return remote(zs.at[lax.rem(q, 2), zk[k]], zr.at[q, z], sz.at[q, k - 1], rz.at[q, k - 1], dz[k])

    def rows(q, p):
        return pl.ds(pl.multiple_of(((q // 2) * 8 + p * 2 + lax.rem(q, 2)) * 256, 256), 256)

    def copya(q, i):
        p, who = ((p0, d1), (p0, d2), (p1, d2))[i]
        src = agv.at[lax.rem(q, 2)] if i < 2 else o_e.at[c, rows(q, p)]
        return remote(src, o_e.at[c, rows(q, p)], sa.at[q, i], ra.at[q, i], who)

    def copys(q, i):
        p = (p0, p1, p2, p3)[i]
        src = agv.at[lax.rem(q, 2)] if i == 0 else o_e.at[c, rows(q, p)]
        return remote(src, o_e.at[c, rows(q, p)], ss.at[q, i], rs.at[q, i], dsib)

    def keep(q):
        return pltpu.make_async_copy(agv.at[lax.rem(q, 2)], o_e.at[c, rows(q, p0)], la.at[q])

    def c_g(k):
        return remote(i_gsum.at[zk[k]], grecv.at[k - 1], s_g.at[k - 1], r_g.at[k - 1], dz[k])

    def c_o(k):
        return remote(i_osum.at[zk[k]], o_op.at[k], s_o.at[k - 1], r_o.at[k - 1], dz[k])

    def c_gr(i):
        blk = gres.at[c, p1 if i == 2 else p0]
        return remote(blk, blk, s_gr.at[i], r_gr.at[i], d1 if i == 0 else d2)

    def c_grc(i):
        p = (p0, p1, p2, p3)[i]
        return remote(gres.at[c, p], gres.at[c, p], s_grc.at[i], r_grc.at[i], dsib)

    def c_sib():
        return remote(dyb.at[0], sibr, s_sib, r_sib, dsib)

    def c_pl(i):
        return remote(dyb.at[1, i], plr.at[i], s_pl.at[i], r_pl.at[i], d2 if i == 1 else d1)

    def c_qz(k):
        return remote(qgp.at[zk[k]], qz.at[k - 1], s_qz.at[k - 1], r_qz.at[k - 1], dz[k])

    def c_qo(i):
        dst = o_qg.at[(p1 if i == 2 else p0) * 2 + c]
        return remote(dst if i == 2 else qgo, dst, s_qo.at[i], r_qo.at[i], d1 if i == 0 else d2)

    def c_qoc(i):
        r = (p0, p1, p2, p3)[i] * 2 + c
        return remote(qgo if i == 0 else o_qg.at[r], o_qg.at[r], s_qoc.at[i], r_qoc.at[i], dsib)

    def c_p1(i):
        return remote(pgp.at[peers[i]], pgr.at[p0], s_p1.at[i], r_p1.at[i], dpl[i])

    def c_p2(k):
        return remote(pgr.at[zk[k]], pq2.at[k - 1], s_p2.at[k - 1], r_p2.at[k - 1], dz[k])

    def c_po(i):
        dst = o_pg.at[c, p1 if i == 2 else p0]
        return remote(dst if i == 2 else pgo, dst, s_po.at[i], r_po.at[i], d1 if i == 0 else d2)

    def c_poc(i):
        p = (p0, p1, p2, p3)[i]
        return remote(pgo if i == 0 else o_pg.at[c, p], o_pg.at[c, p], s_poc.at[i], r_poc.at[i], dsib)

    def lanes_of(zz):
        return pl.ds(pl.multiple_of(zz * 384, 384), 384)

    def c_tz(k):
        return remote(terms.at[:, lanes_of(zk[k])], tz.at[k], s_tz.at[k - 1], r_tz.at[k - 1], dz[k])

    def c_ts():
        return remote(tz.at[0], tsib, s_ts, r_ts, dsib)

    def c_tp(i):
        return remote(tpl.at[p0], tpl.at[p0], s_tp.at[i], r_tp.at[i], dpl[i])

    saves = [pltpu.make_async_copy(gtok, o_gtok, sv.at[0]),
             pltpu.make_async_copy(qgo, o_qg.at[p0 * 2 + c], sv.at[1]),
             pltpu.make_async_copy(pgo, o_pg.at[c, p0], sv.at[2]),
             pltpu.make_async_copy(tout, o_terms, sv.at[3])]
    own_out = pltpu.make_async_copy(i_osum.at[z], o_op.at[0], sv.at[5])
    own_out.start()
    act_load = pltpu.make_async_copy(i_act, xb, sv.at[4])

    for k in (1, 2, 3):
        c_g(k).start()
    loads["gw"].wait()
    loads["r1"].wait()
    loads["x"].wait()
    loads["ggu"].wait()
    loads["dy"].wait()
    loads["hw"].wait()

    def stage1(q):
        @pl.when(lax.rem(q, 2) == 0)
        def _():
            gradient_rows(q // 2, xb, dyb, ggu, hw, gw.at[q // 2])
        for b in range(2):
            copy1(q, b).start()

    def stage2(q):
        @pl.when(q >= 2)
        def _():
            for b in range(2):
                copy1(q, b).wait_recv()

        def one(zz, _):
            send2[lax.rem(q, 2), zz] = (gw[q // 2, p2, lax.rem(q, 2), zz].astype(F32)
                                        + recv1[q, 1, zz].astype(F32)).astype(BF)
            return 0
        lax.fori_loop(0, 4, one, 0)
        copy2(q).start()

    def stage3(q):
        copy2(q).wait()

        def one(zz, _):
            zs[lax.rem(q, 2), zz] = (gw[q // 2, p0, lax.rem(q, 2), zz].astype(F32) + recv1[q, 0, zz].astype(F32)
                                     + recv2[q, zz].astype(F32)).astype(BF)
            return 0
        lax.fori_loop(0, 4, one, 0)
        for k in range(1, 4):
            copyz(q, k).start()
        zr[q, z] = zs[lax.rem(q, 2), z]

    def stage4(q):
        for k in range(1, 4):
            copyz(q, k).wait()

        @pl.when(q >= 2)
        def _():
            copya(q - 2, 0).wait_send()
            copya(q - 2, 1).wait_send()
            copys(q - 2, 0).wait_send()
            keep(q - 2).wait()
        for zz in range(4):
            for j in range(4):
                for l in range(wide // 128):
                    ib[l, pl.ds(zz * 4 + j, 16, stride=EXPERTS), :] = (
                        zr[q, zz, j, :, l * 128 : (l + 1) * 128].astype(F32))
        for l in range(wide // 128):
            agv[lax.rem(q, 2), :, l * 128 : (l + 1) * 128] = ib[l].astype(BF)
        copya(q, 0).start()
        copys(q, 0).start()
        keep(q).start()

    def stage5(q):
        copya(q, 0).wait_recv()
        copya(q, 1).start()
        copya(q, 2).start()
        copys(q, 1).start()

    def stage6(q):
        copya(q, 1).wait_recv()
        copya(q, 2).wait_recv()
        copys(q, 2).start()
        copys(q, 3).start()

    def stage7(q):
        for i in range(4):
            copys(q, i).wait_recv()

    def norm_two():
        r = res[...]
        inv = lax.rsqrt(jnp.mean(r * r, axis=1, keepdims=True) + EPS)
        return inv, r * inv

    def norm_one():
        t = tok[...].astype(F32)
        inv = lax.rsqrt(jnp.mean(t * t, axis=1, keepdims=True) + EPS)
        return inv, t * inv

    def gain(row):
        return jnp.concatenate([smalls[i, row : row + 1, :] for i in range(4)], axis=1).astype(F32)

    def event_residual():
        for name in ("gown", "res", "gates", "kept", "small"):
            loads[name].wait()
        for k in (1, 2, 3):
            c_g(k).wait_recv()

        def gate_part(v):
            return v[:, 1536 : 1536 + EXPERTS].astype(F32) + v[:, 1536 + EXPERTS : 1536 + 2 * EXPERTS].astype(F32)
        gg = (gate_part(gown[...]) + gate_part(grecv[0]) + gate_part(grecv[1]) + gate_part(grecv[2])) * kept[...]
        gt = gates[...]
        gl = (gt * (gg - jnp.sum(gt * gg, axis=1, keepdims=True))).astype(BF)
        router_t = jnp.concatenate([smalls[i, 16:32, :] for i in range(4)], axis=1)
        ga = jnp.dot(gl, router_t, preferred_element_type=F32)
        ga = ga + gown[:, :1536].astype(F32)
        for k in range(3):
            ga = ga + grecv[k, :, :1536].astype(F32)
        inv, normed = norm_two()
        terms[8:24, :] = lax.dot_general(gl, xb[c, z], (((0,), (0,)), ((), ())), preferred_element_type=F32)
        terms[1:2, :] = jnp.sum(ga * normed, axis=0, keepdims=True)
        scaled = ga * gain(1)
        gr = dyb[c, z].astype(F32) + inv * (scaled - normed * jnp.mean(scaled * normed, axis=1, keepdims=True))
        gresf[...] = gr
        gres[c, p0] = gr.astype(BF)
        for i in range(2):
            c_gr(i).start()
        c_grc(0).start()

    def event_share():
        for k in (1, 2, 3):
            c_o(k).start()
        for i in range(3):
            c_gr(i).wait_recv()
            if i == 0:
                c_gr(2).start()
            c_grc(i + 1).start()
        act_load.start()

    scale = 64 ** -0.5

    def event_attention():
        for name in ("projw", "probs", "q", "k", "v", "att", "qkvw"):
            loads[name].wait()
        for i in range(4):
            c_grc(i).wait_recv()

        def one(n, _):
            cc, i = n // 4, lax.rem(n, 4)
            gb = lax.dot_general(gres[cc, i], projw[...], (((1,), (1,)), ((), ())),
                                 preferred_element_type=F32).astype(BF)
            ga = jnp.concatenate([gb[:, h * 64 : (h + 1) * 64] for h in range(3)], axis=0)
            pb = probs[cc, i]
            gv = lax.dot_general(pb.astype(BF), ga, (((0,), (0,)), ((), ())), preferred_element_type=F32)
            gp = lax.dot_general(ga, vs[cc, i], (((1,), (1,)), ((), ())), preferred_element_type=F32)
            gs = (pb * (gp - jnp.sum(pb * gp, axis=-1, keepdims=True))).astype(BF)
            gq = jnp.dot(gs, ks[cc, i], preferred_element_type=F32) * scale
            gk = lax.dot_general(gs, qs[cc, i], (((0,), (0,)), ((), ())), preferred_element_type=F32) * scale
            lo = jnp.concatenate([gq[0:128], gq[128:256]], axis=1)
            hi = jnp.concatenate([gq[256:384], gk], axis=1)
            gproj[cc, i, :, 0:128] = turn(lo, cos_t[...], -sin_t[...]).astype(BF)
            gproj[cc, i, :, 128:256] = turn(hi, cos_t[...], -sin_t[...]).astype(BF)
            gproj[cc, i, :, 256:320] = gv.astype(BF)
            return 0
        lax.fori_loop(0, 8, one, 0)

        def to_sib(i, _):
            dyb[0, i] = lax.dot_general(gproj[1 - c, i], qkvw[...], (((1,), (1,)), ((), ())),
                                        preferred_element_type=F32).astype(BF)
            return 0
        lax.fori_loop(0, 4, to_sib, 0)
        c_sib().start()
        pg = lax.dot_general(att[...].reshape(1024, 192), gres[...].reshape(1024, 1536), (((0,), (0,)), ((), ())),
                             preferred_element_type=F32)
        pgp[...] = pg.astype(BF).reshape(4, 48, 1536)
        for i in range(3):
            c_p1(i).start()
        pgr[p0] = pgp[p0]

    def event_columns():
        act_load.wait()

        def one(zz, _):
            a = xb[:, :, :, lanes_of(zz)].reshape(1024, 384)
            qgp[zz] = lax.dot_general(a, gproj[...].reshape(1024, 320), (((0,), (0,)), ((), ())),
                                      preferred_element_type=F32).astype(BF)
            return 0
        lax.fori_loop(0, 4, one, 0)
        for k in (1, 2, 3):
            c_qz(k).start()
        c_sib().wait()

        def part(p):
            return lax.dot_general(gproj[c, p], qkvw[...], (((1,), (1,)), ((), ())),
                                   preferred_element_type=F32) + sibr[p].astype(F32)
        for i in (2, 0):
            dyb[1, i] = part(peers[i]).astype(BF)
            c_pl(i).start()
        dyb[1, 1] = part(p2).astype(BF)
        gtok[...] = part(p0)
        for i in range(3):
            c_p1(i).wait_recv()
        for k in (1, 2, 3):
            c_p2(k).start()

    def event_second():
        c_pl(2).wait_recv()
        dyb[1, 1] = (dyb[1, 1].astype(F32) + plr[2].astype(F32)).astype(BF)
        c_pl(1).start()
        for k in (1, 2, 3):
            c_qz(k).wait_recv()
        qgo[...] = (qgp[z].astype(F32) + qz[0].astype(F32) + qz[1].astype(F32) + qz[2].astype(F32)).astype(BF)
        for i in range(2):
            c_qo(i).start()
        c_qoc(0).start()
        saves[1].start()
        for k in (1, 2, 3):
            c_p2(k).wait_recv()
        pgo[...] = (pgr[z].astype(F32) + pq2[0].astype(F32) + pq2[1].astype(F32) + pq2[2].astype(F32)).astype(BF)
        for i in range(2):
            c_po(i).start()
        c_poc(0).start()
        saves[2].start()

    def event_tokens():
        ga = gtok[...]
        for i in range(2):
            c_pl(i).wait_recv()
            ga = ga + plr[i].astype(F32)
        inv, normed = norm_one()
        terms[0:1, :] = jnp.sum(ga * normed, axis=0, keepdims=True)
        scaled = ga * gain(0)
        gtok[...] = gresf[...] + inv * (scaled - normed * jnp.mean(scaled * normed, axis=1, keepdims=True))
        saves[0].start()
        for k in (1, 2, 3):
            c_tz(k).start()
        for copy, over in ((c_qo, c_qoc), (c_po, c_poc)):
            copy(0).wait_recv()
            copy(2).start()
            over(1).start()
            copy(1).wait_recv()
            over(2).start()

    def event_terms():
        for k in (1, 2, 3):
            c_tz(k).wait_recv()
        tz[0] = terms[:, lanes_of(z)] + tz[1] + tz[2] + tz[3]
        c_ts().start()
        for copy, over in ((c_qo, c_qoc), (c_po, c_poc)):
            copy(2).wait_recv()
            over(3).start()
        c_ts().wait()
        tpl[p0] = tz[0] + tsib[...]
        for i in range(3):
            c_tp(i).start()

    def event_last():
        for i in range(3):
            c_tp(i).wait_recv()
        tout[...] = tpl[0] + tpl[1] + tpl[2] + tpl[3]
        saves[3].start()
        for i in range(4):
            c_qoc(i).wait_recv()
            c_poc(i).wait_recv()
        for k in (1, 2, 3):
            c_o(k).wait_recv()

    stages = (stage1, stage2, stage3, stage4, stage5, stage6, stage7)
    lead = 4
    for q in (2, 3):
        stage1(jnp.int32(q))
    for q in range(1):
        stage2(jnp.int32(q))
    events = {2: event_residual, 3: event_share, 4: event_attention, 5: event_columns, 6: event_second,
              7: event_tokens, 8: event_terms, 9: event_last}

    def step(t, _):
        for i, stage in enumerate(stages):
            q = t + lead if i == 0 else t + 2 - i

            @pl.when((q >= 0) & (q < nq))
            def _(stage=stage, q=q):
                stage(q)
        for at, event in events.items():
            @pl.when(t == at)
            def _(event=event):
                event()
        return 0

    lax.fori_loop(0, nq + len(stages) - 2, step, 0)

    def left(q, _):
        @pl.when(q >= 2)
        def _():
            for b in range(2):
                copy1(q, b).wait_send()
        for i in range(1, 4):
            copys(q, i).wait_send()
        copya(q, 2).wait_send()

        @pl.when(q >= nq - 2)
        def _():
            copya(q, 0).wait_send()
            copya(q, 1).wait_send()
            copys(q, 0).wait_send()
            keep(q).wait()
        return 0
    lax.fori_loop(0, nq, left, 0)
    for k in (1, 2, 3):
        for one in (c_g(k), c_o(k), c_qz(k), c_p2(k), c_tz(k)):
            one.wait_send()
    for i in range(3):
        for one in (c_gr(i), c_pl(i), c_qo(i), c_p1(i), c_po(i), c_tp(i)):
            one.wait_send()
    for i in range(4):
        for one in (c_grc(i), c_qoc(i), c_poc(i)):
            one.wait_send()
    for one in saves + [own_out]:
        one.wait()


def back(front_outs, tok, cos_t, sin_t):
    nq, wide = 6, 3 * HID // 2
    sem, vm = pltpu.SemaphoreType.DMA, pltpu.VMEM
    out = lambda shape, kind=BF: jax.ShapeDtypeStruct(shape, kind)
    piece = (4, 4, 16, wide)
    outs = (out((2, 6144, wide)), out((128, 1536), F32), out((8, 384, 320)), out((2, 4, 48, 1536)),
            out((24, 384), F32), out((4, 128, 1536)))
    block, quad, three = vm((2, 4, 128, 1536), BF), vm((4, 128, 1536), BF), vm((3, 128, 1536), BF)
    scratch = [
        block, block, vm((4, 1024, 512), BF), vm((4, 1024, 256), BF), vm((2, 4, 384, 64), BF),
        vm((2, 4, 128, 64), BF), vm((2, 4, 128, 64), BF), vm((2, 4, 384, 128), F32), vm((2, 4, 128, 192), BF),
        vm((1536, 320), BF), vm((192, 1536), BF), vm((4, 32, 384), BF), vm((128, 1536), F32), vm((128, 16), F32), vm((128, 16), F32),
        vm((128, 1664), BF), vm((3, 128, 1664), BF),
        vm((3, 4, 2) + piece, BF), vm((nq, 2) + piece, BF), vm((2,) + piece, BF), vm((nq,) + piece, BF),
        vm((2,) + piece, BF), vm((nq,) + piece, BF), vm((wide // 128, 256, 128), F32), vm((2, 256, wide), BF),
        block, vm((128, 1536), F32), vm((2, 4, 128, 320), BF), quad, three, vm((4, 384, 320), BF),
        vm((3, 384, 320), BF), vm((384, 320), BF), vm((4, 48, 1536), BF), vm((4, 48, 1536), BF),
        vm((3, 48, 1536), BF), vm((48, 1536), BF), vm((24, 1536), F32), vm((4, 24, 384), F32),
        vm((24, 384), F32), vm((4, 24, 384), F32), vm((24, 384), F32), vm((128, 1536), F32),
    ]
    n3, n4, one = sem((3,)), sem((4,)), sem(())
    sems = [
        sem((nq, 2)), sem((nq, 2)), sem((nq,)), sem((nq,)), sem((nq, 3)), sem((nq, 3)), sem((nq, 3)), sem((nq, 3)),
        sem((nq, 4)), sem((nq, 4)), sem((nq,)),
        n3, n3, n3, n3, n4, n4, one, one, n3, n3, n3, n3, n3, n3,
        n4, n4, n3, n3, n3, n3, n3, n3, n4, n4, n3, n3, one, one,
        n3, n3, n3, n3, sem((18,)), sem((6,)),
    ]
    vmem, any_ = pl.BlockSpec(memory_space=pltpu.VMEM), pl.BlockSpec(memory_space=pl.ANY)
    return pl.pallas_call(
        back_kernel,
        out_shape=outs,
        in_specs=[any_] * 20 + [vmem] * 3,
        out_specs=[any_] * len(outs),
        scratch_shapes=scratch + sems,
        compiler_params=pltpu.CompilerParams(
            collective_id=2, has_side_effects=True, vmem_limit_bytes=62 * 1024 * 1024),
        name="back",
    )(*front_outs, tok, cos_t, sin_t)


def finish_kernel(v, qkv, proj, res, parts, terms, gu, dn, g_qkv, g_proj, out, g_router):
    half = HID // 2
    for c in range(2):
        gu[:, c * half : (c + 1) * half] = v[c, :, :half].astype(F32)
        gu[:, HID + c * half : HID + (c + 1) * half] = v[c, :, half : 2 * half].astype(F32)
        dn[:, c * half : (c + 1) * half] = v[c, :, 2 * half :].astype(F32)
    heads = range(qkv.shape[0])
    g_qkv[...] = jnp.concatenate(
        [qkv[h, :, lo:hi].astype(F32) for lo, hi in ((0, 192), (192, 256), (256, 320)) for h in heads], axis=1)
    g_proj[...] = proj[...].astype(F32)

    @pl.when(pl.program_id(0) == 0)
    def _():
        total = res[...]
        for k in range(4):
            total = total + parts[k].astype(F32)
        out[...] = total.astype(BF)
        g_router[...] = terms[8:, :]


def finish(v, qkv, proj, res, parts, terms):
    steps, own, width = 8, proj.shape[0], proj.shape[1]
    row, some = v.shape[1] // steps, own // steps
    once = lambda n: (lambda i: (0,) * n)
    return pl.pallas_call(
        finish_kernel,
        grid=(steps,),
        out_shape=(
            jax.ShapeDtypeStruct((v.shape[1], 2 * HID), F32), jax.ShapeDtypeStruct((v.shape[1], HID), F32),
            jax.ShapeDtypeStruct((own, 2560), F32), jax.ShapeDtypeStruct((own, width), F32),
            jax.ShapeDtypeStruct(res.shape, BF), jax.ShapeDtypeStruct((EXPERTS, own), F32)),
        in_specs=[
            pl.BlockSpec((2, row, v.shape[2]), lambda i: (0, i, 0)),
            pl.BlockSpec((8, some, 320), lambda i: (0, i, 0)), pl.BlockSpec((some, width), lambda i: (i, 0)),
            pl.BlockSpec(res.shape, once(2)), pl.BlockSpec(parts.shape, once(3)),
            pl.BlockSpec(terms.shape, once(2))],
        out_specs=[
            pl.BlockSpec((row, 2 * HID), lambda i: (i, 0)), pl.BlockSpec((row, HID), lambda i: (i, 0)),
            pl.BlockSpec((some, 2560), lambda i: (i, 0)), pl.BlockSpec((some, width), lambda i: (i, 0)),
            pl.BlockSpec(res.shape, once(2)), pl.BlockSpec((EXPERTS, own), once(2))],
        compiler_params=pltpu.CompilerParams(vmem_limit_bytes=62 * 1024 * 1024),
        name="finish",
    )(v, qkv, proj, res, parts, terms)


def expert_grads_general(reps, grps, xs, dys, ggu, hw):
    local, half, width = ggu.shape[0], HID // 2, xs.shape[1]
    own = width // grps
    chips = reps // 2
    piece = own // chips
    same_core = [[2 * i + c for i in range(chips)] for c in range(2)]
    pairs = [[2 * i, 2 * i + 1] for i in range(chips)]
    up = jnp.einsum("td,eth->edh", xs, ggu, preferred_element_type=F32).astype(BF)
    down = jnp.einsum("td,eth->edh", dys, hw, preferred_element_type=F32).astype(BF)
    gw = jnp.concatenate([up, down], axis=2)
    gw = gw.reshape(local, grps, chips, piece, 3 * half).transpose(2, 1, 3, 0, 4)
    gw = gw.reshape(chips * grps * piece, local * 3 * half)
    gw = lax.psum_scatter(gw, "rep", scatter_dimension=0, tiled=True, axis_index_groups=same_core)
    gw = lax.all_to_all(gw.reshape(grps, piece, local, 3 * half), "grp", 0, 0, tiled=True)
    gw = gw.transpose(1, 0, 2, 3).reshape(piece, EXPERTS, 3 * half)
    gw = lax.all_gather(gw, "rep", axis=0, tiled=True, axis_index_groups=same_core)
    gw = lax.all_gather(gw, "rep", axis=0, tiled=False, axis_index_groups=pairs).astype(F32)
    gw = gw.reshape(2, own * EXPERTS, 3, half)
    gw = jnp.moveaxis(gw, 0, 2).reshape(own * EXPERTS, 3 * HID)
    return gw[:, : 2 * HID], gw[:, 2 * HID :]


def shards_general(
    reps,
    grps,
    tokens,
    attn_gain,
    query_key_value_weight,
    attn_proj,
    mlp_gain,
    w_router,
    w_gate_up,
    w_down,
    prefix_len,
    expert_ids,
    priority,
    cotangent,
):
    seq, width = tokens.shape
    own = width // grps
    local_experts = EXPERTS // grps
    heads = KEY_VALUE_HEADS
    groups = None if reps == heads else [list(range(i, i + heads)) for i in range(0, reps, heads)]
    rep, grp = lax.axis_index("rep"), lax.axis_index("grp")
    head = lax.rem(rep, heads)
    qw, hw = QPK * HEAD_WIDTH, HEAD_WIDTH
    q_all = QUERY_HEADS * HEAD_WIDTH

    small = jnp.concatenate([attn_gain[:, None], mlp_gain[:, None], w_router], axis=1)
    small = lax.all_gather(small, "grp", axis=0, tiled=True)
    gain_one, gain_two = small[:, 0].astype(F32)[None, :], small[:, 1].astype(F32)[None, :]
    router = small[:, 2:]
    qkv_cols = jnp.concatenate(
        [
            lax.dynamic_slice_in_dim(query_key_value_weight, head * qw, qw, 1),
            lax.dynamic_slice_in_dim(query_key_value_weight, q_all + head * hw, hw, 1),
            lax.dynamic_slice_in_dim(query_key_value_weight, q_all + heads * hw + head * hw, hw, 1),
        ],
        axis=1,
    )
    qkv_head = lax.all_gather(qkv_cols, "grp", axis=0, tiled=True)
    row = head * qw + jnp.arange(qw)
    mine = (row // own) == grp
    proj_rows = jnp.where(mine[:, None], jnp.take(attn_proj, jnp.where(mine, row - grp * own, 0), axis=0), 0)
    proj_head = lax.psum(proj_rows, "grp")

    core, chip, chips, half = lax.rem(rep, 2), rep // 2, reps // 2, HID // 2
    pairs = [[2 * i, 2 * i + 1] for i in range(chips)]
    same_core = [[2 * i + c for i in range(chips)] for c in range(2)]
    piece = own // chips
    gu_piece = lax.dynamic_slice_in_dim(w_gate_up, chip * piece, piece, 0)
    dn_piece = lax.dynamic_slice_in_dim(w_down, chip * piece, piece, 0)
    both = jnp.concatenate(
        [
            lax.dynamic_slice_in_dim(gu_piece, core * half, half, 2),
            lax.dynamic_slice_in_dim(gu_piece, HID + core * half, half, 2),
            lax.dynamic_slice_in_dim(dn_piece, core * half, half, 2),
        ],
        axis=2,
    )
    both = both.reshape(piece, grps, local_experts, 3 * half).transpose(1, 2, 0, 3)
    both = lax.all_to_all(both, "grp", 0, 0, tiled=True)
    both = lax.all_gather(both, "rep", axis=0, tiled=False, axis_index_groups=same_core)
    both = both.transpose(2, 1, 0, 3, 4).reshape(local_experts, width, 3 * half)
    wgu, wdn = both[:, :, : 2 * half], both[:, :, 2 * half :]

    tokens_f = tokens.astype(F32)
    inverse_one = lax.rsqrt(jnp.mean(tokens_f * tokens_f, axis=1, keepdims=True) + EPS)
    normed_one = tokens_f * inverse_one
    act_one = (normed_one * gain_one).astype(BF)
    act_plane = lax.all_gather(act_one, "rep", axis=0, tiled=True, axis_index_groups=groups)
    prefix_plane = lax.all_gather(prefix_len, "rep", axis=0, tiled=True, axis_index_groups=groups)
    cos, sin = rope_tables(seq)
    projected = dot(act_plane, qkv_head).reshape(heads, seq, QPK + 2, HEAD_WIDTH)
    cos_b, sin_b = cos[None, :, None, :], sin[None, :, None, :]
    turned = rotate(projected[:, :, : QPK + 1], cos_b, sin_b).astype(BF)
    query = turned[:, :, :QPK]
    key = turned[:, :, QPK]
    value = projected[:, :, QPK + 1].astype(BF)
    scale = HEAD_WIDTH ** (-0.5)
    row_pos, col_pos = jnp.arange(seq)[:, None], jnp.arange(seq)[None, :]
    allowed = (col_pos <= row_pos)[None] | (col_pos[None] < prefix_plane[:, None, None])
    scores = jnp.einsum("bsgd,btd->bgst", query, key, preferred_element_type=F32) * scale
    scores = jnp.where(allowed[:, None], scores, -1e30)
    exps = jnp.exp(scores - jnp.max(scores, axis=-1, keepdims=True))
    probs = exps / jnp.sum(exps, axis=-1, keepdims=True)
    probs_low = probs.astype(BF)
    attended = jnp.einsum("bgst,btd->bsgd", probs_low, value, preferred_element_type=F32)
    attended = attended.astype(BF).reshape(heads * seq, qw)
    part = dot(attended, proj_head).astype(BF)
    part = lax.psum_scatter(part, "rep", scatter_dimension=0, tiled=True, axis_index_groups=groups)
    residual = tokens_f + part.astype(F32)
    inverse_two = lax.rsqrt(jnp.mean(residual * residual, axis=1, keepdims=True) + EPS)
    normed_two = residual * inverse_two
    act_two = (normed_two * gain_two).astype(BF)
    gates, kept = routing(expert_ids, priority, dot(act_two, router))

    def column(v):
        v = lax.all_gather(v, "grp", axis=0, tiled=True)
        return lax.all_gather(v, "rep", axis=0, tiled=True, axis_index_groups=pairs)

    def to_owners(v):
        v = lax.psum_scatter(v, "rep", scatter_dimension=0, tiled=True, axis_index_groups=pairs)
        return lax.psum_scatter(v, "grp", scatter_dimension=0, tiled=True).astype(F32)

    dy_all = column(cotangent)
    x_all = column(act_two)
    weight = column(jnp.where(kept, gates, 0.0))
    weight = lax.dynamic_slice_in_dim(weight, grp * local_experts, local_experts, 1).T[:, :, None]
    gate_up = jnp.einsum("td,edh->eth", x_all, wgu, preferred_element_type=F32)
    g, u = gate_up[..., :half], gate_up[..., half:]
    sig = jax.nn.sigmoid(g)
    silu = g * sig
    hidden = silu * u
    hidden_w = (hidden * weight).astype(BF)
    back = jnp.einsum("td,edh->eth", dy_all, wdn, preferred_element_type=F32)
    grad_gate_part = jnp.sum(back * hidden, axis=2)
    grad_hidden = back * weight
    ggu = jnp.concatenate(
        [grad_hidden * u * sig * (1.0 + g * (1.0 - sig)), grad_hidden * silu], axis=2
    ).astype(BF)
    out_part = jnp.einsum("eth,edh->td", hidden_w, wdn, preferred_element_type=F32).astype(BF)
    gact_part = jnp.einsum("eth,edh->td", ggu, wgu, preferred_element_type=F32).astype(BF)
    gact = to_owners(gact_part)
    grad_gates = lax.psum_scatter(
        grad_gate_part.T, "rep", scatter_dimension=0, tiled=True, axis_index_groups=pairs
    )
    grad_gates = lax.all_to_all(grad_gates, "grp", 0, 1, tiled=True)
    grad_gates = jnp.where(kept, grad_gates, 0.0)
    out = to_owners(out_part)
    output = (residual + out).astype(BF)
    grad_gu, grad_dn = expert_grads_general(reps, grps, x_all, dy_all, ggu, hidden_w)
    grad_gu = grad_gu.reshape(own, EXPERTS, 2 * HID)
    grad_dn = grad_dn.reshape(own, EXPERTS, HID)

    grad_logits = (gates * (grad_gates - jnp.sum(gates * grad_gates, axis=1, keepdims=True))).astype(BF)
    gact = gact + dot(grad_logits, router.T)
    router_term = dot(act_two.T, grad_logits)
    gain_two_term = jnp.sum(gact * normed_two, axis=0)
    scaled = gact * gain_two
    dy = cotangent.astype(F32)
    grad_residual = dy + inverse_two * (
        scaled - normed_two * jnp.mean(scaled * normed_two, axis=1, keepdims=True)
    )
    gres_low = grad_residual.astype(BF)

    gres_plane = lax.all_gather(gres_low, "rep", axis=0, tiled=True, axis_index_groups=groups)
    proj_term = dot(attended.T, gres_plane)
    grad_att = dot(gres_plane, proj_head.T).astype(BF).reshape(heads, seq, QPK, HEAD_WIDTH)
    grad_value = jnp.einsum("bgst,bsgd->btd", probs_low, grad_att, preferred_element_type=F32)
    grad_probs = jnp.einsum("bsgd,btd->bgst", grad_att, value, preferred_element_type=F32)
    grad_scores = (
        probs * (grad_probs - jnp.sum(probs * grad_probs, axis=-1, keepdims=True))
    ).astype(BF)
    grad_query = jnp.einsum("bgst,btd->bsgd", grad_scores, key, preferred_element_type=F32) * scale
    grad_key = jnp.einsum("bgst,bsgd->btd", grad_scores, query, preferred_element_type=F32) * scale
    turned_back = rotate(
        jnp.concatenate([grad_query, grad_key[:, :, None]], axis=2), cos_b, -sin_b
    )
    gproj = jnp.concatenate([turned_back, grad_value[:, :, None]], axis=2).astype(BF)
    gproj = gproj.reshape(heads * seq, qw + 2 * hw)
    qkv_term = dot(act_plane.T, gproj)
    gact_one = dot(gproj, qkv_head.T).astype(BF)
    gact_one = lax.psum_scatter(
        gact_one, "rep", scatter_dimension=0, tiled=True, axis_index_groups=groups
    ).astype(F32)
    gain_one_term = jnp.sum(gact_one * normed_one, axis=0)
    scaled_one = gact_one * gain_one
    grad_tokens = grad_residual + inverse_one * (
        scaled_one - normed_one * jnp.mean(scaled_one * normed_one, axis=1, keepdims=True)
    )

    qkv_own = lax.psum_scatter(qkv_term.astype(BF), "grp", scatter_dimension=0, tiled=True)
    proj_sum = lax.psum(proj_term.astype(BF), "grp")
    if groups is not None:
        across = [[i + heads * j for j in range(reps // heads)] for i in range(heads)]
        qkv_own = lax.psum(qkv_own, "rep", axis_index_groups=across)
        proj_sum = lax.psum(proj_sum, "rep", axis_index_groups=across)
    qkv_own = lax.all_gather(qkv_own, "rep", axis=0, tiled=False, axis_index_groups=groups)
    qkv_own = qkv_own.astype(F32)
    grad_qkv = jnp.concatenate(
        [
            qkv_own[:, :, lo:hi].transpose(1, 0, 2).reshape(own, -1)
            for lo, hi in ((0, qw), (qw, qw + hw), (qw + hw, qw + 2 * hw))
        ],
        axis=1,
    )
    proj_all = lax.all_gather(proj_sum, "rep", axis=0, tiled=True, axis_index_groups=groups)
    grad_proj = lax.dynamic_slice_in_dim(proj_all, grp * own, own, 0).astype(F32)
    terms = jnp.concatenate([gain_one_term[:, None], gain_two_term[:, None], router_term], axis=1)
    terms = lax.psum(lax.psum_scatter(terms, "grp", scatter_dimension=0, tiled=True), "rep")
    return (
        output,
        grad_tokens,
        terms[:, 0],
        grad_qkv,
        grad_proj,
        terms[:, 1],
        terms[:, 2:],
        grad_gu,
        grad_dn,
    )


def shards(
    tokens,
    attn_gain,
    query_key_value_weight,
    attn_proj,
    mlp_gain,
    w_router,
    w_gate_up,
    w_down,
    prefix_len,
    expert_ids,
    priority,
    cotangent,
):
    own, width = attn_gain.shape[0], tokens.shape[1]
    small = jnp.concatenate(
        [attn_gain[None], mlp_gain[None], jnp.zeros((14, own), BF), w_router.T], axis=0
    )
    prefix = jnp.broadcast_to(prefix_len.astype(F32), (8, 128))
    half = HEAD_WIDTH // 2
    inverse_freq = np.float32(10000.0) ** (-np.arange(half, dtype=np.float32) * np.float32(2.0 / HEAD_WIDTH))
    angles = np.arange(tokens.shape[0], dtype=np.float32)[:, None] * inverse_freq[None, :]
    cos_t = jnp.asarray(np.tile(np.cos(angles), (1, 4)), F32)
    sin = np.sin(angles)
    sin_t = jnp.asarray(np.tile(np.concatenate([-sin, sin], axis=1), (1, 2)), F32)
    parts = front(
        tokens, cotangent, w_gate_up, w_down, query_key_value_weight, attn_proj, small, expert_ids.T,
        priority.reshape(expert_ids.shape), prefix, cos_t, sin_t)
    wide, grad_tokens, qkv_own, proj_own, terms, out_parts = back(parts, tokens, cos_t, sin_t)
    grad_gu, grad_dn, grad_qkv, grad_proj, output, grad_router = finish(
        wide, qkv_own, proj_own.reshape(own, width), parts[13], out_parts, terms)
    return (
        output,
        grad_tokens,
        terms[0],
        grad_qkv,
        grad_proj,
        terms[1],
        grad_router.T,
        grad_gu.reshape(own, EXPERTS, 2 * HID),
        grad_dn.reshape(own, EXPERTS, HID),
    )


def solution(mesh):
    tok, par = ("rep", "grp"), "grp"
    in_specs = (
        P(tok, None),
        P(par),
        P(par, None),
        P(par, None),
        P(par),
        P(par, None),
        P(par, None, None),
        P(par, None, None),
        P(tok),
        P(tok, None),
        P(tok, None),
        P(tok, None),
    )
    out_specs = (
        P(tok, None),
        P(tok, None),
        P(par),
        P(par, None),
        P(par, None),
        P(par),
        P(par, None),
        P(par, None, None),
        P(par, None, None),
    )
    reps, grps = mesh.shape["rep"], mesh.shape["grp"]

    def body(*args):
        if (reps, grps) == (8, 4):
            return shards(*args)
        return shards_general(reps, grps, *args)

    return jax.shard_map(body, mesh=mesh, in_specs=in_specs, out_specs=out_specs, check_vma=False)
```

```python
import jax
import jax.numpy as jnp
import numpy as np
from jax import lax
from jax.experimental import pallas as pl
from jax.experimental.pallas import tpu as pltpu
from jax.sharding import PartitionSpec as P

QUERY_HEADS = 24
KEY_VALUE_HEADS = 8
HEAD_WIDTH = 64
HID = 512
EXPERTS = 16
CAP = 72
EPS = 1e-05
BF = jnp.bfloat16
F32 = jnp.float32
QPK = QUERY_HEADS // KEY_VALUE_HEADS
BIG = 1 << 20
MESH = pl.DeviceIdType.MESH


def dot(a, b):
    return jnp.dot(a, b, preferred_element_type=F32)


def rope_tables(length):
    half = HEAD_WIDTH // 2
    position = jnp.arange(length, dtype=F32)[:, None]
    inverse_freq = 10000.0 ** (-jnp.arange(half, dtype=F32) * 2.0 / HEAD_WIDTH)
    angles = position * inverse_freq[None, :]
    return jnp.cos(angles), jnp.sin(angles)


def rotate(v, cos, sin):
    half = HEAD_WIDTH // 2
    a, b = v[..., :half], v[..., half:]
    return jnp.concatenate([a * cos - b * sin, b * cos + a * sin], axis=-1)


def choices(expert_ids, priority):
    seq, top = expert_ids.shape
    choose = expert_ids[:, :, None] == jnp.arange(EXPERTS, dtype=jnp.int32)[None, None, :]
    chosen = jnp.any(choose, axis=1)
    rank_of = jnp.sum(jnp.where(choose, priority.reshape(seq, top)[:, :, None], 0), axis=1)
    rank_of = jnp.where(chosen, rank_of, BIG)
    slot = jnp.sum((rank_of[None, :, :] < rank_of[:, None, :]).astype(jnp.int32), axis=1)
    return chosen, chosen & (slot < CAP)


def routing(expert_ids, priority, logits):
    chosen, kept = choices(expert_ids, priority)
    top_logit = jnp.max(jnp.where(chosen, logits, -jnp.inf), axis=1, keepdims=True)
    gate_exp = jnp.where(chosen, jnp.exp(jnp.where(chosen, logits - top_logit, 0.0)), 0.0)
    gates = gate_exp / jnp.sum(gate_exp, axis=1, keepdims=True)
    return gates, kept


def place():
    r, z = lax.axis_index("rep"), lax.axis_index("grp")
    return r // 4, (r // 2) % 2, r % 2, z


def flip(bit, by):
    return bit + by * (1 - 2 * bit)


def turn(v, cos, sin):
    lane = lax.broadcasted_iota(jnp.int32, v.shape, 1)
    partner = jnp.where(lax.rem(lane, 64) < 32, pltpu.roll(v, 96, 1), pltpu.roll(v, 32, 1))
    return v * cos + partner * sin


def gradient_rows(q3, x, dy, ggu, hw, gw):
    half = HID // 2

    def side(ref):
        return jnp.concatenate(
            [ref[:, :, :, pl.ds(pl.multiple_of(zz * 384 + q3 * 128, 128), 128)].reshape(1024, 128)
             for zz in range(4)], axis=1)
    xs, ds = side(x), side(dy)

    def one(j, _):
        up = lax.dot_general(xs, ggu[j], (((0,), (0,)), ((), ())), preferred_element_type=F32).astype(BF)
        dn = lax.dot_general(ds, hw[j], (((0,), (0,)), ((), ())), preferred_element_type=F32).astype(BF)
        for zz in range(4):
            for p in range(4):
                for h in range(2):
                    at = zz * 128 + p * 32 + h * 16
                    gw[p, h, zz, j, :, : 2 * half] = up[at : at + 16]
                    gw[p, h, zz, j, :, 2 * half :] = dn[at : at + 16]
        return 0
    lax.fori_loop(0, 4, one, 0)


def front_kernel(tok, dy, w_gu, w_dn, qkv, proj, small, ids_t, prio, prefix, cos_t, sin_t,
                 o_x, o_dy, o_ggu, o_hw, o_act, o_q, o_k, o_v, o_probs, o_att, o_qkvw, o_projw,
                 o_small, o_res, o_gates, o_kept, o_gsum, o_osum, o_gw, o_r1,
                 smalls, qkvw, projw, projq, actp, pre, pr, qs, ks, vs, probs, att, part, sibr, sums, plr,
                 xall, dyall, wbuf, ggu, hw, gpart, ggp, gsib,
                 gsum, res, gates, kept, qwin, wst, wcol, wpiece, gw,
                 s_small, r_small, s_qkv, r_qkv, s_pz, r_pz, s_pq, r_pq, s_wz, r_wz, s_wp, r_wp,
                 s_act, r_act, s_pre, r_pre, s_actc, r_actc, s_prec, r_prec, s_sib, r_sib, s_pl, r_pl,
                 s_x, r_x, s_xc, r_xc, s_y, r_y, s_yc, r_yc,
                 s_gc, r_gc, s_oc, r_oc, s1, r1, sl):
    y, x, c, z = place()
    half = HID // 2

    def slot(a, b):
        return flip(y, a * c + b * (1 - c)) * 2 + flip(x, a * (1 - c) + b * c)

    p0, p1, p2, p3 = slot(0, 0), slot(1, 0), slot(0, 1), slot(1, 1)
    peers = (p1, p2, p3)
    d1, d2, dsib = (p1 * 2 + c, z), (p2 * 2 + c, z), (p0 * 2 + 1 - c, z)
    dpl = [(p * 2 + c, z) for p in peers]
    zk = [lax.rem(z + k, 4) for k in range(4)]
    zf = [lax.rem(z + 4 - k, 4) for k in range(4)]
    dz = [(p0 * 2 + c, zz) for zz in zk]

    barrier = pltpu.get_barrier_semaphore()
    for to in dpl + dz[1:] + [dsib]:
        pl.semaphore_signal(barrier, 1, device_id=to, device_id_type=MESH)
    pl.semaphore_wait(barrier, 7)

    def remote(src, dst, s, r, to):
        return pltpu.make_async_remote_copy(src, dst, s, r, device_id=to, device_id_type=MESH)

    def c_small(k):
        return remote(small, smalls.at[z], s_small.at[k - 1], r_small.at[k - 1], dz[k])

    def rows(zz, pp):
        return pl.ds(pl.multiple_of(zz * 384 + pp * 96, 96), 96)

    def c_wz(k):
        return remote(wpiece.at[zk[k]], wbuf.at[:, rows(z, p0)], s_wz.at[k - 1], r_wz.at[k - 1], dz[k])

    def c_wp(k, i):
        zz = zf[k]
        who, pp = ((d1, p0), (d2, p0), (d2, p1))[i]
        src = wpiece.at[z] if (k == 0 and i < 2) else wbuf.at[:, rows(zz, pp)]
        return remote(src, wbuf.at[:, rows(zz, pp)], s_wp.at[k, i], r_wp.at[k, i], who)

    def quarter(p):
        return pl.ds(pl.multiple_of(p * 48, 48), 48)

    def c_pz(k):
        src = proj.at[pl.ds(pl.multiple_of(c * 192 + p0 * 48, 48), 48)]
        return remote(src, projq.at[k - 1], s_pz.at[k - 1], r_pz.at[k - 1], dz[k])

    def c_pq(k, owner):
        return remote(projq.at[k - 1], projw.at[quarter(p0)], s_pq.at[k - 1], r_pq.at[p0], (owner * 2 + c, z))

    def c_pq_in(i):
        return remote(projq.at[0], projw.at[quarter(peers[i])], s_pq.at[0], r_pq.at[peers[i]], dpl[i])

    def c_act(i):
        blk = actp.at[c, p1 if i == 2 else p0]
        return remote(blk, blk, s_act.at[i], r_act.at[i], d1 if i == 0 else d2)

    def c_pre(i):
        blk = pre.at[c, p1 if i == 2 else p0]
        return remote(blk, blk, s_pre.at[i], r_pre.at[i], d1 if i == 0 else d2)

    def c_actc(i):
        p = (p0, p1, p2, p3)[i]
        return remote(actp.at[c, p], actp.at[c, p], s_actc.at[i], r_actc.at[i], dsib)

    def c_prec(i):
        p = (p0, p1, p2, p3)[i]
        return remote(pre.at[c, p], pre.at[c, p], s_prec.at[i], r_prec.at[i], dsib)

    def c_sib():
        return remote(part, sibr, s_sib, r_sib, dsib)

    def c_pl(i):
        return remote(sums.at[i], plr.at[i], s_pl.at[i], r_pl.at[i], d2 if i == 1 else d1)

    def chain(at, s, r, sc=None, rc=None):
        def hop(h, d, send):
            block = z - (h - 1) if d == 0 else z + (h - 1)
            if not send:
                block = z - h if d == 0 else z + h
            return remote(at(block), at(block), s.at[d, h - 1], r.at[d, h - 1],
                          (p0 * 2 + c, z + 1 if d == 0 else z - 1))

        def may(h, d, send):
            if send:
                return (z < 3) & (z >= h - 1) if d == 0 else (z > 0) & (z <= 4 - h)
            return z >= h if d == 0 else z <= 3 - h

        def across(h, d):
            block = z - h if d == 0 else z + h
            return remote(at(block), at(block), sc.at[d, h - 1], rc.at[d, h - 1], dsib)

        def over():
            return remote(at(z), at(z), sc.at[2, 0], rc.at[2, 0], dsib)

        def send(h):
            for d in range(2):
                @pl.when(may(h, d, True))
                def _(d=d):
                    hop(h, d, True).start()
            if h == 1 and sc is not None:
                over().start()

        def recv(h):
            for d in range(2):
                @pl.when(may(h, d, False))
                def _(d=d):
                    hop(h, d, False).wait_recv()
                    if sc is not None:
                        across(h, d).start()

        def finish():
            over().wait_recv()
            for h in (1, 2, 3):
                for d in range(2):
                    @pl.when(may(h, d, False))
                    def _(d=d, h=h):
                        across(h, d).wait_recv()

        def sent():
            if sc is not None:
                over().wait_send()
            for h in (1, 2, 3):
                for d in range(2):
                    @pl.when(may(h, d, True))
                    def _(d=d, h=h):
                        hop(h, d, True).wait_send()
                    if sc is not None:
                        @pl.when(may(h, d, False))
                        def _(d=d, h=h):
                            across(h, d).wait_send()
        return send, recv, finish, sent

    x_send, x_recv, x_finish, x_sent = chain(lambda b: xall.at[c, b], s_x, r_x, s_xc, r_xc)
    y_send, y_recv, y_finish, y_sent = chain(lambda b: dyall.at[c, b], s_y, r_y, s_yc, r_yc)
    q_send, q_recv, _, q_sent = chain(
        lambda b: qkvw.at[pl.ds(pl.multiple_of(b * 384, 384), 384)], s_qkv, r_qkv)

    opart, osib, osum = part, sibr, sums

    def copy1(h, b):
        return remote(gw.at[slot(1, b), h], o_r1.at[h, b], s1.at[h, b], r1.at[h, b], d1)
    g_c = remote(gpart, gsib, s_gc, r_gc, dsib)
    o_c = remote(opart, osib, s_oc, r_oc, dsib)

    def weights_a(k):
        if k:
            c_wz(k).wait_recv()
        c_wp(k, 0).start()
        if k == 0:
            c_wp(0, 1).start()

    def weights_b(k):
        c_wp(k, 0).wait_recv()
        if k:
            c_wp(k, 1).start()
        c_wp(k, 2).start()

    for k in (1, 2, 3):
        c_small(k).start()
    local = [pltpu.make_async_copy(small, smalls.at[z], sl.at[0]),
             pltpu.make_async_copy(dy, dyall.at[c, z], sl.at[3])]

    def window(off, width, at, n):
        src = qkv.at[:, pl.ds(pl.multiple_of(off, 128), width)]
        return pltpu.make_async_copy(src, qwin.at[:, pl.ds(at, width)], sl.at[n])
    mine = p0 * 96
    windows = [window(384 * p0 + 128 * c, 256, 0, 1), window(1536 + 128 * p0, 128, 256, 2),
               window(2048 + 128 * p0, 128, 384, 5)]
    pieces = [pltpu.make_async_copy(
        ref.at[pl.ds(pl.multiple_of(mine, 96), 96), :, pl.ds(pl.multiple_of(off, half), half)],
        wst.at[:, :, pl.ds(i * half, half)], sl.at[6 + i])
        for i, (ref, off) in enumerate(((w_gu, c * half), (w_gu, HID + c * half), (w_dn, c * half)))]
    for one in local + windows + pieces:
        one.start()
    own_proj = pltpu.make_async_copy(proj.at[pl.ds(pl.multiple_of(c * 192, 192), 192)], projw, sl.at[4])

    @pl.when(z == p0)
    def _():
        own_proj.start()
    for one in windows:
        one.wait()
    cols = qwin[...].astype(F32)
    own_rows = pl.ds(pl.multiple_of(z * 384, 384), 384)
    for at, lo, width in ((0, 0, 256), (192, 256, 128), (256, 384, 128)):
        part_ = cols[:, lo : lo + width]
        part_ = jnp.where(c == 0, part_, pltpu.roll(part_, width - 64, 1)).astype(BF)
        qkvw[own_rows, at : at + (192 if at == 0 else 64)] = part_[:, : 192 if at == 0 else 64]

    tok_f = tok[...].astype(F32)
    inv1 = lax.rsqrt(jnp.mean(tok_f * tok_f, axis=1, keepdims=True) + EPS)
    for k in (1, 2, 3):
        c_small(k).wait_recv()
    q_send(1)
    local[0].wait()
    gain1 = jnp.concatenate([smalls[i, 0:1, :] for i in range(4)], axis=1).astype(F32)
    actp[c, p0] = (tok_f * inv1 * gain1).astype(BF)
    pre[c, p0] = jnp.full((8, 128), prefix[0], jnp.int32).astype(F32)
    for i in range(2):
        c_act(i).start()
        c_pre(i).start()
    c_actc(0).start()
    c_prec(0).start()
    chosen_f = jnp.zeros((128, 128), F32)
    rank_of = jnp.zeros((128, 128), F32)
    lane_e = lax.broadcasted_iota(jnp.int32, (128, 128), 1)
    ids = ids_t[...].astype(F32).T
    spread = jnp.concatenate(
        [jnp.broadcast_to(prio[i : i + 1, :].astype(F32), (16, 128)) for i in range(8)], axis=0)
    token = lax.broadcasted_iota(jnp.int32, (128, 128), 0)
    spread = jnp.where(lane_e // 8 == lax.rem(token, 16), spread, 0.0)
    for k in range(8):
        hit = ids[:, k : k + 1] == lane_e.astype(F32)
        chosen_f = jnp.where(hit, 1.0, chosen_f)
        own_prio = jnp.sum(jnp.where(lax.rem(lane_e, 8) == k, spread, 0.0), axis=1, keepdims=True)
        rank_of = jnp.where(hit, own_prio, rank_of)
    rank_of = jnp.where(chosen_f > 0.0, rank_of, 65536.0)
    rank_t = rank_of.T
    slots = jnp.zeros((128, 128), F32)
    for e in range(EXPERTS):
        before = jnp.sum((rank_t[e : e + 1, :] < rank_of[:, e : e + 1]).astype(F32), axis=1, keepdims=True)
        slots = jnp.where(lane_e == e, before, slots)
    kept_f = jnp.where(slots < CAP, chosen_f, 0.0)
    kept[...] = kept_f[:, :EXPERTS]
    q_recv(1)
    q_send(2)

    for one in pieces:
        one.wait()

    def expert_rows(l, _):
        wcol[...] = wst[:, :, pl.ds(pl.multiple_of(l * 128, 128), 128)].astype(F32).reshape(1536, 128)
        for e in range(EXPERTS):
            wpiece[e // 4, e % 4, :, pl.ds(pl.multiple_of(l * 128, 128), 128)] = (
                wcol[pl.ds(e, 96, stride=EXPERTS), :].astype(BF))
        return 0
    lax.fori_loop(0, 6, expert_rows, 0)
    own_piece = pltpu.make_async_copy(wpiece.at[z], wbuf.at[:, rows(z, p0)], sl.at[30])
    own_piece.start()
    weights_a(0)
    q_recv(2)
    q_send(3)
    for k in (1, 2, 3):
        c_pz(k).start()
    for i in range(3):
        c_act(i).wait_recv()
        c_pre(i).wait_recv()
        if i == 0:
            c_act(2).start()
            c_pre(2).start()
        c_actc(i + 1).start()
        c_prec(i + 1).start()
    q_recv(3)
    weights_b(0)
    local[1].wait()

    row = lax.broadcasted_iota(jnp.int32, (128, 128), 0)
    col = lax.broadcasted_iota(jnp.int32, (128, 128), 1)
    causal = col <= row
    col_f = col.astype(F32)

    def attention(cc):
        pr[...] = jnp.dot(actp[cc].reshape(512, 1536), qkvw[...], preferred_element_type=F32).reshape(4, 128, 320)

        def one(i, _):
            lo = turn(pr[i, :, 0:128], cos_t[...], sin_t[...]).astype(BF)
            hi = turn(pr[i, :, 128:256], cos_t[...], sin_t[...]).astype(BF)
            qs[cc, i, 0:128] = lo[:, 0:64]
            qs[cc, i, 128:256] = lo[:, 64:128]
            qs[cc, i, 256:384] = hi[:, 0:64]
            ks[cc, i] = hi[:, 64:128]
            vs[cc, i] = pr[i, :, 256:320].astype(BF)
            sc = lax.dot_general(qs[cc, i], ks[cc, i], (((1,), (1,)), ((), ())), preferred_element_type=F32)
            allowed = causal | (col_f < pre[cc, i, 0:1, :])
            sc = jnp.where(allowed[None], sc.reshape(3, 128, 128) * (64 ** -0.5), -1e30)
            ex = jnp.exp(sc - jnp.max(sc, axis=-1, keepdims=True))
            pb = (ex / jnp.sum(ex, axis=-1, keepdims=True)).reshape(384, 128)
            probs[cc, i] = pb
            at = jnp.dot(pb.astype(BF), vs[cc, i], preferred_element_type=F32).astype(BF)
            for h in range(3):
                att[cc, i, :, h * 64 : (h + 1) * 64] = at[h * 128 : (h + 1) * 128]
            return 0
        lax.fori_loop(0, 4, one, 0)

    attention(c)
    for k in (1, 3, 2):
        c_wz(k).start()
    for i in range(4):
        c_actc(i).wait_recv()
        c_prec(i).wait_recv()
    attention(1 - c)
    for k in (1, 2, 3):
        c_pz(k).wait_recv()
        owner = zf[k]

        @pl.when(owner != p0)
        def _(k=k, owner=owner):
            c_pq(k, owner).start()

        @pl.when(owner == p0)
        def _(k=k):
            projw[quarter(p0)] = projq[k - 1]

    @pl.when(z == p0)
    def _():
        own_proj.wait()

    @pl.when(z != p0)
    def _():
        for i in range(3):
            c_pq_in(i).wait_recv()

    def to_sib(i, _):
        part[i] = jnp.dot(att[1 - c, i], projw[...], preferred_element_type=F32).astype(BF)
        return 0
    lax.fori_loop(0, 4, to_sib, 0)
    c_sib().start()
    c_sib().wait_recv()
    def mixed(p):
        return jnp.dot(att[c, p], projw[...], preferred_element_type=F32) + sibr[p].astype(F32)

    for i in (2, 0):
        sums[i] = mixed(peers[i]).astype(BF)
        c_pl(i).start()
    to_second = mixed(p2)
    residual = tok_f + mixed(p0)
    c_pl(2).wait_recv()
    sums[1] = (to_second + plr[2].astype(F32)).astype(BF)
    c_pl(1).start()
    for i in range(2):
        c_pl(i).wait_recv()
        residual = residual + plr[i].astype(F32)
    res[...] = residual
    inv2 = lax.rsqrt(jnp.mean(residual * residual, axis=1, keepdims=True) + EPS)
    gain2 = jnp.concatenate([smalls[i, 1:2, :] for i in range(4)], axis=1).astype(F32)
    act2 = (residual * inv2 * gain2).astype(BF)
    router = jnp.concatenate([smalls[i, 16:32, :] for i in range(4)], axis=1)
    logits = lax.dot_general(act2, router, (((1,), (1,)), ((), ())), preferred_element_type=F32)
    chosen = chosen_f[:, :EXPERTS] > 0.0
    top = jnp.max(jnp.where(chosen, logits, -1e30), axis=1, keepdims=True)
    ge = jnp.where(chosen, jnp.exp(jnp.where(chosen, logits - top, 0.0)), 0.0)
    gt = ge / jnp.sum(ge, axis=1, keepdims=True)
    gates[...] = gt
    kept_gates = gt * kept[...]
    gate_hi = kept_gates.astype(BF)
    gate_lo = (kept_gates - gate_hi.astype(F32)).astype(BF)
    xall[c, z, :, :1536] = act2
    xall[c, z, :, 1536:] = jnp.concatenate([gate_hi, gate_lo, jnp.zeros((128, 96), BF)], axis=1)
    x_send(1)
    y_send(1)
    weights_a(1)
    weights_a(3)
    weights_b(1)
    weights_b(3)
    x_recv(1)
    x_send(2)
    weights_a(2)
    y_recv(1)
    y_send(2)
    x_recv(2)
    x_send(3)
    weights_b(2)
    y_recv(2)
    y_send(3)
    x_recv(3)
    y_recv(3)
    own_piece.wait()
    for k in range(4):
        c_wp(k, 1).wait_recv()
        c_wp(k, 2).wait_recv()
    x_finish()
    y_finish()

    lane = lax.broadcasted_iota(jnp.int32, (512, 128), 1)
    ggp[...] = jnp.zeros_like(ggp)

    def expert(n, _):
        j, t = n // 2, lax.rem(n, 2)
        gu = jnp.dot(xall[t, :, :, :1536].reshape(512, 1536), wbuf[j, :, : 2 * half], preferred_element_type=F32)
        bk = jnp.dot(dyall[t].reshape(512, 1536), wbuf[j, :, 2 * half :], preferred_element_type=F32)
        mine = lane == z * 4 + j
        both = xall[t, :, :, 1536:].astype(F32).reshape(512, 128)
        w = jnp.sum(jnp.where(mine | (lane == EXPERTS + z * 4 + j), both, 0.0), axis=1, keepdims=True)
        g, u = gu[:, :half], gu[:, half:]
        sg = 1.0 / (1.0 + jnp.exp(-g))
        silu = g * sg
        hid = silu * u
        hw[j, pl.ds(pl.multiple_of(t * 512, 512), 512)] = (hid * w).astype(BF)
        ggp[t] = ggp[t] + jnp.where(mine, jnp.sum(bk * hid, axis=1, keepdims=True), 0.0).reshape(4, 128, 128)
        gh = bk * w
        at = pl.ds(pl.multiple_of(t * 512, 512), 512)
        ggu[j, at, :half] = (gh * u * sg * (1.0 + g * (1.0 - sg))).astype(BF)
        ggu[j, at, half:] = (gh * silu).astype(BF)
        return 0
    lax.fori_loop(0, 8, expert, 0)

    gradient_rows(0, xall, dyall, ggu, hw, gw)
    for h in range(2):
        for b in range(2):
            copy1(h, b).start()
    saves = []

    def save(src, dst):
        one = pltpu.make_async_copy(src, dst, sl.at[9 + len(saves)])
        one.start()
        saves.append(one)
    for src, dst in ((xall, o_x), (dyall, o_dy), (ggu, o_ggu), (hw, o_hw), (actp, o_act), (qs, o_q), (ks, o_k),
                     (vs, o_v), (probs, o_probs), (att, o_att), (qkvw, o_qkvw), (projw, o_projw),
                     (smalls, o_small), (res, o_res), (gates, o_gates), (kept, o_kept)):
        save(src, dst)

    def block(grad, t, n):
        at = pl.ds(pl.multiple_of(t * 512, 512), 512)
        lanes = pl.ds(pl.multiple_of(n * 256, 256), 256)
        acc = jnp.zeros((512, 256), F32)
        for j in range(4):
            a = ggu[j, at] if grad else hw[j, at]
            b = wbuf[j, lanes, : 2 * half] if grad else wbuf[j, lanes, 2 * half :]
            acc = acc + lax.dot_general(a, b, (((1,), (1,)), ((), ())), preferred_element_type=F32)
        return acc.reshape(4, 128, 256), lanes

    def partial(grad, buf):
        def one(n, _):
            v, lanes = block(grad, 1 - c, n)
            buf[:, :, lanes] = v.astype(BF)
            return 0
        lax.fori_loop(0, 6, one, 0)

    def own(grad, sib, dst):
        def one(n, _):
            v, lanes = block(grad, c, n)
            dst[:, :, lanes] = (v + sib[:, :, lanes].astype(F32)).astype(BF)
            return 0
        lax.fori_loop(0, 6, one, 0)

    def put_gate_grads(dst, v):
        hi = v.astype(BF).astype(F32)
        lo = pltpu.roll((v - hi).reshape(512, 128), EXPERTS, 1)
        dst[:, :, 1536:] = jnp.where(lane < EXPERTS, hi.reshape(512, 128), lo).astype(BF).reshape(4, 128, 128)

    def gate_grads(v):
        both = v[..., 1536:].astype(F32).reshape(512, 128)
        return jnp.where(lane < EXPERTS, both + pltpu.roll(both, 128 - EXPERTS, 1), 0.0).reshape(4, 128, 128)

    c_sib().wait_send()
    for i in range(3):
        c_pl(i).wait_send()
    put_gate_grads(gpart, ggp[1 - c])
    partial(True, gpart)
    g_c.start()
    partial(False, opart)
    o_c.start()
    g_c.wait_recv()
    put_gate_grads(gsum, ggp[c] + gate_grads(gsib))
    own(True, gsib, gsum)
    save(gsum, o_gsum)
    o_c.wait_recv()
    own(False, osib, osum)
    save(osum, o_osum)
    save(gw, o_gw)
    for h in range(2):
        for b in range(2):
            copy1(h, b).wait()

    for k in (1, 2, 3):
        for one in (c_small(k), c_pz(k), c_wz(k)):
            one.wait_send()

        @pl.when(zf[k] != p0)
        def _(k=k):
            c_pq(k, zf[k]).wait_send()
    for k in range(4):
        for i in range(3):
            c_wp(k, i).wait_send()
        for one in (c_actc(k), c_prec(k)):
            one.wait_send()
    for i in range(3):
        for one in (c_act(i), c_pre(i)):
            one.wait_send()
    for one in (g_c, o_c):
        one.wait_send()
    x_sent()
    y_sent()
    q_sent()
    for one in saves:
        one.wait()


def front(*args):
    sem, vm = pltpu.SemaphoreType.DMA, pltpu.VMEM
    out = lambda shape, kind=BF: jax.ShapeDtypeStruct(shape, kind)
    outs = (
        out((2, 4, 128, 1664)), out((2, 4, 128, 1536)), out((4, 1024, 512)), out((4, 1024, 256)),
        out((2, 4, 128, 1536)), out((2, 4, 384, 64)), out((2, 4, 128, 64)), out((2, 4, 128, 64)),
        out((2, 4, 384, 128), F32), out((2, 4, 128, 192)), out((1536, 320)), out((192, 1536)),
        out((4, 32, 384)), out((128, 1536), F32), out((128, 16), F32), out((128, 16), F32), out((4, 128, 1664)),
        out((4, 128, 1536)), out((4, 2, 4, 4, 16, 768)), out((2, 2, 4, 4, 16, 768)),
    )
    block, quad = vm((2, 4, 128, 1536), BF), vm((4, 128, 1536), BF)
    three = vm((3, 128, 1536), BF)
    quad_g = vm((4, 128, 1664), BF)
    scratch = [
        vm((4, 32, 384), BF), vm((1536, 320), BF), vm((192, 1536), BF), vm((3, 48, 1536), BF),
        block, vm((2, 4, 8, 128), F32),
        vm((4, 128, 320), F32), vm((2, 4, 384, 64), BF), vm((2, 4, 128, 64), BF), vm((2, 4, 128, 64), BF),
        vm((2, 4, 384, 128), F32), vm((2, 4, 128, 192), BF), quad, quad, quad, three,
        vm((2, 4, 128, 1664), BF), block, vm((4, 1536, 768), BF), vm((4, 1024, 512), BF),
        vm((4, 1024, 256), BF), quad_g, vm((2, 4, 128, 128), F32), quad_g,
        quad_g, vm((128, 1536), F32), vm((128, 16), F32), vm((128, 16), F32),
        vm((384, 512), BF), vm((96, 16, 768), BF), vm((1536, 128), F32), vm((4, 4, 96, 768), BF),
        vm((4, 2, 4, 4, 16, 768), BF),
    ]
    n3, n4, one = sem((3,)), sem((4,)), sem(())
    hops = [sem((2, 3)), sem((2, 3)), sem((3, 3)), sem((3, 3))]
    sems = [
        n3, n3, sem((2, 3)), sem((2, 3)), n3, n3, n3, n4, n3, n3, sem((4, 3)), sem((4, 3)),
        n3, n3, n3, n3, n4, n4, n4, n4, one, one, n3, n3,
        *hops, *hops, one, one, one, one, sem((2, 2)), sem((2, 2)), sem((31,)),
    ]
    vmem, any_ = pl.BlockSpec(memory_space=pltpu.VMEM), pl.BlockSpec(memory_space=pl.ANY)
    return pl.pallas_call(
        front_kernel,
        out_shape=outs,
        in_specs=[vmem, any_, any_, any_, any_, any_, any_, vmem, vmem,
                  pl.BlockSpec(memory_space=pltpu.SMEM), vmem, vmem],
        out_specs=[any_] * len(outs),
        scratch_shapes=scratch + sems,
        compiler_params=pltpu.CompilerParams(
            collective_id=1, has_side_effects=True, vmem_limit_bytes=62 * 1024 * 1024),
        name="front",
    )(*args)


def back_kernel(i_x, i_dy, i_ggu, i_hw, i_act, i_q, i_k, i_v, i_probs, i_att, i_qkvw, i_projw, i_small,
                i_res, i_gates, i_kept, i_gsum, i_osum, i_gw, i_r1, tok, cos_t, sin_t,
                o_e, o_gtok, o_qg, o_pg, o_terms, o_op,
                xb, dyb, ggu, hw, qs, ks, vs, probs, att, qkvw, projw, smalls, res, gates, kept, gown, grecv,
                gw, recv1, send2, recv2, zs, zr, ib, agv,
                gres, gresf, gproj, sibr, plr, qgp, qz, qgo, pgp, pgr, pq2, pgo, terms, tz, tsib, tpl, tout, gtok,
                s1, r1, s2, r2, sz, rz, sa, ra, ss, rs, la,
                s_g, r_g, s_gr, r_gr, s_grc, r_grc, s_sib, r_sib, s_pl, r_pl, s_qz, r_qz, s_qo, r_qo,
                s_qoc, r_qoc, s_p1, r_p1, s_p2, r_p2, s_po, r_po, s_poc, r_poc, s_tz, r_tz, s_ts, r_ts,
                s_tp, r_tp, s_o, r_o, ld, sv):
    y, x, c, z = place()
    half = HID // 2
    wide = 3 * half
    nq = 6

    def slot(a, b):
        return flip(y, a * c + b * (1 - c)) * 2 + flip(x, a * (1 - c) + b * c)

    p0, p1, p2, p3 = slot(0, 0), slot(1, 0), slot(0, 1), slot(1, 1)
    peers = (p1, p2, p3)
    d1, d2, dsib = (p1 * 2 + c, z), (p2 * 2 + c, z), (p0 * 2 + 1 - c, z)
    dpl = [(p * 2 + c, z) for p in peers]
    zk = [lax.rem(z + k, 4) for k in range(4)]
    dz = [(p0 * 2 + c, zz) for zz in zk]

    loads = {}

    def load(name, src, dst):
        loads[name] = pltpu.make_async_copy(src, dst, ld.at[len(loads)])
        loads[name].start()
    load("gw", i_gw, gw.at[0])
    load("r1", i_r1, recv1.at[pl.ds(0, 2)])
    load("x", i_x.at[:, :, :, pl.ds(0, 1536)], xb)
    load("ggu", i_ggu, ggu)
    load("dy", i_dy, dyb)
    load("hw", i_hw, hw)
    load("gown", i_gsum.at[z], gown)
    for name, src, dst in (("res", i_res, res), ("gates", i_gates, gates), ("kept", i_kept, kept),
                           ("small", i_small, smalls),
                           ("projw", i_projw, projw), ("probs", i_probs, probs), ("q", i_q, qs), ("k", i_k, ks),
                           ("v", i_v, vs), ("att", i_att, att), ("qkvw", i_qkvw, qkvw)):
        load(name, src, dst)

    barrier = pltpu.get_barrier_semaphore()
    for to in dpl + dz[1:] + [dsib]:
        pl.semaphore_signal(barrier, 1, device_id=to, device_id_type=MESH)
    pl.semaphore_wait(barrier, 7)

    def remote(src, dst, s, r, to):
        return pltpu.make_async_remote_copy(src, dst, s, r, device_id=to, device_id_type=MESH)

    def copy1(q, b):
        return remote(gw.at[q // 2, slot(1, b), lax.rem(q, 2)], recv1.at[q, b], s1.at[q, b], r1.at[q, b], d1)

    def copy2(q):
        return remote(send2.at[lax.rem(q, 2)], recv2.at[q], s2.at[q], r2.at[q], d2)

    def copyz(q, k):
        return remote(zs.at[lax.rem(q, 2), zk[k]], zr.at[q, z], sz.at[q, k - 1], rz.at[q, k - 1], dz[k])

    def rows(q, p):
        return pl.ds(pl.multiple_of(((q // 2) * 8 + p * 2 + lax.rem(q, 2)) * 256, 256), 256)

    def copya(q, i):
        p, who = ((p0, d1), (p0, d2), (p1, d2))[i]
        src = agv.at[lax.rem(q, 2)] if i < 2 else o_e.at[c, rows(q, p)]
        return remote(src, o_e.at[c, rows(q, p)], sa.at[q, i], ra.at[q, i], who)

    def copys(q, i):
        p = (p0, p1, p2, p3)[i]
        src = agv.at[lax.rem(q, 2)] if i == 0 else o_e.at[c, rows(q, p)]
        return remote(src, o_e.at[c, rows(q, p)], ss.at[q, i], rs.at[q, i], dsib)

    def keep(q):
        return pltpu.make_async_copy(agv.at[lax.rem(q, 2)], o_e.at[c, rows(q, p0)], la.at[q])

    def c_g(k):
        return remote(i_gsum.at[zk[k]], grecv.at[k - 1], s_g.at[k - 1], r_g.at[k - 1], dz[k])

    def c_o(k):
        return remote(i_osum.at[zk[k]], o_op.at[k], s_o.at[k - 1], r_o.at[k - 1], dz[k])

    def c_gr(i):
        blk = gres.at[c, p1 if i == 2 else p0]
        return remote(blk, blk, s_gr.at[i], r_gr.at[i], d1 if i == 0 else d2)

    def c_grc(i):
        p = (p0, p1, p2, p3)[i]
        return remote(gres.at[c, p], gres.at[c, p], s_grc.at[i], r_grc.at[i], dsib)

    def c_sib():
        return remote(dyb.at[0], sibr, s_sib, r_sib, dsib)

    def c_pl(i):
        return remote(dyb.at[1, i], plr.at[i], s_pl.at[i], r_pl.at[i], d2 if i == 1 else d1)

    def c_qz(k):
        return remote(qgp.at[zk[k]], qz.at[k - 1], s_qz.at[k - 1], r_qz.at[k - 1], dz[k])

    def c_qo(i):
        dst = o_qg.at[(p1 if i == 2 else p0) * 2 + c]
        return remote(dst if i == 2 else qgo, dst, s_qo.at[i], r_qo.at[i], d1 if i == 0 else d2)

    def c_qoc(i):
        r = (p0, p1, p2, p3)[i] * 2 + c
        return remote(qgo if i == 0 else o_qg.at[r], o_qg.at[r], s_qoc.at[i], r_qoc.at[i], dsib)

    def c_p1(i):
        return remote(pgp.at[peers[i]], pgr.at[p0], s_p1.at[i], r_p1.at[i], dpl[i])

    def c_p2(k):
        return remote(pgr.at[zk[k]], pq2.at[k - 1], s_p2.at[k - 1], r_p2.at[k - 1], dz[k])

    def c_po(i):
        dst = o_pg.at[c, p1 if i == 2 else p0]
        return remote(dst if i == 2 else pgo, dst, s_po.at[i], r_po.at[i], d1 if i == 0 else d2)

    def c_poc(i):
        p = (p0, p1, p2, p3)[i]
        return remote(pgo if i == 0 else o_pg.at[c, p], o_pg.at[c, p], s_poc.at[i], r_poc.at[i], dsib)

    def lanes_of(zz):
        return pl.ds(pl.multiple_of(zz * 384, 384), 384)

    def c_tz(k):
        return remote(terms.at[:, lanes_of(zk[k])], tz.at[k], s_tz.at[k - 1], r_tz.at[k - 1], dz[k])

    def c_ts():
        return remote(tz.at[0], tsib, s_ts, r_ts, dsib)

    def c_tp(i):
        return remote(tpl.at[p0], tpl.at[p0], s_tp.at[i], r_tp.at[i], dpl[i])

    saves = [pltpu.make_async_copy(gtok, o_gtok, sv.at[0]),
             pltpu.make_async_copy(qgo, o_qg.at[p0 * 2 + c], sv.at[1]),
             pltpu.make_async_copy(pgo, o_pg.at[c, p0], sv.at[2]),
             pltpu.make_async_copy(tout, o_terms, sv.at[3])]
    own_out = pltpu.make_async_copy(i_osum.at[z], o_op.at[0], sv.at[5])
    own_out.start()
    act_load = pltpu.make_async_copy(i_act, xb, sv.at[4])

    for k in (1, 2, 3):
        c_g(k).start()
    loads["gw"].wait()
    loads["r1"].wait()
    loads["x"].wait()
    loads["ggu"].wait()
    loads["dy"].wait()
    loads["hw"].wait()

    def stage1(q):
        @pl.when(lax.rem(q, 2) == 0)
        def _():
            gradient_rows(q // 2, xb, dyb, ggu, hw, gw.at[q // 2])
        for b in range(2):
            copy1(q, b).start()

    def stage2(q):
        @pl.when(q >= 2)
        def _():
            for b in range(2):
                copy1(q, b).wait_recv()

        def one(zz, _):
            send2[lax.rem(q, 2), zz] = (gw[q // 2, p2, lax.rem(q, 2), zz].astype(F32)
                                        + recv1[q, 1, zz].astype(F32)).astype(BF)
            return 0
        lax.fori_loop(0, 4, one, 0)
        copy2(q).start()

    def stage3(q):
        copy2(q).wait()

        def one(zz, _):
            zs[lax.rem(q, 2), zz] = (gw[q // 2, p0, lax.rem(q, 2), zz].astype(F32) + recv1[q, 0, zz].astype(F32)
                                     + recv2[q, zz].astype(F32)).astype(BF)
            return 0
        lax.fori_loop(0, 4, one, 0)
        for k in range(1, 4):
            copyz(q, k).start()
        zr[q, z] = zs[lax.rem(q, 2), z]

    def stage4(q):
        for k in range(1, 4):
            copyz(q, k).wait()

        @pl.when(q >= 2)
        def _():
            copya(q - 2, 0).wait_send()
            copya(q - 2, 1).wait_send()
            copys(q - 2, 0).wait_send()
            keep(q - 2).wait()
        for zz in range(4):
            for j in range(4):
                for l in range(wide // 128):
                    ib[l, pl.ds(zz * 4 + j, 16, stride=EXPERTS), :] = (
                        zr[q, zz, j, :, l * 128 : (l + 1) * 128].astype(F32))
        for l in range(wide // 128):
            agv[lax.rem(q, 2), :, l * 128 : (l + 1) * 128] = ib[l].astype(BF)
        copya(q, 0).start()
        copys(q, 0).start()
        keep(q).start()

    def stage5(q):
        copya(q, 0).wait_recv()
        copya(q, 1).start()
        copya(q, 2).start()
        copys(q, 1).start()

    def stage6(q):
        copya(q, 1).wait_recv()
        copya(q, 2).wait_recv()
        copys(q, 2).start()
        copys(q, 3).start()

    def stage7(q):
        for i in range(4):
            copys(q, i).wait_recv()

    def norm_two():
        r = res[...]
        inv = lax.rsqrt(jnp.mean(r * r, axis=1, keepdims=True) + EPS)
        return inv, r * inv

    def norm_one():
        t = tok[...].astype(F32)
        inv = lax.rsqrt(jnp.mean(t * t, axis=1, keepdims=True) + EPS)
        return inv, t * inv

    def gain(row):
        return jnp.concatenate([smalls[i, row : row + 1, :] for i in range(4)], axis=1).astype(F32)

    def event_residual():
        for name in ("gown", "res", "gates", "kept", "small"):
            loads[name].wait()
        for k in (1, 2, 3):
            c_g(k).wait_recv()

        def gate_part(v):
            return v[:, 1536 : 1536 + EXPERTS].astype(F32) + v[:, 1536 + EXPERTS : 1536 + 2 * EXPERTS].astype(F32)
        gg = (gate_part(gown[...]) + gate_part(grecv[0]) + gate_part(grecv[1]) + gate_part(grecv[2])) * kept[...]
        gt = gates[...]
        gl = (gt * (gg - jnp.sum(gt * gg, axis=1, keepdims=True))).astype(BF)
        router_t = jnp.concatenate([smalls[i, 16:32, :] for i in range(4)], axis=1)
        ga = jnp.dot(gl, router_t, preferred_element_type=F32)
        ga = ga + gown[:, :1536].astype(F32)
        for k in range(3):
            ga = ga + grecv[k, :, :1536].astype(F32)
        inv, normed = norm_two()
        terms[8:24, :] = lax.dot_general(gl, xb[c, z], (((0,), (0,)), ((), ())), preferred_element_type=F32)
        terms[1:2, :] = jnp.sum(ga * normed, axis=0, keepdims=True)
        scaled = ga * gain(1)
        gr = dyb[c, z].astype(F32) + inv * (scaled - normed * jnp.mean(scaled * normed, axis=1, keepdims=True))
        gresf[...] = gr
        gres[c, p0] = gr.astype(BF)
        for i in range(2):
            c_gr(i).start()
        c_grc(0).start()

    def event_share():
        for k in (1, 2, 3):
            c_o(k).start()
        for i in range(3):
            c_gr(i).wait_recv()
            if i == 0:
                c_gr(2).start()
            c_grc(i + 1).start()
        act_load.start()

    scale = 64 ** -0.5

    def event_attention():
        for name in ("projw", "probs", "q", "k", "v", "att", "qkvw"):
            loads[name].wait()
        for i in range(4):
            c_grc(i).wait_recv()

        def one(n, _):
            cc, i = n // 4, lax.rem(n, 4)
            gb = lax.dot_general(gres[cc, i], projw[...], (((1,), (1,)), ((), ())),
                                 preferred_element_type=F32).astype(BF)
            ga = jnp.concatenate([gb[:, h * 64 : (h + 1) * 64] for h in range(3)], axis=0)
            pb = probs[cc, i]
            gv = lax.dot_general(pb.astype(BF), ga, (((0,), (0,)), ((), ())), preferred_element_type=F32)
            gp = lax.dot_general(ga, vs[cc, i], (((1,), (1,)), ((), ())), preferred_element_type=F32)
            gs = (pb * (gp - jnp.sum(pb * gp, axis=-1, keepdims=True))).astype(BF)
            gq = jnp.dot(gs, ks[cc, i], preferred_element_type=F32) * scale
            gk = lax.dot_general(gs, qs[cc, i], (((0,), (0,)), ((), ())), preferred_element_type=F32) * scale
            lo = jnp.concatenate([gq[0:128], gq[128:256]], axis=1)
            hi = jnp.concatenate([gq[256:384], gk], axis=1)
            gproj[cc, i, :, 0:128] = turn(lo, cos_t[...], -sin_t[...]).astype(BF)
            gproj[cc, i, :, 128:256] = turn(hi, cos_t[...], -sin_t[...]).astype(BF)
            gproj[cc, i, :, 256:320] = gv.astype(BF)
            return 0
        lax.fori_loop(0, 8, one, 0)

        def to_sib(i, _):
            dyb[0, i] = lax.dot_general(gproj[1 - c, i], qkvw[...], (((1,), (1,)), ((), ())),
                                        preferred_element_type=F32).astype(BF)
            return 0
        lax.fori_loop(0, 4, to_sib, 0)
        c_sib().start()
        pg = lax.dot_general(att[...].reshape(1024, 192), gres[...].reshape(1024, 1536), (((0,), (0,)), ((), ())),
                             preferred_element_type=F32)
        pgp[...] = pg.astype(BF).reshape(4, 48, 1536)
        for i in range(3):
            c_p1(i).start()
        pgr[p0] = pgp[p0]

    def event_columns():
        act_load.wait()

        def one(zz, _):
            a = xb[:, :, :, lanes_of(zz)].reshape(1024, 384)
            qgp[zz] = lax.dot_general(a, gproj[...].reshape(1024, 320), (((0,), (0,)), ((), ())),
                                      preferred_element_type=F32).astype(BF)
            return 0
        lax.fori_loop(0, 4, one, 0)
        for k in (1, 2, 3):
            c_qz(k).start()
        c_sib().wait()

        def part(p):
            return lax.dot_general(gproj[c, p], qkvw[...], (((1,), (1,)), ((), ())),
                                   preferred_element_type=F32) + sibr[p].astype(F32)
        for i in (2, 0):
            dyb[1, i] = part(peers[i]).astype(BF)
            c_pl(i).start()
        dyb[1, 1] = part(p2).astype(BF)
        gtok[...] = part(p0)
        for i in range(3):
            c_p1(i).wait_recv()
        for k in (1, 2, 3):
            c_p2(k).start()

    def event_second():
        c_pl(2).wait_recv()
        dyb[1, 1] = (dyb[1, 1].astype(F32) + plr[2].astype(F32)).astype(BF)
        c_pl(1).start()
        for k in (1, 2, 3):
            c_qz(k).wait_recv()
        qgo[...] = (qgp[z].astype(F32) + qz[0].astype(F32) + qz[1].astype(F32) + qz[2].astype(F32)).astype(BF)
        for i in range(2):
            c_qo(i).start()
        c_qoc(0).start()
        saves[1].start()
        for k in (1, 2, 3):
            c_p2(k).wait_recv()
        pgo[...] = (pgr[z].astype(F32) + pq2[0].astype(F32) + pq2[1].astype(F32) + pq2[2].astype(F32)).astype(BF)
        for i in range(2):
            c_po(i).start()
        c_poc(0).start()
        saves[2].start()

    def event_tokens():
        ga = gtok[...]
        for i in range(2):
            c_pl(i).wait_recv()
            ga = ga + plr[i].astype(F32)
        inv, normed = norm_one()
        terms[0:1, :] = jnp.sum(ga * normed, axis=0, keepdims=True)
        scaled = ga * gain(0)
        gtok[...] = gresf[...] + inv * (scaled - normed * jnp.mean(scaled * normed, axis=1, keepdims=True))
        saves[0].start()
        for k in (1, 2, 3):
            c_tz(k).start()
        for copy, over in ((c_qo, c_qoc), (c_po, c_poc)):
            copy(0).wait_recv()
            copy(2).start()
            over(1).start()
            copy(1).wait_recv()
            over(2).start()

    def event_terms():
        for k in (1, 2, 3):
            c_tz(k).wait_recv()
        tz[0] = terms[:, lanes_of(z)] + tz[1] + tz[2] + tz[3]
        c_ts().start()
        for copy, over in ((c_qo, c_qoc), (c_po, c_poc)):
            copy(2).wait_recv()
            over(3).start()
        c_ts().wait()
        tpl[p0] = tz[0] + tsib[...]
        for i in range(3):
            c_tp(i).start()

    def event_last():
        for i in range(3):
            c_tp(i).wait_recv()
        tout[...] = tpl[0] + tpl[1] + tpl[2] + tpl[3]
        saves[3].start()
        for i in range(4):
            c_qoc(i).wait_recv()
            c_poc(i).wait_recv()
        for k in (1, 2, 3):
            c_o(k).wait_recv()

    stages = (stage1, stage2, stage3, stage4, stage5, stage6, stage7)
    lead = 4
    for q in (2, 3):
        stage1(jnp.int32(q))
    for q in range(1):
        stage2(jnp.int32(q))
    events = {2: event_residual, 3: event_share, 4: event_attention, 5: event_columns, 6: event_second,
              7: event_tokens, 8: event_terms, 9: event_last}

    def step(t, _):
        for i, stage in enumerate(stages):
            q = t + lead if i == 0 else t + 2 - i

            @pl.when((q >= 0) & (q < nq))
            def _(stage=stage, q=q):
                stage(q)
        for at, event in events.items():
            @pl.when(t == at)
            def _(event=event):
                event()
        return 0

    lax.fori_loop(0, nq + len(stages) - 2, step, 0)

    def left(q, _):
        @pl.when(q >= 2)
        def _():
            for b in range(2):
                copy1(q, b).wait_send()
        for i in range(1, 4):
            copys(q, i).wait_send()
        copya(q, 2).wait_send()

        @pl.when(q >= nq - 2)
        def _():
            copya(q, 0).wait_send()
            copya(q, 1).wait_send()
            copys(q, 0).wait_send()
            keep(q).wait()
        return 0
    lax.fori_loop(0, nq, left, 0)
    for k in (1, 2, 3):
        for one in (c_g(k), c_o(k), c_qz(k), c_p2(k), c_tz(k)):
            one.wait_send()
    for i in range(3):
        for one in (c_gr(i), c_pl(i), c_qo(i), c_p1(i), c_po(i), c_tp(i)):
            one.wait_send()
    for i in range(4):
        for one in (c_grc(i), c_qoc(i), c_poc(i)):
            one.wait_send()
    for one in saves + [own_out]:
        one.wait()


def back(front_outs, tok, cos_t, sin_t):
    nq, wide = 6, 3 * HID // 2
    sem, vm = pltpu.SemaphoreType.DMA, pltpu.VMEM
    out = lambda shape, kind=BF: jax.ShapeDtypeStruct(shape, kind)
    piece = (4, 4, 16, wide)
    outs = (out((2, 6144, wide)), out((128, 1536), F32), out((8, 384, 320)), out((2, 4, 48, 1536)),
            out((24, 384), F32), out((4, 128, 1536)))
    block, quad, three = vm((2, 4, 128, 1536), BF), vm((4, 128, 1536), BF), vm((3, 128, 1536), BF)
    scratch = [
        block, block, vm((4, 1024, 512), BF), vm((4, 1024, 256), BF), vm((2, 4, 384, 64), BF),
        vm((2, 4, 128, 64), BF), vm((2, 4, 128, 64), BF), vm((2, 4, 384, 128), F32), vm((2, 4, 128, 192), BF),
        vm((1536, 320), BF), vm((192, 1536), BF), vm((4, 32, 384), BF), vm((128, 1536), F32), vm((128, 16), F32), vm((128, 16), F32),
        vm((128, 1664), BF), vm((3, 128, 1664), BF),
        vm((3, 4, 2) + piece, BF), vm((nq, 2) + piece, BF), vm((2,) + piece, BF), vm((nq,) + piece, BF),
        vm((2,) + piece, BF), vm((nq,) + piece, BF), vm((wide // 128, 256, 128), F32), vm((2, 256, wide), BF),
        block, vm((128, 1536), F32), vm((2, 4, 128, 320), BF), quad, three, vm((4, 384, 320), BF),
        vm((3, 384, 320), BF), vm((384, 320), BF), vm((4, 48, 1536), BF), vm((4, 48, 1536), BF),
        vm((3, 48, 1536), BF), vm((48, 1536), BF), vm((24, 1536), F32), vm((4, 24, 384), F32),
        vm((24, 384), F32), vm((4, 24, 384), F32), vm((24, 384), F32), vm((128, 1536), F32),
    ]
    n3, n4, one = sem((3,)), sem((4,)), sem(())
    sems = [
        sem((nq, 2)), sem((nq, 2)), sem((nq,)), sem((nq,)), sem((nq, 3)), sem((nq, 3)), sem((nq, 3)), sem((nq, 3)),
        sem((nq, 4)), sem((nq, 4)), sem((nq,)),
        n3, n3, n3, n3, n4, n4, one, one, n3, n3, n3, n3, n3, n3,
        n4, n4, n3, n3, n3, n3, n3, n3, n4, n4, n3, n3, one, one,
        n3, n3, n3, n3, sem((18,)), sem((6,)),
    ]
    vmem, any_ = pl.BlockSpec(memory_space=pltpu.VMEM), pl.BlockSpec(memory_space=pl.ANY)
    return pl.pallas_call(
        back_kernel,
        out_shape=outs,
        in_specs=[any_] * 20 + [vmem] * 3,
        out_specs=[any_] * len(outs),
        scratch_shapes=scratch + sems,
        compiler_params=pltpu.CompilerParams(
            collective_id=2, has_side_effects=True, vmem_limit_bytes=62 * 1024 * 1024),
        name="back",
    )(*front_outs, tok, cos_t, sin_t)


def finish_kernel(v, qkv, proj, res, parts, terms, gu, dn, g_qkv, g_proj, out, g_router):
    half = HID // 2
    for c in range(2):
        gu[:, c * half : (c + 1) * half] = v[c, :, :half].astype(F32)
        gu[:, HID + c * half : HID + (c + 1) * half] = v[c, :, half : 2 * half].astype(F32)
        dn[:, c * half : (c + 1) * half] = v[c, :, 2 * half :].astype(F32)
    heads = range(qkv.shape[0])
    g_qkv[...] = jnp.concatenate(
        [qkv[h, :, lo:hi].astype(F32) for lo, hi in ((0, 192), (192, 256), (256, 320)) for h in heads], axis=1)
    g_proj[...] = proj[...].astype(F32)

    @pl.when(pl.program_id(0) == 0)
    def _():
        total = res[...]
        for k in range(4):
            total = total + parts[k].astype(F32)
        out[...] = total.astype(BF)
        g_router[...] = terms[8:, :]


def finish(v, qkv, proj, res, parts, terms):
    steps, own, width = 3, proj.shape[0], proj.shape[1]
    row, some = v.shape[1] // steps, own // steps
    once = lambda n: (lambda i: (0,) * n)
    return pl.pallas_call(
        finish_kernel,
        grid=(steps,),
        out_shape=(
            jax.ShapeDtypeStruct((v.shape[1], 2 * HID), F32), jax.ShapeDtypeStruct((v.shape[1], HID), F32),
            jax.ShapeDtypeStruct((own, 2560), F32), jax.ShapeDtypeStruct((own, width), F32),
            jax.ShapeDtypeStruct(res.shape, BF), jax.ShapeDtypeStruct((EXPERTS, own), F32)),
        in_specs=[
            pl.BlockSpec((2, row, v.shape[2]), lambda i: (0, i, 0)),
            pl.BlockSpec((8, some, 320), lambda i: (0, i, 0)), pl.BlockSpec((some, width), lambda i: (i, 0)),
            pl.BlockSpec(res.shape, once(2)), pl.BlockSpec(parts.shape, once(3)),
            pl.BlockSpec(terms.shape, once(2))],
        out_specs=[
            pl.BlockSpec((row, 2 * HID), lambda i: (i, 0)), pl.BlockSpec((row, HID), lambda i: (i, 0)),
            pl.BlockSpec((some, 2560), lambda i: (i, 0)), pl.BlockSpec((some, width), lambda i: (i, 0)),
            pl.BlockSpec(res.shape, once(2)), pl.BlockSpec((EXPERTS, own), once(2))],
        compiler_params=pltpu.CompilerParams(vmem_limit_bytes=62 * 1024 * 1024),
        name="finish",
    )(v, qkv, proj, res, parts, terms)


def expert_grads_general(reps, grps, xs, dys, ggu, hw):
    local, half, width = ggu.shape[0], HID // 2, xs.shape[1]
    own = width // grps
    chips = reps // 2
    piece = own // chips
    same_core = [[2 * i + c for i in range(chips)] for c in range(2)]
    pairs = [[2 * i, 2 * i + 1] for i in range(chips)]
    up = jnp.einsum("td,eth->edh", xs, ggu, preferred_element_type=F32).astype(BF)
    down = jnp.einsum("td,eth->edh", dys, hw, preferred_element_type=F32).astype(BF)
    gw = jnp.concatenate([up, down], axis=2)
    gw = gw.reshape(local, grps, chips, piece, 3 * half).transpose(2, 1, 3, 0, 4)
    gw = gw.reshape(chips * grps * piece, local * 3 * half)
    gw = lax.psum_scatter(gw, "rep", scatter_dimension=0, tiled=True, axis_index_groups=same_core)
    gw = lax.all_to_all(gw.reshape(grps, piece, local, 3 * half), "grp", 0, 0, tiled=True)
    gw = gw.transpose(1, 0, 2, 3).reshape(piece, EXPERTS, 3 * half)
    gw = lax.all_gather(gw, "rep", axis=0, tiled=True, axis_index_groups=same_core)
    gw = lax.all_gather(gw, "rep", axis=0, tiled=False, axis_index_groups=pairs).astype(F32)
    gw = gw.reshape(2, own * EXPERTS, 3, half)
    gw = jnp.moveaxis(gw, 0, 2).reshape(own * EXPERTS, 3 * HID)
    return gw[:, : 2 * HID], gw[:, 2 * HID :]


def shards_general(
    reps,
    grps,
    tokens,
    attn_gain,
    query_key_value_weight,
    attn_proj,
    mlp_gain,
    w_router,
    w_gate_up,
    w_down,
    prefix_len,
    expert_ids,
    priority,
    cotangent,
):
    seq, width = tokens.shape
    own = width // grps
    local_experts = EXPERTS // grps
    heads = KEY_VALUE_HEADS
    groups = None if reps == heads else [list(range(i, i + heads)) for i in range(0, reps, heads)]
    rep, grp = lax.axis_index("rep"), lax.axis_index("grp")
    head = lax.rem(rep, heads)
    qw, hw = QPK * HEAD_WIDTH, HEAD_WIDTH
    q_all = QUERY_HEADS * HEAD_WIDTH

    small = jnp.concatenate([attn_gain[:, None], mlp_gain[:, None], w_router], axis=1)
    small = lax.all_gather(small, "grp", axis=0, tiled=True)
    gain_one, gain_two = small[:, 0].astype(F32)[None, :], small[:, 1].astype(F32)[None, :]
    router = small[:, 2:]
    qkv_cols = jnp.concatenate(
        [
            lax.dynamic_slice_in_dim(query_key_value_weight, head * qw, qw, 1),
            lax.dynamic_slice_in_dim(query_key_value_weight, q_all + head * hw, hw, 1),
            lax.dynamic_slice_in_dim(query_key_value_weight, q_all + heads * hw + head * hw, hw, 1),
        ],
        axis=1,
    )
    qkv_head = lax.all_gather(qkv_cols, "grp", axis=0, tiled=True)
    row = head * qw + jnp.arange(qw)
    mine = (row // own) == grp
    proj_rows = jnp.where(mine[:, None], jnp.take(attn_proj, jnp.where(mine, row - grp * own, 0), axis=0), 0)
    proj_head = lax.psum(proj_rows, "grp")

    core, chip, chips, half = lax.rem(rep, 2), rep // 2, reps // 2, HID // 2
    pairs = [[2 * i, 2 * i + 1] for i in range(chips)]
    same_core = [[2 * i + c for i in range(chips)] for c in range(2)]
    piece = own // chips
    gu_piece = lax.dynamic_slice_in_dim(w_gate_up, chip * piece, piece, 0)
    dn_piece = lax.dynamic_slice_in_dim(w_down, chip * piece, piece, 0)
    both = jnp.concatenate(
        [
            lax.dynamic_slice_in_dim(gu_piece, core * half, half, 2),
            lax.dynamic_slice_in_dim(gu_piece, HID + core * half, half, 2),
            lax.dynamic_slice_in_dim(dn_piece, core * half, half, 2),
        ],
        axis=2,
    )
    both = both.reshape(piece, grps, local_experts, 3 * half).transpose(1, 2, 0, 3)
    both = lax.all_to_all(both, "grp", 0, 0, tiled=True)
    both = lax.all_gather(both, "rep", axis=0, tiled=False, axis_index_groups=same_core)
    both = both.transpose(2, 1, 0, 3, 4).reshape(local_experts, width, 3 * half)
    wgu, wdn = both[:, :, : 2 * half], both[:, :, 2 * half :]

    tokens_f = tokens.astype(F32)
    inverse_one = lax.rsqrt(jnp.mean(tokens_f * tokens_f, axis=1, keepdims=True) + EPS)
    normed_one = tokens_f * inverse_one
    act_one = (normed_one * gain_one).astype(BF)
    act_plane = lax.all_gather(act_one, "rep", axis=0, tiled=True, axis_index_groups=groups)
    prefix_plane = lax.all_gather(prefix_len, "rep", axis=0, tiled=True, axis_index_groups=groups)
    cos, sin = rope_tables(seq)
    projected = dot(act_plane, qkv_head).reshape(heads, seq, QPK + 2, HEAD_WIDTH)
    cos_b, sin_b = cos[None, :, None, :], sin[None, :, None, :]
    turned = rotate(projected[:, :, : QPK + 1], cos_b, sin_b).astype(BF)
    query = turned[:, :, :QPK]
    key = turned[:, :, QPK]
    value = projected[:, :, QPK + 1].astype(BF)
    scale = HEAD_WIDTH ** (-0.5)
    row_pos, col_pos = jnp.arange(seq)[:, None], jnp.arange(seq)[None, :]
    allowed = (col_pos <= row_pos)[None] | (col_pos[None] < prefix_plane[:, None, None])
    scores = jnp.einsum("bsgd,btd->bgst", query, key, preferred_element_type=F32) * scale
    scores = jnp.where(allowed[:, None], scores, -1e30)
    exps = jnp.exp(scores - jnp.max(scores, axis=-1, keepdims=True))
    probs = exps / jnp.sum(exps, axis=-1, keepdims=True)
    probs_low = probs.astype(BF)
    attended = jnp.einsum("bgst,btd->bsgd", probs_low, value, preferred_element_type=F32)
    attended = attended.astype(BF).reshape(heads * seq, qw)
    part = dot(attended, proj_head).astype(BF)
    part = lax.psum_scatter(part, "rep", scatter_dimension=0, tiled=True, axis_index_groups=groups)
    residual = tokens_f + part.astype(F32)
    inverse_two = lax.rsqrt(jnp.mean(residual * residual, axis=1, keepdims=True) + EPS)
    normed_two = residual * inverse_two
    act_two = (normed_two * gain_two).astype(BF)
    gates, kept = routing(expert_ids, priority, dot(act_two, router))

    def column(v):
        v = lax.all_gather(v, "grp", axis=0, tiled=True)
        return lax.all_gather(v, "rep", axis=0, tiled=True, axis_index_groups=pairs)

    def to_owners(v):
        v = lax.psum_scatter(v, "rep", scatter_dimension=0, tiled=True, axis_index_groups=pairs)
        return lax.psum_scatter(v, "grp", scatter_dimension=0, tiled=True).astype(F32)

    dy_all = column(cotangent)
    x_all = column(act_two)
    weight = column(jnp.where(kept, gates, 0.0))
    weight = lax.dynamic_slice_in_dim(weight, grp * local_experts, local_experts, 1).T[:, :, None]
    gate_up = jnp.einsum("td,edh->eth", x_all, wgu, preferred_element_type=F32)
    g, u = gate_up[..., :half], gate_up[..., half:]
    sig = jax.nn.sigmoid(g)
    silu = g * sig
    hidden = silu * u
    hidden_w = (hidden * weight).astype(BF)
    back = jnp.einsum("td,edh->eth", dy_all, wdn, preferred_element_type=F32)
    grad_gate_part = jnp.sum(back * hidden, axis=2)
    grad_hidden = back * weight
    ggu = jnp.concatenate(
        [grad_hidden * u * sig * (1.0 + g * (1.0 - sig)), grad_hidden * silu], axis=2
    ).astype(BF)
    out_part = jnp.einsum("eth,edh->td", hidden_w, wdn, preferred_element_type=F32).astype(BF)
    gact_part = jnp.einsum("eth,edh->td", ggu, wgu, preferred_element_type=F32).astype(BF)
    gact = to_owners(gact_part)
    grad_gates = lax.psum_scatter(
        grad_gate_part.T, "rep", scatter_dimension=0, tiled=True, axis_index_groups=pairs
    )
    grad_gates = lax.all_to_all(grad_gates, "grp", 0, 1, tiled=True)
    grad_gates = jnp.where(kept, grad_gates, 0.0)
    out = to_owners(out_part)
    output = (residual + out).astype(BF)
    grad_gu, grad_dn = expert_grads_general(reps, grps, x_all, dy_all, ggu, hidden_w)
    grad_gu = grad_gu.reshape(own, EXPERTS, 2 * HID)
    grad_dn = grad_dn.reshape(own, EXPERTS, HID)

    grad_logits = (gates * (grad_gates - jnp.sum(gates * grad_gates, axis=1, keepdims=True))).astype(BF)
    gact = gact + dot(grad_logits, router.T)
    router_term = dot(act_two.T, grad_logits)
    gain_two_term = jnp.sum(gact * normed_two, axis=0)
    scaled = gact * gain_two
    dy = cotangent.astype(F32)
    grad_residual = dy + inverse_two * (
        scaled - normed_two * jnp.mean(scaled * normed_two, axis=1, keepdims=True)
    )
    gres_low = grad_residual.astype(BF)

    gres_plane = lax.all_gather(gres_low, "rep", axis=0, tiled=True, axis_index_groups=groups)
    proj_term = dot(attended.T, gres_plane)
    grad_att = dot(gres_plane, proj_head.T).astype(BF).reshape(heads, seq, QPK, HEAD_WIDTH)
    grad_value = jnp.einsum("bgst,bsgd->btd", probs_low, grad_att, preferred_element_type=F32)
    grad_probs = jnp.einsum("bsgd,btd->bgst", grad_att, value, preferred_element_type=F32)
    grad_scores = (
        probs * (grad_probs - jnp.sum(probs * grad_probs, axis=-1, keepdims=True))
    ).astype(BF)
    grad_query = jnp.einsum("bgst,btd->bsgd", grad_scores, key, preferred_element_type=F32) * scale
    grad_key = jnp.einsum("bgst,bsgd->btd", grad_scores, query, preferred_element_type=F32) * scale
    turned_back = rotate(
        jnp.concatenate([grad_query, grad_key[:, :, None]], axis=2), cos_b, -sin_b
    )
    gproj = jnp.concatenate([turned_back, grad_value[:, :, None]], axis=2).astype(BF)
    gproj = gproj.reshape(heads * seq, qw + 2 * hw)
    qkv_term = dot(act_plane.T, gproj)
    gact_one = dot(gproj, qkv_head.T).astype(BF)
    gact_one = lax.psum_scatter(
        gact_one, "rep", scatter_dimension=0, tiled=True, axis_index_groups=groups
    ).astype(F32)
    gain_one_term = jnp.sum(gact_one * normed_one, axis=0)
    scaled_one = gact_one * gain_one
    grad_tokens = grad_residual + inverse_one * (
        scaled_one - normed_one * jnp.mean(scaled_one * normed_one, axis=1, keepdims=True)
    )

    qkv_own = lax.psum_scatter(qkv_term.astype(BF), "grp", scatter_dimension=0, tiled=True)
    proj_sum = lax.psum(proj_term.astype(BF), "grp")
    if groups is not None:
        across = [[i + heads * j for j in range(reps // heads)] for i in range(heads)]
        qkv_own = lax.psum(qkv_own, "rep", axis_index_groups=across)
        proj_sum = lax.psum(proj_sum, "rep", axis_index_groups=across)
    qkv_own = lax.all_gather(qkv_own, "rep", axis=0, tiled=False, axis_index_groups=groups)
    qkv_own = qkv_own.astype(F32)
    grad_qkv = jnp.concatenate(
        [
            qkv_own[:, :, lo:hi].transpose(1, 0, 2).reshape(own, -1)
            for lo, hi in ((0, qw), (qw, qw + hw), (qw + hw, qw + 2 * hw))
        ],
        axis=1,
    )
    proj_all = lax.all_gather(proj_sum, "rep", axis=0, tiled=True, axis_index_groups=groups)
    grad_proj = lax.dynamic_slice_in_dim(proj_all, grp * own, own, 0).astype(F32)
    terms = jnp.concatenate([gain_one_term[:, None], gain_two_term[:, None], router_term], axis=1)
    terms = lax.psum(lax.psum_scatter(terms, "grp", scatter_dimension=0, tiled=True), "rep")
    return (
        output,
        grad_tokens,
        terms[:, 0],
        grad_qkv,
        grad_proj,
        terms[:, 1],
        terms[:, 2:],
        grad_gu,
        grad_dn,
    )


def shards(
    tokens,
    attn_gain,
    query_key_value_weight,
    attn_proj,
    mlp_gain,
    w_router,
    w_gate_up,
    w_down,
    prefix_len,
    expert_ids,
    priority,
    cotangent,
):
    own, width = attn_gain.shape[0], tokens.shape[1]
    small = jnp.concatenate(
        [attn_gain[None], mlp_gain[None], jnp.zeros((14, own), BF), w_router.T], axis=0
    )
    half = HEAD_WIDTH // 2
    inverse_freq = np.float32(10000.0) ** (-np.arange(half, dtype=np.float32) * np.float32(2.0 / HEAD_WIDTH))
    angles = np.arange(tokens.shape[0], dtype=np.float32)[:, None] * inverse_freq[None, :]
    cos_t = jnp.asarray(np.tile(np.cos(angles), (1, 4)), F32)
    sin = np.sin(angles)
    sin_t = jnp.asarray(np.tile(np.concatenate([-sin, sin], axis=1), (1, 2)), F32)
    parts = front(
        tokens, cotangent, w_gate_up, w_down, query_key_value_weight, attn_proj, small, expert_ids.T,
        priority.reshape(8, 128), prefix_len, cos_t, sin_t)
    wide, grad_tokens, qkv_own, proj_own, terms, out_parts = back(parts, tokens, cos_t, sin_t)
    grad_gu, grad_dn, grad_qkv, grad_proj, output, grad_router = finish(
        wide, qkv_own, proj_own.reshape(own, width), parts[13], out_parts, terms)
    return (
        output,
        grad_tokens,
        terms[0],
        grad_qkv,
        grad_proj,
        terms[1],
        grad_router.T,
        grad_gu.reshape(own, EXPERTS, 2 * HID),
        grad_dn.reshape(own, EXPERTS, HID),
    )


def solution(mesh):
    tok, par = ("rep", "grp"), "grp"
    in_specs = (
        P(tok, None),
        P(par),
        P(par, None),
        P(par, None),
        P(par),
        P(par, None),
        P(par, None, None),
        P(par, None, None),
        P(tok),
        P(tok, None),
        P(tok, None),
        P(tok, None),
    )
    out_specs = (
        P(tok, None),
        P(tok, None),
        P(par),
        P(par, None),
        P(par, None),
        P(par),
        P(par, None),
        P(par, None, None),
        P(par, None, None),
    )
    reps, grps = mesh.shape["rep"], mesh.shape["grp"]

    def body(*args):
        if (reps, grps) == (8, 4):
            return shards(*args)
        return shards_general(reps, grps, *args)

    return jax.shard_map(body, mesh=mesh, in_specs=in_specs, out_specs=out_specs, check_vma=False)
```

```python
import jax
import jax.numpy as jnp
import numpy as np
from jax import lax
from jax.experimental import pallas as pl
from jax.experimental.pallas import tpu as pltpu
from jax.sharding import PartitionSpec as P

QUERY_HEADS = 24
KEY_VALUE_HEADS = 8
HEAD_WIDTH = 64
HID = 512
EXPERTS = 16
CAP = 72
EPS = 1e-05
BF = jnp.bfloat16
F32 = jnp.float32
QPK = QUERY_HEADS // KEY_VALUE_HEADS
BIG = 1 << 20
MESH = pl.DeviceIdType.MESH


def dot(a, b):
    return jnp.dot(a, b, preferred_element_type=F32)


def rope_tables(length):
    half = HEAD_WIDTH // 2
    position = jnp.arange(length, dtype=F32)[:, None]
    inverse_freq = 10000.0 ** (-jnp.arange(half, dtype=F32) * 2.0 / HEAD_WIDTH)
    angles = position * inverse_freq[None, :]
    return jnp.cos(angles), jnp.sin(angles)


def rotate(v, cos, sin):
    half = HEAD_WIDTH // 2
    a, b = v[..., :half], v[..., half:]
    return jnp.concatenate([a * cos - b * sin, b * cos + a * sin], axis=-1)


def choices(expert_ids, priority):
    seq, top = expert_ids.shape
    choose = expert_ids[:, :, None] == jnp.arange(EXPERTS, dtype=jnp.int32)[None, None, :]
    chosen = jnp.any(choose, axis=1)
    rank_of = jnp.sum(jnp.where(choose, priority.reshape(seq, top)[:, :, None], 0), axis=1)
    rank_of = jnp.where(chosen, rank_of, BIG)
    slot = jnp.sum((rank_of[None, :, :] < rank_of[:, None, :]).astype(jnp.int32), axis=1)
    return chosen, chosen & (slot < CAP)


def routing(expert_ids, priority, logits):
    chosen, kept = choices(expert_ids, priority)
    top_logit = jnp.max(jnp.where(chosen, logits, -jnp.inf), axis=1, keepdims=True)
    gate_exp = jnp.where(chosen, jnp.exp(jnp.where(chosen, logits - top_logit, 0.0)), 0.0)
    gates = gate_exp / jnp.sum(gate_exp, axis=1, keepdims=True)
    return gates, kept


def place():
    r, z = lax.axis_index("rep"), lax.axis_index("grp")
    return r // 4, (r // 2) % 2, r % 2, z


def flip(bit, by):
    return bit + by * (1 - 2 * bit)


def turn(v, cos, sin):
    lane = lax.broadcasted_iota(jnp.int32, v.shape, 1)
    partner = jnp.where(lax.rem(lane, 64) < 32, pltpu.roll(v, 96, 1), pltpu.roll(v, 32, 1))
    return v * cos + partner * sin


def gradient_rows(q3, x, dy, ggu, hw, gw):
    half = HID // 2

    def side(ref):
        return jnp.concatenate(
            [ref[:, :, :, pl.ds(pl.multiple_of(zz * 384 + q3 * 128, 128), 128)].reshape(1024, 128)
             for zz in range(4)], axis=1)
    xs, ds = side(x), side(dy)

    def one(j, _):
        up = lax.dot_general(xs, ggu[j], (((0,), (0,)), ((), ())), preferred_element_type=F32).astype(BF)
        dn = lax.dot_general(ds, hw[j], (((0,), (0,)), ((), ())), preferred_element_type=F32).astype(BF)
        for zz in range(4):
            for p in range(4):
                for h in range(2):
                    at = zz * 128 + p * 32 + h * 16
                    gw[p, h, zz, j, :, : 2 * half] = up[at : at + 16]
                    gw[p, h, zz, j, :, 2 * half :] = dn[at : at + 16]
        return 0
    lax.fori_loop(0, 4, one, 0)


def front_kernel(tok, dy, w_gu, w_dn, qkv, proj, small, ids_t, prio, prefix, cos_t, sin_t,
                 o_x, o_dy, o_ggu, o_hw, o_act, o_q, o_k, o_v, o_probs, o_att, o_qkvw, o_projw,
                 o_small, o_res, o_gates, o_kept, o_gsum, o_osum, o_gw, o_r1,
                 smalls, qkvw, projw, projq, actp, pre, pr, qs, ks, vs, probs, att, part, sibr, sums, plr,
                 xall, dyall, wbuf, ggu, hw, gpart, ggp, gsib,
                 gsum, res, gates, kept, qwin, wst, wcol, wpiece, gw,
                 s_small, r_small, s_qkv, r_qkv, s_pz, r_pz, s_pq, r_pq, s_wz, r_wz, s_wp, r_wp,
                 s_act, r_act, s_pre, r_pre, s_actc, r_actc, s_prec, r_prec, s_sib, r_sib, s_pl, r_pl,
                 s_x, r_x, s_xc, r_xc, s_y, r_y, s_yc, r_yc,
                 s_gc, r_gc, s_oc, r_oc, s1, r1, sl):
    y, x, c, z = place()
    half = HID // 2

    def slot(a, b):
        return flip(y, a * c + b * (1 - c)) * 2 + flip(x, a * (1 - c) + b * c)

    p0, p1, p2, p3 = slot(0, 0), slot(1, 0), slot(0, 1), slot(1, 1)
    peers = (p1, p2, p3)
    d1, d2, dsib = (p1 * 2 + c, z), (p2 * 2 + c, z), (p0 * 2 + 1 - c, z)
    dpl = [(p * 2 + c, z) for p in peers]
    zk = [lax.rem(z + k, 4) for k in range(4)]
    zf = [lax.rem(z + 4 - k, 4) for k in range(4)]
    dz = [(p0 * 2 + c, zz) for zz in zk]

    barrier = pltpu.get_barrier_semaphore()
    for to in dpl + dz[1:] + [dsib]:
        pl.semaphore_signal(barrier, 1, device_id=to, device_id_type=MESH)
    pl.semaphore_wait(barrier, 7)

    def remote(src, dst, s, r, to):
        return pltpu.make_async_remote_copy(src, dst, s, r, device_id=to, device_id_type=MESH)

    def c_small(k):
        return remote(small, smalls.at[z], s_small.at[k - 1], r_small.at[k - 1], dz[k])

    def rows(zz, pp):
        return pl.ds(pl.multiple_of(zz * 384 + pp * 96, 96), 96)

    def c_wz(k):
        return remote(wpiece.at[zk[k]], wbuf.at[:, rows(z, p0)], s_wz.at[k - 1], r_wz.at[k - 1], dz[k])

    def c_wp(k, i):
        zz = zf[k]
        who, pp = ((d1, p0), (d2, p0), (d2, p1))[i]
        src = wpiece.at[z] if (k == 0 and i < 2) else wbuf.at[:, rows(zz, pp)]
        return remote(src, wbuf.at[:, rows(zz, pp)], s_wp.at[k, i], r_wp.at[k, i], who)

    def quarter(p):
        return pl.ds(pl.multiple_of(p * 48, 48), 48)

    def c_pz(k):
        src = proj.at[pl.ds(pl.multiple_of(c * 192 + p0 * 48, 48), 48)]
        return remote(src, projq.at[k - 1], s_pz.at[k - 1], r_pz.at[k - 1], dz[k])

    def c_pq(k, owner):
        return remote(projq.at[k - 1], projw.at[quarter(p0)], s_pq.at[k - 1], r_pq.at[p0], (owner * 2 + c, z))

    def c_pq_in(i):
        return remote(projq.at[0], projw.at[quarter(peers[i])], s_pq.at[0], r_pq.at[peers[i]], dpl[i])

    def c_act(i):
        blk = actp.at[c, p1 if i == 2 else p0]
        return remote(blk, blk, s_act.at[i], r_act.at[i], d1 if i == 0 else d2)

    def c_pre(i):
        blk = pre.at[c, p1 if i == 2 else p0]
        return remote(blk, blk, s_pre.at[i], r_pre.at[i], d1 if i == 0 else d2)

    def c_actc(i):
        p = (p0, p1, p2, p3)[i]
        return remote(actp.at[c, p], actp.at[c, p], s_actc.at[i], r_actc.at[i], dsib)

    def c_prec(i):
        p = (p0, p1, p2, p3)[i]
        return remote(pre.at[c, p], pre.at[c, p], s_prec.at[i], r_prec.at[i], dsib)

    def c_sib():
        return remote(part, sibr, s_sib, r_sib, dsib)

    def c_pl(i):
        return remote(sums.at[i], plr.at[i], s_pl.at[i], r_pl.at[i], d2 if i == 1 else d1)

    def chain(at, s, r, sc=None, rc=None):
        def hop(h, d, send):
            block = z - (h - 1) if d == 0 else z + (h - 1)
            if not send:
                block = z - h if d == 0 else z + h
            return remote(at(block), at(block), s.at[d, h - 1], r.at[d, h - 1],
                          (p0 * 2 + c, z + 1 if d == 0 else z - 1))

        def may(h, d, send):
            if send:
                return (z < 3) & (z >= h - 1) if d == 0 else (z > 0) & (z <= 4 - h)
            return z >= h if d == 0 else z <= 3 - h

        def across(h, d):
            block = z - h if d == 0 else z + h
            return remote(at(block), at(block), sc.at[d, h - 1], rc.at[d, h - 1], dsib)

        def over():
            return remote(at(z), at(z), sc.at[2, 0], rc.at[2, 0], dsib)

        def send(h):
            for d in range(2):
                @pl.when(may(h, d, True))
                def _(d=d):
                    hop(h, d, True).start()
            if h == 1 and sc is not None:
                over().start()

        def recv(h):
            for d in range(2):
                @pl.when(may(h, d, False))
                def _(d=d):
                    hop(h, d, False).wait_recv()
                    if sc is not None:
                        across(h, d).start()

        def finish():
            over().wait_recv()
            for h in (1, 2, 3):
                for d in range(2):
                    @pl.when(may(h, d, False))
                    def _(d=d, h=h):
                        across(h, d).wait_recv()

        def sent():
            if sc is not None:
                over().wait_send()
            for h in (1, 2, 3):
                for d in range(2):
                    @pl.when(may(h, d, True))
                    def _(d=d, h=h):
                        hop(h, d, True).wait_send()
                    if sc is not None:
                        @pl.when(may(h, d, False))
                        def _(d=d, h=h):
                            across(h, d).wait_send()
        return send, recv, finish, sent

    x_send, x_recv, x_finish, x_sent = chain(lambda b: xall.at[c, b], s_x, r_x, s_xc, r_xc)
    y_send, y_recv, y_finish, y_sent = chain(lambda b: dyall.at[c, b], s_y, r_y, s_yc, r_yc)
    q_send, q_recv, _, q_sent = chain(
        lambda b: qkvw.at[pl.ds(pl.multiple_of(b * 384, 384), 384)], s_qkv, r_qkv)

    opart, osib, osum = part, sibr, sums

    def copy1(h, b):
        return remote(gw.at[slot(1, b), h], o_r1.at[h, b], s1.at[h, b], r1.at[h, b], d1)
    g_c = remote(gpart, gsib, s_gc, r_gc, dsib)
    o_c = remote(opart, osib, s_oc, r_oc, dsib)

    def weights_a(k):
        if k:
            c_wz(k).wait_recv()
        c_wp(k, 0).start()
        if k == 0:
            c_wp(0, 1).start()

    def weights_b(k):
        c_wp(k, 0).wait_recv()
        if k:
            c_wp(k, 1).start()
        c_wp(k, 2).start()

    for k in (1, 2, 3):
        c_small(k).start()
    local = [pltpu.make_async_copy(small, smalls.at[z], sl.at[0]),
             pltpu.make_async_copy(dy, dyall.at[c, z], sl.at[3])]

    def window(off, width, at, n):
        src = qkv.at[:, pl.ds(pl.multiple_of(off, 128), width)]
        return pltpu.make_async_copy(src, qwin.at[:, pl.ds(at, width)], sl.at[n])
    mine = p0 * 96
    windows = [window(384 * p0 + 128 * c, 256, 0, 1), window(1536 + 128 * p0, 128, 256, 2),
               window(2048 + 128 * p0, 128, 384, 5)]
    pieces = [pltpu.make_async_copy(
        ref.at[pl.ds(pl.multiple_of(mine, 96), 96), :, pl.ds(pl.multiple_of(off, half), half)],
        wst.at[:, :, pl.ds(i * half, half)], sl.at[6 + i])
        for i, (ref, off) in enumerate(((w_gu, c * half), (w_gu, HID + c * half), (w_dn, c * half)))]
    for one in local + windows + pieces:
        one.start()
    own_proj = pltpu.make_async_copy(proj.at[pl.ds(pl.multiple_of(c * 192, 192), 192)], projw, sl.at[4])

    @pl.when(z == p0)
    def _():
        own_proj.start()
    for one in windows:
        one.wait()
    cols = qwin[...].astype(F32)
    own_rows = pl.ds(pl.multiple_of(z * 384, 384), 384)
    for at, lo, width in ((0, 0, 256), (192, 256, 128), (256, 384, 128)):
        part_ = cols[:, lo : lo + width]
        part_ = jnp.where(c == 0, part_, pltpu.roll(part_, width - 64, 1)).astype(BF)
        qkvw[own_rows, at : at + (192 if at == 0 else 64)] = part_[:, : 192 if at == 0 else 64]

    tok_f = tok[...].astype(F32)
    inv1 = lax.rsqrt(jnp.mean(tok_f * tok_f, axis=1, keepdims=True) + EPS)
    for k in (1, 2, 3):
        c_small(k).wait_recv()
    q_send(1)
    local[0].wait()
    gain1 = jnp.concatenate([smalls[i, 0:1, :] for i in range(4)], axis=1).astype(F32)
    actp[c, p0] = (tok_f * inv1 * gain1).astype(BF)
    pre[c, p0] = jnp.full((8, 128), prefix[0], jnp.int32).astype(F32)
    for i in range(2):
        c_act(i).start()
        c_pre(i).start()
    c_actc(0).start()
    c_prec(0).start()
    chosen_f = jnp.zeros((128, 128), F32)
    rank_of = jnp.zeros((128, 128), F32)
    lane_e = lax.broadcasted_iota(jnp.int32, (128, 128), 1)
    ids = ids_t[...].astype(F32).T
    spread = jnp.concatenate(
        [jnp.broadcast_to(prio[i : i + 1, :].astype(F32), (16, 128)) for i in range(8)], axis=0)
    token = lax.broadcasted_iota(jnp.int32, (128, 128), 0)
    spread = jnp.where(lane_e // 8 == lax.rem(token, 16), spread, 0.0)
    for k in range(8):
        hit = ids[:, k : k + 1] == lane_e.astype(F32)
        chosen_f = jnp.where(hit, 1.0, chosen_f)
        own_prio = jnp.sum(jnp.where(lax.rem(lane_e, 8) == k, spread, 0.0), axis=1, keepdims=True)
        rank_of = jnp.where(hit, own_prio, rank_of)
    rank_of = jnp.where(chosen_f > 0.0, rank_of, 65536.0)
    rank_t = rank_of.T
    slots = jnp.zeros((128, 128), F32)
    for e in range(EXPERTS):
        before = jnp.sum((rank_t[e : e + 1, :] < rank_of[:, e : e + 1]).astype(F32), axis=1, keepdims=True)
        slots = jnp.where(lane_e == e, before, slots)
    kept_f = jnp.where(slots < CAP, chosen_f, 0.0)
    kept[...] = kept_f[:, :EXPERTS]
    q_recv(1)
    q_send(2)

    for one in pieces:
        one.wait()

    def expert_rows(l, _):
        wcol[...] = wst[:, :, pl.ds(pl.multiple_of(l * 128, 128), 128)].astype(F32).reshape(1536, 128)
        for e in range(EXPERTS):
            wpiece[e // 4, e % 4, :, pl.ds(pl.multiple_of(l * 128, 128), 128)] = (
                wcol[pl.ds(e, 96, stride=EXPERTS), :].astype(BF))
        return 0
    lax.fori_loop(0, 6, expert_rows, 0)
    own_piece = pltpu.make_async_copy(wpiece.at[z], wbuf.at[:, rows(z, p0)], sl.at[30])
    own_piece.start()
    weights_a(0)
    q_recv(2)
    q_send(3)
    for k in (1, 2, 3):
        c_pz(k).start()
    for i in range(3):
        c_act(i).wait_recv()
        c_pre(i).wait_recv()
        if i == 0:
            c_act(2).start()
            c_pre(2).start()
        c_actc(i + 1).start()
        c_prec(i + 1).start()
    q_recv(3)
    weights_b(0)
    local[1].wait()

    row = lax.broadcasted_iota(jnp.int32, (128, 128), 0)
    col = lax.broadcasted_iota(jnp.int32, (128, 128), 1)
    causal = col <= row
    col_f = col.astype(F32)

    def attention(cc):
        pr[...] = jnp.dot(actp[cc].reshape(512, 1536), qkvw[...], preferred_element_type=F32).reshape(4, 128, 320)

        def one(i, _):
            lo = turn(pr[i, :, 0:128], cos_t[...], sin_t[...]).astype(BF)
            hi = turn(pr[i, :, 128:256], cos_t[...], sin_t[...]).astype(BF)
            qs[cc, i, 0:128] = lo[:, 0:64]
            qs[cc, i, 128:256] = lo[:, 64:128]
            qs[cc, i, 256:384] = hi[:, 0:64]
            ks[cc, i] = hi[:, 64:128]
            vs[cc, i] = pr[i, :, 256:320].astype(BF)
            sc = lax.dot_general(qs[cc, i], ks[cc, i], (((1,), (1,)), ((), ())), preferred_element_type=F32)
            allowed = causal | (col_f < pre[cc, i, 0:1, :])
            sc = jnp.where(allowed[None], sc.reshape(3, 128, 128) * (64 ** -0.5), -1e30)
            ex = jnp.exp(sc - jnp.max(sc, axis=-1, keepdims=True))
            pb = (ex / jnp.sum(ex, axis=-1, keepdims=True)).reshape(384, 128)
            probs[cc, i] = pb
            at = jnp.dot(pb.astype(BF), vs[cc, i], preferred_element_type=F32).astype(BF)
            for h in range(3):
                att[cc, i, :, h * 64 : (h + 1) * 64] = at[h * 128 : (h + 1) * 128]
            return 0
        lax.fori_loop(0, 4, one, 0)

    attention(c)
    for k in (1, 3, 2):
        c_wz(k).start()
    for i in range(4):
        c_actc(i).wait_recv()
        c_prec(i).wait_recv()
    attention(1 - c)
    for k in (1, 2, 3):
        c_pz(k).wait_recv()
        owner = zf[k]

        @pl.when(owner != p0)
        def _(k=k, owner=owner):
            c_pq(k, owner).start()

        @pl.when(owner == p0)
        def _(k=k):
            projw[quarter(p0)] = projq[k - 1]

    @pl.when(z == p0)
    def _():
        own_proj.wait()

    @pl.when(z != p0)
    def _():
        for i in range(3):
            c_pq_in(i).wait_recv()

    def to_sib(i, _):
        part[i] = jnp.dot(att[1 - c, i], projw[...], preferred_element_type=F32).astype(BF)
        return 0
    lax.fori_loop(0, 4, to_sib, 0)
    c_sib().start()
    c_sib().wait_recv()
    def mixed(p):
        return jnp.dot(att[c, p], projw[...], preferred_element_type=F32) + sibr[p].astype(F32)

    for i in (2, 0):
        sums[i] = mixed(peers[i]).astype(BF)
        c_pl(i).start()
    to_second = mixed(p2)
    residual = tok_f + mixed(p0)
    c_pl(2).wait_recv()
    sums[1] = (to_second + plr[2].astype(F32)).astype(BF)
    c_pl(1).start()
    for i in range(2):
        c_pl(i).wait_recv()
        residual = residual + plr[i].astype(F32)
    res[...] = residual
    inv2 = lax.rsqrt(jnp.mean(residual * residual, axis=1, keepdims=True) + EPS)
    gain2 = jnp.concatenate([smalls[i, 1:2, :] for i in range(4)], axis=1).astype(F32)
    act2 = (residual * inv2 * gain2).astype(BF)
    router = jnp.concatenate([smalls[i, 16:32, :] for i in range(4)], axis=1)
    logits = lax.dot_general(act2, router, (((1,), (1,)), ((), ())), preferred_element_type=F32)
    chosen = chosen_f[:, :EXPERTS] > 0.0
    top = jnp.max(jnp.where(chosen, logits, -1e30), axis=1, keepdims=True)
    ge = jnp.where(chosen, jnp.exp(jnp.where(chosen, logits - top, 0.0)), 0.0)
    gt = ge / jnp.sum(ge, axis=1, keepdims=True)
    gates[...] = gt
    kept_gates = gt * kept[...]
    gate_hi = kept_gates.astype(BF)
    gate_lo = (kept_gates - gate_hi.astype(F32)).astype(BF)
    xall[c, z, :, :1536] = act2
    xall[c, z, :, 1536:] = jnp.concatenate([gate_hi, gate_lo, jnp.zeros((128, 96), BF)], axis=1)
    x_send(1)
    y_send(1)
    weights_a(1)
    weights_a(3)
    weights_b(1)
    weights_b(3)
    x_recv(1)
    x_send(2)
    weights_a(2)
    y_recv(1)
    y_send(2)
    x_recv(2)
    x_send(3)
    weights_b(2)
    y_recv(2)
    y_send(3)
    x_recv(3)
    y_recv(3)
    own_piece.wait()
    for k in range(4):
        c_wp(k, 1).wait_recv()
        c_wp(k, 2).wait_recv()
    x_finish()
    y_finish()

    lane = lax.broadcasted_iota(jnp.int32, (512, 128), 1)
    ggp[...] = jnp.zeros_like(ggp)

    def expert(n, _):
        j, t = n // 2, lax.rem(n, 2)
        gu = jnp.dot(xall[t, :, :, :1536].reshape(512, 1536), wbuf[j, :, : 2 * half], preferred_element_type=F32)
        bk = jnp.dot(dyall[t].reshape(512, 1536), wbuf[j, :, 2 * half :], preferred_element_type=F32)
        mine = lane == z * 4 + j
        both = xall[t, :, :, 1536:].astype(F32).reshape(512, 128)
        w = jnp.sum(jnp.where(mine | (lane == EXPERTS + z * 4 + j), both, 0.0), axis=1, keepdims=True)
        g, u = gu[:, :half], gu[:, half:]
        sg = 1.0 / (1.0 + jnp.exp(-g))
        silu = g * sg
        hid = silu * u
        hw[j, pl.ds(pl.multiple_of(t * 512, 512), 512)] = (hid * w).astype(BF)
        ggp[t] = ggp[t] + jnp.where(mine, jnp.sum(bk * hid, axis=1, keepdims=True), 0.0).reshape(4, 128, 128)
        gh = bk * w
        at = pl.ds(pl.multiple_of(t * 512, 512), 512)
        ggu[j, at, :half] = (gh * u * sg * (1.0 + g * (1.0 - sg))).astype(BF)
        ggu[j, at, half:] = (gh * silu).astype(BF)
        return 0
    lax.fori_loop(0, 8, expert, 0)

    gradient_rows(0, xall, dyall, ggu, hw, gw)
    for h in range(2):
        for b in range(2):
            copy1(h, b).start()
    saves = []

    def save(src, dst):
        one = pltpu.make_async_copy(src, dst, sl.at[9 + len(saves)])
        one.start()
        saves.append(one)
    for src, dst in ((gw, o_gw), (xall, o_x), (dyall, o_dy), (ggu, o_ggu), (hw, o_hw), (actp, o_act), (qs, o_q), (ks, o_k),
                     (vs, o_v), (probs, o_probs), (att, o_att), (qkvw, o_qkvw), (projw, o_projw),
                     (smalls, o_small), (res, o_res), (gates, o_gates), (kept, o_kept)):
        save(src, dst)

    def block(grad, t, n):
        at = pl.ds(pl.multiple_of(t * 512, 512), 512)
        lanes = pl.ds(pl.multiple_of(n * 256, 256), 256)
        acc = jnp.zeros((512, 256), F32)
        for j in range(4):
            a = ggu[j, at] if grad else hw[j, at]
            b = wbuf[j, lanes, : 2 * half] if grad else wbuf[j, lanes, 2 * half :]
            acc = acc + lax.dot_general(a, b, (((1,), (1,)), ((), ())), preferred_element_type=F32)
        return acc.reshape(4, 128, 256), lanes

    def partial(grad, buf):
        def one(n, _):
            v, lanes = block(grad, 1 - c, n)
            buf[:, :, lanes] = v.astype(BF)
            return 0
        lax.fori_loop(0, 6, one, 0)

    def own(grad, sib, dst):
        def one(n, _):
            v, lanes = block(grad, c, n)
            dst[:, :, lanes] = (v + sib[:, :, lanes].astype(F32)).astype(BF)
            return 0
        lax.fori_loop(0, 6, one, 0)

    def put_gate_grads(dst, v):
        hi = v.astype(BF).astype(F32)
        lo = pltpu.roll((v - hi).reshape(512, 128), EXPERTS, 1)
        dst[:, :, 1536:] = jnp.where(lane < EXPERTS, hi.reshape(512, 128), lo).astype(BF).reshape(4, 128, 128)

    def gate_grads(v):
        both = v[..., 1536:].astype(F32).reshape(512, 128)
        return jnp.where(lane < EXPERTS, both + pltpu.roll(both, 128 - EXPERTS, 1), 0.0).reshape(4, 128, 128)

    c_sib().wait_send()
    for i in range(3):
        c_pl(i).wait_send()
    put_gate_grads(gpart, ggp[1 - c])
    partial(True, gpart)
    g_c.start()
    partial(False, opart)
    o_c.start()
    g_c.wait_recv()
    put_gate_grads(gsum, ggp[c] + gate_grads(gsib))
    own(True, gsib, gsum)
    save(gsum, o_gsum)
    o_c.wait_recv()
    own(False, osib, osum)
    save(osum, o_osum)
    for h in range(2):
        for b in range(2):
            copy1(h, b).wait()

    for k in (1, 2, 3):
        for one in (c_small(k), c_pz(k), c_wz(k)):
            one.wait_send()

        @pl.when(zf[k] != p0)
        def _(k=k):
            c_pq(k, zf[k]).wait_send()
    for k in range(4):
        for i in range(3):
            c_wp(k, i).wait_send()
        for one in (c_actc(k), c_prec(k)):
            one.wait_send()
    for i in range(3):
        for one in (c_act(i), c_pre(i)):
            one.wait_send()
    for one in (g_c, o_c):
        one.wait_send()
    x_sent()
    y_sent()
    q_sent()
    for one in saves:
        one.wait()


def front(*args):
    sem, vm = pltpu.SemaphoreType.DMA, pltpu.VMEM
    out = lambda shape, kind=BF: jax.ShapeDtypeStruct(shape, kind)
    outs = (
        out((2, 4, 128, 1664)), out((2, 4, 128, 1536)), out((4, 1024, 512)), out((4, 1024, 256)),
        out((2, 4, 128, 1536)), out((2, 4, 384, 64)), out((2, 4, 128, 64)), out((2, 4, 128, 64)),
        out((2, 4, 384, 128), F32), out((2, 4, 128, 192)), out((1536, 320)), out((192, 1536)),
        out((4, 32, 384)), out((128, 1536), F32), out((128, 16), F32), out((128, 16), F32), out((4, 128, 1664)),
        out((4, 128, 1536)), out((4, 2, 4, 4, 16, 768)), out((2, 2, 4, 4, 16, 768)),
    )
    block, quad = vm((2, 4, 128, 1536), BF), vm((4, 128, 1536), BF)
    three = vm((3, 128, 1536), BF)
    quad_g = vm((4, 128, 1664), BF)
    scratch = [
        vm((4, 32, 384), BF), vm((1536, 320), BF), vm((192, 1536), BF), vm((3, 48, 1536), BF),
        block, vm((2, 4, 8, 128), F32),
        vm((4, 128, 320), F32), vm((2, 4, 384, 64), BF), vm((2, 4, 128, 64), BF), vm((2, 4, 128, 64), BF),
        vm((2, 4, 384, 128), F32), vm((2, 4, 128, 192), BF), quad, quad, quad, three,
        vm((2, 4, 128, 1664), BF), block, vm((4, 1536, 768), BF), vm((4, 1024, 512), BF),
        vm((4, 1024, 256), BF), quad_g, vm((2, 4, 128, 128), F32), quad_g,
        quad_g, vm((128, 1536), F32), vm((128, 16), F32), vm((128, 16), F32),
        vm((384, 512), BF), vm((96, 16, 768), BF), vm((1536, 128), F32), vm((4, 4, 96, 768), BF),
        vm((4, 2, 4, 4, 16, 768), BF),
    ]
    n3, n4, one = sem((3,)), sem((4,)), sem(())
    hops = [sem((2, 3)), sem((2, 3)), sem((3, 3)), sem((3, 3))]
    sems = [
        n3, n3, sem((2, 3)), sem((2, 3)), n3, n3, n3, n4, n3, n3, sem((4, 3)), sem((4, 3)),
        n3, n3, n3, n3, n4, n4, n4, n4, one, one, n3, n3,
        *hops, *hops, one, one, one, one, sem((2, 2)), sem((2, 2)), sem((31,)),
    ]
    vmem, any_ = pl.BlockSpec(memory_space=pltpu.VMEM), pl.BlockSpec(memory_space=pl.ANY)
    return pl.pallas_call(
        front_kernel,
        out_shape=outs,
        in_specs=[vmem, any_, any_, any_, any_, any_, any_, vmem, vmem,
                  pl.BlockSpec(memory_space=pltpu.SMEM), vmem, vmem],
        out_specs=[any_] * len(outs),
        scratch_shapes=scratch + sems,
        compiler_params=pltpu.CompilerParams(
            collective_id=1, has_side_effects=True, vmem_limit_bytes=62 * 1024 * 1024),
        name="front",
    )(*args)


def back_kernel(i_x, i_dy, i_ggu, i_hw, i_act, i_q, i_k, i_v, i_probs, i_att, i_qkvw, i_projw, i_small,
                i_res, i_gates, i_kept, i_gsum, i_osum, i_gw, i_r1, tok, cos_t, sin_t,
                o_e, o_gtok, o_qg, o_pg, o_terms, o_op,
                xb, dyb, ggu, hw, qs, ks, vs, probs, att, qkvw, projw, smalls, res, gates, kept, gown, grecv,
                gw, recv1, send2, recv2, zs, zr, ib, agv,
                gres, gresf, gproj, sibr, plr, qgp, qz, qgo, pgp, pgr, pq2, pgo, terms, tz, tsib, tpl, tout, gtok,
                s1, r1, s2, r2, sz, rz, sa, ra, ss, rs, la,
                s_g, r_g, s_gr, r_gr, s_grc, r_grc, s_sib, r_sib, s_pl, r_pl, s_qz, r_qz, s_qo, r_qo,
                s_qoc, r_qoc, s_p1, r_p1, s_p2, r_p2, s_po, r_po, s_poc, r_poc, s_tz, r_tz, s_ts, r_ts,
                s_tp, r_tp, s_o, r_o, ld, sv):
    y, x, c, z = place()
    half = HID // 2
    wide = 3 * half
    nq = 6

    def slot(a, b):
        return flip(y, a * c + b * (1 - c)) * 2 + flip(x, a * (1 - c) + b * c)

    p0, p1, p2, p3 = slot(0, 0), slot(1, 0), slot(0, 1), slot(1, 1)
    peers = (p1, p2, p3)
    d1, d2, dsib = (p1 * 2 + c, z), (p2 * 2 + c, z), (p0 * 2 + 1 - c, z)
    dpl = [(p * 2 + c, z) for p in peers]
    zk = [lax.rem(z + k, 4) for k in range(4)]
    dz = [(p0 * 2 + c, zz) for zz in zk]

    loads = {}

    def load(name, src, dst):
        loads[name] = pltpu.make_async_copy(src, dst, ld.at[len(loads)])
        loads[name].start()
    load("gw", i_gw, gw.at[0])
    load("r1", i_r1, recv1.at[pl.ds(0, 2)])
    load("x", i_x.at[:, :, :, pl.ds(0, 1536)], xb)
    load("ggu", i_ggu, ggu)
    load("dy", i_dy, dyb)
    load("hw", i_hw, hw)
    load("gown", i_gsum.at[z], gown)
    for name, src, dst in (("res", i_res, res), ("gates", i_gates, gates), ("kept", i_kept, kept),
                           ("small", i_small, smalls),
                           ("projw", i_projw, projw), ("probs", i_probs, probs), ("q", i_q, qs), ("k", i_k, ks),
                           ("v", i_v, vs), ("att", i_att, att), ("qkvw", i_qkvw, qkvw)):
        load(name, src, dst)

    barrier = pltpu.get_barrier_semaphore()
    for to in dpl + dz[1:] + [dsib]:
        pl.semaphore_signal(barrier, 1, device_id=to, device_id_type=MESH)
    pl.semaphore_wait(barrier, 7)

    def remote(src, dst, s, r, to):
        return pltpu.make_async_remote_copy(src, dst, s, r, device_id=to, device_id_type=MESH)

    def copy1(q, b):
        return remote(gw.at[q // 2, slot(1, b), lax.rem(q, 2)], recv1.at[q, b], s1.at[q, b], r1.at[q, b], d1)

    def copy2(q):
        return remote(send2.at[lax.rem(q, 2)], recv2.at[q], s2.at[q], r2.at[q], d2)

    def copyz(q, k):
        return remote(zs.at[lax.rem(q, 2), zk[k]], zr.at[q, z], sz.at[q, k - 1], rz.at[q, k - 1], dz[k])

    def rows(q, p):
        return pl.ds(pl.multiple_of(((q // 2) * 8 + p * 2 + lax.rem(q, 2)) * 256, 256), 256)

    def copya(q, i):
        p, who = ((p0, d1), (p0, d2), (p1, d2))[i]
        src = agv.at[lax.rem(q, 2)] if i < 2 else o_e.at[c, rows(q, p)]
        return remote(src, o_e.at[c, rows(q, p)], sa.at[q, i], ra.at[q, i], who)

    def copys(q, i):
        p = (p0, p1, p2, p3)[i]
        src = agv.at[lax.rem(q, 2)] if i == 0 else o_e.at[c, rows(q, p)]
        return remote(src, o_e.at[c, rows(q, p)], ss.at[q, i], rs.at[q, i], dsib)

    def keep(q):
        return pltpu.make_async_copy(agv.at[lax.rem(q, 2)], o_e.at[c, rows(q, p0)], la.at[q])

    def c_g(k):
        return remote(i_gsum.at[zk[k]], grecv.at[k - 1], s_g.at[k - 1], r_g.at[k - 1], dz[k])

    def c_o(k):
        return remote(i_osum.at[zk[k]], o_op.at[k], s_o.at[k - 1], r_o.at[k - 1], dz[k])

    def c_gr(i):
        blk = gres.at[c, p1 if i == 2 else p0]
        return remote(blk, blk, s_gr.at[i], r_gr.at[i], d1 if i == 0 else d2)

    def c_grc(i):
        p = (p0, p1, p2, p3)[i]
        return remote(gres.at[c, p], gres.at[c, p], s_grc.at[i], r_grc.at[i], dsib)

    def c_sib():
        return remote(dyb.at[0], sibr, s_sib, r_sib, dsib)

    def c_pl(i):
        return remote(dyb.at[1, i], plr.at[i], s_pl.at[i], r_pl.at[i], d2 if i == 1 else d1)

    def c_qz(k):
        return remote(qgp.at[zk[k]], qz.at[k - 1], s_qz.at[k - 1], r_qz.at[k - 1], dz[k])

    def c_qo(i):
        dst = o_qg.at[(p1 if i == 2 else p0) * 2 + c]
        return remote(dst if i == 2 else qgo, dst, s_qo.at[i], r_qo.at[i], d1 if i == 0 else d2)

    def c_qoc(i):
        r = (p0, p1, p2, p3)[i] * 2 + c
        return remote(qgo if i == 0 else o_qg.at[r], o_qg.at[r], s_qoc.at[i], r_qoc.at[i], dsib)

    def c_p1(i):
        return remote(pgp.at[peers[i]], pgr.at[p0], s_p1.at[i], r_p1.at[i], dpl[i])

    def c_p2(k):
        return remote(pgr.at[zk[k]], pq2.at[k - 1], s_p2.at[k - 1], r_p2.at[k - 1], dz[k])

    def c_po(i):
        dst = o_pg.at[c, p1 if i == 2 else p0]
        return remote(dst if i == 2 else pgo, dst, s_po.at[i], r_po.at[i], d1 if i == 0 else d2)

    def c_poc(i):
        p = (p0, p1, p2, p3)[i]
        return remote(pgo if i == 0 else o_pg.at[c, p], o_pg.at[c, p], s_poc.at[i], r_poc.at[i], dsib)

    def lanes_of(zz):
        return pl.ds(pl.multiple_of(zz * 384, 384), 384)

    def c_tz(k):
        return remote(terms.at[:, lanes_of(zk[k])], tz.at[k], s_tz.at[k - 1], r_tz.at[k - 1], dz[k])

    def c_ts():
        return remote(tz.at[0], tsib, s_ts, r_ts, dsib)

    def c_tp(i):
        return remote(tpl.at[p0], tpl.at[p0], s_tp.at[i], r_tp.at[i], dpl[i])

    saves = [pltpu.make_async_copy(gtok, o_gtok, sv.at[0]),
             pltpu.make_async_copy(qgo, o_qg.at[p0 * 2 + c], sv.at[1]),
             pltpu.make_async_copy(pgo, o_pg.at[c, p0], sv.at[2]),
             pltpu.make_async_copy(tout, o_terms, sv.at[3])]
    own_out = pltpu.make_async_copy(i_osum.at[z], o_op.at[0], sv.at[5])
    own_out.start()
    act_load = pltpu.make_async_copy(i_act, xb, sv.at[4])

    for k in (1, 2, 3):
        c_g(k).start()
    loads["gw"].wait()
    loads["r1"].wait()
    loads["x"].wait()
    loads["ggu"].wait()
    loads["dy"].wait()
    loads["hw"].wait()

    def stage1(q):
        @pl.when(lax.rem(q, 2) == 0)
        def _():
            gradient_rows(q // 2, xb, dyb, ggu, hw, gw.at[q // 2])
        for b in range(2):
            copy1(q, b).start()

    def stage2(q):
        @pl.when(q >= 2)
        def _():
            for b in range(2):
                copy1(q, b).wait_recv()

        def one(zz, _):
            send2[lax.rem(q, 2), zz] = (gw[q // 2, p2, lax.rem(q, 2), zz].astype(F32)
                                        + recv1[q, 1, zz].astype(F32)).astype(BF)
            return 0
        lax.fori_loop(0, 4, one, 0)
        copy2(q).start()

    def stage3(q):
        copy2(q).wait()

        def one(zz, _):
            zs[lax.rem(q, 2), zz] = (gw[q // 2, p0, lax.rem(q, 2), zz].astype(F32) + recv1[q, 0, zz].astype(F32)
                                     + recv2[q, zz].astype(F32)).astype(BF)
            return 0
        lax.fori_loop(0, 4, one, 0)
        for k in range(1, 4):
            copyz(q, k).start()
        zr[q, z] = zs[lax.rem(q, 2), z]

    def stage4(q):
        for k in range(1, 4):
            copyz(q, k).wait()

        @pl.when(q >= 2)
        def _():
            copya(q - 2, 0).wait_send()
            copya(q - 2, 1).wait_send()
            copys(q - 2, 0).wait_send()
            keep(q - 2).wait()
        for zz in range(4):
            for j in range(4):
                for l in range(wide // 128):
                    ib[l, pl.ds(zz * 4 + j, 16, stride=EXPERTS), :] = (
                        zr[q, zz, j, :, l * 128 : (l + 1) * 128].astype(F32))
        for l in range(wide // 128):
            agv[lax.rem(q, 2), :, l * 128 : (l + 1) * 128] = ib[l].astype(BF)
        copya(q, 0).start()
        copys(q, 0).start()
        keep(q).start()

    def stage5(q):
        copya(q, 0).wait_recv()
        copya(q, 1).start()
        copya(q, 2).start()
        copys(q, 1).start()

    def stage6(q):
        copya(q, 1).wait_recv()
        copya(q, 2).wait_recv()
        copys(q, 2).start()
        copys(q, 3).start()

    def stage7(q):
        for i in range(4):
            copys(q, i).wait_recv()

    def norm_two():
        r = res[...]
        inv = lax.rsqrt(jnp.mean(r * r, axis=1, keepdims=True) + EPS)
        return inv, r * inv

    def norm_one():
        t = tok[...].astype(F32)
        inv = lax.rsqrt(jnp.mean(t * t, axis=1, keepdims=True) + EPS)
        return inv, t * inv

    def gain(row):
        return jnp.concatenate([smalls[i, row : row + 1, :] for i in range(4)], axis=1).astype(F32)

    def event_residual():
        for name in ("gown", "res", "gates", "kept", "small"):
            loads[name].wait()
        for k in (1, 2, 3):
            c_g(k).wait_recv()

        def gate_part(v):
            return v[:, 1536 : 1536 + EXPERTS].astype(F32) + v[:, 1536 + EXPERTS : 1536 + 2 * EXPERTS].astype(F32)
        gg = (gate_part(gown[...]) + gate_part(grecv[0]) + gate_part(grecv[1]) + gate_part(grecv[2])) * kept[...]
        gt = gates[...]
        gl = (gt * (gg - jnp.sum(gt * gg, axis=1, keepdims=True))).astype(BF)
        router_t = jnp.concatenate([smalls[i, 16:32, :] for i in range(4)], axis=1)
        ga = jnp.dot(gl, router_t, preferred_element_type=F32)
        ga = ga + gown[:, :1536].astype(F32)
        for k in range(3):
            ga = ga + grecv[k, :, :1536].astype(F32)
        inv, normed = norm_two()
        terms[8:24, :] = lax.dot_general(gl, xb[c, z], (((0,), (0,)), ((), ())), preferred_element_type=F32)
        terms[1:2, :] = jnp.sum(ga * normed, axis=0, keepdims=True)
        scaled = ga * gain(1)
        gr = dyb[c, z].astype(F32) + inv * (scaled - normed * jnp.mean(scaled * normed, axis=1, keepdims=True))
        gresf[...] = gr
        gres[c, p0] = gr.astype(BF)
        for i in range(2):
            c_gr(i).start()
        c_grc(0).start()

    def event_share():
        for k in (1, 2, 3):
            c_o(k).start()
        for i in range(3):
            c_gr(i).wait_recv()
            if i == 0:
                c_gr(2).start()
            c_grc(i + 1).start()
        act_load.start()

    scale = 64 ** -0.5

    def event_attention():
        for name in ("projw", "probs", "q", "k", "v", "att", "qkvw"):
            loads[name].wait()
        for i in range(4):
            c_grc(i).wait_recv()

        def one(n, _):
            cc, i = n // 4, lax.rem(n, 4)
            gb = lax.dot_general(gres[cc, i], projw[...], (((1,), (1,)), ((), ())),
                                 preferred_element_type=F32).astype(BF)
            ga = jnp.concatenate([gb[:, h * 64 : (h + 1) * 64] for h in range(3)], axis=0)
            pb = probs[cc, i]
            gv = lax.dot_general(pb.astype(BF), ga, (((0,), (0,)), ((), ())), preferred_element_type=F32)
            gp = lax.dot_general(ga, vs[cc, i], (((1,), (1,)), ((), ())), preferred_element_type=F32)
            gs = (pb * (gp - jnp.sum(pb * gp, axis=-1, keepdims=True))).astype(BF)
            gq = jnp.dot(gs, ks[cc, i], preferred_element_type=F32) * scale
            gk = lax.dot_general(gs, qs[cc, i], (((0,), (0,)), ((), ())), preferred_element_type=F32) * scale
            lo = jnp.concatenate([gq[0:128], gq[128:256]], axis=1)
            hi = jnp.concatenate([gq[256:384], gk], axis=1)
            gproj[cc, i, :, 0:128] = turn(lo, cos_t[...], -sin_t[...]).astype(BF)
            gproj[cc, i, :, 128:256] = turn(hi, cos_t[...], -sin_t[...]).astype(BF)
            gproj[cc, i, :, 256:320] = gv.astype(BF)
            return 0
        lax.fori_loop(0, 8, one, 0)

        def to_sib(i, _):
            dyb[0, i] = lax.dot_general(gproj[1 - c, i], qkvw[...], (((1,), (1,)), ((), ())),
                                        preferred_element_type=F32).astype(BF)
            return 0
        lax.fori_loop(0, 4, to_sib, 0)
        c_sib().start()
        pg = lax.dot_general(att[...].reshape(1024, 192), gres[...].reshape(1024, 1536), (((0,), (0,)), ((), ())),
                             preferred_element_type=F32)
        pgp[...] = pg.astype(BF).reshape(4, 48, 1536)
        for i in range(3):
            c_p1(i).start()
        pgr[p0] = pgp[p0]

    def event_columns():
        act_load.wait()

        def one(zz, _):
            a = xb[:, :, :, lanes_of(zz)].reshape(1024, 384)
            qgp[zz] = lax.dot_general(a, gproj[...].reshape(1024, 320), (((0,), (0,)), ((), ())),
                                      preferred_element_type=F32).astype(BF)
            return 0
        lax.fori_loop(0, 4, one, 0)
        for k in (1, 2, 3):
            c_qz(k).start()
        c_sib().wait()

        def part(p):
            return lax.dot_general(gproj[c, p], qkvw[...], (((1,), (1,)), ((), ())),
                                   preferred_element_type=F32) + sibr[p].astype(F32)
        for i in (2, 0):
            dyb[1, i] = part(peers[i]).astype(BF)
            c_pl(i).start()
        dyb[1, 1] = part(p2).astype(BF)
        gtok[...] = part(p0)
        for i in range(3):
            c_p1(i).wait_recv()
        for k in (1, 2, 3):
            c_p2(k).start()

    def event_second():
        c_pl(2).wait_recv()
        dyb[1, 1] = (dyb[1, 1].astype(F32) + plr[2].astype(F32)).astype(BF)
        c_pl(1).start()
        for k in (1, 2, 3):
            c_qz(k).wait_recv()
        qgo[...] = (qgp[z].astype(F32) + qz[0].astype(F32) + qz[1].astype(F32) + qz[2].astype(F32)).astype(BF)
        for i in range(2):
            c_qo(i).start()
        c_qoc(0).start()
        saves[1].start()
        for k in (1, 2, 3):
            c_p2(k).wait_recv()
        pgo[...] = (pgr[z].astype(F32) + pq2[0].astype(F32) + pq2[1].astype(F32) + pq2[2].astype(F32)).astype(BF)
        for i in range(2):
            c_po(i).start()
        c_poc(0).start()
        saves[2].start()

    def event_tokens():
        ga = gtok[...]
        for i in range(2):
            c_pl(i).wait_recv()
            ga = ga + plr[i].astype(F32)
        inv, normed = norm_one()
        terms[0:1, :] = jnp.sum(ga * normed, axis=0, keepdims=True)
        scaled = ga * gain(0)
        gtok[...] = gresf[...] + inv * (scaled - normed * jnp.mean(scaled * normed, axis=1, keepdims=True))
        saves[0].start()
        for k in (1, 2, 3):
            c_tz(k).start()
        for copy, over in ((c_qo, c_qoc), (c_po, c_poc)):
            copy(0).wait_recv()
            copy(2).start()
            over(1).start()
            copy(1).wait_recv()
            over(2).start()

    def event_terms():
        for k in (1, 2, 3):
            c_tz(k).wait_recv()
        tz[0] = terms[:, lanes_of(z)] + tz[1] + tz[2] + tz[3]
        c_ts().start()
        for copy, over in ((c_qo, c_qoc), (c_po, c_poc)):
            copy(2).wait_recv()
            over(3).start()
        c_ts().wait()
        tpl[p0] = tz[0] + tsib[...]
        for i in range(3):
            c_tp(i).start()

    def event_last():
        for i in range(3):
            c_tp(i).wait_recv()
        tout[...] = tpl[0] + tpl[1] + tpl[2] + tpl[3]
        saves[3].start()
        for i in range(4):
            c_qoc(i).wait_recv()
            c_poc(i).wait_recv()
        for k in (1, 2, 3):
            c_o(k).wait_recv()

    stages = (stage1, stage2, stage3, stage4, stage5, stage6, stage7)
    lead = 4
    for q in (2, 3):
        stage1(jnp.int32(q))
    for q in range(1):
        stage2(jnp.int32(q))
    events = {2: event_residual, 3: event_share, 4: event_attention, 5: event_columns, 6: event_second,
              7: event_tokens, 8: event_terms, 9: event_last}

    def step(t, _):
        for i, stage in enumerate(stages):
            q = t + lead if i == 0 else t + 2 - i

            @pl.when((q >= 0) & (q < nq))
            def _(stage=stage, q=q):
                stage(q)
        for at, event in events.items():
            @pl.when(t == at)
            def _(event=event):
                event()
        return 0

    lax.fori_loop(0, nq + len(stages) - 2, step, 0)

    def left(q, _):
        @pl.when(q >= 2)
        def _():
            for b in range(2):
                copy1(q, b).wait_send()
        for i in range(1, 4):
            copys(q, i).wait_send()
        copya(q, 2).wait_send()

        @pl.when(q >= nq - 2)
        def _():
            copya(q, 0).wait_send()
            copya(q, 1).wait_send()
            copys(q, 0).wait_send()
            keep(q).wait()
        return 0
    lax.fori_loop(0, nq, left, 0)
    for k in (1, 2, 3):
        for one in (c_g(k), c_o(k), c_qz(k), c_p2(k), c_tz(k)):
            one.wait_send()
    for i in range(3):
        for one in (c_gr(i), c_pl(i), c_qo(i), c_p1(i), c_po(i), c_tp(i)):
            one.wait_send()
    for i in range(4):
        for one in (c_grc(i), c_qoc(i), c_poc(i)):
            one.wait_send()
    for one in saves + [own_out]:
        one.wait()


def back(front_outs, tok, cos_t, sin_t):
    nq, wide = 6, 3 * HID // 2
    sem, vm = pltpu.SemaphoreType.DMA, pltpu.VMEM
    out = lambda shape, kind=BF: jax.ShapeDtypeStruct(shape, kind)
    piece = (4, 4, 16, wide)
    outs = (out((2, 6144, wide)), out((128, 1536), F32), out((8, 384, 320)), out((2, 4, 48, 1536)),
            out((24, 384), F32), out((4, 128, 1536)))
    block, quad, three = vm((2, 4, 128, 1536), BF), vm((4, 128, 1536), BF), vm((3, 128, 1536), BF)
    scratch = [
        block, block, vm((4, 1024, 512), BF), vm((4, 1024, 256), BF), vm((2, 4, 384, 64), BF),
        vm((2, 4, 128, 64), BF), vm((2, 4, 128, 64), BF), vm((2, 4, 384, 128), F32), vm((2, 4, 128, 192), BF),
        vm((1536, 320), BF), vm((192, 1536), BF), vm((4, 32, 384), BF), vm((128, 1536), F32), vm((128, 16), F32), vm((128, 16), F32),
        vm((128, 1664), BF), vm((3, 128, 1664), BF),
        vm((3, 4, 2) + piece, BF), vm((nq, 2) + piece, BF), vm((2,) + piece, BF), vm((nq,) + piece, BF),
        vm((2,) + piece, BF), vm((nq,) + piece, BF), vm((wide // 128, 256, 128), F32), vm((2, 256, wide), BF),
        block, vm((128, 1536), F32), vm((2, 4, 128, 320), BF), quad, three, vm((4, 384, 320), BF),
        vm((3, 384, 320), BF), vm((384, 320), BF), vm((4, 48, 1536), BF), vm((4, 48, 1536), BF),
        vm((3, 48, 1536), BF), vm((48, 1536), BF), vm((24, 1536), F32), vm((4, 24, 384), F32),
        vm((24, 384), F32), vm((4, 24, 384), F32), vm((24, 384), F32), vm((128, 1536), F32),
    ]
    n3, n4, one = sem((3,)), sem((4,)), sem(())
    sems = [
        sem((nq, 2)), sem((nq, 2)), sem((nq,)), sem((nq,)), sem((nq, 3)), sem((nq, 3)), sem((nq, 3)), sem((nq, 3)),
        sem((nq, 4)), sem((nq, 4)), sem((nq,)),
        n3, n3, n3, n3, n4, n4, one, one, n3, n3, n3, n3, n3, n3,
        n4, n4, n3, n3, n3, n3, n3, n3, n4, n4, n3, n3, one, one,
        n3, n3, n3, n3, sem((18,)), sem((6,)),
    ]
    vmem, any_ = pl.BlockSpec(memory_space=pltpu.VMEM), pl.BlockSpec(memory_space=pl.ANY)
    return pl.pallas_call(
        back_kernel,
        out_shape=outs,
        in_specs=[any_] * 20 + [vmem] * 3,
        out_specs=[any_] * len(outs),
        scratch_shapes=scratch + sems,
        compiler_params=pltpu.CompilerParams(
            collective_id=2, has_side_effects=True, vmem_limit_bytes=62 * 1024 * 1024),
        name="back",
    )(*front_outs, tok, cos_t, sin_t)


def finish_kernel(v, qkv, proj, res, parts, terms, gu, dn, g_qkv, g_proj, out, g_router):
    half = HID // 2
    for c in range(2):
        gu[:, c * half : (c + 1) * half] = v[c, :, :half].astype(F32)
        gu[:, HID + c * half : HID + (c + 1) * half] = v[c, :, half : 2 * half].astype(F32)
        dn[:, c * half : (c + 1) * half] = v[c, :, 2 * half :].astype(F32)
    heads = range(qkv.shape[0])
    g_qkv[...] = jnp.concatenate(
        [qkv[h, :, lo:hi].astype(F32) for lo, hi in ((0, 192), (192, 256), (256, 320)) for h in heads], axis=1)
    g_proj[...] = proj[...].astype(F32)

    @pl.when(pl.program_id(0) == 0)
    def _():
        total = res[...]
        for k in range(4):
            total = total + parts[k].astype(F32)
        out[...] = total.astype(BF)
        g_router[...] = terms[8:, :]


def finish(v, qkv, proj, res, parts, terms):
    steps, own, width = 3, proj.shape[0], proj.shape[1]
    row, some = v.shape[1] // steps, own // steps
    once = lambda n: (lambda i: (0,) * n)
    return pl.pallas_call(
        finish_kernel,
        grid=(steps,),
        out_shape=(
            jax.ShapeDtypeStruct((v.shape[1], 2 * HID), F32), jax.ShapeDtypeStruct((v.shape[1], HID), F32),
            jax.ShapeDtypeStruct((own, 2560), F32), jax.ShapeDtypeStruct((own, width), F32),
            jax.ShapeDtypeStruct(res.shape, BF), jax.ShapeDtypeStruct((EXPERTS, own), F32)),
        in_specs=[
            pl.BlockSpec((2, row, v.shape[2]), lambda i: (0, i, 0)),
            pl.BlockSpec((8, some, 320), lambda i: (0, i, 0)), pl.BlockSpec((some, width), lambda i: (i, 0)),
            pl.BlockSpec(res.shape, once(2)), pl.BlockSpec(parts.shape, once(3)),
            pl.BlockSpec(terms.shape, once(2))],
        out_specs=[
            pl.BlockSpec((row, 2 * HID), lambda i: (i, 0)), pl.BlockSpec((row, HID), lambda i: (i, 0)),
            pl.BlockSpec((some, 2560), lambda i: (i, 0)), pl.BlockSpec((some, width), lambda i: (i, 0)),
            pl.BlockSpec(res.shape, once(2)), pl.BlockSpec((EXPERTS, own), once(2))],
        compiler_params=pltpu.CompilerParams(vmem_limit_bytes=62 * 1024 * 1024),
        name="finish",
    )(v, qkv, proj, res, parts, terms)


def expert_grads_general(reps, grps, xs, dys, ggu, hw):
    local, half, width = ggu.shape[0], HID // 2, xs.shape[1]
    own = width // grps
    chips = reps // 2
    piece = own // chips
    same_core = [[2 * i + c for i in range(chips)] for c in range(2)]
    pairs = [[2 * i, 2 * i + 1] for i in range(chips)]
    up = jnp.einsum("td,eth->edh", xs, ggu, preferred_element_type=F32).astype(BF)
    down = jnp.einsum("td,eth->edh", dys, hw, preferred_element_type=F32).astype(BF)
    gw = jnp.concatenate([up, down], axis=2)
    gw = gw.reshape(local, grps, chips, piece, 3 * half).transpose(2, 1, 3, 0, 4)
    gw = gw.reshape(chips * grps * piece, local * 3 * half)
    gw = lax.psum_scatter(gw, "rep", scatter_dimension=0, tiled=True, axis_index_groups=same_core)
    gw = lax.all_to_all(gw.reshape(grps, piece, local, 3 * half), "grp", 0, 0, tiled=True)
    gw = gw.transpose(1, 0, 2, 3).reshape(piece, EXPERTS, 3 * half)
    gw = lax.all_gather(gw, "rep", axis=0, tiled=True, axis_index_groups=same_core)
    gw = lax.all_gather(gw, "rep", axis=0, tiled=False, axis_index_groups=pairs).astype(F32)
    gw = gw.reshape(2, own * EXPERTS, 3, half)
    gw = jnp.moveaxis(gw, 0, 2).reshape(own * EXPERTS, 3 * HID)
    return gw[:, : 2 * HID], gw[:, 2 * HID :]


def shards_general(
    reps,
    grps,
    tokens,
    attn_gain,
    query_key_value_weight,
    attn_proj,
    mlp_gain,
    w_router,
    w_gate_up,
    w_down,
    prefix_len,
    expert_ids,
    priority,
    cotangent,
):
    seq, width = tokens.shape
    own = width // grps
    local_experts = EXPERTS // grps
    heads = KEY_VALUE_HEADS
    groups = None if reps == heads else [list(range(i, i + heads)) for i in range(0, reps, heads)]
    rep, grp = lax.axis_index("rep"), lax.axis_index("grp")
    head = lax.rem(rep, heads)
    qw, hw = QPK * HEAD_WIDTH, HEAD_WIDTH
    q_all = QUERY_HEADS * HEAD_WIDTH

    small = jnp.concatenate([attn_gain[:, None], mlp_gain[:, None], w_router], axis=1)
    small = lax.all_gather(small, "grp", axis=0, tiled=True)
    gain_one, gain_two = small[:, 0].astype(F32)[None, :], small[:, 1].astype(F32)[None, :]
    router = small[:, 2:]
    qkv_cols = jnp.concatenate(
        [
            lax.dynamic_slice_in_dim(query_key_value_weight, head * qw, qw, 1),
            lax.dynamic_slice_in_dim(query_key_value_weight, q_all + head * hw, hw, 1),
            lax.dynamic_slice_in_dim(query_key_value_weight, q_all + heads * hw + head * hw, hw, 1),
        ],
        axis=1,
    )
    qkv_head = lax.all_gather(qkv_cols, "grp", axis=0, tiled=True)
    row = head * qw + jnp.arange(qw)
    mine = (row // own) == grp
    proj_rows = jnp.where(mine[:, None], jnp.take(attn_proj, jnp.where(mine, row - grp * own, 0), axis=0), 0)
    proj_head = lax.psum(proj_rows, "grp")

    core, chip, chips, half = lax.rem(rep, 2), rep // 2, reps // 2, HID // 2
    pairs = [[2 * i, 2 * i + 1] for i in range(chips)]
    same_core = [[2 * i + c for i in range(chips)] for c in range(2)]
    piece = own // chips
    gu_piece = lax.dynamic_slice_in_dim(w_gate_up, chip * piece, piece, 0)
    dn_piece = lax.dynamic_slice_in_dim(w_down, chip * piece, piece, 0)
    both = jnp.concatenate(
        [
            lax.dynamic_slice_in_dim(gu_piece, core * half, half, 2),
            lax.dynamic_slice_in_dim(gu_piece, HID + core * half, half, 2),
            lax.dynamic_slice_in_dim(dn_piece, core * half, half, 2),
        ],
        axis=2,
    )
    both = both.reshape(piece, grps, local_experts, 3 * half).transpose(1, 2, 0, 3)
    both = lax.all_to_all(both, "grp", 0, 0, tiled=True)
    both = lax.all_gather(both, "rep", axis=0, tiled=False, axis_index_groups=same_core)
    both = both.transpose(2, 1, 0, 3, 4).reshape(local_experts, width, 3 * half)
    wgu, wdn = both[:, :, : 2 * half], both[:, :, 2 * half :]

    tokens_f = tokens.astype(F32)
    inverse_one = lax.rsqrt(jnp.mean(tokens_f * tokens_f, axis=1, keepdims=True) + EPS)
    normed_one = tokens_f * inverse_one
    act_one = (normed_one * gain_one).astype(BF)
    act_plane = lax.all_gather(act_one, "rep", axis=0, tiled=True, axis_index_groups=groups)
    prefix_plane = lax.all_gather(prefix_len, "rep", axis=0, tiled=True, axis_index_groups=groups)
    cos, sin = rope_tables(seq)
    projected = dot(act_plane, qkv_head).reshape(heads, seq, QPK + 2, HEAD_WIDTH)
    cos_b, sin_b = cos[None, :, None, :], sin[None, :, None, :]
    turned = rotate(projected[:, :, : QPK + 1], cos_b, sin_b).astype(BF)
    query = turned[:, :, :QPK]
    key = turned[:, :, QPK]
    value = projected[:, :, QPK + 1].astype(BF)
    scale = HEAD_WIDTH ** (-0.5)
    row_pos, col_pos = jnp.arange(seq)[:, None], jnp.arange(seq)[None, :]
    allowed = (col_pos <= row_pos)[None] | (col_pos[None] < prefix_plane[:, None, None])
    scores = jnp.einsum("bsgd,btd->bgst", query, key, preferred_element_type=F32) * scale
    scores = jnp.where(allowed[:, None], scores, -1e30)
    exps = jnp.exp(scores - jnp.max(scores, axis=-1, keepdims=True))
    probs = exps / jnp.sum(exps, axis=-1, keepdims=True)
    probs_low = probs.astype(BF)
    attended = jnp.einsum("bgst,btd->bsgd", probs_low, value, preferred_element_type=F32)
    attended = attended.astype(BF).reshape(heads * seq, qw)
    part = dot(attended, proj_head).astype(BF)
    part = lax.psum_scatter(part, "rep", scatter_dimension=0, tiled=True, axis_index_groups=groups)
    residual = tokens_f + part.astype(F32)
    inverse_two = lax.rsqrt(jnp.mean(residual * residual, axis=1, keepdims=True) + EPS)
    normed_two = residual * inverse_two
    act_two = (normed_two * gain_two).astype(BF)
    gates, kept = routing(expert_ids, priority, dot(act_two, router))

    def column(v):
        v = lax.all_gather(v, "grp", axis=0, tiled=True)
        return lax.all_gather(v, "rep", axis=0, tiled=True, axis_index_groups=pairs)

    def to_owners(v):
        v = lax.psum_scatter(v, "rep", scatter_dimension=0, tiled=True, axis_index_groups=pairs)
        return lax.psum_scatter(v, "grp", scatter_dimension=0, tiled=True).astype(F32)

    dy_all = column(cotangent)
    x_all = column(act_two)
    weight = column(jnp.where(kept, gates, 0.0))
    weight = lax.dynamic_slice_in_dim(weight, grp * local_experts, local_experts, 1).T[:, :, None]
    gate_up = jnp.einsum("td,edh->eth", x_all, wgu, preferred_element_type=F32)
    g, u = gate_up[..., :half], gate_up[..., half:]
    sig = jax.nn.sigmoid(g)
    silu = g * sig
    hidden = silu * u
    hidden_w = (hidden * weight).astype(BF)
    back = jnp.einsum("td,edh->eth", dy_all, wdn, preferred_element_type=F32)
    grad_gate_part = jnp.sum(back * hidden, axis=2)
    grad_hidden = back * weight
    ggu = jnp.concatenate(
        [grad_hidden * u * sig * (1.0 + g * (1.0 - sig)), grad_hidden * silu], axis=2
    ).astype(BF)
    out_part = jnp.einsum("eth,edh->td", hidden_w, wdn, preferred_element_type=F32).astype(BF)
    gact_part = jnp.einsum("eth,edh->td", ggu, wgu, preferred_element_type=F32).astype(BF)
    gact = to_owners(gact_part)
    grad_gates = lax.psum_scatter(
        grad_gate_part.T, "rep", scatter_dimension=0, tiled=True, axis_index_groups=pairs
    )
    grad_gates = lax.all_to_all(grad_gates, "grp", 0, 1, tiled=True)
    grad_gates = jnp.where(kept, grad_gates, 0.0)
    out = to_owners(out_part)
    output = (residual + out).astype(BF)
    grad_gu, grad_dn = expert_grads_general(reps, grps, x_all, dy_all, ggu, hidden_w)
    grad_gu = grad_gu.reshape(own, EXPERTS, 2 * HID)
    grad_dn = grad_dn.reshape(own, EXPERTS, HID)

    grad_logits = (gates * (grad_gates - jnp.sum(gates * grad_gates, axis=1, keepdims=True))).astype(BF)
    gact = gact + dot(grad_logits, router.T)
    router_term = dot(act_two.T, grad_logits)
    gain_two_term = jnp.sum(gact * normed_two, axis=0)
    scaled = gact * gain_two
    dy = cotangent.astype(F32)
    grad_residual = dy + inverse_two * (
        scaled - normed_two * jnp.mean(scaled * normed_two, axis=1, keepdims=True)
    )
    gres_low = grad_residual.astype(BF)

    gres_plane = lax.all_gather(gres_low, "rep", axis=0, tiled=True, axis_index_groups=groups)
    proj_term = dot(attended.T, gres_plane)
    grad_att = dot(gres_plane, proj_head.T).astype(BF).reshape(heads, seq, QPK, HEAD_WIDTH)
    grad_value = jnp.einsum("bgst,bsgd->btd", probs_low, grad_att, preferred_element_type=F32)
    grad_probs = jnp.einsum("bsgd,btd->bgst", grad_att, value, preferred_element_type=F32)
    grad_scores = (
        probs * (grad_probs - jnp.sum(probs * grad_probs, axis=-1, keepdims=True))
    ).astype(BF)
    grad_query = jnp.einsum("bgst,btd->bsgd", grad_scores, key, preferred_element_type=F32) * scale
    grad_key = jnp.einsum("bgst,bsgd->btd", grad_scores, query, preferred_element_type=F32) * scale
    turned_back = rotate(
        jnp.concatenate([grad_query, grad_key[:, :, None]], axis=2), cos_b, -sin_b
    )
    gproj = jnp.concatenate([turned_back, grad_value[:, :, None]], axis=2).astype(BF)
    gproj = gproj.reshape(heads * seq, qw + 2 * hw)
    qkv_term = dot(act_plane.T, gproj)
    gact_one = dot(gproj, qkv_head.T).astype(BF)
    gact_one = lax.psum_scatter(
        gact_one, "rep", scatter_dimension=0, tiled=True, axis_index_groups=groups
    ).astype(F32)
    gain_one_term = jnp.sum(gact_one * normed_one, axis=0)
    scaled_one = gact_one * gain_one
    grad_tokens = grad_residual + inverse_one * (
        scaled_one - normed_one * jnp.mean(scaled_one * normed_one, axis=1, keepdims=True)
    )

    qkv_own = lax.psum_scatter(qkv_term.astype(BF), "grp", scatter_dimension=0, tiled=True)
    proj_sum = lax.psum(proj_term.astype(BF), "grp")
    if groups is not None:
        across = [[i + heads * j for j in range(reps // heads)] for i in range(heads)]
        qkv_own = lax.psum(qkv_own, "rep", axis_index_groups=across)
        proj_sum = lax.psum(proj_sum, "rep", axis_index_groups=across)
    qkv_own = lax.all_gather(qkv_own, "rep", axis=0, tiled=False, axis_index_groups=groups)
    qkv_own = qkv_own.astype(F32)
    grad_qkv = jnp.concatenate(
        [
            qkv_own[:, :, lo:hi].transpose(1, 0, 2).reshape(own, -1)
            for lo, hi in ((0, qw), (qw, qw + hw), (qw + hw, qw + 2 * hw))
        ],
        axis=1,
    )
    proj_all = lax.all_gather(proj_sum, "rep", axis=0, tiled=True, axis_index_groups=groups)
    grad_proj = lax.dynamic_slice_in_dim(proj_all, grp * own, own, 0).astype(F32)
    terms = jnp.concatenate([gain_one_term[:, None], gain_two_term[:, None], router_term], axis=1)
    terms = lax.psum(lax.psum_scatter(terms, "grp", scatter_dimension=0, tiled=True), "rep")
    return (
        output,
        grad_tokens,
        terms[:, 0],
        grad_qkv,
        grad_proj,
        terms[:, 1],
        terms[:, 2:],
        grad_gu,
        grad_dn,
    )


def shards(
    tokens,
    attn_gain,
    query_key_value_weight,
    attn_proj,
    mlp_gain,
    w_router,
    w_gate_up,
    w_down,
    prefix_len,
    expert_ids,
    priority,
    cotangent,
):
    own, width = attn_gain.shape[0], tokens.shape[1]
    small = jnp.concatenate(
        [jnp.concatenate([attn_gain, mlp_gain, jnp.zeros((14 * own,), BF)]).reshape(16, own), w_router.T], axis=0
    )
    half = HEAD_WIDTH // 2
    inverse_freq = np.float32(10000.0) ** (-np.arange(half, dtype=np.float32) * np.float32(2.0 / HEAD_WIDTH))
    angles = np.arange(tokens.shape[0], dtype=np.float32)[:, None] * inverse_freq[None, :]
    cos_t = jnp.asarray(np.tile(np.cos(angles), (1, 4)), F32)
    sin = np.sin(angles)
    sin_t = jnp.asarray(np.tile(np.concatenate([-sin, sin], axis=1), (1, 2)), F32)
    parts = front(
        tokens, cotangent, w_gate_up, w_down, query_key_value_weight, attn_proj, small, expert_ids.T,
        priority.reshape(8, 128), prefix_len, cos_t, sin_t)
    wide, grad_tokens, qkv_own, proj_own, terms, out_parts = back(parts, tokens, cos_t, sin_t)
    grad_gu, grad_dn, grad_qkv, grad_proj, output, grad_router = finish(
        wide, qkv_own, proj_own.reshape(own, width), parts[13], out_parts, terms)
    return (
        output,
        grad_tokens,
        terms[0],
        grad_qkv,
        grad_proj,
        terms[1],
        grad_router.T,
        grad_gu.reshape(own, EXPERTS, 2 * HID),
        grad_dn.reshape(own, EXPERTS, HID),
    )


def solution(mesh):
    tok, par = ("rep", "grp"), "grp"
    in_specs = (
        P(tok, None),
        P(par),
        P(par, None),
        P(par, None),
        P(par),
        P(par, None),
        P(par, None, None),
        P(par, None, None),
        P(tok),
        P(tok, None),
        P(tok, None),
        P(tok, None),
    )
    out_specs = (
        P(tok, None),
        P(tok, None),
        P(par),
        P(par, None),
        P(par, None),
        P(par),
        P(par, None),
        P(par, None, None),
        P(par, None, None),
    )
    reps, grps = mesh.shape["rep"], mesh.shape["grp"]

    def body(*args):
        if (reps, grps) == (8, 4):
            return shards(*args)
        return shards_general(reps, grps, *args)

    return jax.shard_map(body, mesh=mesh, in_specs=in_specs, out_specs=out_specs, check_vma=False)
```
